32 devices in a mesh: batch: 4 (over x, core), blk: 8 (over z, y).
Axes of the slice: x: 2, y: 2, z: 4, core: 2. Of those that a mesh axis runs over, the one named last changes fastest.
Arguments:
- tokens: bfloat16 [4, 1024, 1024], P('batch', 'blk'), may hold values from -6 to 6
- lengths: int32 [4], P('batch'), may hold values from 897 to 1024, as said below
- w_qkv: bfloat16 [1024, 3072], replicated, may hold values from -0.1875 to 0.1875
- qv_bias: float32 [2, 1024], replicated, may hold values from -1.5 to 1.5
- w_attn: bfloat16 [1024, 1024], replicated, may hold values from -3 to 3
- out_bias: float32 [2, 1024], replicated, may hold values from -1.5 to 1.5
- w_in: bfloat16 [1024, 4096], replicated, may hold values from -0.1875 to 0.1875
- in_bias: float32 [4096], replicated, may hold values from -1.5 to 1.5
- w_back: bfloat16 [4096, 1024], replicated, may hold values from -0.09375 to 0.09375
- norm_gain: float32 [2, 1024], replicated, may hold values from 0.1 to 1.9
- norm_shift: float32 [2, 1024], replicated, may hold values from -1.5 to 1.5
- cotangent: bfloat16 [4, 1024, 1024], P('batch', 'blk'), may hold values from -6 to 6
Outputs:
- mixed: bfloat16 [4, 1024, 1024], P('batch', 'blk')
- grad_tokens: bfloat16 [4, 1024, 1024], P('batch', 'blk')
- grad_qkv: float32 [1024, 3072], P('blk')
- grad_qv_bias: float32 [2, 1024], P(None, 'blk')
- grad_attn: float32 [1024, 1024], P('blk')
- grad_out_bias: float32 [2, 1024], P(None, 'blk')
- grad_in: float32 [1024, 4096], P('blk')
- grad_in_bias: float32 [4096], P('blk')
- grad_back: float32 [4096, 1024], P(None, 'blk')
- grad_gain: float32 [2, 1024], P(None, 'blk')
- grad_shift: float32 [2, 1024], P(None, 'blk')
The draws below stay inside these ranges and needn't reach their ends.
Inputs may be any that keep to these rules, and one draw needn't show every extreme that they name: `lengths`: one sequence, drawn from the seed, has the full length 1024; every sequence has valid positions on the last device of its row.
All inputs are finite; a program needn't handle non-finite values.
Results may differ from the reference program's by a relative error of at most 0.025.
Values may be sent and summed in bfloat16 or wider, within the bound.
A program may use at most 448 MiB of HBM per device.

```python
import jax
import jax.numpy as jnp
from jax import lax

D = 1024
HEADS = 16
FF = 4096
CH = 128
LEN = 1024
SEQS = 4
TOKS = 1024
N_BATCH = 4


def draw_lengths(key, part):
    key = jax.random.fold_in(key, 7)
    base_key, full_key = jax.random.split(key)
    drawn = jax.random.randint(base_key, (SEQS,), LEN - CH + 1, LEN + 1)
    chosen = jax.random.randint(full_key, (1,), 0, SEQS)
    places = lax.broadcasted_iota(jnp.int32, (SEQS,), 0)
    return jnp.where(places == chosen, LEN, drawn).astype(jnp.int32)


def spiked(result, own_key, source, target, blocks, factor):
    owner, partner = [(jnp.arange(result.shape[axis_at]) // (result.shape[axis_at] // blocks)).reshape([-1 if axis == axis_at else 1 for axis in range(result.ndim)]) for axis_at in (source, target)]
    chosen = jax.random.permutation(own_key, blocks)[partner]
    strong = (owner == chosen) | (owner == (partner + blocks // 2) % blocks)
    return jnp.where(strong, factor * result, result)


def block_levels(stream_key, shape, cuts, least, high):
    level = 1.0
    for dim, blocks in cuts:
        heights = jax.random.uniform(jax.random.fold_in(jax.random.fold_in(stream_key, 6), dim), (blocks,), jnp.float32, least / len(cuts), high / len(cuts))
        level = level * jnp.repeat(jnp.exp(heights), shape[dim] // blocks).reshape((-1,) + (1,) * (len(shape) - 1 - dim))
    return level


def normal_values(own_key, extent, spread, limit, cuts=(), kind=jnp.bfloat16):
    entries = jax.random.normal(own_key, extent, jnp.float32) * spread
    if len(cuts) > 0:
        entries = block_levels(own_key, extent, cuts, -0.22, 0.18) * entries
    return jnp.clip(entries, min=-limit, max=limit).astype(kind)


def bell_draw_with(key, extent, deviation, reach, cuts, heavy, dtype=jnp.bfloat16):
    result = deviation * jax.random.normal(key, extent, jnp.float32)
    if cuts:
        result = result * block_levels(key, extent, cuts, -0.22, 0.18)
    return jnp.clip(spiked(result, jax.random.fold_in(key, 3), *heavy), -reach, reach).astype(dtype)


def setup_inputs(seed: int = 0) -> dict:
    key_list = jax.random.split(jax.random.key(seed), 13)
    return {
        "tokens": bell_draw_with(key_list[0], (N_BATCH, TOKS, D), 1.0, 6.0, ((0, 4), (1, 8)), (1, 2, 8, 2.0)),
        "lengths": draw_lengths(jax.random.fold_in(key_list[12], 71), 0),
        "w_qkv": normal_values(key_list[2], (D, 3 * D), D ** -0.5, 0.1875),
        "qv_bias": normal_values(key_list[3], (2, D), 0.3, 1.5, (), jnp.float32),
        "w_attn": normal_values(key_list[4], (D, D), (max(4 * D // LEN, 1)) ** -0.5, 3.0),
        "out_bias": normal_values(key_list[5], (2, D), 0.3, 1.5, (), jnp.float32),
        "w_in": normal_values(key_list[6], (D, FF), D ** -0.5, 0.1875),
        "in_bias": normal_values(key_list[7], (FF,), 0.3, 1.5, (), jnp.float32),
        "w_back": normal_values(key_list[8], (FF, D), FF ** -0.5, 0.09375),
        "norm_gain": jnp.clip(1.0 + 0.18 * jax.random.normal(key_list[9], (2, D), jnp.float32), 0.1, 1.9),
        "norm_shift": normal_values(key_list[10], (2, D), 0.3, 1.5, (), jnp.float32),
        "cotangent": bell_draw_with(key_list[11], (N_BATCH, TOKS, D), 1.0, 6.0, ((0, 4), (1, 8)), (1, 2, 8, 2.0)),
    }


@jax.custom_vjp
def low(v):
    return lax.optimization_barrier(v.astype(jnp.bfloat16)).astype(jnp.float32)

@jax.custom_vjp
def low_back(v):
    return v

def low_keep(v):
    return (low(v), None)

def low_pass(kept, grad):
    return (grad,)

def back_keep(v):
    return (v, None)

def back_low(kept, grad):
    return (low(grad),)
low.defvjp(low_keep, low_pass)
low_back.defvjp(back_keep, back_low)
eps = 1e-12
highest = lax.Precision.HIGHEST

def round_both(values):
    return low_back(low(values))

def matmul(left, right):
    return jnp.dot(left, right, precision=highest, preferred_element_type=jnp.float32)

def normalize(values, gain, shift):
    centered = values - lax.optimization_barrier(jnp.mean(values, axis=-1, keepdims=True))
    variance = lax.optimization_barrier(jnp.mean(centered * centered, axis=-1, keepdims=True))
    return centered * lax.rsqrt(variance + eps) * gain + shift

def attend_one(operands):
    queries, key_rows, values, length = operands
    seq_len, model_width = queries.shape
    head_size = model_width // HEADS

    def heads_of(matrix):
        return matrix.reshape(seq_len, HEADS, head_size).transpose(1, 0, 2)
    scores = jnp.einsum('hqd,hkd->hqk', heads_of(queries), heads_of(key_rows), precision=highest) * head_size ** (-0.5)
    scores = low_back(scores)
    key_valid = jnp.arange(seq_len) < length
    masked = jnp.where(key_valid, scores, -1e+30)
    row_max = lax.optimization_barrier(jnp.max(masked, axis=-1, keepdims=True))
    exp_scores = jnp.where(key_valid, jnp.exp(masked - row_max), 0.0)
    prob_low = low(exp_scores / lax.optimization_barrier(jnp.sum(exp_scores, axis=-1, keepdims=True)))
    output = jnp.einsum('hqk,hkd->hqd', prob_low, heads_of(values), precision=highest)
    return output.transpose(1, 0, 2).reshape(seq_len, model_width)

def encoder_layer(hidden, params, lengths):
    w_qkv, qv_bias, w_attn, out_bias, w_in, in_bias, w_back, norm_gain, norm_shift = params
    model_width = hidden.shape[1]
    seq_count = lengths.shape[0]
    hidden_low = low(hidden)
    bias_row = jnp.concatenate([qv_bias[0], jnp.zeros_like(qv_bias[0]), qv_bias[1]])
    projected = round_both(matmul(hidden_low, w_qkv) + bias_row)
    queries = projected[:, :model_width].reshape(seq_count, -1, model_width)
    key_rows = projected[:, model_width:2 * model_width].reshape(seq_count, -1, model_width)
    values = projected[:, 2 * model_width:].reshape(seq_count, -1, model_width)
    attended = lax.map(jax.checkpoint(attend_one), (queries, key_rows, values, lengths))
    attended = round_both(attended.reshape(-1, model_width))
    branch = low_back(matmul(attended, w_attn) + out_bias[0])
    first_norm = normalize(hidden + branch, norm_gain[0], norm_shift[0])
    inner_pre = low_back(matmul(low(first_norm), w_in) + in_bias)
    activated = low(jax.nn.gelu(inner_pre, approximate=False))
    branch_two = low_back(matmul(activated, w_back) + out_bias[1])
    return normalize(first_norm + branch_two, norm_gain[1], norm_shift[1])

def reference(tokens, lengths, w_qkv, qv_bias, w_attn, out_bias, w_in, in_bias, w_back, norm_gain, norm_shift, cotangent):
    model_width = tokens.shape[2]
    flat_tokens = tokens.astype(jnp.float32).reshape(-1, model_width)
    weights = tuple((weight_arg.astype(jnp.float32) for weight_arg in (w_qkv, qv_bias, w_attn, out_bias, w_in, in_bias, w_back, norm_gain, norm_shift)))

    def network(values, params):
        return encoder_layer(encoder_layer(values, params, lengths), params, lengths)
    output, pull_back = jax.vjp(network, flat_tokens, weights)
    grad_flat, grad_list = pull_back(cotangent.astype(jnp.float32).reshape(-1, model_width))
    return (output.astype(jnp.bfloat16).reshape(tokens.shape), grad_flat.astype(jnp.bfloat16).reshape(tokens.shape), grad_list[0], grad_list[1], grad_list[2], grad_list[3], grad_list[4], grad_list[5], grad_list[6], grad_list[7], grad_list[8])
```

```python
import functools

import jax
import jax.numpy as jnp
from jax import lax
from jax.experimental import pallas as pl
from jax.experimental.pallas import tpu as pltpu
from jax.sharding import PartitionSpec as P

HEADS = 16


eps = 1e-12


def from_partner(x, axis, distance):
    return lax.ppermute(x, axis, [(i, i ^ 1 << distance) for i in range(lax.axis_size(axis))])


def normalize(values, gain, shift):
    centered = values - jnp.mean(values, axis=-1, keepdims=True)
    variance = jnp.mean(centered * centered, axis=-1, keepdims=True)
    return centered * lax.rsqrt(variance + eps) * gain + shift


def gelu_exact(values):
    return jax.nn.gelu(values, approximate=False)


def head_split(matrix, head_count):
    row_count, model_width = matrix.shape
    return matrix.reshape(row_count, head_count // 4, 4, model_width // head_count).transpose(
        1, 2, 0, 3
    )


def head_merge(stacked):
    group_count, group_size, row_count, head_size = stacked.shape
    return stacked.transpose(2, 0, 1, 3).reshape(row_count, group_count * group_size * head_size)


def core_forward(query_part, key_part, value_part, key_valid, scale):
    scores = (
        jnp.einsum("hqd,hkd->hqk", query_part, key_part, preferred_element_type=jnp.float32) * scale
    )
    masked = jnp.where(key_valid, scores, -1e30)
    row_max = jnp.max(masked, axis=-1, keepdims=True)
    exp_scores = jnp.where(key_valid, jnp.exp(masked - row_max), 0.0)
    row_total = jnp.sum(exp_scores, axis=-1, keepdims=True)
    prob_low = (exp_scores / row_total).astype(jnp.bfloat16)
    output = jnp.einsum("hqk,hkd->hqd", prob_low, value_part, preferred_element_type=jnp.float32)
    return (output, (row_max + jnp.log(row_total))[..., 0])


def core_backward(query_part, key_part, value_part, grad_part, log_part, key_valid, scale):
    scores = (
        jnp.einsum("hqd,hkd->hqk", query_part, key_part, preferred_element_type=jnp.float32) * scale
    )
    probs = jnp.where(key_valid, jnp.exp(scores - log_part[..., None]), 0.0)
    grad_probs = jnp.einsum(
        "hqd,hkd->hqk", grad_part, value_part, preferred_element_type=jnp.float32
    )
    inner_sum = jnp.sum(probs * grad_probs, axis=-1, keepdims=True)
    grad_scores = (probs * (grad_probs - inner_sum)).astype(jnp.bfloat16)
    grad_query = (
        jnp.einsum("hqk,hkd->hqd", grad_scores, key_part, preferred_element_type=jnp.float32)
        * scale
    )
    grad_key = (
        jnp.einsum("hqk,hqd->hkd", grad_scores, query_part, preferred_element_type=jnp.float32)
        * scale
    )
    grad_value = jnp.einsum(
        "hqk,hqd->hkd", probs.astype(jnp.bfloat16), grad_part, preferred_element_type=jnp.float32
    )
    return (grad_query, grad_key, grad_value)


def gather_group(kv_pair, position, bit_count):
    buffer_rows = kv_pair
    for step_bit in range(bit_count):
        received = from_partner(buffer_rows, "blk", step_bit)
        high_side = position >> step_bit & 1 == 1
        buffer_rows = jnp.where(
            high_side,
            jnp.concatenate([received, buffer_rows], 0),
            jnp.concatenate([buffer_rows, received], 0),
        )
    return buffer_rows


def spread_group(partials, position, bit_count):
    for step_bit in reversed(range(bit_count)):
        half_rows = partials.shape[0] // 2
        high_side = position >> step_bit & 1 == 1
        lower_part = partials[:half_rows]
        upper_part = partials[half_rows:]
        kept_part = jnp.where(high_side, upper_part, lower_part)
        sent_part = jnp.where(high_side, lower_part, upper_part)
        partials = kept_part + from_partner(sent_part.astype(jnp.bfloat16), "blk", step_bit).astype(
            sent_part.dtype
        )
    return partials


def attend_forward(queries, gathered, key_valid, head_count):
    model_width = queries.shape[1]
    scale = (model_width // head_count) ** (-0.5)
    query_heads = head_split(queries, head_count)
    key_heads = head_split(gathered[:, :model_width], head_count)
    value_heads = head_split(gathered[:, model_width:], head_count)

    def one_group(operands):
        query_part, key_part, value_part = operands
        return core_forward(query_part, key_part, value_part, key_valid, scale)

    outputs, log_sums = lax.map(one_group, (query_heads, key_heads, value_heads))
    return (head_merge(outputs), log_sums)


def attend_backward(queries, gathered, key_valid, log_sums, grad_attended, head_count):
    model_width = queries.shape[1]
    scale = (model_width // head_count) ** (-0.5)
    query_heads = head_split(queries, head_count)
    key_heads = head_split(gathered[:, :model_width], head_count)
    value_heads = head_split(gathered[:, model_width:], head_count)
    grad_heads = head_split(grad_attended, head_count)

    def one_group(operands):
        query_part, key_part, value_part, grad_part, log_part = operands
        return core_backward(
            query_part, key_part, value_part, grad_part, log_part, key_valid, scale
        )

    grad_query, grad_key, grad_value = lax.map(
        one_group, (query_heads, key_heads, value_heads, grad_heads, log_sums)
    )
    return (
        head_merge(grad_query),
        jnp.concatenate([head_merge(grad_key), head_merge(grad_value)], 1),
    )


def layer_forward(hidden, params, key_valid, position, bit_count, head_count):
    w_qkv, qv_bias, w_attn, out_bias, w_in, in_bias, w_back, norm_gain, norm_shift = params
    model_width = hidden.shape[1]
    hidden_low = hidden.astype(jnp.bfloat16)
    bias_row = jnp.concatenate([qv_bias[0], jnp.zeros_like(qv_bias[0]), qv_bias[1]])
    projected = (jnp.dot(hidden_low, w_qkv, preferred_element_type=jnp.float32) + bias_row).astype(
        jnp.bfloat16
    )
    gathered = gather_group(projected[:, model_width:], position, bit_count)
    attended, log_sums = attend_forward(projected[:, :model_width], gathered, key_valid, head_count)
    attended_low = attended.astype(jnp.bfloat16)
    first_sum = (
        hidden + jnp.dot(attended_low, w_attn, preferred_element_type=jnp.float32) + out_bias[0]
    )
    first_norm = normalize(first_sum, norm_gain[0], norm_shift[0])
    first_low = first_norm.astype(jnp.bfloat16)
    inner_pre = jnp.dot(first_low, w_in, preferred_element_type=jnp.float32) + in_bias
    activated = gelu_exact(inner_pre).astype(jnp.bfloat16)
    second_sum = (
        first_norm + jnp.dot(activated, w_back, preferred_element_type=jnp.float32) + out_bias[1]
    )
    output = normalize(second_sum, norm_gain[1], norm_shift[1])
    saved_state = (
        hidden_low,
        projected,
        gathered,
        log_sums,
        attended_low,
        first_sum,
        first_low,
        inner_pre,
        activated,
        second_sum,
    )
    return (output, saved_state)


def layer_backward(grad_output, saved_state, params, key_valid, position, bit_count, head_count):
    w_qkv, qv_bias, w_attn, out_bias, w_in, in_bias, w_back, norm_gain, norm_shift = params
    (
        hidden_low,
        projected,
        gathered,
        log_sums,
        attended_low,
        first_sum,
        first_low,
        inner_pre,
        activated,
        second_sum,
    ) = saved_state
    model_width = hidden_low.shape[1]
    unused_two, pull_two = jax.vjp(normalize, second_sum, norm_gain[1], norm_shift[1])
    grad_second, gain_two, shift_two = pull_two(grad_output)
    grad_branch_two = grad_second.astype(jnp.bfloat16)
    back_grad = jnp.einsum(
        "ra,rb->ab", activated, grad_branch_two, preferred_element_type=jnp.float32
    )
    bias_two = jnp.sum(grad_branch_two.astype(jnp.float32), axis=0)
    grad_act = jnp.dot(grad_branch_two, w_back.T, preferred_element_type=jnp.float32)
    unused_gelu, pull_gelu = jax.vjp(gelu_exact, inner_pre)
    grad_inner = pull_gelu(grad_act)[0].astype(jnp.bfloat16)
    in_grad = jnp.einsum("ra,rb->ab", first_low, grad_inner, preferred_element_type=jnp.float32)
    in_bias_grad = jnp.sum(grad_inner.astype(jnp.float32), axis=0)
    grad_first_norm = grad_second + jnp.dot(grad_inner, w_in.T, preferred_element_type=jnp.float32)
    unused_one, pull_one = jax.vjp(normalize, first_sum, norm_gain[0], norm_shift[0])
    grad_first, gain_one, shift_one = pull_one(grad_first_norm)
    grad_branch = grad_first.astype(jnp.bfloat16)
    attn_grad = jnp.einsum(
        "ra,rb->ab", attended_low, grad_branch, preferred_element_type=jnp.float32
    )
    bias_one = jnp.sum(grad_branch.astype(jnp.float32), axis=0)
    grad_attended = jnp.dot(grad_branch, w_attn.T, preferred_element_type=jnp.float32).astype(
        jnp.bfloat16
    )
    grad_query, grad_pairs = attend_backward(
        projected[:, :model_width], gathered, key_valid, log_sums, grad_attended, head_count
    )
    own_pairs = spread_group(grad_pairs, position, bit_count)
    grad_proj = jnp.concatenate([grad_query, own_pairs], 1).astype(jnp.bfloat16)
    qkv_grad = jnp.einsum("ra,rb->ab", hidden_low, grad_proj, preferred_element_type=jnp.float32)
    column_sums = jnp.sum(grad_proj.astype(jnp.float32), axis=0)
    qv_grad = jnp.stack([column_sums[:model_width], column_sums[2 * model_width :]])
    grad_hidden = grad_first + jnp.dot(grad_proj, w_qkv.T, preferred_element_type=jnp.float32)
    grad_list = (
        qkv_grad,
        qv_grad,
        attn_grad,
        jnp.stack([bias_one, bias_two]),
        in_grad,
        in_bias_grad,
        back_grad,
        jnp.stack([gain_one, gain_two]),
        jnp.stack([shift_one, shift_two]),
    )
    return (grad_hidden, grad_list)


def scatter_once(grad_list):
    (
        qkv_grad,
        qv_grad,
        attn_grad,
        bias_grad,
        in_grad,
        in_bias_grad,
        back_grad,
        gain_grad,
        shift_grad,
    ) = grad_list
    return (
        lax.psum_scatter(qkv_grad, "blk", scatter_dimension=0, tiled=True),
        lax.psum_scatter(qv_grad, "blk", scatter_dimension=1, tiled=True),
        lax.psum_scatter(attn_grad, "blk", scatter_dimension=0, tiled=True),
        lax.psum_scatter(bias_grad, "blk", scatter_dimension=1, tiled=True),
        lax.psum_scatter(in_grad, "blk", scatter_dimension=0, tiled=True),
        lax.psum_scatter(in_bias_grad, "blk", scatter_dimension=0, tiled=True),
        lax.psum_scatter(back_grad, "blk", scatter_dimension=1, tiled=True),
        lax.psum_scatter(gain_grad, "blk", scatter_dimension=1, tiled=True),
        lax.psum_scatter(shift_grad, "blk", scatter_dimension=1, tiled=True),
    )


def body(
    tokens,
    lengths,
    w_qkv,
    qv_bias,
    w_attn,
    out_bias,
    w_in,
    in_bias,
    w_back,
    norm_gain,
    norm_shift,
    cotangent,
):
    row_count = tokens.shape[1]
    head_count = HEADS
    cycle_size = lax.axis_size("blk")
    bit_count = cycle_size.bit_length() - 1
    position = lax.axis_index("blk")
    length = lengths[0]
    key_valid = jnp.arange(cycle_size * row_count) < length
    params = (w_qkv, qv_bias, w_attn, out_bias, w_in, in_bias, w_back, norm_gain, norm_shift)
    out_one, saved_one = layer_forward(
        tokens[0].astype(jnp.float32), params, key_valid, position, bit_count, head_count
    )
    out_two, saved_two = layer_forward(out_one, params, key_valid, position, bit_count, head_count)
    grad_hidden, grads_two = layer_backward(
        cotangent[0].astype(jnp.float32),
        saved_two,
        params,
        key_valid,
        position,
        bit_count,
        head_count,
    )
    grad_hidden, grads_one = layer_backward(
        grad_hidden, saved_one, params, key_valid, position, bit_count, head_count
    )
    shards = scatter_once(jax.tree.map(jnp.add, grads_two, grads_one))
    (
        qkv_part,
        qv_part,
        attn_part,
        bias_part,
        in_part,
        in_bias_part,
        back_part,
        gain_part,
        shift_part,
    ) = shards
    totals = (
        lax.psum(qkv_part.astype(jnp.bfloat16), "batch").astype(jnp.float32),
        lax.psum(qv_part.astype(jnp.bfloat16), "batch").astype(jnp.float32),
        lax.psum(attn_part.astype(jnp.bfloat16), "batch").astype(jnp.float32),
        lax.psum(bias_part.astype(jnp.bfloat16), "batch").astype(jnp.float32),
        lax.psum(in_part.astype(jnp.bfloat16), "batch").astype(jnp.float32),
        lax.psum(in_bias_part.astype(jnp.bfloat16), "batch").astype(jnp.float32),
        lax.psum(back_part.astype(jnp.bfloat16), "batch").astype(jnp.float32),
        lax.psum(gain_part.astype(jnp.bfloat16), "batch").astype(jnp.float32),
        lax.psum(shift_part.astype(jnp.bfloat16), "batch").astype(jnp.float32),
    )
    return (
        out_two.astype(jnp.bfloat16)[None],
        grad_hidden.astype(jnp.bfloat16)[None],
        totals[0],
        totals[1],
        totals[2],
        totals[3],
        totals[4],
        totals[5],
        totals[6],
        totals[7],
        totals[8],
    )


MESH = pl.DeviceIdType.MESH
f32 = jnp.float32
bf16 = jnp.bfloat16


def member(j):
    return {"blk": j}


def place():
    return lax.axis_index("blk")


def exchange_kernel(group, columns, spread, src, dst, send_sem, recv_sem, own_sem):
    me = place()
    rows = 128
    groups = columns // 128
    barrier = pltpu.get_barrier_semaphore()
    for step in range(1, group):
        pl.semaphore_signal(
            barrier, inc=1, device_id=member(lax.rem(me + step, group)), device_id_type=MESH
        )
    pl.semaphore_wait(barrier, group - 1)

    def views(target, source):
        for part in range(groups):
            wide_t = pl.ds(pl.multiple_of(part * 128 * group + target * 128, 128), 128)
            wide_s = pl.ds(pl.multiple_of(part * 128 * group + source * 128, 128), 128)
            narrow = pl.ds(part * 128, 128)
            row_s = pl.ds(pl.multiple_of(source * rows, rows), rows)
            row_t = pl.ds(pl.multiple_of(target * rows, rows), rows)
            if spread:
                yield src.at[:, wide_t], dst.at[row_s, narrow]
            else:
                yield src.at[row_t, narrow], dst.at[:, wide_s]

    copies = []
    for step in range(1, group):
        target = lax.rem(me + step, group)
        for part, (here, there) in enumerate(views(target, me)):
            copy = pltpu.make_async_remote_copy(
                src_ref=here,
                dst_ref=there,
                send_sem=send_sem.at[step - 1, part],
                recv_sem=recv_sem.at[step - 1, part],
                device_id=member(target),
                device_id_type=MESH,
            )
            copy.start()
            copies.append(copy)
    for part, (here, there) in enumerate(views(me, me)):
        copy = pltpu.make_async_copy(here, there, own_sem.at[part])
        copy.start()
        copies.append(copy)
    for copy in copies:
        copy.wait()


def exchange(x, group, spread, ident):
    if spread:
        groups = x.shape[1] // (128 * group)
        out = (128 * group, groups * 128)
    else:
        groups = x.shape[1] // 128
        out = (128, groups * 128 * group)
    return pl.pallas_call(
        functools.partial(exchange_kernel, group, groups * 128, spread),
        out_shape=jax.ShapeDtypeStruct(out, x.dtype),
        in_specs=[pl.BlockSpec(memory_space=pl.ANY)],
        out_specs=pl.BlockSpec(memory_space=pl.ANY),
        scratch_shapes=[
            pltpu.SemaphoreType.DMA((group - 1, groups)),
            pltpu.SemaphoreType.DMA((group - 1, groups)),
            pltpu.SemaphoreType.DMA((groups,)),
        ],
        compiler_params=pltpu.CompilerParams(collective_id=ident, has_side_effects=True),
    )(x)


def dot_t(a, b):
    return lax.dot_general(a, b, (((1,), (1,)), ((), ())), preferred_element_type=f32)


def dot_0(a, b):
    return lax.dot_general(a, b, (((0,), (0,)), ((), ())), preferred_element_type=f32)


def attend_kernel(len_ref, qkv_ref, o_ref, lse_ref):
    count = qkv_ref.shape[0]
    limit = len_ref[0]
    keys = qkv_ref[:, 128:256]
    values = qkv_ref[:, 256:384]
    low_half = lax.broadcasted_iota(jnp.int32, (1, 128), 1) < 64
    valid = lax.broadcasted_iota(jnp.int32, (1, count), 1) < limit
    step = 256
    for start in range(0, count, step):
        rows = pl.ds(start, step)
        queries = qkv_ref[rows, 0:128]
        outs, lses = [], []
        for half in range(2):
            mine = low_half if half == 0 else jnp.logical_not(low_half)
            part = jnp.where(mine, queries, jnp.zeros_like(queries)) * jnp.asarray(0.125, bf16)
            scores = jnp.where(valid, dot_t(part, keys), -1e30)
            top = jnp.max(scores, axis=1, keepdims=True)
            expd = jnp.exp(scores - top)
            total = jnp.sum(expd, axis=1, keepdims=True)
            probs = (expd * (1.0 / total)).astype(bf16)
            outs.append(jnp.dot(probs, values, preferred_element_type=f32))
            lses.append(top + jnp.log(total))
        o_ref[rows, :] = jnp.where(low_half, outs[0], outs[1]).astype(bf16)
        lse_ref[rows, :] = jnp.where(low_half, lses[0], lses[1])


def attend(length, qkv):
    count = qkv.shape[0]
    return pl.pallas_call(
        attend_kernel,
        out_shape=(
            jax.ShapeDtypeStruct((count, 128), bf16),
            jax.ShapeDtypeStruct((count, 128), f32),
        ),
        in_specs=[
            pl.BlockSpec(memory_space=pltpu.SMEM),
            pl.BlockSpec(memory_space=pltpu.VMEM),
        ],
        out_specs=(
            pl.BlockSpec(memory_space=pltpu.VMEM),
            pl.BlockSpec(memory_space=pltpu.VMEM),
        ),
        compiler_params=pltpu.CompilerParams(vmem_limit_bytes=48 * 2**20),
        cost_estimate=pl.CostEstimate(
            flops=4 * count * count * 128, bytes_accessed=count * 2048, transcendentals=2 * count * count
        ),
    )(length, qkv)


def attend_back_kernel(len_ref, qkv_ref, do_ref, lse_ref, dqkv_ref, dk_ref, dv_ref):
    count = qkv_ref.shape[0]
    limit = len_ref[0]
    keys = qkv_ref[:, 128:256]
    values = qkv_ref[:, 256:384]
    low_half = lax.broadcasted_iota(jnp.int32, (1, 128), 1) < 64
    valid = lax.broadcasted_iota(jnp.int32, (1, count), 1) < limit
    step = 256
    for start in range(0, count, step):
        rows = pl.ds(start, step)
        queries = qkv_ref[rows, 0:128]
        grads = do_ref[rows, :]
        lse = lse_ref[rows, :]
        dqs, dks, dvs = [], [], []
        for half in range(2):
            mine = low_half if half == 0 else jnp.logical_not(low_half)
            q_part = jnp.where(mine, queries, jnp.zeros_like(queries)) * jnp.asarray(0.125, bf16)
            g_part = jnp.where(mine, grads, jnp.zeros_like(grads))
            scores = dot_t(q_part, keys)
            probs = jnp.where(valid, jnp.exp(scores - lse[:, 64 * half : 64 * half + 1]), 0.0)
            dp = dot_t(g_part, values)
            delta = jnp.sum(probs * dp, axis=1, keepdims=True)
            ds = (probs * (dp - delta)).astype(bf16)
            dqs.append(jnp.dot(ds, keys, preferred_element_type=f32))
            dks.append(dot_0(ds, q_part))
            dvs.append(dot_0(probs.astype(bf16), g_part))
        dqkv_ref[rows, 0:128] = (jnp.where(low_half, dqs[0], dqs[1]) * 0.125).astype(bf16)
        dk = dks[0] + dks[1]
        dv = dvs[0] + dvs[1]
        if start == 0:
            dk_ref[...] = dk
            dv_ref[...] = dv
        else:
            dk_ref[...] += dk
            dv_ref[...] += dv
    dqkv_ref[:, 128:256] = dk_ref[...].astype(bf16)
    dqkv_ref[:, 256:384] = dv_ref[...].astype(bf16)


def attend_back(length, qkv, grads, lse):
    count = qkv.shape[0]
    return pl.pallas_call(
        attend_back_kernel,
        out_shape=jax.ShapeDtypeStruct((count, 384), bf16),
        in_specs=[pl.BlockSpec(memory_space=pltpu.SMEM)]
        + [pl.BlockSpec(memory_space=pltpu.VMEM)] * 3,
        out_specs=pl.BlockSpec(memory_space=pltpu.VMEM),
        scratch_shapes=[pltpu.VMEM((count, 128), f32), pltpu.VMEM((count, 128), f32)],
        compiler_params=pltpu.CompilerParams(vmem_limit_bytes=48 * 2**20),
        cost_estimate=pl.CostEstimate(
            flops=10 * count * count * 128, bytes_accessed=count * 3072, transcendentals=2 * count * count
        ),
    )(length, qkv, grads, lse)


def fast_forward(hidden, params, length, group):
    w_qkv, qv_bias, w_attn, out_bias, w_in, in_bias, w_back, norm_gain, norm_shift = params
    hidden_low = hidden.astype(bf16)
    bias_row = jnp.concatenate([qv_bias[0], jnp.zeros_like(qv_bias[0]), qv_bias[1]])
    projected = (jnp.dot(hidden_low, w_qkv, preferred_element_type=f32) + bias_row).astype(bf16)
    qkv = exchange(projected, group, True, 1)
    heads_out, lse = attend(length, qkv)
    attended = exchange(heads_out, group, False, 2)
    first_sum = hidden + jnp.dot(attended, w_attn, preferred_element_type=f32) + out_bias[0]
    first_norm = normalize(first_sum, norm_gain[0], norm_shift[0])
    first_low = first_norm.astype(bf16)
    inner_pre = jnp.dot(first_low, w_in, preferred_element_type=f32) + in_bias
    activated = gelu_exact(inner_pre).astype(bf16)
    second_sum = first_norm + jnp.dot(activated, w_back, preferred_element_type=f32) + out_bias[1]
    output = normalize(second_sum, norm_gain[1], norm_shift[1])
    return output, (
        hidden_low, qkv, lse, attended, first_sum, first_low, inner_pre, activated, second_sum,
    )


def back_normalize(values, gain, grad):
    centered = values - jnp.mean(values, axis=-1, keepdims=True)
    inverse = lax.rsqrt(jnp.mean(centered * centered, axis=-1, keepdims=True) + eps)
    unit = centered * inverse
    scaled = grad * gain
    inner = jnp.mean(scaled * unit, axis=-1, keepdims=True)
    return (
        inverse * (scaled - jnp.mean(scaled, axis=-1, keepdims=True) - unit * inner),
        jnp.sum(grad * unit, axis=0),
        jnp.sum(grad, axis=0),
    )


def fast_backward(grad_output, saved, params, length, group):
    w_qkv, qv_bias, w_attn, out_bias, w_in, in_bias, w_back, norm_gain, norm_shift = params
    hidden_low, qkv, lse, attended, first_sum, first_low, inner_pre, activated, second_sum = saved
    grad_second, gain_two, shift_two = back_normalize(second_sum, norm_gain[1], grad_output)
    dz_two = grad_second.astype(bf16)
    grad_act = dot_t(dz_two, w_back)
    unused_gelu, pull_gelu = jax.vjp(gelu_exact, inner_pre)
    du = pull_gelu(grad_act)[0].astype(bf16)
    grad_first_norm = grad_second + dot_t(du, w_in)
    grad_first, gain_one, shift_one = back_normalize(first_sum, norm_gain[0], grad_first_norm)
    dz = grad_first.astype(bf16)
    grad_attended = dot_t(dz, w_attn).astype(bf16)
    head_grads = exchange(grad_attended, group, True, 3)
    dqkv_heads = attend_back(length, qkv, head_grads, lse)
    dqkv = exchange(dqkv_heads, group, False, 4)
    grad_hidden = grad_first + dot_t(dqkv, w_qkv)

    def column_sum(x):
        return jnp.sum(x.astype(f32), axis=0)

    width = hidden_low.shape[1]
    sums = column_sum(dqkv)
    vectors = (
        sums[:width], sums[2 * width :], column_sum(dz), column_sum(dz_two), column_sum(du),
        gain_one, gain_two, shift_one, shift_two,
    )
    pairs = ((hidden_low, dqkv), (attended, dz), (first_low, du), (dz_two, activated))
    return grad_hidden, vectors, pairs


def swap(x, axis, bit):
    return from_partner(x, axis, bit)


def add_low(kept, received):
    return (kept.astype(f32) + received.astype(f32)).astype(bf16)


def pick(x, at, axis):
    return lax.dynamic_index_in_dim(x, at, axis, keepdims=False)


def fold(x, axis, index, mesh_axis, bit):
    sent = pick(x, 1 - index, axis)
    kept = pick(x, index, axis)
    return add_low(kept, swap(sent, mesh_axis, bit))


def join(x, index, mesh_axis, bit):
    other = swap(x, mesh_axis, bit)
    return jnp.where(index == 0, jnp.stack([x, other]), jnp.stack([other, x]))


def reduce_yxz(total, position, row):
    columns = total.shape[1]
    z_hi, z_lo, y = position >> 2, position >> 1 & 1, position & 1
    x_at = row >> 1
    cut = total.reshape(2, 2, 2, 128, columns)
    part = fold(cut, 2, y, "blk", 0)
    part = part.reshape(2, 2, 2, 64, columns)
    part = fold(part, 2, x_at, "batch", 1)
    part = fold(part, 1, z_lo, "blk", 1)
    part = fold(part, 0, z_hi, "blk", 2)
    return join(part, x_at, "batch", 1).reshape(128, columns)


def reduce_zyx(total, position, row):
    columns = total.shape[1]
    z_hi, z_lo, y = position >> 2, position >> 1 & 1, position & 1
    cut = total.reshape(2, 2, 2, 128, columns)
    part = fold(cut, 1, z_lo, "blk", 1)
    part = fold(part, 0, z_hi, "blk", 2)
    part = fold(part, 0, y, "blk", 0)
    return add_low(part, swap(part, "batch", 1))


def fast_body(tokens, lengths, *rest):
    params, cotangent = rest[:-1], rest[-1]
    group = lax.axis_size("blk")
    position = lax.axis_index("blk")
    row = lax.axis_index("batch")
    core = row & 1
    out_one, saved_one = fast_forward(tokens[0].astype(f32), params, lengths, group)
    out_two, saved_two = fast_forward(out_one, params, lengths, group)
    grad, vec_two, pairs_two = fast_backward(cotangent[0].astype(f32), saved_two, params, lengths, group)
    grad, vec_one, pairs_one = fast_backward(grad, saved_one, params, lengths, group)

    def half_grad(pair_two, pair_one):
        def both(two, one, split):
            mine = jnp.concatenate([two, one], 0)
            if split:
                halves = mine.reshape(mine.shape[0], 2, mine.shape[1] // 2)
                mine, sent = pick(halves, core, 1), pick(halves, 1 - core, 1)
            else:
                sent = mine
            return jnp.concatenate([mine, swap(sent, "batch", 0)], 0)

        left = both(pair_two[0], pair_one[0], False)
        right = both(pair_two[1], pair_one[1], True)
        return dot_0(left, right).astype(bf16)

    qkv_half, attn_half, in_half, back_half = [
        half_grad(two, one) for two, one in zip(pairs_two, pairs_one)
    ]
    vectors = [a + b for a, b in zip(vec_two, vec_one)]
    stacked = jnp.concatenate(
        [jnp.stack(vectors[:4] + vectors[5:]).reshape(8, 8, 128),
         vectors[4].reshape(8, 4, 128).transpose(1, 0, 2)], 0
    )
    pieces = stacked.transpose(1, 2, 0).reshape(1024, 12)
    pieces = pieces + swap(pieces, "batch", 0)
    pieces = jnp.pad(pieces, ((0, 0), (0, 116))).astype(bf16)
    back_part = reduce_yxz(back_half, position, row)
    in_part = reduce_yxz(in_half, position, row)
    tail = reduce_zyx(jnp.concatenate([attn_half, qkv_half, pieces], 1), position, row)

    def whole(part):
        both = join(part, core, "batch", 0)
        return both.transpose(1, 0, 2).reshape(128, -1).astype(f32)

    back_grad = whole(back_part).T
    in_grad = whole(in_part)
    attn_grad = whole(tail[:, :512])
    qkv_grad = whole(tail[:, 512:2048])
    small = tail[:, 2048:2060].astype(f32).T
    return (
        out_two.astype(bf16)[None],
        grad.astype(bf16)[None],
        qkv_grad,
        small[0:2],
        attn_grad,
        small[2:4],
        in_grad,
        small[8:12].reshape(512),
        back_grad,
        small[4:6],
        small[6:8],
    )


def solution(mesh):
    placed = (
        P("batch", "blk", None),
        P("batch"),
        P(),
        P(),
        P(),
        P(),
        P(),
        P(),
        P(),
        P(),
        P(),
        P("batch", "blk", None),
    )
    fast = dict(mesh.shape) == {"batch": 4, "blk": 8}
    return jax.shard_map(
        fast_body if fast else body,
        mesh=mesh,
        in_specs=placed,
        out_specs=(
            P("batch", "blk", None),
            P("batch", "blk", None),
            P("blk", None),
            P(None, "blk"),
            P("blk", None),
            P(None, "blk"),
            P("blk", None),
            P("blk"),
            P(None, "blk"),
            P(None, "blk"),
            P(None, "blk"),
        ),
        check_vma=False,
    )
```

```python
import functools

import jax
import jax.numpy as jnp
from jax import lax
from jax.experimental import pallas as pl
from jax.experimental.pallas import tpu as pltpu
from jax.sharding import PartitionSpec as P

HEADS = 16


eps = 1e-12


def from_partner(x, axis, distance):
    return lax.ppermute(x, axis, [(i, i ^ 1 << distance) for i in range(lax.axis_size(axis))])


def normalize(values, gain, shift):
    centered = values - jnp.mean(values, axis=-1, keepdims=True)
    variance = jnp.mean(centered * centered, axis=-1, keepdims=True)
    return centered * lax.rsqrt(variance + eps) * gain + shift


def gelu_exact(values):
    return jax.nn.gelu(values, approximate=False)


def head_split(matrix, head_count):
    row_count, model_width = matrix.shape
    return matrix.reshape(row_count, head_count // 4, 4, model_width // head_count).transpose(
        1, 2, 0, 3
    )


def head_merge(stacked):
    group_count, group_size, row_count, head_size = stacked.shape
    return stacked.transpose(2, 0, 1, 3).reshape(row_count, group_count * group_size * head_size)


def core_forward(query_part, key_part, value_part, key_valid, scale):
    scores = (
        jnp.einsum("hqd,hkd->hqk", query_part, key_part, preferred_element_type=jnp.float32) * scale
    )
    masked = jnp.where(key_valid, scores, -1e30)
    row_max = jnp.max(masked, axis=-1, keepdims=True)
    exp_scores = jnp.where(key_valid, jnp.exp(masked - row_max), 0.0)
    row_total = jnp.sum(exp_scores, axis=-1, keepdims=True)
    prob_low = (exp_scores / row_total).astype(jnp.bfloat16)
    output = jnp.einsum("hqk,hkd->hqd", prob_low, value_part, preferred_element_type=jnp.float32)
    return (output, (row_max + jnp.log(row_total))[..., 0])


def core_backward(query_part, key_part, value_part, grad_part, log_part, key_valid, scale):
    scores = (
        jnp.einsum("hqd,hkd->hqk", query_part, key_part, preferred_element_type=jnp.float32) * scale
    )
    probs = jnp.where(key_valid, jnp.exp(scores - log_part[..., None]), 0.0)
    grad_probs = jnp.einsum(
        "hqd,hkd->hqk", grad_part, value_part, preferred_element_type=jnp.float32
    )
    inner_sum = jnp.sum(probs * grad_probs, axis=-1, keepdims=True)
    grad_scores = (probs * (grad_probs - inner_sum)).astype(jnp.bfloat16)
    grad_query = (
        jnp.einsum("hqk,hkd->hqd", grad_scores, key_part, preferred_element_type=jnp.float32)
        * scale
    )
    grad_key = (
        jnp.einsum("hqk,hqd->hkd", grad_scores, query_part, preferred_element_type=jnp.float32)
        * scale
    )
    grad_value = jnp.einsum(
        "hqk,hqd->hkd", probs.astype(jnp.bfloat16), grad_part, preferred_element_type=jnp.float32
    )
    return (grad_query, grad_key, grad_value)


def gather_group(kv_pair, position, bit_count):
    buffer_rows = kv_pair
    for step_bit in range(bit_count):
        received = from_partner(buffer_rows, "blk", step_bit)
        high_side = position >> step_bit & 1 == 1
        buffer_rows = jnp.where(
            high_side,
            jnp.concatenate([received, buffer_rows], 0),
            jnp.concatenate([buffer_rows, received], 0),
        )
    return buffer_rows


def spread_group(partials, position, bit_count):
    for step_bit in reversed(range(bit_count)):
        half_rows = partials.shape[0] // 2
        high_side = position >> step_bit & 1 == 1
        lower_part = partials[:half_rows]
        upper_part = partials[half_rows:]
        kept_part = jnp.where(high_side, upper_part, lower_part)
        sent_part = jnp.where(high_side, lower_part, upper_part)
        partials = kept_part + from_partner(sent_part.astype(jnp.bfloat16), "blk", step_bit).astype(
            sent_part.dtype
        )
    return partials


def attend_forward(queries, gathered, key_valid, head_count):
    model_width = queries.shape[1]
    scale = (model_width // head_count) ** (-0.5)
    query_heads = head_split(queries, head_count)
    key_heads = head_split(gathered[:, :model_width], head_count)
    value_heads = head_split(gathered[:, model_width:], head_count)

    def one_group(operands):
        query_part, key_part, value_part = operands
        return core_forward(query_part, key_part, value_part, key_valid, scale)

    outputs, log_sums = lax.map(one_group, (query_heads, key_heads, value_heads))
    return (head_merge(outputs), log_sums)


def attend_backward(queries, gathered, key_valid, log_sums, grad_attended, head_count):
    model_width = queries.shape[1]
    scale = (model_width // head_count) ** (-0.5)
    query_heads = head_split(queries, head_count)
    key_heads = head_split(gathered[:, :model_width], head_count)
    value_heads = head_split(gathered[:, model_width:], head_count)
    grad_heads = head_split(grad_attended, head_count)

    def one_group(operands):
        query_part, key_part, value_part, grad_part, log_part = operands
        return core_backward(
            query_part, key_part, value_part, grad_part, log_part, key_valid, scale
        )

    grad_query, grad_key, grad_value = lax.map(
        one_group, (query_heads, key_heads, value_heads, grad_heads, log_sums)
    )
    return (
        head_merge(grad_query),
        jnp.concatenate([head_merge(grad_key), head_merge(grad_value)], 1),
    )


def layer_forward(hidden, params, key_valid, position, bit_count, head_count):
    w_qkv, qv_bias, w_attn, out_bias, w_in, in_bias, w_back, norm_gain, norm_shift = params
    model_width = hidden.shape[1]
    hidden_low = hidden.astype(jnp.bfloat16)
    bias_row = jnp.concatenate([qv_bias[0], jnp.zeros_like(qv_bias[0]), qv_bias[1]])
    projected = (jnp.dot(hidden_low, w_qkv, preferred_element_type=jnp.float32) + bias_row).astype(
        jnp.bfloat16
    )
    gathered = gather_group(projected[:, model_width:], position, bit_count)
    attended, log_sums = attend_forward(projected[:, :model_width], gathered, key_valid, head_count)
    attended_low = attended.astype(jnp.bfloat16)
    first_sum = (
        hidden + jnp.dot(attended_low, w_attn, preferred_element_type=jnp.float32) + out_bias[0]
    )
    first_norm = normalize(first_sum, norm_gain[0], norm_shift[0])
    first_low = first_norm.astype(jnp.bfloat16)
    inner_pre = jnp.dot(first_low, w_in, preferred_element_type=jnp.float32) + in_bias
    activated = gelu_exact(inner_pre).astype(jnp.bfloat16)
    second_sum = (
        first_norm + jnp.dot(activated, w_back, preferred_element_type=jnp.float32) + out_bias[1]
    )
    output = normalize(second_sum, norm_gain[1], norm_shift[1])
    saved_state = (
        hidden_low,
        projected,
        gathered,
        log_sums,
        attended_low,
        first_sum,
        first_low,
        inner_pre,
        activated,
        second_sum,
    )
    return (output, saved_state)


def layer_backward(grad_output, saved_state, params, key_valid, position, bit_count, head_count):
    w_qkv, qv_bias, w_attn, out_bias, w_in, in_bias, w_back, norm_gain, norm_shift = params
    (
        hidden_low,
        projected,
        gathered,
        log_sums,
        attended_low,
        first_sum,
        first_low,
        inner_pre,
        activated,
        second_sum,
    ) = saved_state
    model_width = hidden_low.shape[1]
    unused_two, pull_two = jax.vjp(normalize, second_sum, norm_gain[1], norm_shift[1])
    grad_second, gain_two, shift_two = pull_two(grad_output)
    grad_branch_two = grad_second.astype(jnp.bfloat16)
    back_grad = jnp.einsum(
        "ra,rb->ab", activated, grad_branch_two, preferred_element_type=jnp.float32
    )
    bias_two = jnp.sum(grad_branch_two.astype(jnp.float32), axis=0)
    grad_act = jnp.dot(grad_branch_two, w_back.T, preferred_element_type=jnp.float32)
    unused_gelu, pull_gelu = jax.vjp(gelu_exact, inner_pre)
    grad_inner = pull_gelu(grad_act)[0].astype(jnp.bfloat16)
    in_grad = jnp.einsum("ra,rb->ab", first_low, grad_inner, preferred_element_type=jnp.float32)
    in_bias_grad = jnp.sum(grad_inner.astype(jnp.float32), axis=0)
    grad_first_norm = grad_second + jnp.dot(grad_inner, w_in.T, preferred_element_type=jnp.float32)
    unused_one, pull_one = jax.vjp(normalize, first_sum, norm_gain[0], norm_shift[0])
    grad_first, gain_one, shift_one = pull_one(grad_first_norm)
    grad_branch = grad_first.astype(jnp.bfloat16)
    attn_grad = jnp.einsum(
        "ra,rb->ab", attended_low, grad_branch, preferred_element_type=jnp.float32
    )
    bias_one = jnp.sum(grad_branch.astype(jnp.float32), axis=0)
    grad_attended = jnp.dot(grad_branch, w_attn.T, preferred_element_type=jnp.float32).astype(
        jnp.bfloat16
    )
    grad_query, grad_pairs = attend_backward(
        projected[:, :model_width], gathered, key_valid, log_sums, grad_attended, head_count
    )
    own_pairs = spread_group(grad_pairs, position, bit_count)
    grad_proj = jnp.concatenate([grad_query, own_pairs], 1).astype(jnp.bfloat16)
    qkv_grad = jnp.einsum("ra,rb->ab", hidden_low, grad_proj, preferred_element_type=jnp.float32)
    column_sums = jnp.sum(grad_proj.astype(jnp.float32), axis=0)
    qv_grad = jnp.stack([column_sums[:model_width], column_sums[2 * model_width :]])
    grad_hidden = grad_first + jnp.dot(grad_proj, w_qkv.T, preferred_element_type=jnp.float32)
    grad_list = (
        qkv_grad,
        qv_grad,
        attn_grad,
        jnp.stack([bias_one, bias_two]),
        in_grad,
        in_bias_grad,
        back_grad,
        jnp.stack([gain_one, gain_two]),
        jnp.stack([shift_one, shift_two]),
    )
    return (grad_hidden, grad_list)


def scatter_once(grad_list):
    (
        qkv_grad,
        qv_grad,
        attn_grad,
        bias_grad,
        in_grad,
        in_bias_grad,
        back_grad,
        gain_grad,
        shift_grad,
    ) = grad_list
    return (
        lax.psum_scatter(qkv_grad, "blk", scatter_dimension=0, tiled=True),
        lax.psum_scatter(qv_grad, "blk", scatter_dimension=1, tiled=True),
        lax.psum_scatter(attn_grad, "blk", scatter_dimension=0, tiled=True),
        lax.psum_scatter(bias_grad, "blk", scatter_dimension=1, tiled=True),
        lax.psum_scatter(in_grad, "blk", scatter_dimension=0, tiled=True),
        lax.psum_scatter(in_bias_grad, "blk", scatter_dimension=0, tiled=True),
        lax.psum_scatter(back_grad, "blk", scatter_dimension=1, tiled=True),
        lax.psum_scatter(gain_grad, "blk", scatter_dimension=1, tiled=True),
        lax.psum_scatter(shift_grad, "blk", scatter_dimension=1, tiled=True),
    )


def body(
    tokens,
    lengths,
    w_qkv,
    qv_bias,
    w_attn,
    out_bias,
    w_in,
    in_bias,
    w_back,
    norm_gain,
    norm_shift,
    cotangent,
):
    row_count = tokens.shape[1]
    head_count = HEADS
    cycle_size = lax.axis_size("blk")
    bit_count = cycle_size.bit_length() - 1
    position = lax.axis_index("blk")
    length = lengths[0]
    key_valid = jnp.arange(cycle_size * row_count) < length
    params = (w_qkv, qv_bias, w_attn, out_bias, w_in, in_bias, w_back, norm_gain, norm_shift)
    out_one, saved_one = layer_forward(
        tokens[0].astype(jnp.float32), params, key_valid, position, bit_count, head_count
    )
    out_two, saved_two = layer_forward(out_one, params, key_valid, position, bit_count, head_count)
    grad_hidden, grads_two = layer_backward(
        cotangent[0].astype(jnp.float32),
        saved_two,
        params,
        key_valid,
        position,
        bit_count,
        head_count,
    )
    grad_hidden, grads_one = layer_backward(
        grad_hidden, saved_one, params, key_valid, position, bit_count, head_count
    )
    shards = scatter_once(jax.tree.map(jnp.add, grads_two, grads_one))
    (
        qkv_part,
        qv_part,
        attn_part,
        bias_part,
        in_part,
        in_bias_part,
        back_part,
        gain_part,
        shift_part,
    ) = shards
    totals = (
        lax.psum(qkv_part.astype(jnp.bfloat16), "batch").astype(jnp.float32),
        lax.psum(qv_part.astype(jnp.bfloat16), "batch").astype(jnp.float32),
        lax.psum(attn_part.astype(jnp.bfloat16), "batch").astype(jnp.float32),
        lax.psum(bias_part.astype(jnp.bfloat16), "batch").astype(jnp.float32),
        lax.psum(in_part.astype(jnp.bfloat16), "batch").astype(jnp.float32),
        lax.psum(in_bias_part.astype(jnp.bfloat16), "batch").astype(jnp.float32),
        lax.psum(back_part.astype(jnp.bfloat16), "batch").astype(jnp.float32),
        lax.psum(gain_part.astype(jnp.bfloat16), "batch").astype(jnp.float32),
        lax.psum(shift_part.astype(jnp.bfloat16), "batch").astype(jnp.float32),
    )
    return (
        out_two.astype(jnp.bfloat16)[None],
        grad_hidden.astype(jnp.bfloat16)[None],
        totals[0],
        totals[1],
        totals[2],
        totals[3],
        totals[4],
        totals[5],
        totals[6],
        totals[7],
        totals[8],
    )


MESH = pl.DeviceIdType.MESH
f32 = jnp.float32
bf16 = jnp.bfloat16


def member(j):
    return {"blk": j}


def place():
    return lax.axis_index("blk")


def exchange_kernel(group, columns, spread, src, dst, send_sem, recv_sem, own_sem):
    me = place()
    rows = 128
    groups = columns // 128
    barrier = pltpu.get_barrier_semaphore()
    for step in range(1, group):
        pl.semaphore_signal(
            barrier, inc=1, device_id=member(lax.rem(me + step, group)), device_id_type=MESH
        )
    pl.semaphore_wait(barrier, group - 1)

    def views(target, source):
        for part in range(groups):
            wide_t = pl.ds(pl.multiple_of(part * 128 * group + target * 128, 128), 128)
            wide_s = pl.ds(pl.multiple_of(part * 128 * group + source * 128, 128), 128)
            narrow = pl.ds(part * 128, 128)
            row_s = pl.ds(pl.multiple_of(source * rows, rows), rows)
            row_t = pl.ds(pl.multiple_of(target * rows, rows), rows)
            if spread:
                yield src.at[:, wide_t], dst.at[row_s, narrow]
            else:
                yield src.at[row_t, narrow], dst.at[:, wide_s]

    copies = []
    for step in range(1, group):
        target = lax.rem(me + step, group)
        for part, (here, there) in enumerate(views(target, me)):
            copy = pltpu.make_async_remote_copy(
                src_ref=here,
                dst_ref=there,
                send_sem=send_sem.at[step - 1, part],
                recv_sem=recv_sem.at[step - 1, part],
                device_id=member(target),
                device_id_type=MESH,
            )
            copy.start()
            copies.append(copy)
    for part, (here, there) in enumerate(views(me, me)):
        copy = pltpu.make_async_copy(here, there, own_sem.at[part])
        copy.start()
        copies.append(copy)
    for copy in copies:
        copy.wait()


def exchange(x, group, spread, ident):
    if spread:
        groups = x.shape[1] // (128 * group)
        out = (128 * group, groups * 128)
    else:
        groups = x.shape[1] // 128
        out = (128, groups * 128 * group)
    return pl.pallas_call(
        functools.partial(exchange_kernel, group, groups * 128, spread),
        out_shape=jax.ShapeDtypeStruct(out, x.dtype),
        in_specs=[pl.BlockSpec(memory_space=pl.ANY)],
        out_specs=pl.BlockSpec(memory_space=pl.ANY),
        scratch_shapes=[
            pltpu.SemaphoreType.DMA((group - 1, groups)),
            pltpu.SemaphoreType.DMA((group - 1, groups)),
            pltpu.SemaphoreType.DMA((groups,)),
        ],
        compiler_params=pltpu.CompilerParams(collective_id=ident, has_side_effects=True),
    )(x)


def dot_t(a, b):
    return lax.dot_general(a, b, (((1,), (1,)), ((), ())), preferred_element_type=f32)


def dot_0(a, b):
    return lax.dot_general(a, b, (((0,), (0,)), ((), ())), preferred_element_type=f32)


def attend_kernel(len_ref, qkv_ref, o_ref, lse_ref):
    count = qkv_ref.shape[0]
    limit = len_ref[0]
    keys = qkv_ref[:, 128:256]
    values = qkv_ref[:, 256:384]
    low_half = lax.broadcasted_iota(jnp.int32, (1, 128), 1) < 64
    valid = lax.broadcasted_iota(jnp.int32, (1, count), 1) < limit
    step = 256
    for start in range(0, count, step):
        rows = pl.ds(start, step)
        queries = qkv_ref[rows, 0:128]
        outs, lses = [], []
        for half in range(2):
            mine = low_half if half == 0 else jnp.logical_not(low_half)
            part = jnp.where(mine, queries, jnp.zeros_like(queries)) * jnp.asarray(0.125, bf16)
            scores = jnp.where(valid, dot_t(part, keys), -1e30)
            top = jnp.max(scores, axis=1, keepdims=True)
            expd = jnp.exp(scores - top)
            total = jnp.sum(expd, axis=1, keepdims=True)
            probs = (expd * (1.0 / total)).astype(bf16)
            outs.append(jnp.dot(probs, values, preferred_element_type=f32))
            lses.append(top + jnp.log(total))
        o_ref[rows, :] = jnp.where(low_half, outs[0], outs[1]).astype(bf16)
        lse_ref[rows, :] = jnp.where(low_half, lses[0], lses[1])


def attend(length, qkv):
    count = qkv.shape[0]
    return pl.pallas_call(
        attend_kernel,
        out_shape=(
            jax.ShapeDtypeStruct((count, 128), bf16),
            jax.ShapeDtypeStruct((count, 128), f32),
        ),
        in_specs=[
            pl.BlockSpec(memory_space=pltpu.SMEM),
            pl.BlockSpec(memory_space=pltpu.VMEM),
        ],
        out_specs=(
            pl.BlockSpec(memory_space=pltpu.VMEM),
            pl.BlockSpec(memory_space=pltpu.VMEM),
        ),
        compiler_params=pltpu.CompilerParams(vmem_limit_bytes=48 * 2**20),
        cost_estimate=pl.CostEstimate(
            flops=4 * count * count * 128, bytes_accessed=count * 2048, transcendentals=2 * count * count
        ),
    )(length, qkv)


def attend_back_kernel(len_ref, qkv_ref, do_ref, lse_ref, dqkv_ref, dk_ref, dv_ref):
    count = qkv_ref.shape[0]
    limit = len_ref[0]
    keys = qkv_ref[:, 128:256]
    values = qkv_ref[:, 256:384]
    low_half = lax.broadcasted_iota(jnp.int32, (1, 128), 1) < 64
    valid = lax.broadcasted_iota(jnp.int32, (1, count), 1) < limit
    step = 256
    for start in range(0, count, step):
        rows = pl.ds(start, step)
        queries = qkv_ref[rows, 0:128]
        grads = do_ref[rows, :]
        lse = lse_ref[rows, :]
        dqs, dks, dvs = [], [], []
        for half in range(2):
            mine = low_half if half == 0 else jnp.logical_not(low_half)
            q_part = jnp.where(mine, queries, jnp.zeros_like(queries)) * jnp.asarray(0.125, bf16)
            g_part = jnp.where(mine, grads, jnp.zeros_like(grads))
            scores = dot_t(q_part, keys)
            probs = jnp.where(valid, jnp.exp(scores - lse[:, 64 * half : 64 * half + 1]), 0.0)
            dp = dot_t(g_part, values)
            delta = jnp.sum(probs * dp, axis=1, keepdims=True)
            ds = (probs * (dp - delta)).astype(bf16)
            dqs.append(jnp.dot(ds, keys, preferred_element_type=f32))
            dks.append(dot_0(ds, q_part))
            dvs.append(dot_0(probs.astype(bf16), g_part))
        dqkv_ref[rows, 0:128] = (jnp.where(low_half, dqs[0], dqs[1]) * 0.125).astype(bf16)
        dk = dks[0] + dks[1]
        dv = dvs[0] + dvs[1]
        if start == 0:
            dk_ref[...] = dk
            dv_ref[...] = dv
        else:
            dk_ref[...] += dk
            dv_ref[...] += dv
    dqkv_ref[:, 128:256] = dk_ref[...].astype(bf16)
    dqkv_ref[:, 256:384] = dv_ref[...].astype(bf16)


def attend_back(length, qkv, grads, lse):
    count = qkv.shape[0]
    return pl.pallas_call(
        attend_back_kernel,
        out_shape=jax.ShapeDtypeStruct((count, 384), bf16),
        in_specs=[pl.BlockSpec(memory_space=pltpu.SMEM)]
        + [pl.BlockSpec(memory_space=pltpu.VMEM)] * 3,
        out_specs=pl.BlockSpec(memory_space=pltpu.VMEM),
        scratch_shapes=[pltpu.VMEM((count, 128), f32), pltpu.VMEM((count, 128), f32)],
        compiler_params=pltpu.CompilerParams(vmem_limit_bytes=48 * 2**20),
        cost_estimate=pl.CostEstimate(
            flops=10 * count * count * 128, bytes_accessed=count * 3072, transcendentals=2 * count * count
        ),
    )(length, qkv, grads, lse)


def fast_forward(hidden, params, length, group):
    w_qkv, qv_bias, w_attn, out_bias, w_in, in_bias, w_back, norm_gain, norm_shift = params
    hidden_low = hidden.astype(bf16)
    bias_row = jnp.concatenate([qv_bias[0], jnp.zeros_like(qv_bias[0]), qv_bias[1]])
    projected = (jnp.dot(hidden_low, w_qkv, preferred_element_type=f32) + bias_row).astype(bf16)
    qkv = exchange(projected, group, True, 1)
    heads_out, lse = attend(length, qkv)
    attended = exchange(heads_out, group, False, 2)
    first_sum = hidden + jnp.dot(attended, w_attn, preferred_element_type=f32) + out_bias[0]
    first_norm = normalize(first_sum, norm_gain[0], norm_shift[0])
    first_low = first_norm.astype(bf16)
    inner_pre = jnp.dot(first_low, w_in, preferred_element_type=f32) + in_bias
    activated = gelu_exact(inner_pre).astype(bf16)
    second_sum = first_norm + jnp.dot(activated, w_back, preferred_element_type=f32) + out_bias[1]
    output = normalize(second_sum, norm_gain[1], norm_shift[1])
    return output, (
        hidden_low, qkv, lse, attended, first_sum, first_low, inner_pre, activated, second_sum,
    )


def back_normalize(values, gain, grad):
    centered = values - jnp.mean(values, axis=-1, keepdims=True)
    inverse = lax.rsqrt(jnp.mean(centered * centered, axis=-1, keepdims=True) + eps)
    unit = centered * inverse
    scaled = grad * gain
    inner = jnp.mean(scaled * unit, axis=-1, keepdims=True)
    return (
        inverse * (scaled - jnp.mean(scaled, axis=-1, keepdims=True) - unit * inner),
        jnp.sum(grad * unit, axis=0),
        jnp.sum(grad, axis=0),
    )


def fast_backward(grad_output, saved, params, length, group):
    w_qkv, qv_bias, w_attn, out_bias, w_in, in_bias, w_back, norm_gain, norm_shift = params
    hidden_low, qkv, lse, attended, first_sum, first_low, inner_pre, activated, second_sum = saved
    grad_second, gain_two, shift_two = back_normalize(second_sum, norm_gain[1], grad_output)
    dz_two = grad_second.astype(bf16)
    grad_act = dot_t(dz_two, w_back)
    unused_gelu, pull_gelu = jax.vjp(gelu_exact, inner_pre)
    du = pull_gelu(grad_act)[0].astype(bf16)
    grad_first_norm = grad_second + dot_t(du, w_in)
    grad_first, gain_one, shift_one = back_normalize(first_sum, norm_gain[0], grad_first_norm)
    dz = grad_first.astype(bf16)
    grad_attended = dot_t(dz, w_attn).astype(bf16)
    head_grads = exchange(grad_attended, group, True, 3)
    dqkv_heads = attend_back(length, qkv, head_grads, lse)
    dqkv = exchange(dqkv_heads, group, False, 4)
    grad_hidden = grad_first + dot_t(dqkv, w_qkv)

    def column_sum(x):
        return jnp.sum(x.astype(f32), axis=0)

    width = hidden_low.shape[1]
    sums = column_sum(dqkv)
    vectors = (
        sums[:width], sums[2 * width :], column_sum(dz), column_sum(dz_two), column_sum(du),
        gain_one, gain_two, shift_one, shift_two,
    )
    pairs = ((hidden_low, dqkv), (attended, dz), (first_low, du), (dz_two, activated))
    return grad_hidden, vectors, pairs


PATHS = {"A": "yxabXC", "B": "xyabXC", "C": "abysC"}
CHUNK_PATHS = "BCAACBBCABAA"
WIDE = 512
ORDER = (
    (0, -1), (1, -1), (2, -1), (3, -1), (0, 0), (4, -1), (1, 0), (5, -1), (2, 0), (6, -1), (3, 0), (7, -1), (4, 0), (8, -1), (5, 0), (9, -1), (0, 1), (2, 1), (1, 1), (8, 0), (10, -1), (7, 0), (11, -1), (6, 0), (5, 1), (3, 1), (1, 2), (0, 2), (2, 2), (4, 1), (9, 0), (10, 0), (5, 2), (3, 2), (7, 1), (8, 1), (0, 3), (1, 3), (2, 3), (1, 4), (11, 0), (5, 3), (10, 1), (3, 3), (0, 4), (8, 2), (2, 4), (0, 5), (6, 1), (2, 5), (10, 2), (4, 2), (8, 3), (11, 1), (6, 2), (5, 4), (3, 4), (5, 5), (9, 1), (10, 3), (3, 5), (11, 2), (4, 3), (7, 2), (8, 4), (4, 4), (6, 3), (10, 4), (8, 5), (9, 2), (10, 5), (7, 3), (11, 3), (6, 4), (7, 4), (6, 5), (9, 3), (11, 4), (11, 5), (9, 4), (9, 5),
)


def plan(path, rows):
    slabs, width, steps = 8, WIDE, []
    for stage in path:
        if stage in "yab":
            slabs //= 2
        elif stage == "x":
            width //= 2
        elif stage == "X":
            width *= 2
        steps.append((stage, slabs, width))
    return steps


def grad_kernel(*refs):
    count = len(CHUNK_PATHS)
    lefts, rights = refs[0:8], refs[8:16]
    vec_ref, out = refs[16], refs[17]
    it = iter(refs[18:])
    left_buf = [next(it) for _ in range(4)]
    right_buf = [next(it) for _ in range(4)]
    turned = next(it)
    chunk_buf = [next(it) for _ in range(count)]
    landing = {}
    for c, name in enumerate(CHUNK_PATHS):
        for i, (stage, _, _) in enumerate(plan(PATHS[name], 128)):
            if stage in "yabxs":
                landing[c, i] = next(it)
    send_sem, recv_sem, in_send, in_recv, in_own, vec_sem = it

    row, position = lax.axis_index("batch"), lax.axis_index("blk")
    core, x_at = row % 2, row // 2
    y, z_lo, z_hi = position % 2, (position // 2) % 2, position // 4
    bits = {"y": y, "a": z_lo, "b": z_hi}
    across = {
        "C": {"batch": row + 1 - 2 * core},
        "x": {"batch": row + 2 - 4 * x_at},
        "y": {"blk": position + 1 - 2 * y},
        "a": {"blk": position + 2 - 4 * z_lo},
        "b": {"blk": position + 4 - 8 * z_hi},
    }
    across["X"] = across["s"] = across["x"]
    barrier = pltpu.get_barrier_semaphore()
    for who in "Cxyab":
        pl.semaphore_signal(barrier, inc=1, device_id=across[who], device_id_type=MESH)

    order_of = (3, 2, 1, 0)
    own_copies, in_copies = {}, {}
    for k in order_of:
        for d in range(2):
            half = right_buf[k].shape[2]
            mine = pl.ds(pl.multiple_of(core * half, 128), half)
            for side, (src, dst) in enumerate(
                ((lefts[2 * k + d], left_buf[k].at[d]), (rights[2 * k + d].at[:, mine], right_buf[k].at[d]))
            ):
                copy = pltpu.make_async_copy(src, dst, in_own.at[k, d, side])
                copy.start()
                own_copies[k, d, side] = copy
    vec_c = count - 1
    vec_copy = pltpu.make_async_copy(vec_ref, chunk_buf[vec_c].at[:, 128:144], vec_sem)
    vec_copy.start()
    pl.semaphore_wait(barrier, 5)
    for k in order_of:
        for d in range(2):
            half = right_buf[k].shape[2]
            theirs = pl.ds(pl.multiple_of((1 - core) * half, 128), half)
            for side, (src, dst) in enumerate(
                ((lefts[2 * k + d], left_buf[k].at[2 + d]), (rights[2 * k + d].at[:, theirs], right_buf[k].at[2 + d]))
            ):
                copy = pltpu.make_async_remote_copy(
                    src_ref=src, dst_ref=dst, send_sem=in_send.at[k, d, side],
                    recv_sem=in_recv.at[k, d, side], device_id=across["C"], device_id_type=MESH,
                )
                copy.start()
                in_copies[k, d, side] = copy

    def weight_of(c):
        return (3, c, 2048) if c < 4 else (2, c - 4, 2048) if c < 8 else (1, 0, 512) if c < 9 else (0, c - 9, 1536)

    base = {3: 0, 2: 4096, 1: 8192, 0: 9216}
    ready = set()

    def prepare(k):
        for d in range(2):
            for side in range(2):
                own_copies[k, d, side].wait()
                in_copies[k, d, side].wait_recv()
        for g in range(4):
            turned[:, pl.ds(128 * g, 128)] = left_buf[k][g].T

    def compute(c):
        k, at, _ = weight_of(c)
        if k not in ready:
            prepare(k)
            ready.add(k)
        path = [s for s in PATHS[CHUNK_PATHS[c]] if s in "yab"]
        right = right_buf[k][:, :, pl.ds(at * WIDE, WIDE)].reshape(512, WIDE)

        def piece(i, carry):
            product = jnp.dot(
                turned[pl.ds(pl.multiple_of(i * 256, 256), 256), :], right, preferred_element_type=f32
            ).astype(bf16)
            for low in range(2):
                bit = {"y": low, "a": i % 2, "b": i // 2}
                spot = (bit[path[0]] * 2 + bit[path[1]]) * 2 + bit[path[2]]
                chunk_buf[c][spot, 0:128] = product[128 * low : 128 * low + 128]
            return carry

        lax.fori_loop(0, 4, piece, 0)
        if c == vec_c:
            vec_copy.wait()

    current, copies = {}, {}
    steps = {c: plan(PATHS[name], 128) for c, name in enumerate(CHUNK_PATHS)}
    sem_at = {}
    for c in range(count):
        for i in range(len(steps[c])):
            sem_at[c, i] = len(sem_at)

    def spot_of(c):
        k, at, half = weight_of(c)
        return base[k] + core * half + at * WIDE

    def rows_of(c):
        return 144 if c == vec_c else 128

    def send(c, i):
        stage, slabs, width = steps[c][i]
        if stage in "yab":
            src = current[c].at[pl.ds((1 - bits[stage]) * slabs, slabs)]
            dst = landing[c, i]
        elif stage == "x":
            src = current[c].at[:, :, pl.ds(pl.multiple_of((1 - x_at) * width, 128), width)]
            dst = landing[c, i]
        elif stage == "s":
            src, dst = current[c], landing[c, i]
        else:
            start = spot_of(c) + (x_at * (width // 2) if stage == "X" else 0)
            width = width // 2 if stage == "X" else width
            src = dst = out.at[pl.ds(0, rows_of(c)), pl.ds(pl.multiple_of(start, 128), width)]
        copy = pltpu.make_async_remote_copy(
            src_ref=src, dst_ref=dst, send_sem=send_sem.at[sem_at[c, i]],
            recv_sem=recv_sem.at[sem_at[c, i]], device_id=across[stage], device_id_type=MESH,
        )
        copy.start()
        copies[c, i] = copy

    def advance(c, i):
        stage, slabs, width = steps[c][i]
        copies[c, i].wait_recv()
        if stage in "XC":
            return
        got, old = landing[c, i], current[c]

        def add(n, carry):
            if stage in "yab":
                kept = old[bits[stage] * slabs + n]
            elif stage == "x":
                kept = old[n, :, pl.ds(pl.multiple_of(x_at * width, 128), width)]
            else:
                kept = old[n]
            got[n] = (got[n].astype(f32) + kept.astype(f32)).astype(bf16)
            return carry

        lax.fori_loop(0, slabs, add, 0)
        current[c] = got
        if steps[c][i + 1][0] in "XC":
            start = spot_of(c) + (x_at * width if steps[c][i + 1][0] == "X" else 0)
            out[pl.ds(0, rows_of(c)), pl.ds(pl.multiple_of(start, 128), width)] = got[0]

    for c, i in ORDER:
        if i < 0:
            compute(c)
            current[c] = chunk_buf[c]
        else:
            advance(c, i)
        if i + 1 < len(steps[c]):
            send(c, i + 1)
    for copy in copies.values():
        copy.wait_send()
    for copy in in_copies.values():
        copy.wait_send()


def weight_grads(pairs_two, pairs_one, vectors):
    lefts, rights = [], []
    for two, one in zip(pairs_two, pairs_one):
        lefts += [two[0], one[0]]
        rights += [two[1], one[1]]
    scratch = [pltpu.VMEM((4, 128, 1024), bf16) for _ in range(4)]
    scratch += [pltpu.VMEM((4, 128, rights[2 * k].shape[1] // 2), bf16) for k in range(4)]
    scratch += [pltpu.VMEM((1024, 512), bf16)]
    total = 0
    rows = [144 if c == len(CHUNK_PATHS) - 1 else 128 for c in range(len(CHUNK_PATHS))]
    scratch += [pltpu.VMEM((8, r, WIDE), bf16) for r in rows]
    for c, name in enumerate(CHUNK_PATHS):
        for stage, slabs, width in plan(PATHS[name], 128):
            total += 1
            if stage in "yabxs":
                scratch.append(pltpu.VMEM((slabs, rows[c], width), bf16))
    dma = pltpu.SemaphoreType.DMA
    scratch += [dma((total,)), dma((total,)), dma((4, 2, 2)), dma((4, 2, 2)), dma((4, 2, 2)), dma(())]
    return pl.pallas_call(
        grad_kernel,
        out_shape=jax.ShapeDtypeStruct((144, 12288), bf16),
        in_specs=[pl.BlockSpec(memory_space=pl.ANY)] * 17,
        out_specs=pl.BlockSpec(memory_space=pltpu.VMEM),
        scratch_shapes=scratch,
        compiler_params=pltpu.CompilerParams(
            collective_id=5, has_side_effects=True, vmem_limit_bytes=56 * 2**20
        ),
    )(*lefts, *rights, vectors)


def fast_body(tokens, lengths, *rest):
    params, cotangent = rest[:-1], rest[-1]
    group = lax.axis_size("blk")
    out_one, saved_one = fast_forward(tokens[0].astype(f32), params, lengths, group)
    out_two, saved_two = fast_forward(out_one, params, lengths, group)
    grad, vec_two, pairs_two = fast_backward(cotangent[0].astype(f32), saved_two, params, lengths, group)
    grad, vec_one, pairs_one = fast_backward(grad, saved_one, params, lengths, group)
    vectors = [a + b for a, b in zip(vec_two, vec_one)]
    stacked = jnp.concatenate(
        [jnp.stack(vectors[:4] + vectors[5:]).reshape(8, 8, 128),
         vectors[4].reshape(8, 4, 128).transpose(1, 0, 2)], 0
    )
    pieces = stacked.reshape(3, 4, 2, 2, 2, 128).transpose(4, 3, 2, 0, 1, 5).reshape(8, 3, 512)
    pieces = jnp.pad(pieces, ((0, 0), (0, 13), (0, 0))).astype(bf16)
    sums = weight_grads(pairs_two, pairs_one, pieces)
    back_grad = sums[:128, :4096].astype(f32).T
    in_grad = sums[:128, 4096:8192].astype(f32)
    attn_grad = sums[:128, 8192:9216].astype(f32)
    qkv_grad = sums[:128, 9216:].astype(f32)
    small = sums[128:131, 10240:10752].astype(f32) + sums[128:131, 11776:12288].astype(f32)
    small = small.reshape(12, 128)
    return (
        out_two.astype(bf16)[None],
        grad.astype(bf16)[None],
        qkv_grad,
        small[0:2],
        attn_grad,
        small[2:4],
        in_grad,
        small[8:12].reshape(512),
        back_grad,
        small[4:6],
        small[6:8],
    )


def solution(mesh):
    placed = (
        P("batch", "blk", None),
        P("batch"),
        P(),
        P(),
        P(),
        P(),
        P(),
        P(),
        P(),
        P(),
        P(),
        P("batch", "blk", None),
    )
    fast = dict(mesh.shape) == {"batch": 4, "blk": 8}
    return jax.shard_map(
        fast_body if fast else body,
        mesh=mesh,
        in_specs=placed,
        out_specs=(
            P("batch", "blk", None),
            P("batch", "blk", None),
            P("blk", None),
            P(None, "blk"),
            P("blk", None),
            P(None, "blk"),
            P("blk", None),
            P("blk"),
            P(None, "blk"),
            P(None, "blk"),
            P(None, "blk"),
        ),
        check_vma=False,
    )
```

```python
import jax
import jax.numpy as jnp
from jax import lax
from jax.experimental import pallas as pl
from jax.experimental.pallas import tpu as pltpu
from jax.sharding import PartitionSpec as P

HEADS = 16


eps = 1e-12


def from_partner(x, axis, distance):
    return lax.ppermute(x, axis, [(i, i ^ 1 << distance) for i in range(lax.axis_size(axis))])


def normalize(values, gain, shift):
    centered = values - jnp.mean(values, axis=-1, keepdims=True)
    variance = jnp.mean(centered * centered, axis=-1, keepdims=True)
    return centered * lax.rsqrt(variance + eps) * gain + shift


def gelu_exact(values):
    return jax.nn.gelu(values, approximate=False)


def head_split(matrix, head_count):
    row_count, model_width = matrix.shape
    return matrix.reshape(row_count, head_count // 4, 4, model_width // head_count).transpose(
        1, 2, 0, 3
    )


def head_merge(stacked):
    group_count, group_size, row_count, head_size = stacked.shape
    return stacked.transpose(2, 0, 1, 3).reshape(row_count, group_count * group_size * head_size)


def core_forward(query_part, key_part, value_part, key_valid, scale):
    scores = (
        jnp.einsum("hqd,hkd->hqk", query_part, key_part, preferred_element_type=jnp.float32) * scale
    )
    masked = jnp.where(key_valid, scores, -1e30)
    row_max = jnp.max(masked, axis=-1, keepdims=True)
    exp_scores = jnp.where(key_valid, jnp.exp(masked - row_max), 0.0)
    row_total = jnp.sum(exp_scores, axis=-1, keepdims=True)
    prob_low = (exp_scores / row_total).astype(jnp.bfloat16)
    output = jnp.einsum("hqk,hkd->hqd", prob_low, value_part, preferred_element_type=jnp.float32)
    return (output, (row_max + jnp.log(row_total))[..., 0])


def core_backward(query_part, key_part, value_part, grad_part, log_part, key_valid, scale):
    scores = (
        jnp.einsum("hqd,hkd->hqk", query_part, key_part, preferred_element_type=jnp.float32) * scale
    )
    probs = jnp.where(key_valid, jnp.exp(scores - log_part[..., None]), 0.0)
    grad_probs = jnp.einsum(
        "hqd,hkd->hqk", grad_part, value_part, preferred_element_type=jnp.float32
    )
    inner_sum = jnp.sum(probs * grad_probs, axis=-1, keepdims=True)
    grad_scores = (probs * (grad_probs - inner_sum)).astype(jnp.bfloat16)
    grad_query = (
        jnp.einsum("hqk,hkd->hqd", grad_scores, key_part, preferred_element_type=jnp.float32)
        * scale
    )
    grad_key = (
        jnp.einsum("hqk,hqd->hkd", grad_scores, query_part, preferred_element_type=jnp.float32)
        * scale
    )
    grad_value = jnp.einsum(
        "hqk,hqd->hkd", probs.astype(jnp.bfloat16), grad_part, preferred_element_type=jnp.float32
    )
    return (grad_query, grad_key, grad_value)


def gather_group(kv_pair, position, bit_count):
    buffer_rows = kv_pair
    for step_bit in range(bit_count):
        received = from_partner(buffer_rows, "blk", step_bit)
        high_side = position >> step_bit & 1 == 1
        buffer_rows = jnp.where(
            high_side,
            jnp.concatenate([received, buffer_rows], 0),
            jnp.concatenate([buffer_rows, received], 0),
        )
    return buffer_rows


def spread_group(partials, position, bit_count):
    for step_bit in reversed(range(bit_count)):
        half_rows = partials.shape[0] // 2
        high_side = position >> step_bit & 1 == 1
        lower_part = partials[:half_rows]
        upper_part = partials[half_rows:]
        kept_part = jnp.where(high_side, upper_part, lower_part)
        sent_part = jnp.where(high_side, lower_part, upper_part)
        partials = kept_part + from_partner(sent_part.astype(jnp.bfloat16), "blk", step_bit).astype(
            sent_part.dtype
        )
    return partials


def attend_forward(queries, gathered, key_valid, head_count):
    model_width = queries.shape[1]
    scale = (model_width // head_count) ** (-0.5)
    query_heads = head_split(queries, head_count)
    key_heads = head_split(gathered[:, :model_width], head_count)
    value_heads = head_split(gathered[:, model_width:], head_count)

    def one_group(operands):
        query_part, key_part, value_part = operands
        return core_forward(query_part, key_part, value_part, key_valid, scale)

    outputs, log_sums = lax.map(one_group, (query_heads, key_heads, value_heads))
    return (head_merge(outputs), log_sums)


def attend_backward(queries, gathered, key_valid, log_sums, grad_attended, head_count):
    model_width = queries.shape[1]
    scale = (model_width // head_count) ** (-0.5)
    query_heads = head_split(queries, head_count)
    key_heads = head_split(gathered[:, :model_width], head_count)
    value_heads = head_split(gathered[:, model_width:], head_count)
    grad_heads = head_split(grad_attended, head_count)

    def one_group(operands):
        query_part, key_part, value_part, grad_part, log_part = operands
        return core_backward(
            query_part, key_part, value_part, grad_part, log_part, key_valid, scale
        )

    grad_query, grad_key, grad_value = lax.map(
        one_group, (query_heads, key_heads, value_heads, grad_heads, log_sums)
    )
    return (
        head_merge(grad_query),
        jnp.concatenate([head_merge(grad_key), head_merge(grad_value)], 1),
    )


def layer_forward(hidden, params, key_valid, position, bit_count, head_count):
    w_qkv, qv_bias, w_attn, out_bias, w_in, in_bias, w_back, norm_gain, norm_shift = params
    model_width = hidden.shape[1]
    hidden_low = hidden.astype(jnp.bfloat16)
    bias_row = jnp.concatenate([qv_bias[0], jnp.zeros_like(qv_bias[0]), qv_bias[1]])
    projected = (jnp.dot(hidden_low, w_qkv, preferred_element_type=jnp.float32) + bias_row).astype(
        jnp.bfloat16
    )
    gathered = gather_group(projected[:, model_width:], position, bit_count)
    attended, log_sums = attend_forward(projected[:, :model_width], gathered, key_valid, head_count)
    attended_low = attended.astype(jnp.bfloat16)
    first_sum = (
        hidden + jnp.dot(attended_low, w_attn, preferred_element_type=jnp.float32) + out_bias[0]
    )
    first_norm = normalize(first_sum, norm_gain[0], norm_shift[0])
    first_low = first_norm.astype(jnp.bfloat16)
    inner_pre = jnp.dot(first_low, w_in, preferred_element_type=jnp.float32) + in_bias
    activated = gelu_exact(inner_pre).astype(jnp.bfloat16)
    second_sum = (
        first_norm + jnp.dot(activated, w_back, preferred_element_type=jnp.float32) + out_bias[1]
    )
    output = normalize(second_sum, norm_gain[1], norm_shift[1])
    saved_state = (
        hidden_low,
        projected,
        gathered,
        log_sums,
        attended_low,
        first_sum,
        first_low,
        inner_pre,
        activated,
        second_sum,
    )
    return (output, saved_state)


def layer_backward(grad_output, saved_state, params, key_valid, position, bit_count, head_count):
    w_qkv, qv_bias, w_attn, out_bias, w_in, in_bias, w_back, norm_gain, norm_shift = params
    (
        hidden_low,
        projected,
        gathered,
        log_sums,
        attended_low,
        first_sum,
        first_low,
        inner_pre,
        activated,
        second_sum,
    ) = saved_state
    model_width = hidden_low.shape[1]
    unused_two, pull_two = jax.vjp(normalize, second_sum, norm_gain[1], norm_shift[1])
    grad_second, gain_two, shift_two = pull_two(grad_output)
    grad_branch_two = grad_second.astype(jnp.bfloat16)
    back_grad = jnp.einsum(
        "ra,rb->ab", activated, grad_branch_two, preferred_element_type=jnp.float32
    )
    bias_two = jnp.sum(grad_branch_two.astype(jnp.float32), axis=0)
    grad_act = jnp.dot(grad_branch_two, w_back.T, preferred_element_type=jnp.float32)
    unused_gelu, pull_gelu = jax.vjp(gelu_exact, inner_pre)
    grad_inner = pull_gelu(grad_act)[0].astype(jnp.bfloat16)
    in_grad = jnp.einsum("ra,rb->ab", first_low, grad_inner, preferred_element_type=jnp.float32)
    in_bias_grad = jnp.sum(grad_inner.astype(jnp.float32), axis=0)
    grad_first_norm = grad_second + jnp.dot(grad_inner, w_in.T, preferred_element_type=jnp.float32)
    unused_one, pull_one = jax.vjp(normalize, first_sum, norm_gain[0], norm_shift[0])
    grad_first, gain_one, shift_one = pull_one(grad_first_norm)
    grad_branch = grad_first.astype(jnp.bfloat16)
    attn_grad = jnp.einsum(
        "ra,rb->ab", attended_low, grad_branch, preferred_element_type=jnp.float32
    )
    bias_one = jnp.sum(grad_branch.astype(jnp.float32), axis=0)
    grad_attended = jnp.dot(grad_branch, w_attn.T, preferred_element_type=jnp.float32).astype(
        jnp.bfloat16
    )
    grad_query, grad_pairs = attend_backward(
        projected[:, :model_width], gathered, key_valid, log_sums, grad_attended, head_count
    )
    own_pairs = spread_group(grad_pairs, position, bit_count)
    grad_proj = jnp.concatenate([grad_query, own_pairs], 1).astype(jnp.bfloat16)
    qkv_grad = jnp.einsum("ra,rb->ab", hidden_low, grad_proj, preferred_element_type=jnp.float32)
    column_sums = jnp.sum(grad_proj.astype(jnp.float32), axis=0)
    qv_grad = jnp.stack([column_sums[:model_width], column_sums[2 * model_width :]])
    grad_hidden = grad_first + jnp.dot(grad_proj, w_qkv.T, preferred_element_type=jnp.float32)
    grad_list = (
        qkv_grad,
        qv_grad,
        attn_grad,
        jnp.stack([bias_one, bias_two]),
        in_grad,
        in_bias_grad,
        back_grad,
        jnp.stack([gain_one, gain_two]),
        jnp.stack([shift_one, shift_two]),
    )
    return (grad_hidden, grad_list)


def scatter_once(grad_list):
    (
        qkv_grad,
        qv_grad,
        attn_grad,
        bias_grad,
        in_grad,
        in_bias_grad,
        back_grad,
        gain_grad,
        shift_grad,
    ) = grad_list
    return (
        lax.psum_scatter(qkv_grad, "blk", scatter_dimension=0, tiled=True),
        lax.psum_scatter(qv_grad, "blk", scatter_dimension=1, tiled=True),
        lax.psum_scatter(attn_grad, "blk", scatter_dimension=0, tiled=True),
        lax.psum_scatter(bias_grad, "blk", scatter_dimension=1, tiled=True),
        lax.psum_scatter(in_grad, "blk", scatter_dimension=0, tiled=True),
        lax.psum_scatter(in_bias_grad, "blk", scatter_dimension=0, tiled=True),
        lax.psum_scatter(back_grad, "blk", scatter_dimension=1, tiled=True),
        lax.psum_scatter(gain_grad, "blk", scatter_dimension=1, tiled=True),
        lax.psum_scatter(shift_grad, "blk", scatter_dimension=1, tiled=True),
    )


def body(
    tokens,
    lengths,
    w_qkv,
    qv_bias,
    w_attn,
    out_bias,
    w_in,
    in_bias,
    w_back,
    norm_gain,
    norm_shift,
    cotangent,
):
    row_count = tokens.shape[1]
    head_count = HEADS
    cycle_size = lax.axis_size("blk")
    bit_count = cycle_size.bit_length() - 1
    position = lax.axis_index("blk")
    length = lengths[0]
    key_valid = jnp.arange(cycle_size * row_count) < length
    params = (w_qkv, qv_bias, w_attn, out_bias, w_in, in_bias, w_back, norm_gain, norm_shift)
    out_one, saved_one = layer_forward(
        tokens[0].astype(jnp.float32), params, key_valid, position, bit_count, head_count
    )
    out_two, saved_two = layer_forward(out_one, params, key_valid, position, bit_count, head_count)
    grad_hidden, grads_two = layer_backward(
        cotangent[0].astype(jnp.float32),
        saved_two,
        params,
        key_valid,
        position,
        bit_count,
        head_count,
    )
    grad_hidden, grads_one = layer_backward(
        grad_hidden, saved_one, params, key_valid, position, bit_count, head_count
    )
    shards = scatter_once(jax.tree.map(jnp.add, grads_two, grads_one))
    (
        qkv_part,
        qv_part,
        attn_part,
        bias_part,
        in_part,
        in_bias_part,
        back_part,
        gain_part,
        shift_part,
    ) = shards
    totals = (
        lax.psum(qkv_part.astype(jnp.bfloat16), "batch").astype(jnp.float32),
        lax.psum(qv_part.astype(jnp.bfloat16), "batch").astype(jnp.float32),
        lax.psum(attn_part.astype(jnp.bfloat16), "batch").astype(jnp.float32),
        lax.psum(bias_part.astype(jnp.bfloat16), "batch").astype(jnp.float32),
        lax.psum(in_part.astype(jnp.bfloat16), "batch").astype(jnp.float32),
        lax.psum(in_bias_part.astype(jnp.bfloat16), "batch").astype(jnp.float32),
        lax.psum(back_part.astype(jnp.bfloat16), "batch").astype(jnp.float32),
        lax.psum(gain_part.astype(jnp.bfloat16), "batch").astype(jnp.float32),
        lax.psum(shift_part.astype(jnp.bfloat16), "batch").astype(jnp.float32),
    )
    return (
        out_two.astype(jnp.bfloat16)[None],
        grad_hidden.astype(jnp.bfloat16)[None],
        totals[0],
        totals[1],
        totals[2],
        totals[3],
        totals[4],
        totals[5],
        totals[6],
        totals[7],
        totals[8],
    )


MESH = pl.DeviceIdType.MESH
f32 = jnp.float32
bf16 = jnp.bfloat16
FLIPS = ((0, 0), (1, 0), (0, 1), (1, 1))
GROUPS = len(FLIPS)
PART = 4096 // GROUPS
WIDE = 256
ROWS, D, FF, LEN, VEC = 128, 1024, 4096, 1024, 144


def dot(a, b):
    return jnp.dot(a, b, preferred_element_type=f32)


def dot_t(a, b):
    return lax.dot_general(a, b, (((1,), (1,)), ((), ())), preferred_element_type=f32)


def dot_0(a, b):
    return lax.dot_general(a, b, (((0,), (0,)), ((), ())), preferred_element_type=f32)


def span(at, size):
    return pl.ds(pl.multiple_of(at * size, size), size)


def flip(bit, by):
    return bit + by * (1 - 2 * bit)


def group(ref, n):
    return ref.at[pl.ds(n * ROWS, ROWS)]


class Spot:
    def __init__(self):
        self.row, self.pos = lax.axis_index("batch"), lax.axis_index("blk")
        self.x, self.c = self.row // 2, self.row % 2
        self.z, self.y = self.pos // 2, self.pos % 2
        self.zl, self.zh = self.z % 2, self.z // 2
        self.place = self.row * 2 + self.y

    def flipped(self, c=0, x=0, y=0, zl=0, zh=0):
        row = flip(self.x, x) * 2 + flip(self.c, c)
        pos = flip(self.zh, zh) * 4 + flip(self.zl, zl) * 2 + flip(self.y, y)
        return {"batch": row, "blk": pos}

    def member(self, place):
        return {"batch": place // 2, "blk": self.z * 2 + place % 2}

    def worker(self):
        return {"batch": self.z, "blk": (self.row + 3) % 4 * 2 + self.y}

    def owner(self):
        return {"batch": (self.z + 1) % 4, "blk": self.row * 2 + self.y}


class Link:
    def __init__(self, send_sem, recv_sem, own_sem):
        self.send_sem, self.recv_sem, self.own_sem = send_sem, recv_sem, own_sem
        self.count, self.own_count = 0, 0
        self.pending_send, self.pending_recv, self.pending_own = [], [], []

    def put(self, src, dst, device):
        at = self.count
        self.count += 1
        copy = pltpu.make_async_remote_copy(
            src_ref=src, dst_ref=dst, send_sem=self.send_sem.at[at], recv_sem=self.recv_sem.at[at],
            device_id=device, device_id_type=MESH,
        )
        copy.start()
        self.pending_send.append(copy)
        self.pending_recv.append(copy)
        return copy

    def keep(self, src, dst):
        copy = pltpu.make_async_copy(src, dst, self.own_sem.at[self.own_count])
        self.own_count += 1
        copy.start()
        self.pending_own.append(copy)
        return copy

    def arrive(self, copies):
        for copy in copies:
            if any(copy is other for other in self.pending_own):
                self.pending_own = [other for other in self.pending_own if other is not copy]
                copy.wait()
            else:
                self.pending_recv = [other for other in self.pending_recv if other is not copy]
                copy.wait_recv()

    def finish(self):
        self.arrive(self.pending_own + self.pending_recv)
        for copy in self.pending_send:
            copy.wait_send()


def signal_all(devices):
    barrier = pltpu.get_barrier_semaphore()
    for device in devices:
        pl.semaphore_signal(barrier, inc=1, device_id=device, device_id_type=MESH)
    return barrier, len(devices)


def standard(values):
    centered = values - jnp.mean(values, axis=-1, keepdims=True)
    inverse = lax.rsqrt(jnp.mean(centered * centered, axis=-1, keepdims=True) + eps)
    return centered * inverse, inverse


def standard_back(unit, inverse, gain, grad):
    scaled = grad * gain
    inner = jnp.mean(scaled * unit, axis=-1, keepdims=True)
    return inverse * (scaled - jnp.mean(scaled, axis=-1, keepdims=True) - unit * inner)


def column_sum(x):
    return jnp.sum(x.astype(f32), axis=0, keepdims=True)


def gelu_pair(u):
    t = 1.0 / (1.0 + 0.23164188 * jnp.abs(u))
    bell = jnp.exp(-0.5 * u * u)
    poly = t * (0.127414796 + t * (-0.142248368 + t * (0.7107068705 + t * (-0.7265760135 + t * 0.5307027145))))
    tail = poly * bell
    cdf = jnp.where(u < 0, tail, 1.0 - tail)
    return u * cdf, cdf + u * bell * 0.3989422804


def low_lanes():
    return lax.broadcasted_iota(jnp.int32, (1, 128), 1) < 64


def valid_keys(length):
    return lax.broadcasted_iota(jnp.int32, (1, LEN), 1).astype(f32) < length


def attention_rows(qkv, rows, valid):
    queries, keys, values = qkv[rows, 0:128], qkv[:, 128:256], qkv[:, 256:384]
    low_half = low_lanes()
    outs, lses = [], []
    for half in range(2):
        mine = low_half if half == 0 else jnp.logical_not(low_half)
        part = jnp.where(mine, queries, jnp.zeros_like(queries)) * jnp.asarray(0.125, bf16)
        scores = jnp.where(valid, dot_t(part, keys), -1e30)
        top = jnp.max(scores, axis=1, keepdims=True)
        expd = jnp.exp(scores - top)
        total = jnp.sum(expd, axis=1, keepdims=True)
        probs = (expd * (1.0 / total)).astype(bf16)
        outs.append(dot(probs, values))
        lses.append(top + jnp.log(total))
    return (
        jnp.where(low_half, outs[0], outs[1]).astype(bf16),
        jnp.where(low_half, lses[0], lses[1]),
    )


def attention_back_rows(qkv, grads_ref, lse_ref, rows, valid):
    keys, values = qkv[:, 128:256], qkv[:, 256:384]
    low_half = low_lanes()
    queries, grads, lse = qkv[rows, 0:128], grads_ref[rows, :], lse_ref[rows, :]
    dqs, dk, dv = [], None, None
    for half in range(2):
        mine = low_half if half == 0 else jnp.logical_not(low_half)
        q_part = jnp.where(mine, queries, jnp.zeros_like(queries)) * jnp.asarray(0.125, bf16)
        g_part = jnp.where(mine, grads, jnp.zeros_like(grads))
        scores = dot_t(q_part, keys)
        probs = jnp.where(valid, jnp.exp(scores - lse[:, 64 * half : 64 * half + 1]), 0.0)
        dp = dot_t(g_part, values)
        delta = jnp.sum(probs * dp, axis=1, keepdims=True)
        ds = (probs * (dp - delta)).astype(bf16)
        dqs.append(dot(ds, keys))
        dk_part, dv_part = dot_0(ds, q_part), dot_0(probs.astype(bf16), g_part)
        dk = dk_part if dk is None else dk + dk_part
        dv = dv_part if dv is None else dv + dv_part
    dq = (jnp.where(low_half, dqs[0], dqs[1]) * 0.125).astype(bf16)
    return dq, dk, dv


def send_columns(link, spot, source, target, part, landing):
    copies = []
    for step in list(range(1, 8)) + [0]:
        to = (spot.place + step) % 8
        src = source.at[:, pl.ds(pl.multiple_of(part * D + to * 128, 128), 128)]
        dst = target.at[span(spot.place, ROWS), pl.ds(landing * 128, 128)]
        copies.append(link.put(src, dst, spot.member(to)) if step else link.keep(src, dst))
    return copies


def pair_rows(spot, step):
    return span((spot.place // 2 + step) % 4, 256)


def send_rows(link, spot, source, target, step, part):
    same = (spot.place + 2 * step) % 8
    copies = []
    for n, to in enumerate((same, same + 1 - 2 * spot.y)):
        src = source.at[span(to, ROWS), pl.ds(part * 128, 128)]
        dst = target.at[:, pl.ds(pl.multiple_of(part * D + spot.place * 128, 128), 128)]
        copies.append(link.put(src, dst, spot.member(to)) if step or n else link.keep(src, dst))
    return copies


PAIR_STEPS = (1, 2, 3, 0)


def spec(**named):
    return named


def two(*entry):
    return [entry, entry]


MAIN_OUT = spec(
    mixed=((ROWS, D), bf16), qkv1=((LEN, 384), bf16), lse1=((LEN, 128), f32),
    left_attn=((4, ROWS, D), bf16), right_attn=((4 * ROWS, 512), bf16),
    left_back=((2 * GROUPS, ROWS, D), bf16), right_back=((2 * GROUPS * ROWS, PART), bf16),
    left_in=((2 * GROUPS, ROWS, D), bf16), right_in=((2 * GROUPS * ROWS, PART), bf16),
    hidden=((2, LEN, D), bf16), dqkv2=((LEN, 384), bf16),
    dzb1=((ROWS, D), bf16), du1=((ROWS, FF), bf16), dza1=((ROWS, D), bf16),
    do1=((ROWS, D), bf16), dr1=((ROWS, D), f32), vec=((8, D), f32), inb=((1, FF), f32),
    length=((8, 128), f32),
)
MAIN_SCRATCH = spec(
    w_qkv=((D, 3 * D), bf16), w_attn=((D, D), bf16), w_in=((D, FF), bf16), w_back=((FF, D), bf16),
    tok=((ROWS, D), bf16), cot=((ROWS, D), bf16), length=((8, 128), f32), sent_length=((8, 128), f32),
    proj=two((ROWS, 3 * D), bf16), qkv=two((LEN, 384), bf16), lse=two((LEN, 128), f32),
    o=two((LEN, 128), bf16), att=two((ROWS, D), bf16), n=two((ROWS, D), bf16),
    act=two((ROWS, FF), bf16), slope=two((ROWS, FF), bf16),
    unit_a=two((ROWS, D), f32), unit_b=two((ROWS, D), f32),
    inv_a=two((ROWS, 128), f32), inv_b=two((ROWS, 128), f32),
    hq2=((ROWS, D), bf16), h=((ROWS, D), f32), acc=((ROWS, D), f32), mixed=((ROWS, D), bf16),
    dzb=two((ROWS, D), bf16), du=two((ROWS, FF), bf16), dza=two((ROWS, D), bf16), do=two((ROWS, D), bf16),
    doh=((LEN, 128), bf16), dqkvh=((LEN, 384), bf16), dk=((LEN, 128), f32), dv=((LEN, 128), f32),
    dqkv=((ROWS, 3 * D), bf16), dr1=((ROWS, D), f32), vec=((8, D), f32), inb=((1, FF), f32),
)


class Refs:
    pass


def flat(entries):
    out = []
    for entry in entries.values():
        out += entry if isinstance(entry, list) else [entry]
    return out


def bind(entries, refs):
    got, it = Refs(), iter(refs)
    for name, entry in entries.items():
        setattr(got, name, [next(it) for _ in entry] if isinstance(entry, list) else next(it))
    return got


def main_kernel(*refs):
    (len_ref, tokens, cotangent, w_qkv, w_attn, w_in, w_back,
     qv_bias, out_bias, in_bias, gain, shift) = refs[:12]
    outs = bind(MAIN_OUT, refs[12 : 12 + len(MAIN_OUT)])
    rest = refs[12 + len(MAIN_OUT) :]
    s = bind(MAIN_SCRATCH, rest[:-4])
    load_sem, send_sem, recv_sem, own_sem = rest[-4:]
    spot = Spot()
    link = Link(send_sem, recv_sem, own_sem)
    others = [spot.member((spot.place + step) % 8) for step in range(1, 8)]
    others += [spot.flipped(c=dc, zl=dz) for dc, dz in FLIPS if dz]
    others += [spot.worker(), spot.owner()]
    barrier, expected = signal_all(others)

    loads = []
    for n, (src, dst) in enumerate(
        [(w_qkv.at[:, pl.ds(D * part, D)], s.w_qkv.at[:, pl.ds(D * part, D)]) for part in (1, 2, 0)]
        + [(w_attn, s.w_attn), (w_in, s.w_in), (w_back, s.w_back)]
    ):
        loads.append(pltpu.make_async_copy(src, dst, load_sem.at[n]))
        loads[n].start()
    loaded = set()

    def need(n):
        if n not in loaded:
            loaded.add(n)
            loads[n].wait()

    s.sent_length[...] = jnp.full((8, 128), len_ref[0], jnp.int32).astype(f32)
    pl.semaphore_wait(barrier, expected)
    first_in = [link.put(tokens, s.tok, spot.worker()), link.put(s.sent_length, s.length, spot.worker())]
    cot_in = link.put(cotangent, s.cot, spot.worker())
    link.arrive(first_in)
    valid = valid_keys(s.length[0:1, 0:1])

    def share(source, left, d):
        link.keep(source, left.at[d])
        for n, (dc, dz) in enumerate(FLIPS[1:], 1):
            link.put(source, left.at[2 * n + d], spot.flipped(c=dc, zl=dz))

    def part_of(c, zl):
        return c if GROUPS == 2 else c * 2 + zl

    def deal(source, right, d):
        link.keep(source.at[:, span(part_of(spot.c, spot.zl), PART)], group(right, d))
        for n, (dc, dz) in enumerate(FLIPS[1:], 1):
            cols = span(part_of(flip(spot.c, dc), flip(spot.zl, dz)), PART)
            link.put(source.at[:, cols], group(right, 2 * n + d), spot.flipped(c=dc, zl=dz))

    def gather(hq, d, part):
        rows = pl.ds(part * 64, 64)
        block = outs.hidden.at[d, pl.ds(pl.multiple_of(spot.place * ROWS + part * 64, 64), 64)]
        for dx, dy in ((1, 0), (0, 1), (1, 1)):
            link.put(hq.at[rows], block, spot.flipped(x=dx, y=dy))
        link.keep(hq.at[rows], block)

    def forward(d, hq, h):
        to_heads = []
        for part, number in ((1, 0), (2, 1), (0, 2)):
            need(number)

            def tile(i, carry):
                cols = span(2 * part + i, 512)
                value = dot(hq[...], s.w_qkv[:, cols])
                if part != 1:
                    value += qv_bias[part // 2 : part // 2 + 1, span(i, 512)]
                s.proj[d][:, cols] = value.astype(bf16)
                return carry

            lax.fori_loop(0, 2, tile, 0)
            to_heads += send_columns(link, spot, s.proj[d], s.qkv[d], part, part)
        link.arrive(to_heads)
        to_rows = []
        for step in PAIR_STEPS:
            rows = pair_rows(spot, step)
            s.o[d][rows, :], s.lse[d][rows, :] = attention_rows(s.qkv[d], rows, valid)
            to_rows += send_rows(link, spot, s.o[d], s.att[d], step, 0)
        if d == 0:
            link.keep(s.qkv[0], outs.qkv1)
            link.keep(s.lse[0], outs.lse1)
        link.arrive(to_rows)
        gather(s.tok, 0, d)
        need(3)
        unit, inverse = standard(h[...].astype(f32) + dot(s.att[d][...], s.w_attn[...]) + out_bias[0:1])
        link.keep(s.att[d], outs.left_attn.at[d])
        link.put(s.att[d], outs.left_attn.at[2 + d], spot.flipped(c=1))
        s.unit_a[d][...] = unit
        s.inv_a[d][...] = jnp.broadcast_to(inverse, (ROWS, 128))
        first = unit * gain[0:1] + shift[0:1]
        s.n[d][...] = first.astype(bf16)
        share(s.n[d], outs.left_in, d)
        s.acc[...] = first + out_bias[1:2]
        need(4)
        need(5)

        def inner(i, carry):
            cols = span(i, 512)
            act, slope = gelu_pair(dot(s.n[d][...], s.w_in[:, cols]) + in_bias[:, cols])
            act = act.astype(bf16)
            s.act[d][:, cols] = act
            s.slope[d][:, cols] = slope.astype(bf16)
            s.acc[...] += dot(act, s.w_back[cols, :])
            return carry

        lax.fori_loop(0, 8, inner, 0)
        deal(s.act[d], outs.right_back, d)
        unit, inverse = standard(s.acc[...])
        s.unit_b[d][...] = unit
        s.inv_b[d][...] = jnp.broadcast_to(inverse, (ROWS, 128))
        return unit * gain[1:2] + shift[1:2]

    def add_vec(at, value, fresh):
        s.vec[at : at + 1, :] = value if fresh else s.vec[at : at + 1, :] + value

    def backward(d, grad, fresh):
        unit = s.unit_b[d][...]
        add_vec(3, column_sum(grad * unit), fresh)
        add_vec(5, column_sum(grad), fresh)
        dr = standard_back(unit, s.inv_b[d][:, 0:1], gain[1:2], grad)
        s.acc[...] = dr
        low = dr.astype(bf16)
        s.dzb[d][...] = low
        if d:
            share(s.dzb[d], outs.left_back, d)
        else:
            link.keep(s.dzb[d], outs.dzb1)
        add_vec(1, column_sum(low), fresh)

        def inner(i, carry):
            cols = span(i, 512)
            du = (dot_t(s.dzb[d][...], s.w_back[cols, :]) * s.slope[d][:, cols].astype(f32)).astype(bf16)
            s.du[d][:, cols] = du
            total = column_sum(du)
            s.inb[:, cols] = total if fresh else s.inb[:, cols] + total
            s.acc[...] += dot_t(du, s.w_in[:, cols])
            return carry

        lax.fori_loop(0, 8, inner, 0)
        if d:
            deal(s.du[d], outs.right_in, d)
        else:
            link.keep(s.du[d], outs.du1)
        grad = s.acc[...]
        unit = s.unit_a[d][...]
        add_vec(2, column_sum(grad * unit), fresh)
        add_vec(4, column_sum(grad), fresh)
        dr = standard_back(unit, s.inv_a[d][:, 0:1], gain[0:1], grad)
        s.dr1[...] = dr
        low = dr.astype(bf16)
        s.dza[d][...] = low
        if d:
            link.keep(s.dza[d].at[:, span(spot.c, 512)], group(outs.right_attn, d))
            link.put(s.dza[d].at[:, span(1 - spot.c, 512)], group(outs.right_attn, 2 + d), spot.flipped(c=1))
        else:
            link.keep(s.dza[d], outs.dza1)
        add_vec(0, column_sum(low), fresh)
        s.do[d][...] = dot_t(low, s.w_attn[...]).astype(bf16)

    out = forward(0, s.tok, s.tok)
    s.h[...] = out
    s.hq2[...] = out.astype(bf16)
    out = forward(1, s.hq2, s.h)
    s.mixed[...] = out.astype(bf16)
    link.put(s.mixed, outs.mixed, spot.owner())
    link.arrive([cot_in])
    gather(s.hq2, 1, 0)
    backward(1, s.cot[...].astype(f32), True)
    link.arrive(send_columns(link, spot, s.do[1], s.doh, 0, 0))
    to_rows = attention_back(link, spot, s.qkv[1], s.doh, s.lse[1], s.dqkvh, s.dk, s.dv, s.dqkv, valid)
    link.keep(s.dqkvh, outs.dqkv2)
    link.arrive(to_rows)
    gather(s.hq2, 1, 1)
    backward(0, s.dr1[...] + dot_t(s.dqkv[...], s.w_qkv[...]), False)
    link.keep(s.do[0], outs.do1)
    link.keep(s.dr1, outs.dr1)
    link.keep(s.vec, outs.vec)
    link.keep(s.inb, outs.inb)
    link.keep(s.length, outs.length)
    link.finish()


def attention_back_step(link, spot, step, qkv, doh, lse, dqkvh, dk_ref, dv_ref, dqkv, valid):
    rows = pair_rows(spot, step)
    dq, dk, dv = attention_back_rows(qkv, doh, lse, rows, valid)
    dqkvh[rows, 0:128] = dq
    dk_ref[...] = dk if step == PAIR_STEPS[0] else dk_ref[...] + dk
    dv_ref[...] = dv if step == PAIR_STEPS[0] else dv_ref[...] + dv
    return send_rows(link, spot, dqkvh, dqkv, step, 0)


def attention_back_end(link, spot, dqkvh, dk_ref, dv_ref, dqkv):
    dqkvh[:, 128:256] = dk_ref[...].astype(bf16)
    dqkvh[:, 256:384] = dv_ref[...].astype(bf16)
    copies = []
    for part in (1, 2):
        for step in PAIR_STEPS:
            copies += send_rows(link, spot, dqkvh, dqkv, step, part)
    return copies


def attention_back(link, spot, qkv, doh, lse, dqkvh, dk_ref, dv_ref, dqkv, valid):
    copies = []
    for step in PAIR_STEPS:
        copies += attention_back_step(link, spot, step, qkv, doh, lse, dqkvh, dk_ref, dv_ref, dqkv, valid)
    return copies + attention_back_end(link, spot, dqkvh, dk_ref, dv_ref, dqkv)


def main_call(length, tokens, cotangent, params):
    w_qkv, qv_bias, w_attn, out_bias, w_in, in_bias, w_back, gain, shift = params
    dma = pltpu.SemaphoreType.DMA
    vmem, hbm = pl.BlockSpec(memory_space=pltpu.VMEM), pl.BlockSpec(memory_space=pl.ANY)
    results = pl.pallas_call(
        main_kernel,
        out_shape=[jax.ShapeDtypeStruct(*entry) for entry in MAIN_OUT.values()],
        in_specs=[pl.BlockSpec(memory_space=pltpu.SMEM), hbm, hbm] + [hbm] * 4 + [vmem] * 5,
        out_specs=[hbm] * len(MAIN_OUT),
        scratch_shapes=[pltpu.VMEM(*entry) for entry in flat(MAIN_SCRATCH)]
        + [dma((6,)), dma((160,)), dma((160,)), dma((60,))],
        compiler_params=pltpu.CompilerParams(
            collective_id=1, has_side_effects=True, vmem_limit_bytes=60 * 2**20
        ),
    )(length, tokens, cotangent, w_qkv, w_attn, w_in, w_back, qv_bias, out_bias, in_bias[None], gain, shift)
    return bind(MAIN_OUT, results)


PATHS = spec(A="yxabXC", B="xyabXC", C="abysC", D="yxbSWK", E="xybSWK")
CHUNKS = "BEDEEDDDD"
PER = PART // WIDE
ORDER = (
    (100, 12), (0, -1), (100, 13), (100, 1), (100, 2), (100, 3), (100, 4), (100, 14), (1, -1), (2, -1),
    (0, 0), (3, -1), (100, 5), (100, 10), (100, 6), (2, 0), (4, -1), (1, 0), (5, -1), (0, 1),
    (3, 0), (6, -1), (100, 7), (100, 9), (0, 2), (1, 1), (2, 1), (5, 0), (4, 0), (7, -1),
    (8, -1), (3, 1), (100, 8), (6, 0), (5, 1), (0, 3), (4, 1), (1, 2), (2, 2), (7, 0),
    (3, 2), (6, 1), (5, 2), (0, 4), (8, 0), (1, 3), (0, 5), (4, 2), (2, 3), (3, 3),
    (7, 1), (5, 3), (6, 2), (4, 3), (8, 1), (1, 4), (6, 3), (7, 2), (2, 4), (1, 5),
    (3, 4), (2, 5), (7, 3), (8, 2), (5, 4), (3, 5), (4, 4), (5, 5), (8, 3), (6, 4),
    (4, 5), (7, 4), (6, 5), (8, 4), (7, 5), (8, 5),
)
IN_OUT = spec(back=0, fore=FF, attn=2 * FF, qkv=2 * FF + D)


def plan(path, width):
    slabs, steps = 8, []
    for stage in path:
        if stage in "yab":
            slabs //= 2
        elif stage == "x":
            width //= 2
        elif stage in "XW":
            width *= 2
        steps.append((stage, slabs, width))
    return steps


def weight_of(c):
    return (0, 0) if c == 0 else (1 + (c - 1) // PER, (c - 1) % PER)


def chunk_rows(c):
    return VEC if c == 0 else ROWS


WIDTHS = [512] + [WIDE] * (2 * PER)
PLANS = [plan(PATHS[name], width) for name, width in zip(CHUNKS, WIDTHS)]
GRAD_SCRATCH = spec(
    left=[((4, ROWS, D), bf16)] + two((2 * GROUPS, ROWS, D), bf16),
    right=[((4 * ROWS, 512), bf16)] + two((2 * GROUPS * ROWS, PART), bf16),
    turned=[((D, 512), bf16)] + two((D, 256 * GROUPS), bf16),
    chunk=[((8, chunk_rows(c), WIDTHS[c]), bf16) for c in range(len(CHUNKS))],
    landing=[
        ((slabs, chunk_rows(c), width), bf16)
        for c, steps in enumerate(PLANS) for stage, slabs, width in steps if stage in "yabxs"
    ],
    hidden=two((LEN, D), bf16), dqkvh=two((LEN, 384), bf16),
    chunk_q=((8, VEC, 384), bf16), landing_q=[((4, VEC, 384), bf16), ((2, VEC, 384), bf16)],
    qkv=((LEN, 384), bf16), lse=((LEN, 128), f32), doh=((LEN, 128), bf16),
    dk=((LEN, 128), f32), dv=((LEN, 128), f32), dqkv=((ROWS, 3 * D), bf16), w_qkv=((D, 3 * D), bf16),
    dr1=((ROWS, D), f32), grad=((ROWS, D), bf16), vec=((8, D), f32), inb=((1, FF), f32), length=((8, 128), f32),
)


def grad_kernel(*refs):
    src = bind(MAIN_OUT, refs[: len(MAIN_OUT)])
    w_qkv, sums, grad_out = refs[len(MAIN_OUT) : len(MAIN_OUT) + 3]
    rest = refs[len(MAIN_OUT) + 3 :]
    s = bind(GRAD_SCRATCH, rest[:-3])
    s.out = sums
    spot = Spot()
    link = Link(*rest[-3:])
    x, y, c, zl, zh = spot.x, spot.y, spot.c, spot.zl, spot.zh
    others = [spot.member((spot.place + step) % 8) for step in range(1, 8)]
    others += [spot.flipped(zl=1), spot.flipped(c=1, zl=1), spot.flipped(zh=1)]
    others += [spot.worker(), spot.owner()]
    barrier, expected = signal_all(others)

    def part_of(c, zl):
        return c if GROUPS == 2 else c * 2 + zl

    mine = span(part_of(c, zl), PART)
    heads_in = [link.keep(src.qkv1, s.qkv), link.keep(src.lse1, s.lse), link.keep(src.length, s.length)]
    ready = [[], [], []]
    ready[0] += [link.keep(src.left_attn, s.left[0]), link.keep(group(src.right_attn, 1), group(s.right[0], 1))]
    ready[0] += [link.keep(group(src.right_attn, 3), group(s.right[0], 3))]
    ready[0] += [link.keep(src.dza1.at[:, span(c, 512)], group(s.right[0], 0))]
    ready[1] += [link.keep(src.dzb1, s.left[1].at[0]), link.keep(src.right_back, s.right[1])]
    ready[1] += [link.keep(src.left_back.at[2 * n + 1], s.left[1].at[2 * n + 1]) for n in range(GROUPS)]
    ready_left = link.keep(src.left_in, s.left[2])
    ready[2] += [link.keep(src.du1.at[:, mine], group(s.right[2], 0))]
    ready[2] += [link.keep(group(src.right_in, 2 * n + 1), group(s.right[2], 2 * n + 1)) for n in range(GROUPS)]
    vec_in = [link.keep(src.vec, s.vec), link.keep(src.inb, s.inb)]
    hidden_in = []
    halves = [pl.ds(pl.multiple_of(half * 512 + c * 256, 256), 256) for half in range(2)]
    for d in range(2):
        hidden_in += [link.keep(src.hidden.at[d, rows], s.hidden[d].at[rows]) for rows in halves]
    dqkv_in = link.keep(src.dqkv2, s.dqkvh[1])
    close_in = [link.keep(w_qkv, s.w_qkv), link.keep(src.dr1, s.dr1)]
    pl.semaphore_wait(barrier, expected)
    to_heads = send_columns(link, spot, src.do1, s.doh, 0, 0)
    ready[0].append(link.put(src.dza1.at[:, span(1 - c, 512)], group(s.right[0], 2), spot.flipped(c=1)))
    for n, (dc, dz) in enumerate(FLIPS[1:], 1):
        ready[1].append(link.put(src.dzb1, s.left[1].at[2 * n], spot.flipped(c=dc, zl=dz)))
    for n, (dc, dz) in enumerate(FLIPS[1:], 1):
        cols = span(part_of(flip(c, dc), flip(zl, dz)), PART)
        ready[2].append(link.put(src.du1.at[:, cols], group(s.right[2], 2 * n), spot.flipped(c=dc, zl=dz)))

    for d in range(2):
        hidden_in += [link.put(src.hidden.at[d, rows], s.hidden[d].at[rows], spot.flipped(c=1)) for rows in halves]

    bits = spec(y=y, a=zl, b=zh)
    across = spec(
        y=spot.flipped(y=1), a=spot.flipped(zl=1), b=spot.flipped(zh=1), x=spot.flipped(x=1), C=spot.flipped(c=1)
    )
    across.update(spec(S=across["a"], X=across["x"], W=across["x"], s=across["x"], K=across["C"]))
    current, landing, copies = {}, {}, {}
    it = iter(s.landing)
    for n, steps in enumerate(PLANS):
        for i, step in enumerate(steps):
            if step[0] in "yabxs":
                landing[n, i] = next(it)
    waiting = [True, True, True]

    def turn(k):
        link.arrive([ready_left] if k == 2 else ready[k])
        count = s.left[k].shape[0]
        for g in range(count):
            s.turned[k][:, pl.ds(ROWS * g, ROWS)] = s.left[k][g].T

    def compute(n):
        k, at = weight_of(n)
        if k == 2 and waiting[2]:
            waiting[2] = False
            link.arrive(ready[2])
        path = [stage for stage in PATHS[CHUNKS[n]] if stage in "yab"]
        path += [stage for stage in "yab" if stage not in path]
        wide = WIDTHS[n]

        def piece(i, carry):
            product = dot(s.turned[k][span(i, 256), :], s.right[k][:, pl.ds(at * wide, wide)]).astype(bf16)
            for low in range(2):
                bit = spec(y=low, a=i % 2, b=i // 2)
                at_slab = (bit[path[0]] * 2 + bit[path[1]]) * 2 + bit[path[2]]
                s.chunk[n][at_slab, 0:ROWS] = product[ROWS * low : ROWS * (low + 1)]
            return carry

        lax.fori_loop(0, 4, piece, 0)
        if n == 0:
            link.arrive(vec_in)
            for shard in range(8):
                bit = spec(y=shard % 2, a=shard // 2 % 2, b=shard // 4)
                at_slab = (bit[path[0]] * 2 + bit[path[1]]) * 2 + bit[path[2]]
                vec = s.vec[:, pl.ds(shard * 128, 128)]
                top = jnp.concatenate([vec, jnp.zeros((8, 384), f32)], 1)
                low = jnp.broadcast_to(s.inb[:, pl.ds(shard * 512, 512)], (8, 512))
                s.chunk[n][at_slab, ROWS:VEC] = jnp.concatenate([top, low], 0).astype(bf16)
        current[n] = s.chunk[n]

    def base_of(n):
        k, at = weight_of(n)
        if k == 0:
            return IN_OUT["attn"] + c * 512 + at * WIDE, 0
        start = IN_OUT["back"] if k == 1 else IN_OUT["fore"]
        if GROUPS == 2:
            return start + c * PART + at * WIDE, 0
        return start + c * 2 * PART + at * WIDE, PART

    def columns(n, quarter, offset, width):
        start, stride = base_of(n)
        return pl.ds(pl.multiple_of(start + quarter * stride + offset, 128), width)

    def send(n, i):
        stage, slabs, width = PLANS[n][i]
        rows = pl.ds(0, chunk_rows(n))
        now, todo = current[n], []
        if stage in "yab":
            todo.append((now.at[pl.ds((1 - bits[stage]) * slabs, slabs)], landing[n, i]))
        elif stage == "x":
            todo.append((now.at[:, :, pl.ds(pl.multiple_of((1 - x) * width, 128), width)], landing[n, i]))
        elif stage == "s":
            todo.append((now, landing[n, i]))
        elif stage == "S":
            todo.append((now.at[1 - zl], s.out.at[rows, columns(n, zl, x * width, width)]))
        else:
            offset = x * (width // 2) if stage in "XW" else 0
            width = width // 2 if stage in "XW" else width
            for quarter in range(2 if stage in "WK" else 1):
                where = s.out.at[rows, columns(n, quarter, offset, width)]
                todo.append((where, where))
        copies[n, i] = [link.put(here, there, across[stage]) for here, there in todo]

    def advance(n, i):
        stage, slabs, width = PLANS[n][i]
        link.arrive(copies[n, i])
        if stage not in "yabxs":
            return
        got, old = landing[n, i], current[n]

        def add(m, carry):
            if stage in "yab":
                kept = old[bits[stage] * slabs + m]
            elif stage == "x":
                kept = old[m, :, pl.ds(pl.multiple_of(x * width, 128), width)]
            else:
                kept = old[m]
            got[m] = (got[m].astype(f32) + kept.astype(f32)).astype(bf16)
            return carry

        lax.fori_loop(0, slabs, add, 0)
        current[n] = got
        follow = PLANS[n][i + 1][0]
        if follow in "SXC":
            offset = 0 if follow == "C" else x * width
            quarter = zl if follow == "S" else 0
            s.out[0 : chunk_rows(n), columns(n, quarter, offset, width)] = got[zl if follow == "S" else 0]

    state = Refs()
    state.rows = []

    def fold_q(n, bit):
        got = s.landing_q[n]
        slabs = got.shape[0]
        old = s.chunk_q if n == 0 else s.landing_q[0]

        def add(m, carry):
            got[m] = (got[m].astype(f32) + old[bit * slabs + m].astype(f32)).astype(bf16)
            return carry

        lax.fori_loop(0, slabs, add, 0)

    def task(k):
        if k == 1:
            link.arrive(to_heads + heads_in)
            state.valid = valid_keys(s.length[0:1, 0:1])
        if k <= 4:
            state.rows += attention_back_step(
                link, spot, PAIR_STEPS[k - 1], s.qkv, s.doh, s.lse, s.dqkvh[0], s.dk, s.dv, s.dqkv, state.valid
            )
        elif k == 5:
            state.rows += attention_back_end(link, spot, s.dqkvh[0], s.dk, s.dv, s.dqkv)
        elif k == 6:
            link.arrive([dqkv_in])

            def piece(i, carry):
                here = span(i, 256)
                product = dot_0(s.hidden[0][:, here], s.dqkvh[0][...])
                product += dot_0(s.hidden[1][:, here], s.dqkvh[1][...])
                product = product.astype(bf16)
                for low in range(2):
                    at_slab = (i % 2) * 4 + (i // 2) * 2 + low
                    s.chunk_q[at_slab, 0:ROWS] = product[ROWS * low : ROWS * (low + 1)]
                return carry

            lax.fori_loop(0, 4, piece, 0)
            total = column_sum(s.dqkvh[0][...]) + column_sum(s.dqkvh[1][...])
            extra = jnp.broadcast_to(total, (16, 384)).astype(bf16)
            for at_slab in range(8):
                s.chunk_q[at_slab, ROWS:VEC] = extra
            state.q = [link.put(s.chunk_q.at[pl.ds((1 - zl) * 4, 4)], s.landing_q[0], across["a"])]
        elif k == 7:
            link.arrive(state.q)
            fold_q(0, zl)
            state.q = [link.put(s.landing_q[0].at[pl.ds((1 - zh) * 2, 2)], s.landing_q[1], across["b"])]
        elif k == 8:
            link.arrive(state.q)
            fold_q(1, zh)
            cols = pl.ds(pl.multiple_of(IN_OUT["qkv"] + spot.place * 384, 128), 384)
            where = s.out.at[:, cols]
            for dx in range(2):
                for dc in range(2):
                    for dy in range(2):
                        slab = s.landing_q[1].at[flip(y, dy)]
                        if dx + dc + dy:
                            link.put(slab, where, spot.flipped(c=dc, x=dx, y=dy))
            s.out[:, cols] = s.landing_q[1][y]
        elif k == 9:
            link.arrive(state.rows + close_in)
            s.grad[...] = (s.dr1[...] + dot_t(s.dqkv[...], s.w_qkv[...])).astype(bf16)
            link.put(s.grad, grad_out, spot.owner())
        elif k == 10:
            link.arrive(hidden_in)
        elif k in (12, 13, 14):
            turn((0, 2, 1)[k - 12])

    for n, i in ORDER:
        if n == 100:
            task(i)
            continue
        if i < 0:
            compute(n)
        else:
            advance(n, i)
        if i + 1 < len(PLANS[n]):
            send(n, i + 1)
    link.finish()


def grad_call(main, w_qkv):
    dma = pltpu.SemaphoreType.DMA
    hbm = pl.BlockSpec(memory_space=pl.ANY)
    return pl.pallas_call(
        grad_kernel,
        out_shape=[jax.ShapeDtypeStruct((VEC, 12 * D), bf16), jax.ShapeDtypeStruct((ROWS, D), bf16)],
        in_specs=[hbm] * (len(MAIN_OUT) + 1),
        out_specs=[pl.BlockSpec(memory_space=pltpu.VMEM), hbm],
        scratch_shapes=[pltpu.VMEM(*entry) for entry in flat(GRAD_SCRATCH)]
        + [dma((240,)), dma((240,)), dma((60,))],
        compiler_params=pltpu.CompilerParams(
            collective_id=2, has_side_effects=True, vmem_limit_bytes=60 * 2**20
        ),
    )(*[getattr(main, name) for name in MAIN_OUT], w_qkv)


def finish_kernel(sums, qkv, qv, attn, bias, fore, fore_bias, back, gain, shift):
    at = IN_OUT
    for part in range(8):
        rows = pl.ds(part * 512, 512)
        back[rows, :] = sums[0:ROWS, pl.ds(at["back"] + part * 512, 512)].astype(f32).T
        fore[:, rows] = sums[0:ROWS, pl.ds(at["fore"] + part * 512, 512)].astype(f32)
    attn[...] = sums[0:ROWS, pl.ds(at["attn"], D)].astype(f32)
    total = jnp.zeros((16, 384), f32)
    for place in range(8):
        for part in range(3):
            here = pl.ds(at["qkv"] + place * 384 + part * 128, 128)
            qkv[:, pl.ds(part * D + place * 128, 128)] = sums[0:ROWS, here].astype(f32)
    mine = lax.axis_index("blk")
    for place in range(8):
        block = sums[ROWS:VEC, pl.ds(at["qkv"] + place * 384, 384)].astype(f32)
        total = total + jnp.where(mine == place, block, jnp.zeros_like(block))
    qv[0:1, :] = total[0:1, 0:128]
    qv[1:2, :] = total[0:1, 256:384]
    small = sums[ROWS:VEC, pl.ds(at["attn"], 512)].astype(f32) + sums[ROWS:VEC, pl.ds(at["attn"] + 512, 512)].astype(f32)
    bias[...] = small[0:2, 0:128]
    gain[...] = small[2:4, 0:128]
    shift[...] = small[4:6, 0:128]
    fore_bias[...] = small[8:9, :]


def finish_call(sums):
    shapes = [(ROWS, 3 * D), (2, 128), (ROWS, D), (2, 128), (ROWS, FF), (1, 512), (FF, 128), (2, 128), (2, 128)]
    return pl.pallas_call(
        finish_kernel,
        out_shape=[jax.ShapeDtypeStruct(shape, f32) for shape in shapes],
        compiler_params=pltpu.CompilerParams(vmem_limit_bytes=40 * 2**20),
    )(sums)


def fast_body(tokens, lengths, *rest):
    params, cotangent = rest[:-1], rest[-1]
    main = main_call(lengths, tokens[0], cotangent[0], params)
    sums, grad = grad_call(main, params[0])
    qkv, qv, attn, bias, fore, fore_bias, back, gain, shift = finish_call(sums)
    return (
        main.mixed[None], grad[None], qkv, qv, attn, bias, fore, fore_bias.reshape(512), back, gain, shift,
    )


def solution(mesh):
    placed = (
        P("batch", "blk", None),
        P("batch"),
        P(),
        P(),
        P(),
        P(),
        P(),
        P(),
        P(),
        P(),
        P(),
        P("batch", "blk", None),
    )
    fast = dict(mesh.shape) == {"batch": 4, "blk": 8}
    return jax.shard_map(
        fast_body if fast else body,
        mesh=mesh,
        in_specs=placed,
        out_specs=(
            P("batch", "blk", None),
            P("batch", "blk", None),
            P("blk", None),
            P(None, "blk"),
            P("blk", None),
            P(None, "blk"),
            P("blk", None),
            P("blk"),
            P(None, "blk"),
            P(None, "blk"),
            P(None, "blk"),
        ),
        check_vma=False,
    )
```

```python
import math

import jax
import jax.numpy as jnp
from jax import lax
from jax.experimental import pallas as pl
from jax.experimental.pallas import tpu as pltpu
from jax.sharding import PartitionSpec as P

HEADS = 16


eps = 1e-12


def from_partner(x, axis, distance):
    return lax.ppermute(x, axis, [(i, i ^ 1 << distance) for i in range(lax.axis_size(axis))])


def normalize(values, gain, shift):
    centered = values - jnp.mean(values, axis=-1, keepdims=True)
    variance = jnp.mean(centered * centered, axis=-1, keepdims=True)
    return centered * lax.rsqrt(variance + eps) * gain + shift


def gelu_exact(values):
    return jax.nn.gelu(values, approximate=False)


def head_split(matrix, head_count):
    row_count, model_width = matrix.shape
    return matrix.reshape(row_count, head_count // 4, 4, model_width // head_count).transpose(
        1, 2, 0, 3
    )


def head_merge(stacked):
    group_count, group_size, row_count, head_size = stacked.shape
    return stacked.transpose(2, 0, 1, 3).reshape(row_count, group_count * group_size * head_size)


def core_forward(query_part, key_part, value_part, key_valid, scale):
    scores = (
        jnp.einsum("hqd,hkd->hqk", query_part, key_part, preferred_element_type=jnp.float32) * scale
    )
    masked = jnp.where(key_valid, scores, -1e30)
    row_max = jnp.max(masked, axis=-1, keepdims=True)
    exp_scores = jnp.where(key_valid, jnp.exp(masked - row_max), 0.0)
    row_total = jnp.sum(exp_scores, axis=-1, keepdims=True)
    prob_low = (exp_scores / row_total).astype(jnp.bfloat16)
    output = jnp.einsum("hqk,hkd->hqd", prob_low, value_part, preferred_element_type=jnp.float32)
    return (output, (row_max + jnp.log(row_total))[..., 0])


def core_backward(query_part, key_part, value_part, grad_part, log_part, key_valid, scale):
    scores = (
        jnp.einsum("hqd,hkd->hqk", query_part, key_part, preferred_element_type=jnp.float32) * scale
    )
    probs = jnp.where(key_valid, jnp.exp(scores - log_part[..., None]), 0.0)
    grad_probs = jnp.einsum(
        "hqd,hkd->hqk", grad_part, value_part, preferred_element_type=jnp.float32
    )
    inner_sum = jnp.sum(probs * grad_probs, axis=-1, keepdims=True)
    grad_scores = (probs * (grad_probs - inner_sum)).astype(jnp.bfloat16)
    grad_query = (
        jnp.einsum("hqk,hkd->hqd", grad_scores, key_part, preferred_element_type=jnp.float32)
        * scale
    )
    grad_key = (
        jnp.einsum("hqk,hqd->hkd", grad_scores, query_part, preferred_element_type=jnp.float32)
        * scale
    )
    grad_value = jnp.einsum(
        "hqk,hqd->hkd", probs.astype(jnp.bfloat16), grad_part, preferred_element_type=jnp.float32
    )
    return (grad_query, grad_key, grad_value)


def gather_group(kv_pair, position, bit_count):
    buffer_rows = kv_pair
    for step_bit in range(bit_count):
        received = from_partner(buffer_rows, "blk", step_bit)
        high_side = position >> step_bit & 1 == 1
        buffer_rows = jnp.where(
            high_side,
            jnp.concatenate([received, buffer_rows], 0),
            jnp.concatenate([buffer_rows, received], 0),
        )
    return buffer_rows


def spread_group(partials, position, bit_count):
    for step_bit in reversed(range(bit_count)):
        half_rows = partials.shape[0] // 2
        high_side = position >> step_bit & 1 == 1
        lower_part = partials[:half_rows]
        upper_part = partials[half_rows:]
        kept_part = jnp.where(high_side, upper_part, lower_part)
        sent_part = jnp.where(high_side, lower_part, upper_part)
        partials = kept_part + from_partner(sent_part.astype(jnp.bfloat16), "blk", step_bit).astype(
            sent_part.dtype
        )
    return partials


def attend_forward(queries, gathered, key_valid, head_count):
    model_width = queries.shape[1]
    scale = (model_width // head_count) ** (-0.5)
    query_heads = head_split(queries, head_count)
    key_heads = head_split(gathered[:, :model_width], head_count)
    value_heads = head_split(gathered[:, model_width:], head_count)

    def one_group(operands):
        query_part, key_part, value_part = operands
        return core_forward(query_part, key_part, value_part, key_valid, scale)

    outputs, log_sums = lax.map(one_group, (query_heads, key_heads, value_heads))
    return (head_merge(outputs), log_sums)


def attend_backward(queries, gathered, key_valid, log_sums, grad_attended, head_count):
    model_width = queries.shape[1]
    scale = (model_width // head_count) ** (-0.5)
    query_heads = head_split(queries, head_count)
    key_heads = head_split(gathered[:, :model_width], head_count)
    value_heads = head_split(gathered[:, model_width:], head_count)
    grad_heads = head_split(grad_attended, head_count)

    def one_group(operands):
        query_part, key_part, value_part, grad_part, log_part = operands
        return core_backward(
            query_part, key_part, value_part, grad_part, log_part, key_valid, scale
        )

    grad_query, grad_key, grad_value = lax.map(
        one_group, (query_heads, key_heads, value_heads, grad_heads, log_sums)
    )
    return (
        head_merge(grad_query),
        jnp.concatenate([head_merge(grad_key), head_merge(grad_value)], 1),
    )


def layer_forward(hidden, params, key_valid, position, bit_count, head_count):
    w_qkv, qv_bias, w_attn, out_bias, w_in, in_bias, w_back, norm_gain, norm_shift = params
    model_width = hidden.shape[1]
    hidden_low = hidden.astype(jnp.bfloat16)
    bias_row = jnp.concatenate([qv_bias[0], jnp.zeros_like(qv_bias[0]), qv_bias[1]])
    projected = (jnp.dot(hidden_low, w_qkv, preferred_element_type=jnp.float32) + bias_row).astype(
        jnp.bfloat16
    )
    gathered = gather_group(projected[:, model_width:], position, bit_count)
    attended, log_sums = attend_forward(projected[:, :model_width], gathered, key_valid, head_count)
    attended_low = attended.astype(jnp.bfloat16)
    first_sum = (
        hidden + jnp.dot(attended_low, w_attn, preferred_element_type=jnp.float32) + out_bias[0]
    )
    first_norm = normalize(first_sum, norm_gain[0], norm_shift[0])
    first_low = first_norm.astype(jnp.bfloat16)
    inner_pre = jnp.dot(first_low, w_in, preferred_element_type=jnp.float32) + in_bias
    activated = gelu_exact(inner_pre).astype(jnp.bfloat16)
    second_sum = (
        first_norm + jnp.dot(activated, w_back, preferred_element_type=jnp.float32) + out_bias[1]
    )
    output = normalize(second_sum, norm_gain[1], norm_shift[1])
    saved_state = (
        hidden_low,
        projected,
        gathered,
        log_sums,
        attended_low,
        first_sum,
        first_low,
        inner_pre,
        activated,
        second_sum,
    )
    return (output, saved_state)


def layer_backward(grad_output, saved_state, params, key_valid, position, bit_count, head_count):
    w_qkv, qv_bias, w_attn, out_bias, w_in, in_bias, w_back, norm_gain, norm_shift = params
    (
        hidden_low,
        projected,
        gathered,
        log_sums,
        attended_low,
        first_sum,
        first_low,
        inner_pre,
        activated,
        second_sum,
    ) = saved_state
    model_width = hidden_low.shape[1]
    unused_two, pull_two = jax.vjp(normalize, second_sum, norm_gain[1], norm_shift[1])
    grad_second, gain_two, shift_two = pull_two(grad_output)
    grad_branch_two = grad_second.astype(jnp.bfloat16)
    back_grad = jnp.einsum(
        "ra,rb->ab", activated, grad_branch_two, preferred_element_type=jnp.float32
    )
    bias_two = jnp.sum(grad_branch_two.astype(jnp.float32), axis=0)
    grad_act = jnp.dot(grad_branch_two, w_back.T, preferred_element_type=jnp.float32)
    unused_gelu, pull_gelu = jax.vjp(gelu_exact, inner_pre)
    grad_inner = pull_gelu(grad_act)[0].astype(jnp.bfloat16)
    in_grad = jnp.einsum("ra,rb->ab", first_low, grad_inner, preferred_element_type=jnp.float32)
    in_bias_grad = jnp.sum(grad_inner.astype(jnp.float32), axis=0)
    grad_first_norm = grad_second + jnp.dot(grad_inner, w_in.T, preferred_element_type=jnp.float32)
    unused_one, pull_one = jax.vjp(normalize, first_sum, norm_gain[0], norm_shift[0])
    grad_first, gain_one, shift_one = pull_one(grad_first_norm)
    grad_branch = grad_first.astype(jnp.bfloat16)
    attn_grad = jnp.einsum(
        "ra,rb->ab", attended_low, grad_branch, preferred_element_type=jnp.float32
    )
    bias_one = jnp.sum(grad_branch.astype(jnp.float32), axis=0)
    grad_attended = jnp.dot(grad_branch, w_attn.T, preferred_element_type=jnp.float32).astype(
        jnp.bfloat16
    )
    grad_query, grad_pairs = attend_backward(
        projected[:, :model_width], gathered, key_valid, log_sums, grad_attended, head_count
    )
    own_pairs = spread_group(grad_pairs, position, bit_count)
    grad_proj = jnp.concatenate([grad_query, own_pairs], 1).astype(jnp.bfloat16)
    qkv_grad = jnp.einsum("ra,rb->ab", hidden_low, grad_proj, preferred_element_type=jnp.float32)
    column_sums = jnp.sum(grad_proj.astype(jnp.float32), axis=0)
    qv_grad = jnp.stack([column_sums[:model_width], column_sums[2 * model_width :]])
    grad_hidden = grad_first + jnp.dot(grad_proj, w_qkv.T, preferred_element_type=jnp.float32)
    grad_list = (
        qkv_grad,
        qv_grad,
        attn_grad,
        jnp.stack([bias_one, bias_two]),
        in_grad,
        in_bias_grad,
        back_grad,
        jnp.stack([gain_one, gain_two]),
        jnp.stack([shift_one, shift_two]),
    )
    return (grad_hidden, grad_list)


def scatter_once(grad_list):
    (
        qkv_grad,
        qv_grad,
        attn_grad,
        bias_grad,
        in_grad,
        in_bias_grad,
        back_grad,
        gain_grad,
        shift_grad,
    ) = grad_list
    return (
        lax.psum_scatter(qkv_grad, "blk", scatter_dimension=0, tiled=True),
        lax.psum_scatter(qv_grad, "blk", scatter_dimension=1, tiled=True),
        lax.psum_scatter(attn_grad, "blk", scatter_dimension=0, tiled=True),
        lax.psum_scatter(bias_grad, "blk", scatter_dimension=1, tiled=True),
        lax.psum_scatter(in_grad, "blk", scatter_dimension=0, tiled=True),
        lax.psum_scatter(in_bias_grad, "blk", scatter_dimension=0, tiled=True),
        lax.psum_scatter(back_grad, "blk", scatter_dimension=1, tiled=True),
        lax.psum_scatter(gain_grad, "blk", scatter_dimension=1, tiled=True),
        lax.psum_scatter(shift_grad, "blk", scatter_dimension=1, tiled=True),
    )


def body(
    tokens,
    lengths,
    w_qkv,
    qv_bias,
    w_attn,
    out_bias,
    w_in,
    in_bias,
    w_back,
    norm_gain,
    norm_shift,
    cotangent,
):
    row_count = tokens.shape[1]
    head_count = HEADS
    cycle_size = lax.axis_size("blk")
    bit_count = cycle_size.bit_length() - 1
    position = lax.axis_index("blk")
    length = lengths[0]
    key_valid = jnp.arange(cycle_size * row_count) < length
    params = (w_qkv, qv_bias, w_attn, out_bias, w_in, in_bias, w_back, norm_gain, norm_shift)
    out_one, saved_one = layer_forward(
        tokens[0].astype(jnp.float32), params, key_valid, position, bit_count, head_count
    )
    out_two, saved_two = layer_forward(out_one, params, key_valid, position, bit_count, head_count)
    grad_hidden, grads_two = layer_backward(
        cotangent[0].astype(jnp.float32),
        saved_two,
        params,
        key_valid,
        position,
        bit_count,
        head_count,
    )
    grad_hidden, grads_one = layer_backward(
        grad_hidden, saved_one, params, key_valid, position, bit_count, head_count
    )
    shards = scatter_once(jax.tree.map(jnp.add, grads_two, grads_one))
    (
        qkv_part,
        qv_part,
        attn_part,
        bias_part,
        in_part,
        in_bias_part,
        back_part,
        gain_part,
        shift_part,
    ) = shards
    totals = (
        lax.psum(qkv_part.astype(jnp.bfloat16), "batch").astype(jnp.float32),
        lax.psum(qv_part.astype(jnp.bfloat16), "batch").astype(jnp.float32),
        lax.psum(attn_part.astype(jnp.bfloat16), "batch").astype(jnp.float32),
        lax.psum(bias_part.astype(jnp.bfloat16), "batch").astype(jnp.float32),
        lax.psum(in_part.astype(jnp.bfloat16), "batch").astype(jnp.float32),
        lax.psum(in_bias_part.astype(jnp.bfloat16), "batch").astype(jnp.float32),
        lax.psum(back_part.astype(jnp.bfloat16), "batch").astype(jnp.float32),
        lax.psum(gain_part.astype(jnp.bfloat16), "batch").astype(jnp.float32),
        lax.psum(shift_part.astype(jnp.bfloat16), "batch").astype(jnp.float32),
    )
    return (
        out_two.astype(jnp.bfloat16)[None],
        grad_hidden.astype(jnp.bfloat16)[None],
        totals[0],
        totals[1],
        totals[2],
        totals[3],
        totals[4],
        totals[5],
        totals[6],
        totals[7],
        totals[8],
    )


MESH = pl.DeviceIdType.MESH
f32 = jnp.float32
bf16 = jnp.bfloat16
FLIPS = ((0, 0), (1, 0), (0, 1), (1, 1))
GROUPS = len(FLIPS)
PART = 4096 // GROUPS
WIDE = 256
ROWS, D, FF, LEN, VEC = 128, 1024, 4096, 1024, 144


def dot(a, b):
    return jnp.dot(a, b, preferred_element_type=f32)


def dot_t(a, b):
    return lax.dot_general(a, b, (((1,), (1,)), ((), ())), preferred_element_type=f32)


def dot_0(a, b):
    return lax.dot_general(a, b, (((0,), (0,)), ((), ())), preferred_element_type=f32)


def span(at, size):
    return pl.ds(pl.multiple_of(at * size, size), size)


def flip(bit, by):
    return bit + by * (1 - 2 * bit)


def group(ref, n):
    return ref.at[pl.ds(n * ROWS, ROWS)]


class Spot:
    def __init__(self):
        self.row, self.pos = lax.axis_index("batch"), lax.axis_index("blk")
        self.x, self.c = self.row // 2, self.row % 2
        self.z, self.y = self.pos // 2, self.pos % 2
        self.zl, self.zh = self.z % 2, self.z // 2
        self.place = self.c * 4 + self.zl * 2 + self.y
        self.moved = self.c != self.zh

    def flipped(self, c=0, x=0, y=0, zl=0, zh=0):
        row = flip(self.x, x) * 2 + flip(self.c, c)
        pos = flip(self.zh, zh) * 4 + flip(self.zl, zl) * 2 + flip(self.y, y)
        return {"batch": row, "blk": pos}

    def member(self, place):
        return {"batch": self.x * 2 + place // 4, "blk": self.zh * 4 + place % 4}

    def partner(self):
        return {"batch": self.x * 2 + self.zh, "blk": self.c * 4 + self.pos % 4}


BULK = 2**21


class Group:
    def __init__(self, at):
        self.at, self.bytes, self.waited = at, 0, False


def bytes_of(ref):
    return math.prod(ref.shape) * jnp.dtype(ref.dtype).itemsize


class Link:
    def __init__(self, send_sem, recv_sem, own_sem, *meters):
        self.send_sem, self.recv_sem, self.own_sem, self.meters = send_sem, recv_sem, own_sem, meters
        self.count, self.own_count = 0, 0
        self.groups, self.own_groups, self.swaps = [], [], []
        self.bulk, self.own_bulk = self.group(), self.own_group()

    def group(self):
        self.groups.append(Group(self.count))
        self.count += 1
        return self.groups[-1]

    def own_group(self):
        self.own_groups.append(Group(self.own_count))
        self.own_count += 1
        return self.own_groups[-1]

    def put(self, src, dst, device, group=None):
        if group is None:
            if self.bulk.bytes + bytes_of(src) > BULK:
                self.bulk = self.group()
            group = self.bulk
        group.bytes += bytes_of(src)
        pltpu.make_async_remote_copy(
            src_ref=src, dst_ref=dst, send_sem=self.send_sem.at[group.at], recv_sem=self.recv_sem.at[group.at],
            device_id=device, device_id_type=MESH,
        ).start()
        return group

    def keep(self, src, dst, group=None):
        if group is None:
            if self.own_bulk.bytes + bytes_of(src) > BULK:
                self.own_bulk = self.own_group()
            group = self.own_bulk
        group.bytes += bytes_of(src)
        pltpu.make_async_copy(src, dst, self.own_sem.at[group.at]).start()
        return group

    def wait(self, group, sem):
        if group.bytes:
            for meter in self.meters:
                row = bytes_of(meter) // meter.shape[0]
                tile = 8 if meter.dtype == f32 else 16
                if group.bytes % (tile * row) == 0 and group.bytes <= bytes_of(meter):
                    view = meter.at[pl.ds(0, group.bytes // row)]
                    pltpu.make_async_copy(view, view, sem.at[group.at]).wait()
                    return
            raise ValueError(group.bytes)

    def arrive(self, *groups):
        for group in groups:
            if not group.waited:
                group.waited = True
                self.wait(group, self.own_sem if any(group is own for own in self.own_groups) else self.recv_sem)

    def swap(self, spot, src, dst):
        far = pltpu.make_async_remote_copy(
            src_ref=src, dst_ref=dst, send_sem=self.send_sem.at[self.count], recv_sem=self.recv_sem.at[self.count],
            device_id=spot.partner(), device_id_type=MESH,
        )
        near = pltpu.make_async_copy(src, dst, self.own_sem.at[self.own_count])
        self.count += 1
        self.own_count += 1
        pl.when(spot.moved)(far.start)
        pl.when(jnp.logical_not(spot.moved))(near.start)
        self.swaps.append((spot, far, near))
        return far, near

    def arrive_swap(self, spot, pair):
        pl.when(spot.moved)(pair[0].wait_recv)
        pl.when(jnp.logical_not(spot.moved))(pair[1].wait)
        self.swaps = [(one, far, None if far is pair[0] else near) for one, far, near in self.swaps]

    def finish(self):
        self.arrive(*self.groups, *self.own_groups)
        for group in self.groups:
            self.wait(group, self.send_sem)
        for spot, far, near in self.swaps:
            if near is not None:
                self.arrive_swap(spot, (far, near))
            pl.when(spot.moved)(far.wait_send)


def greet(spot, devices):
    barrier = pltpu.get_barrier_semaphore()
    for device in devices:
        pl.semaphore_signal(barrier, inc=1, device_id=device, device_id_type=MESH)

    @pl.when(spot.moved)
    def _():
        pl.semaphore_signal(barrier, inc=1, device_id=spot.partner(), device_id_type=MESH)

    def meet():
        @pl.when(spot.moved)
        def _():
            pl.semaphore_wait(barrier, len(devices) + 1)

        @pl.when(jnp.logical_not(spot.moved))
        def _():
            pl.semaphore_wait(barrier, len(devices))

    return meet


def standard(values):
    centered = values - jnp.mean(values, axis=-1, keepdims=True)
    inverse = lax.rsqrt(jnp.mean(centered * centered, axis=-1, keepdims=True) + eps)
    return centered * inverse, inverse


def standard_back(unit, inverse, gain, grad):
    scaled = grad * gain
    inner = jnp.mean(scaled * unit, axis=-1, keepdims=True)
    return inverse * (scaled - jnp.mean(scaled, axis=-1, keepdims=True) - unit * inner)


def column_sum(x):
    return jnp.sum(x.astype(f32), axis=0, keepdims=True)


def gelu_pair(u):
    t = 1.0 / (1.0 + 0.23164188 * jnp.abs(u))
    bell = jnp.exp(-0.5 * u * u)
    poly = t * (0.127414796 + t * (-0.142248368 + t * (0.7107068705 + t * (-0.7265760135 + t * 0.5307027145))))
    tail = poly * bell
    cdf = jnp.where(u < 0, tail, 1.0 - tail)
    return u * cdf, cdf + u * bell * 0.3989422804


def low_lanes():
    return lax.broadcasted_iota(jnp.int32, (1, 128), 1) < 64


def valid_keys(length):
    return lax.broadcasted_iota(jnp.int32, (1, LEN), 1).astype(f32) < length


def attention_rows(qkv, rows, valid):
    queries, keys, values = qkv[rows, 0:128], qkv[:, 128:256], qkv[:, 256:384]
    low_half = low_lanes()
    outs, lses = [], []
    for half in range(2):
        mine = low_half if half == 0 else jnp.logical_not(low_half)
        part = jnp.where(mine, queries, jnp.zeros_like(queries)) * jnp.asarray(0.125, bf16)
        scores = jnp.where(valid, dot_t(part, keys), -1e30)
        top = jnp.max(scores, axis=1, keepdims=True)
        expd = jnp.exp(scores - top)
        total = jnp.sum(expd, axis=1, keepdims=True)
        probs = (expd * (1.0 / total)).astype(bf16)
        outs.append(dot(probs, values))
        lses.append(top + jnp.log(total))
    return jnp.where(low_half, outs[0], outs[1]), jnp.where(low_half, lses[0], lses[1])


def attention_back_keys(qkv, grads_ref, lse_rows, delta_rows, rows, first, length):
    low_half = low_lanes()
    keys, values = qkv[rows, 128:256], qkv[rows, 256:384]
    at = lax.broadcasted_iota(jnp.int32, (256, 1), 0) + first
    valid = at.astype(f32) < length
    dqs, dk, dv = [], None, None
    for half in range(2):
        mine = low_half if half == 0 else jnp.logical_not(low_half)
        k_part = jnp.where(mine, keys, jnp.zeros_like(keys)) * jnp.asarray(0.125, bf16)
        v_part = jnp.where(mine, values, jnp.zeros_like(values))
        queries, grads = qkv[:, 0:128], grads_ref[...]
        scores = dot_t(k_part, queries)
        probs = jnp.where(valid, jnp.exp(scores - lse_rows[half : half + 1, :]), 0.0)
        dp = dot_t(v_part, grads)
        ds = (probs * (dp - delta_rows[half : half + 1, :])).astype(bf16)
        dv_part = dot(probs.astype(bf16), grads)
        dk_part = dot(ds, queries)
        dv = dv_part if half == 0 else jnp.where(low_half, dv, dv_part)
        dk = dk_part if half == 0 else jnp.where(low_half, dk, dk_part)
        dqs.append(dot_0(ds, keys))
    return jnp.where(low_half, dqs[0], dqs[1]), (dk * 0.125).astype(bf16), dv.astype(bf16)


def attention_back_start(s, o, lse, grads):
    turned = lse[...].T
    s.lse_rows[0:1, :] = turned[0:1, :]
    s.lse_rows[1:2, :] = turned[64:65, :]
    product = (grads[...].astype(f32) * o[...]).T
    s.delta_rows[0:1, :] = jnp.sum(product[0:64, :], axis=0, keepdims=True)
    s.delta_rows[1:2, :] = jnp.sum(product[64:128, :], axis=0, keepdims=True)


def attention_back_step(link, spot, step, s, qkv, grads, dqkvh, group, own):
    pair = (spot.place // 2 + step) % 4
    rows = span(pair, 256)
    dq, dk, dv = attention_back_keys(
        qkv, grads, s.lse_rows, s.delta_rows, rows, pair * 256, s.length[0:1, 0:1]
    )
    dqkvh[rows, 128:256] = dk
    dqkvh[rows, 256:384] = dv
    s.dq[...] = dq if step == PAIR_STEPS[0] else s.dq[...] + dq
    for part in (1, 2):
        send_rows(link, spot, dqkvh, s.dqkv, step, part, group, own)


def attention_back_end(link, spot, s, dqkvh, group, own):
    dqkvh[:, 0:128] = (s.dq[...] * 0.125).astype(bf16)
    for step in PAIR_STEPS:
        send_rows(link, spot, dqkvh, s.dqkv, step, 0, group, own)


def send_columns(link, spot, source, target, part, landing, groups, own):
    for step in range(7, -1, -1):
        to = (spot.place + step) % 8
        src = source.at[:, pl.ds(pl.multiple_of(part * D + to * 128, 128), 128)]
        dst = target.at[span(spot.place, ROWS), pl.ds(landing * 128, 128)]
        if step:
            link.put(src, dst, spot.member(to), groups[step])
        else:
            link.keep(src, dst, own)


def pair_rows(spot, step):
    return span((spot.place // 2 + step) % 4, 256)


def send_rows(link, spot, source, target, step, part, group, own):
    same = (spot.place + 2 * step) % 8
    for n, to in enumerate((same, same + 1 - 2 * spot.y)):
        src = source.at[span(to, ROWS), pl.ds(part * 128, 128)]
        dst = target.at[:, pl.ds(pl.multiple_of(part * D + spot.place * 128, 128), 128)]
        if step or n:
            link.put(src, dst, spot.member(to), group)
        else:
            link.keep(src, dst, own)


PAIR_STEPS = (1, 2, 3, 0)


def spec(**named):
    return named


def two(*entry):
    return [entry, entry]


MAIN_OUT = spec(
    mixed=((ROWS, D), bf16), qkv1=((LEN, 384), bf16), lse1=((LEN, 128), f32), o1=((LEN, 128), f32),
    left_attn=((4, ROWS, D), bf16), right_attn=((4 * ROWS, 512), bf16),
    left_back=((2 * GROUPS, ROWS, D), bf16), right_back=((2 * GROUPS * ROWS, PART), bf16),
    left_in=((2 * GROUPS, ROWS, D), bf16), right_in=((2 * GROUPS * ROWS, PART), bf16),
    hidden=((2, LEN, D), bf16), dqkv2=((LEN, 384), bf16),
    du1=((ROWS, FF), bf16), dza1=((ROWS, D), bf16),
    do1=((ROWS, D), bf16), dr1=((ROWS, D), f32), vec=((8, D), f32), inb=((1, FF), f32),
    length=((16, 128), f32),
)
MAIN_SCRATCH = spec(
    w_qkv=((D, 3 * D), bf16), w_attn=((D, D), bf16), w_in=((D, FF), bf16), w_back=((FF, D), bf16),
    tok=((ROWS, D), bf16), cot=((ROWS, D), bf16), length=((16, 128), f32), sent_length=((16, 128), f32),
    proj=two((ROWS, 3 * D), bf16), qkv=two((LEN, 384), bf16), lse=two((LEN, 128), f32),
    o=two((LEN, 128), bf16), full_o=two((LEN, 128), f32), att=two((ROWS, D), bf16), n=two((ROWS, D), bf16),
    act=two((ROWS, FF), bf16), slope=two((ROWS, FF), bf16),
    unit_a=two((ROWS, D), f32), unit_b=two((ROWS, D), f32),
    inv_a=two((ROWS, 128), f32), inv_b=two((ROWS, 128), f32),
    hq2=((ROWS, D), bf16), h=((ROWS, D), f32), acc=((ROWS, D), f32), mixed=((ROWS, D), bf16),
    dzb=two((ROWS, D), bf16), du=two((ROWS, FF), bf16), dza=two((ROWS, D), bf16), do=two((ROWS, D), bf16),
    doh=((LEN, 128), bf16), dqkvh=((LEN, 384), bf16), dq=((LEN, 128), f32), lse_rows=((8, LEN), f32), delta_rows=((8, LEN), f32),
    dqkv=((ROWS, 3 * D), bf16), dr1=((ROWS, D), f32), vec=((8, D), f32), inb=((1, FF), f32),
)


class Refs:
    pass


def flat(entries):
    out = []
    for entry in entries.values():
        out += entry if isinstance(entry, list) else [entry]
    return out


def bind(entries, refs):
    got, it = Refs(), iter(refs)
    for name, entry in entries.items():
        setattr(got, name, [next(it) for _ in entry] if isinstance(entry, list) else next(it))
    return got


def main_kernel(*refs):
    (len_ref, tokens, cotangent, w_qkv, w_attn, w_in, w_back,
     qv_bias, out_bias, in_bias, gain, shift) = refs[:12]
    outs = bind(MAIN_OUT, refs[12 : 12 + len(MAIN_OUT)])
    rest = refs[12 + len(MAIN_OUT) :]
    s = bind(MAIN_SCRATCH, rest[:-4])
    load_sem, send_sem, recv_sem, own_sem = rest[-4:]
    spot = Spot()
    link = Link(send_sem, recv_sem, own_sem, outs.hidden.at[0], outs.lse1)
    others = [spot.member((spot.place + step) % 8) for step in range(1, 8)]
    others += [spot.flipped(x=1), spot.flipped(c=1, x=1)]
    meet = greet(spot, others)

    loads = []
    for n, (src, dst) in enumerate(
        [(w_qkv.at[:, pl.ds(D * part, D)], s.w_qkv.at[:, pl.ds(D * part, D)]) for part in (1, 2, 0)]
        + [(w_attn, s.w_attn), (w_in, s.w_in), (w_back, s.w_back)]
    ):
        loads.append(pltpu.make_async_copy(src, dst, load_sem.at[n]))
        loads[n].start()
    loaded = set()

    def need(n):
        if n not in loaded:
            loaded.add(n)
            loads[n].wait()

    s.sent_length[...] = jnp.full((16, 128), len_ref[0], jnp.int32).astype(f32)
    meet()
    first_in = [link.swap(spot, tokens, s.tok), link.swap(spot, s.sent_length, s.length)]
    for pair in first_in:
        link.arrive_swap(spot, pair)
    valid = valid_keys(s.length[0:1, 0:1])

    later = []

    def share(source, left, d):
        link.keep(source, left.at[d])
        link.put(source, left.at[2 + d], spot.flipped(c=1))
        return link.put(source, left.at[4 + d], spot.flipped(x=1), link.group())

    def pass_on(came, left, d):
        link.arrive(came)
        link.put(left.at[4 + d], left.at[6 + d], spot.flipped(c=1))

    def deal(source, right, d):
        link.keep(source.at[:, span(spot.c * 2 + spot.x, PART)], group(right, d))
        for n, (dc, dx) in enumerate(FLIPS[1:], 1):
            cols = span(flip(spot.c, dc) * 2 + flip(spot.x, dx), PART)
            link.put(source.at[:, cols], group(right, 2 * n + d), spot.flipped(c=dc, x=dx))

    def gather(hq, d, part):
        rows = pl.ds(part * 64, 64)
        block = outs.hidden.at[d, pl.ds(pl.multiple_of(spot.place * ROWS + part * 64, 64), 64)]
        for dz, dy in ((1, 0), (0, 1), (1, 1)):
            link.put(hq.at[rows], block, spot.flipped(zl=dz, y=dy))
        link.keep(hq.at[rows], block)

    def forward(d, hq, h):
        pair_of = [0, 3, 3, 2, 2, 1, 1, 1]
        both, pairs, own = link.group(), [link.group() for _ in range(4)], link.own_group()
        for part, number in ((1, 0), (2, 1), (0, 2)):
            need(number)

            def tile(i, carry):
                cols = span(2 * part + i, 512)
                value = dot(hq[...], s.w_qkv[:, cols])
                if part != 1:
                    value += qv_bias[part // 2 : part // 2 + 1, span(i, 512)]
                s.proj[d][:, cols] = value.astype(bf16)
                return carry

            lax.fori_loop(0, 2, tile, 0)
            to_groups = [both] * 8 if part else [pairs[pair] for pair in pair_of]
            send_columns(link, spot, s.proj[d], s.qkv[d], part, part, to_groups, own)
        link.arrive(both, own)
        if d == 0:
            later.append(link.swap(spot, cotangent, s.cot))
        to_rows, own_rows = link.group(), link.own_group()
        for step in PAIR_STEPS:
            link.arrive(pairs[step])
            rows = pair_rows(spot, step)
            s.full_o[d][rows, :], s.lse[d][rows, :] = attention_rows(s.qkv[d], rows, valid)
            s.o[d][rows, :] = s.full_o[d][rows, :].astype(bf16)
            send_rows(link, spot, s.o[d], s.att[d], step, 0, to_rows, own_rows)
        if d == 0:
            link.keep(s.qkv[0], outs.qkv1)
            link.keep(s.lse[0], outs.lse1)
            link.keep(s.full_o[0], outs.o1)
        link.arrive(to_rows, own_rows)
        gather(s.tok, 0, d)
        need(3)
        unit, inverse = standard(h[...].astype(f32) + dot(s.att[d][...], s.w_attn[...]) + out_bias[0:1])
        link.keep(s.att[d], outs.left_attn.at[d])
        link.put(s.att[d], outs.left_attn.at[2 + d], spot.flipped(c=1))
        s.unit_a[d][...] = unit
        s.inv_a[d][...] = jnp.broadcast_to(inverse, (ROWS, 128))
        first = unit * gain[0:1] + shift[0:1]
        s.n[d][...] = first.astype(bf16)
        came = share(s.n[d], outs.left_in, d)
        s.acc[...] = first + out_bias[1:2]
        need(4)
        need(5)

        def inner(i, carry):
            cols = span(i, 512)
            act, slope = gelu_pair(dot(s.n[d][...], s.w_in[:, cols]) + in_bias[:, cols])
            act = act.astype(bf16)
            s.act[d][:, cols] = act
            s.slope[d][:, cols] = slope.astype(bf16)
            s.acc[...] += dot(act, s.w_back[cols, :])
            return carry

        lax.fori_loop(0, 8, inner, 0)
        deal(s.act[d], outs.right_back, d)
        pass_on(came, outs.left_in, d)
        unit, inverse = standard(s.acc[...])
        s.unit_b[d][...] = unit
        s.inv_b[d][...] = jnp.broadcast_to(inverse, (ROWS, 128))
        return unit * gain[1:2] + shift[1:2]

    def add_vec(at, value, fresh):
        s.vec[at : at + 1, :] = value if fresh else s.vec[at : at + 1, :] + value

    def backward(d, grad, fresh):
        unit = s.unit_b[d][...]
        add_vec(3, column_sum(grad * unit), fresh)
        add_vec(5, column_sum(grad), fresh)
        dr = standard_back(unit, s.inv_b[d][:, 0:1], gain[1:2], grad)
        s.acc[...] = dr
        low = dr.astype(bf16)
        s.dzb[d][...] = low
        came = share(s.dzb[d], outs.left_back, d)
        add_vec(1, column_sum(low), fresh)

        def inner(i, carry):
            cols = span(i, 512)
            du = (dot_t(s.dzb[d][...], s.w_back[cols, :]) * s.slope[d][:, cols].astype(f32)).astype(bf16)
            s.du[d][:, cols] = du
            total = column_sum(du)
            s.inb[:, cols] = total if fresh else s.inb[:, cols] + total
            s.acc[...] += dot_t(du, s.w_in[:, cols])
            return carry

        lax.fori_loop(0, 8, inner, 0)
        if d:
            deal(s.du[d], outs.right_in, d)
            pass_on(came, outs.left_back, d)
        else:
            link.keep(s.du[d], outs.du1)
        grad = s.acc[...]
        unit = s.unit_a[d][...]
        add_vec(2, column_sum(grad * unit), fresh)
        add_vec(4, column_sum(grad), fresh)
        dr = standard_back(unit, s.inv_a[d][:, 0:1], gain[0:1], grad)
        s.dr1[...] = dr
        low = dr.astype(bf16)
        s.dza[d][...] = low
        if d:
            link.keep(s.dza[d].at[:, span(spot.c, 512)], group(outs.right_attn, d))
            link.put(s.dza[d].at[:, span(1 - spot.c, 512)], group(outs.right_attn, 2 + d), spot.flipped(c=1))
        else:
            link.keep(s.dza[d], outs.dza1)
        add_vec(0, column_sum(low), fresh)
        s.do[d][...] = dot_t(low, s.w_attn[...]).astype(bf16)

    out = forward(0, s.tok, s.tok)
    s.h[...] = out
    s.hq2[...] = out.astype(bf16)
    out = forward(1, s.hq2, s.h)
    s.mixed[...] = out.astype(bf16)
    link.swap(spot, s.mixed, outs.mixed)
    link.arrive_swap(spot, later[0])
    gather(s.hq2, 1, 0)
    backward(1, s.cot[...].astype(f32), True)
    to_heads, own_heads = link.group(), link.own_group()
    send_columns(link, spot, s.do[1], s.doh, 0, 0, [to_heads] * 8, own_heads)
    link.arrive(to_heads, own_heads)
    attention_back_start(s, s.full_o[1], s.lse[1], s.doh)
    to_rows, own_rows, last_rows, own_last = link.group(), link.own_group(), link.group(), link.own_group()
    for step in PAIR_STEPS:
        attention_back_step(link, spot, step, s, s.qkv[1], s.doh, s.dqkvh, to_rows, own_rows)
    attention_back_end(link, spot, s, s.dqkvh, last_rows, own_last)
    link.keep(s.dqkvh, outs.dqkv2)
    link.arrive(to_rows, own_rows)
    s.dr1[...] += dot_t(s.dqkv[:, D:], s.w_qkv[:, D:])
    link.arrive(last_rows, own_last)
    gather(s.hq2, 1, 1)
    backward(0, s.dr1[...] + dot_t(s.dqkv[:, :D], s.w_qkv[:, :D]), False)
    link.keep(s.do[0], outs.do1)
    link.keep(s.dr1, outs.dr1)
    small = link.own_group()
    link.keep(s.vec, outs.vec, small)
    link.keep(s.inb, outs.inb, small)
    link.keep(s.length, outs.length, small)
    link.finish()


def main_call(length, tokens, cotangent, params):
    w_qkv, qv_bias, w_attn, out_bias, w_in, in_bias, w_back, gain, shift = params
    dma = pltpu.SemaphoreType.DMA
    vmem, hbm = pl.BlockSpec(memory_space=pltpu.VMEM), pl.BlockSpec(memory_space=pl.ANY)
    results = pl.pallas_call(
        main_kernel,
        out_shape=[jax.ShapeDtypeStruct(*entry) for entry in MAIN_OUT.values()],
        in_specs=[pl.BlockSpec(memory_space=pltpu.SMEM), hbm, hbm] + [hbm] * 4 + [vmem] * 5,
        out_specs=[hbm] * len(MAIN_OUT),
        scratch_shapes=[pltpu.VMEM(*entry) for entry in flat(MAIN_SCRATCH)]
        + [dma((6,)), dma((32,)), dma((32,)), dma((20,))],
        compiler_params=pltpu.CompilerParams(
            collective_id=1, has_side_effects=True, vmem_limit_bytes=60 * 2**20
        ),
    )(length, tokens, cotangent, w_qkv, w_attn, w_in, w_back, qv_bias, out_bias, in_bias[None], gain, shift)
    return bind(MAIN_OUT, results)


PATHS = spec(A="yxabXC", B="xyabXC", C="abysC", F="yabVK", G="aybVK")
CHUNKS = "BFGFFFGFF"
PER = PART // WIDE
ORDER = (
    (100, 12), (0, -1), (100, 10), (100, 14), (2, -1), (100, 1), (100, 2), (100, 3), (100, 4), (100, 5),
    (100, 6), (1, -1), (100, 13), (100, 9), (0, 0), (6, -1), (2, 0), (8, -1), (1, 0), (7, -1),
    (0, 1), (2, 1), (6, 0), (4, -1), (100, 7), (1, 1), (8, 0), (5, -1), (0, 2), (7, 0),
    (3, -1), (2, 2), (6, 1), (1, 2), (100, 8), (8, 1), (2, 3), (1, 3), (2, 4), (0, 3),
    (1, 4), (4, 0), (7, 1), (0, 4), (6, 2), (0, 5), (5, 0), (6, 3), (6, 4), (8, 2),
    (4, 1), (3, 0), (8, 3), (7, 2), (8, 4), (5, 1), (100, 11), (7, 3), (4, 2), (7, 4),
    (3, 1), (4, 3), (5, 2), (4, 4), (3, 2), (5, 3), (5, 4), (3, 3), (3, 4),
)
IN_OUT = spec(back=0, fore=FF, attn=2 * FF, qkv=2 * FF + D)


def plan(path, width):
    slabs, steps = 8, []
    for stage in path:
        if stage in "yab":
            slabs //= 2
        elif stage == "x":
            width //= 2
        elif stage == "X":
            width *= 2
        steps.append((stage, slabs, width))
    return steps


def weight_of(c):
    return (0, 0) if c == 0 else (1 + (c - 1) // PER, (c - 1) % PER)


def chunk_rows(c):
    return VEC if c == 0 else ROWS


WIDTHS = [512] + [WIDE] * (2 * PER)
SEMS = 20 + sum(len(PATHS[name]) for name in CHUNKS)
PLANS = [plan(PATHS[name], width) for name, width in zip(CHUNKS, WIDTHS)]
GRAD_SCRATCH = spec(
    left=[((4, ROWS, D), bf16)] + two((2 * GROUPS, ROWS, D), bf16),
    right=[((4 * ROWS, 512), bf16)] + two((2 * GROUPS * ROWS, PART), bf16),
    turned=[((D, 512), bf16)] + two((D, 256 * GROUPS), bf16),
    chunk=[((8, chunk_rows(c), WIDTHS[c]), bf16) for c in range(len(CHUNKS))],
    landing=[
        ((slabs, chunk_rows(c), width), bf16)
        for c, steps in enumerate(PLANS) for stage, slabs, width in steps if stage in "yabxs"
    ],
    hidden=two((LEN, D), bf16), dqkvh=two((LEN, 384), bf16),
    chunk_q=((8, VEC, 384), bf16), landing_q=two((4, VEC, 384), bf16),
    qkv=((LEN, 384), bf16), lse=((LEN, 128), f32), doh=((LEN, 128), bf16),
    o=((LEN, 128), f32), dq=((LEN, 128), f32), lse_rows=((8, LEN), f32), delta_rows=((8, LEN), f32),
    dqkv=((ROWS, 3 * D), bf16), w_qkv=((D, 3 * D), bf16),
    dr1=((ROWS, D), f32), grad=((ROWS, D), bf16), vec=((8, D), f32), inb=((1, FF), f32), length=((16, 128), f32),
)


def grad_kernel(*refs):
    src = bind(MAIN_OUT, refs[: len(MAIN_OUT)])
    w_qkv, sums, grad_out = refs[len(MAIN_OUT) : len(MAIN_OUT) + 3]
    rest = refs[len(MAIN_OUT) + 3 :]
    s = bind(GRAD_SCRATCH, rest[:-3])
    s.out = sums
    spot = Spot()
    link = Link(*rest[-3:], src.hidden.at[0], src.lse1, w_qkv)
    x, y, c, zl, zh = spot.x, spot.y, spot.c, spot.zl, spot.zh
    others = [spot.member((spot.place + step) % 8) for step in range(1, 8)]
    others += [spot.flipped(x=1), spot.flipped(c=1, x=1), spot.flipped(zh=1)]
    meet = greet(spot, others)
    mine = span(c * 2 + x, PART)
    heads_in, vec_in, hidden_in, dqkv_in, close_in, left_in, right_in, weight_in = [link.own_group() for _ in range(8)]
    length_in = link.own_group()
    own_ready = [link.own_group() for _ in range(3)]
    for one, other in ((src.o1, s.o), (src.qkv1, s.qkv), (src.lse1, s.lse)):
        link.keep(one, other, heads_in)
    link.keep(src.length, s.length, length_in)
    link.keep(src.left_attn, s.left[0], own_ready[0])
    for n in (1, 3):
        link.keep(group(src.right_attn, n), group(s.right[0], n), own_ready[0])
    link.keep(src.dza1.at[:, span(c, 512)], group(s.right[0], 0), own_ready[0])
    link.keep(src.right_back, s.right[1], right_in)
    for n in (0, 1, 2, 3, 4, 5, 7):
        link.keep(src.left_back.at[n], s.left[1].at[n], own_ready[1])
    link.keep(src.left_in, s.left[2], left_in)
    link.keep(src.du1.at[:, mine], group(s.right[2], 0), own_ready[2])
    for n in range(GROUPS):
        link.keep(group(src.right_in, 2 * n + 1), group(s.right[2], 2 * n + 1), own_ready[2])
    link.keep(src.vec, s.vec, vec_in)
    link.keep(src.inb, s.inb, vec_in)
    rows = span(c, 512)
    for d in range(2):
        link.keep(src.hidden.at[d, rows], s.hidden[d].at[rows], hidden_in)
    link.keep(src.dqkv2, s.dqkvh[1], dqkv_in)
    link.keep(w_qkv, s.w_qkv, weight_in)
    link.keep(src.dr1, s.dr1, close_in)
    meet()
    to_heads, own_heads, far_hidden = link.group(), link.own_group(), link.group()
    far_ready = [link.group() for _ in range(3)]
    send_columns(link, spot, src.do1, s.doh, 0, 0, [to_heads] * 8, own_heads)
    link.put(src.dza1.at[:, span(1 - c, 512)], group(s.right[0], 2), spot.flipped(c=1), far_ready[0])
    link.put(src.left_back.at[4], s.left[1].at[6], spot.flipped(c=1), far_ready[1])
    for n, (dc, dx) in enumerate(FLIPS[1:], 1):
        cols = span(flip(c, dc) * 2 + flip(x, dx), PART)
        link.put(src.du1.at[:, cols], group(s.right[2], 2 * n), spot.flipped(c=dc, x=dx), far_ready[2])
    for d in range(2):
        link.put(src.hidden.at[d, rows], s.hidden[d].at[rows], spot.flipped(c=1), far_hidden)

    bits = spec(y=y, a=zl, b=zh)
    across = spec(
        y=spot.flipped(y=1), a=spot.flipped(zl=1), b=spot.flipped(zh=1), x=spot.flipped(x=1), C=spot.flipped(c=1)
    )
    across.update(spec(X=across["x"], V=across["x"], s=across["x"], K=across["C"]))
    current, landing, copies = {}, {}, {}
    it = iter(s.landing)
    for n, steps in enumerate(PLANS):
        for i, step in enumerate(steps):
            if step[0] in "yabxs":
                landing[n, i] = next(it)
    waiting = [True, True, True]

    def turn(k):
        if k == 2:
            link.arrive(left_in)
        else:
            link.arrive(own_ready[k], far_ready[k])
            if k == 1:
                link.arrive(right_in)
        count = s.left[k].shape[0]
        for g in range(count):
            s.turned[k][:, pl.ds(ROWS * g, ROWS)] = s.left[k][g].T

    def compute(n):
        k, at = weight_of(n)
        if k == 2 and waiting[2]:
            waiting[2] = False
            link.arrive(own_ready[2], far_ready[2])
        path = [stage for stage in PATHS[CHUNKS[n]] if stage in "yab"]
        path += [stage for stage in "yab" if stage not in path]
        wide = WIDTHS[n]

        def piece(i, carry):
            product = dot(s.turned[k][span(i, 256), :], s.right[k][:, pl.ds(at * wide, wide)]).astype(bf16)
            for low in range(2):
                bit = spec(y=low, a=i % 2, b=i // 2)
                at_slab = (bit[path[0]] * 2 + bit[path[1]]) * 2 + bit[path[2]]
                s.chunk[n][at_slab, 0:ROWS] = product[ROWS * low : ROWS * (low + 1)]
            return carry

        lax.fori_loop(0, 4, piece, 0)
        if n == 0:
            link.arrive(vec_in)
            for shard in range(8):
                bit = spec(y=shard % 2, a=shard // 2 % 2, b=shard // 4)
                at_slab = (bit[path[0]] * 2 + bit[path[1]]) * 2 + bit[path[2]]
                vec = s.vec[:, pl.ds(shard * 128, 128)]
                top = jnp.concatenate([vec, jnp.zeros((8, 384), f32)], 1)
                low = jnp.broadcast_to(s.inb[:, pl.ds(shard * 512, 512)], (8, 512))
                s.chunk[n][at_slab, ROWS:VEC] = jnp.concatenate([top, low], 0).astype(bf16)
        current[n] = s.chunk[n]

    def base_of(n):
        k, at = weight_of(n)
        if k == 0:
            return IN_OUT["attn"] + c * 512 + at * WIDE, 0
        return IN_OUT["back" if k == 1 else "fore"] + c * 2 * PART + at * WIDE, PART

    def columns(n, quarter, offset, width):
        start, stride = base_of(n)
        return pl.ds(pl.multiple_of(start + quarter * stride + offset, 128), width)

    def send(n, i):
        stage, slabs, width = PLANS[n][i]
        rows = pl.ds(0, chunk_rows(n))
        now, todo = current[n], []
        if stage in "yab":
            todo.append((now.at[pl.ds((1 - bits[stage]) * slabs, slabs)], landing[n, i]))
        elif stage == "x":
            todo.append((now.at[:, :, pl.ds(pl.multiple_of((1 - x) * width, 128), width)], landing[n, i]))
        elif stage == "s":
            todo.append((now, landing[n, i]))
        else:
            offset = x * (width // 2) if stage == "X" else 0
            width = width // 2 if stage == "X" else width
            for quarter in [x] if stage == "V" else range(2) if stage == "K" else [0]:
                where = s.out.at[rows, columns(n, quarter, offset, width)]
                todo.append((where, where))
        copies[n, i] = link.group()
        for here, there in todo:
            link.put(here, there, across[stage], copies[n, i])

    def advance(n, i):
        stage, slabs, width = PLANS[n][i]
        link.arrive(copies[n, i])
        if stage not in "yabxs":
            return
        got, old = landing[n, i], current[n]

        def add(m, carry):
            if stage in "yab":
                kept = old[bits[stage] * slabs + m]
            elif stage == "x":
                kept = old[m, :, pl.ds(pl.multiple_of(x * width, 128), width)]
            else:
                kept = old[m]
            got[m] = (got[m].astype(f32) + kept.astype(f32)).astype(bf16)
            return carry

        lax.fori_loop(0, slabs, add, 0)
        current[n] = got
        follow = PLANS[n][i + 1][0]
        if follow in "VXC":
            offset = x * width if follow == "X" else 0
            s.out[0 : chunk_rows(n), columns(n, x if follow == "V" else 0, offset, width)] = got[0]

    state = Refs()
    rows_kv, own_kv, rows_q, own_q = link.group(), link.own_group(), link.group(), link.own_group()

    def fold_q(n, bit):
        got = s.landing_q[n]
        slabs = got.shape[0]
        old = s.chunk_q if n == 0 else s.landing_q[0]

        def add(m, carry):
            got[m] = (got[m].astype(f32) + old[bit * slabs + m].astype(f32)).astype(bf16)
            return carry

        lax.fori_loop(0, slabs, add, 0)

    def task(k):
        if k == 1:
            link.arrive(to_heads, own_heads, heads_in, length_in)
            attention_back_start(s, s.o, s.lse, s.doh)
        if k <= 4:
            attention_back_step(link, spot, PAIR_STEPS[k - 1], s, s.qkv, s.doh, s.dqkvh[0], rows_kv, own_kv)
        elif k == 5:
            attention_back_end(link, spot, s, s.dqkvh[0], rows_q, own_q)
        elif k == 6:
            link.arrive(dqkv_in)

            def piece(i, carry):
                here = span(i, 256)
                product = dot_0(s.hidden[0][:, here], s.dqkvh[0][...])
                product += dot_0(s.hidden[1][:, here], s.dqkvh[1][...])
                product = product.astype(bf16)
                for low in range(2):
                    at_slab = i * 2 + low
                    s.chunk_q[at_slab, 0:ROWS] = product[ROWS * low : ROWS * (low + 1)]
                return carry

            lax.fori_loop(0, 4, piece, 0)
            total = column_sum(s.dqkvh[0][...]) + column_sum(s.dqkvh[1][...])
            extra = jnp.broadcast_to(total, (16, 384)).astype(bf16)
            for at_slab in range(8):
                s.chunk_q[at_slab, ROWS:VEC] = extra
            state.q = link.put(s.chunk_q.at[pl.ds((1 - zh) * 4, 4)], s.landing_q[0], across["b"], link.group())
        elif k == 7:
            link.arrive(state.q)
            fold_q(0, zh)
            state.q = link.put(s.landing_q[0], s.landing_q[1], across["x"], link.group())
        elif k == 8:
            link.arrive(state.q)
            fold_q(1, 0)
            cols = pl.ds(pl.multiple_of(IN_OUT["qkv"] + spot.place * 384, 128), 384)
            where = s.out.at[:, cols]
            state.q = link.group()
            for dz, dy in ((1, 1), (1, 0), (0, 1)):
                slab = s.landing_q[1].at[flip(zl, dz) * 2 + flip(y, dy)]
                link.put(slab, where, spot.flipped(zl=dz, y=dy), state.q)
            s.out[:, cols] = s.landing_q[1][zl * 2 + y]
        elif k == 11:
            link.arrive(state.q)
            where = s.out.at[:, pl.ds(pl.multiple_of(IN_OUT["qkv"] + c * 1536, 128), 1536)]
            link.put(where, where, across["C"])
        elif k == 9:
            link.arrive(rows_kv, own_kv, rows_q, own_q, close_in, weight_in)
            s.grad[...] = (s.dr1[...] + dot_t(s.dqkv[...], s.w_qkv[...])).astype(bf16)
            link.swap(spot, s.grad, grad_out)
        elif k == 10:
            link.arrive(hidden_in, far_hidden)
        elif k in (12, 13, 14):
            turn((0, 2, 1)[k - 12])

    for n, i in ORDER:
        if n == 100:
            task(i)
            continue
        if i < 0:
            compute(n)
        else:
            advance(n, i)
        if i + 1 < len(PLANS[n]):
            send(n, i + 1)
    link.finish()


def grad_call(main, w_qkv):
    dma = pltpu.SemaphoreType.DMA
    hbm = pl.BlockSpec(memory_space=pl.ANY)
    return pl.pallas_call(
        grad_kernel,
        out_shape=[jax.ShapeDtypeStruct((VEC, 12 * D), bf16), jax.ShapeDtypeStruct((ROWS, D), bf16)],
        in_specs=[hbm] * (len(MAIN_OUT) + 1),
        out_specs=[pl.BlockSpec(memory_space=pltpu.VMEM), hbm],
        scratch_shapes=[pltpu.VMEM(*entry) for entry in flat(GRAD_SCRATCH)]
        + [dma((SEMS,)), dma((SEMS,)), dma((20,))],
        compiler_params=pltpu.CompilerParams(
            collective_id=2, has_side_effects=True, vmem_limit_bytes=60 * 2**20
        ),
    )(*[getattr(main, name) for name in MAIN_OUT], w_qkv)


def finish_kernel(sums, mixed_in, grad_in, mixed, grad, qkv, qv, attn, bias, fore, fore_bias, back, gain, shift):
    at = IN_OUT
    mixed[...] = mixed_in[...]
    grad[...] = grad_in[...]
    for part in range(8):
        rows = pl.ds(part * 512, 512)
        back[rows, :] = sums[0:ROWS, pl.ds(at["back"] + part * 512, 512)].astype(f32).T
        fore[:, rows] = sums[0:ROWS, pl.ds(at["fore"] + part * 512, 512)].astype(f32)
    attn[...] = sums[0:ROWS, pl.ds(at["attn"], D)].astype(f32)
    total = jnp.zeros((16, 384), f32)
    for place in range(8):
        start = at["qkv"] + place * 384
        for part in range(3):
            here = pl.ds(start + part * 128, 128)
            qkv[:, pl.ds(part * D + place * 128, 128)] = sums[0:ROWS, here].astype(f32)
        block = sums[ROWS:VEC, pl.ds(start, 384)].astype(f32)
        total = total + jnp.where(lax.axis_index("blk") == place, block, 0.0)
    qv[0:1, :] = total[0:1, 0:128]
    qv[1:2, :] = total[0:1, 256:384]
    start = at["attn"]
    small = sums[ROWS:VEC, pl.ds(start, 512)].astype(f32) + sums[ROWS:VEC, pl.ds(start + 512, 512)].astype(f32)
    bias[...] = small[0:2, 0:128]
    gain[...] = small[2:4, 0:128]
    shift[...] = small[4:6, 0:128]
    fore_bias[...] = small[8:9, :]


def finish_call(sums, mixed, grad):
    shapes = [(ROWS, 3 * D), (2, 128), (ROWS, D), (2, 128), (ROWS, FF), (1, 512), (FF, 128), (2, 128), (2, 128)]
    outs = [jax.ShapeDtypeStruct((ROWS, D), bf16)] * 2 + [jax.ShapeDtypeStruct(shape, f32) for shape in shapes]
    return pl.pallas_call(
        finish_kernel,
        out_shape=outs,
        compiler_params=pltpu.CompilerParams(vmem_limit_bytes=40 * 2**20),
    )(sums, mixed, grad)


def fast_body(tokens, lengths, *rest):
    params, cotangent = rest[:-1], rest[-1]
    main = main_call(lengths, tokens[0], cotangent[0], params)
    sums, grad = grad_call(main, params[0])
    mixed, grad, qkv, qv, attn, bias, fore, fore_bias, back, gain, shift = finish_call(sums, main.mixed, grad)
    return (
        mixed[None], grad[None], qkv, qv, attn, bias, fore, fore_bias.reshape(512), back, gain, shift,
    )


def solution(mesh):
    placed = (
        P("batch", "blk", None),
        P("batch"),
        P(),
        P(),
        P(),
        P(),
        P(),
        P(),
        P(),
        P(),
        P(),
        P("batch", "blk", None),
    )
    fast = dict(mesh.shape) == {"batch": 4, "blk": 8}
    return jax.shard_map(
        fast_body if fast else body,
        mesh=mesh,
        in_specs=placed,
        out_specs=(
            P("batch", "blk", None),
            P("batch", "blk", None),
            P("blk", None),
            P(None, "blk"),
            P("blk", None),
            P(None, "blk"),
            P("blk", None),
            P("blk"),
            P(None, "blk"),
            P(None, "blk"),
            P(None, "blk"),
        ),
        check_vma=False,
    )
```

```python
import math

import jax
import jax.numpy as jnp
from jax import lax
from jax.experimental import pallas as pl
from jax.experimental.pallas import tpu as pltpu
from jax.sharding import PartitionSpec as P

HEADS = 16


eps = 1e-12


def from_partner(x, axis, distance):
    return lax.ppermute(x, axis, [(i, i ^ 1 << distance) for i in range(lax.axis_size(axis))])


def normalize(values, gain, shift):
    centered = values - jnp.mean(values, axis=-1, keepdims=True)
    variance = jnp.mean(centered * centered, axis=-1, keepdims=True)
    return centered * lax.rsqrt(variance + eps) * gain + shift


def gelu_exact(values):
    return jax.nn.gelu(values, approximate=False)


def head_split(matrix, head_count):
    row_count, model_width = matrix.shape
    return matrix.reshape(row_count, head_count // 4, 4, model_width // head_count).transpose(
        1, 2, 0, 3
    )


def head_merge(stacked):
    group_count, group_size, row_count, head_size = stacked.shape
    return stacked.transpose(2, 0, 1, 3).reshape(row_count, group_count * group_size * head_size)


def core_forward(query_part, key_part, value_part, key_valid, scale):
    scores = (
        jnp.einsum("hqd,hkd->hqk", query_part, key_part, preferred_element_type=jnp.float32) * scale
    )
    masked = jnp.where(key_valid, scores, -1e30)
    row_max = jnp.max(masked, axis=-1, keepdims=True)
    exp_scores = jnp.where(key_valid, jnp.exp(masked - row_max), 0.0)
    row_total = jnp.sum(exp_scores, axis=-1, keepdims=True)
    prob_low = (exp_scores / row_total).astype(jnp.bfloat16)
    output = jnp.einsum("hqk,hkd->hqd", prob_low, value_part, preferred_element_type=jnp.float32)
    return (output, (row_max + jnp.log(row_total))[..., 0])


def core_backward(query_part, key_part, value_part, grad_part, log_part, key_valid, scale):
    scores = (
        jnp.einsum("hqd,hkd->hqk", query_part, key_part, preferred_element_type=jnp.float32) * scale
    )
    probs = jnp.where(key_valid, jnp.exp(scores - log_part[..., None]), 0.0)
    grad_probs = jnp.einsum(
        "hqd,hkd->hqk", grad_part, value_part, preferred_element_type=jnp.float32
    )
    inner_sum = jnp.sum(probs * grad_probs, axis=-1, keepdims=True)
    grad_scores = (probs * (grad_probs - inner_sum)).astype(jnp.bfloat16)
    grad_query = (
        jnp.einsum("hqk,hkd->hqd", grad_scores, key_part, preferred_element_type=jnp.float32)
        * scale
    )
    grad_key = (
        jnp.einsum("hqk,hqd->hkd", grad_scores, query_part, preferred_element_type=jnp.float32)
        * scale
    )
    grad_value = jnp.einsum(
        "hqk,hqd->hkd", probs.astype(jnp.bfloat16), grad_part, preferred_element_type=jnp.float32
    )
    return (grad_query, grad_key, grad_value)


def gather_group(kv_pair, position, bit_count):
    buffer_rows = kv_pair
    for step_bit in range(bit_count):
        received = from_partner(buffer_rows, "blk", step_bit)
        high_side = position >> step_bit & 1 == 1
        buffer_rows = jnp.where(
            high_side,
            jnp.concatenate([received, buffer_rows], 0),
            jnp.concatenate([buffer_rows, received], 0),
        )
    return buffer_rows


def spread_group(partials, position, bit_count):
    for step_bit in reversed(range(bit_count)):
        half_rows = partials.shape[0] // 2
        high_side = position >> step_bit & 1 == 1
        lower_part = partials[:half_rows]
        upper_part = partials[half_rows:]
        kept_part = jnp.where(high_side, upper_part, lower_part)
        sent_part = jnp.where(high_side, lower_part, upper_part)
        partials = kept_part + from_partner(sent_part.astype(jnp.bfloat16), "blk", step_bit).astype(
            sent_part.dtype
        )
    return partials


def attend_forward(queries, gathered, key_valid, head_count):
    model_width = queries.shape[1]
    scale = (model_width // head_count) ** (-0.5)
    query_heads = head_split(queries, head_count)
    key_heads = head_split(gathered[:, :model_width], head_count)
    value_heads = head_split(gathered[:, model_width:], head_count)

    def one_group(operands):
        query_part, key_part, value_part = operands
        return core_forward(query_part, key_part, value_part, key_valid, scale)

    outputs, log_sums = lax.map(one_group, (query_heads, key_heads, value_heads))
    return (head_merge(outputs), log_sums)


def attend_backward(queries, gathered, key_valid, log_sums, grad_attended, head_count):
    model_width = queries.shape[1]
    scale = (model_width // head_count) ** (-0.5)
    query_heads = head_split(queries, head_count)
    key_heads = head_split(gathered[:, :model_width], head_count)
    value_heads = head_split(gathered[:, model_width:], head_count)
    grad_heads = head_split(grad_attended, head_count)

    def one_group(operands):
        query_part, key_part, value_part, grad_part, log_part = operands
        return core_backward(
            query_part, key_part, value_part, grad_part, log_part, key_valid, scale
        )

    grad_query, grad_key, grad_value = lax.map(
        one_group, (query_heads, key_heads, value_heads, grad_heads, log_sums)
    )
    return (
        head_merge(grad_query),
        jnp.concatenate([head_merge(grad_key), head_merge(grad_value)], 1),
    )


def layer_forward(hidden, params, key_valid, position, bit_count, head_count):
    w_qkv, qv_bias, w_attn, out_bias, w_in, in_bias, w_back, norm_gain, norm_shift = params
    model_width = hidden.shape[1]
    hidden_low = hidden.astype(jnp.bfloat16)
    bias_row = jnp.concatenate([qv_bias[0], jnp.zeros_like(qv_bias[0]), qv_bias[1]])
    projected = (jnp.dot(hidden_low, w_qkv, preferred_element_type=jnp.float32) + bias_row).astype(
        jnp.bfloat16
    )
    gathered = gather_group(projected[:, model_width:], position, bit_count)
    attended, log_sums = attend_forward(projected[:, :model_width], gathered, key_valid, head_count)
    attended_low = attended.astype(jnp.bfloat16)
    first_sum = (
        hidden + jnp.dot(attended_low, w_attn, preferred_element_type=jnp.float32) + out_bias[0]
    )
    first_norm = normalize(first_sum, norm_gain[0], norm_shift[0])
    first_low = first_norm.astype(jnp.bfloat16)
    inner_pre = jnp.dot(first_low, w_in, preferred_element_type=jnp.float32) + in_bias
    activated = gelu_exact(inner_pre).astype(jnp.bfloat16)
    second_sum = (
        first_norm + jnp.dot(activated, w_back, preferred_element_type=jnp.float32) + out_bias[1]
    )
    output = normalize(second_sum, norm_gain[1], norm_shift[1])
    saved_state = (
        hidden_low,
        projected,
        gathered,
        log_sums,
        attended_low,
        first_sum,
        first_low,
        inner_pre,
        activated,
        second_sum,
    )
    return (output, saved_state)


def layer_backward(grad_output, saved_state, params, key_valid, position, bit_count, head_count):
    w_qkv, qv_bias, w_attn, out_bias, w_in, in_bias, w_back, norm_gain, norm_shift = params
    (
        hidden_low,
        projected,
        gathered,
        log_sums,
        attended_low,
        first_sum,
        first_low,
        inner_pre,
        activated,
        second_sum,
    ) = saved_state
    model_width = hidden_low.shape[1]
    unused_two, pull_two = jax.vjp(normalize, second_sum, norm_gain[1], norm_shift[1])
    grad_second, gain_two, shift_two = pull_two(grad_output)
    grad_branch_two = grad_second.astype(jnp.bfloat16)
    back_grad = jnp.einsum(
        "ra,rb->ab", activated, grad_branch_two, preferred_element_type=jnp.float32
    )
    bias_two = jnp.sum(grad_branch_two.astype(jnp.float32), axis=0)
    grad_act = jnp.dot(grad_branch_two, w_back.T, preferred_element_type=jnp.float32)
    unused_gelu, pull_gelu = jax.vjp(gelu_exact, inner_pre)
    grad_inner = pull_gelu(grad_act)[0].astype(jnp.bfloat16)
    in_grad = jnp.einsum("ra,rb->ab", first_low, grad_inner, preferred_element_type=jnp.float32)
    in_bias_grad = jnp.sum(grad_inner.astype(jnp.float32), axis=0)
    grad_first_norm = grad_second + jnp.dot(grad_inner, w_in.T, preferred_element_type=jnp.float32)
    unused_one, pull_one = jax.vjp(normalize, first_sum, norm_gain[0], norm_shift[0])
    grad_first, gain_one, shift_one = pull_one(grad_first_norm)
    grad_branch = grad_first.astype(jnp.bfloat16)
    attn_grad = jnp.einsum(
        "ra,rb->ab", attended_low, grad_branch, preferred_element_type=jnp.float32
    )
    bias_one = jnp.sum(grad_branch.astype(jnp.float32), axis=0)
    grad_attended = jnp.dot(grad_branch, w_attn.T, preferred_element_type=jnp.float32).astype(
        jnp.bfloat16
    )
    grad_query, grad_pairs = attend_backward(
        projected[:, :model_width], gathered, key_valid, log_sums, grad_attended, head_count
    )
    own_pairs = spread_group(grad_pairs, position, bit_count)
    grad_proj = jnp.concatenate([grad_query, own_pairs], 1).astype(jnp.bfloat16)
    qkv_grad = jnp.einsum("ra,rb->ab", hidden_low, grad_proj, preferred_element_type=jnp.float32)
    column_sums = jnp.sum(grad_proj.astype(jnp.float32), axis=0)
    qv_grad = jnp.stack([column_sums[:model_width], column_sums[2 * model_width :]])
    grad_hidden = grad_first + jnp.dot(grad_proj, w_qkv.T, preferred_element_type=jnp.float32)
    grad_list = (
        qkv_grad,
        qv_grad,
        attn_grad,
        jnp.stack([bias_one, bias_two]),
        in_grad,
        in_bias_grad,
        back_grad,
        jnp.stack([gain_one, gain_two]),
        jnp.stack([shift_one, shift_two]),
    )
    return (grad_hidden, grad_list)


def scatter_once(grad_list):
    (
        qkv_grad,
        qv_grad,
        attn_grad,
        bias_grad,
        in_grad,
        in_bias_grad,
        back_grad,
        gain_grad,
        shift_grad,
    ) = grad_list
    return (
        lax.psum_scatter(qkv_grad, "blk", scatter_dimension=0, tiled=True),
        lax.psum_scatter(qv_grad, "blk", scatter_dimension=1, tiled=True),
        lax.psum_scatter(attn_grad, "blk", scatter_dimension=0, tiled=True),
        lax.psum_scatter(bias_grad, "blk", scatter_dimension=1, tiled=True),
        lax.psum_scatter(in_grad, "blk", scatter_dimension=0, tiled=True),
        lax.psum_scatter(in_bias_grad, "blk", scatter_dimension=0, tiled=True),
        lax.psum_scatter(back_grad, "blk", scatter_dimension=1, tiled=True),
        lax.psum_scatter(gain_grad, "blk", scatter_dimension=1, tiled=True),
        lax.psum_scatter(shift_grad, "blk", scatter_dimension=1, tiled=True),
    )


def body(
    tokens,
    lengths,
    w_qkv,
    qv_bias,
    w_attn,
    out_bias,
    w_in,
    in_bias,
    w_back,
    norm_gain,
    norm_shift,
    cotangent,
):
    row_count = tokens.shape[1]
    head_count = HEADS
    cycle_size = lax.axis_size("blk")
    bit_count = cycle_size.bit_length() - 1
    position = lax.axis_index("blk")
    length = lengths[0]
    key_valid = jnp.arange(cycle_size * row_count) < length
    params = (w_qkv, qv_bias, w_attn, out_bias, w_in, in_bias, w_back, norm_gain, norm_shift)
    out_one, saved_one = layer_forward(
        tokens[0].astype(jnp.float32), params, key_valid, position, bit_count, head_count
    )
    out_two, saved_two = layer_forward(out_one, params, key_valid, position, bit_count, head_count)
    grad_hidden, grads_two = layer_backward(
        cotangent[0].astype(jnp.float32),
        saved_two,
        params,
        key_valid,
        position,
        bit_count,
        head_count,
    )
    grad_hidden, grads_one = layer_backward(
        grad_hidden, saved_one, params, key_valid, position, bit_count, head_count
    )
    shards = scatter_once(jax.tree.map(jnp.add, grads_two, grads_one))
    (
        qkv_part,
        qv_part,
        attn_part,
        bias_part,
        in_part,
        in_bias_part,
        back_part,
        gain_part,
        shift_part,
    ) = shards
    totals = (
        lax.psum(qkv_part.astype(jnp.bfloat16), "batch").astype(jnp.float32),
        lax.psum(qv_part.astype(jnp.bfloat16), "batch").astype(jnp.float32),
        lax.psum(attn_part.astype(jnp.bfloat16), "batch").astype(jnp.float32),
        lax.psum(bias_part.astype(jnp.bfloat16), "batch").astype(jnp.float32),
        lax.psum(in_part.astype(jnp.bfloat16), "batch").astype(jnp.float32),
        lax.psum(in_bias_part.astype(jnp.bfloat16), "batch").astype(jnp.float32),
        lax.psum(back_part.astype(jnp.bfloat16), "batch").astype(jnp.float32),
        lax.psum(gain_part.astype(jnp.bfloat16), "batch").astype(jnp.float32),
        lax.psum(shift_part.astype(jnp.bfloat16), "batch").astype(jnp.float32),
    )
    return (
        out_two.astype(jnp.bfloat16)[None],
        grad_hidden.astype(jnp.bfloat16)[None],
        totals[0],
        totals[1],
        totals[2],
        totals[3],
        totals[4],
        totals[5],
        totals[6],
        totals[7],
        totals[8],
    )


MESH = pl.DeviceIdType.MESH
f32 = jnp.float32
bf16 = jnp.bfloat16
FLIPS = ((0, 0), (1, 0), (0, 1), (1, 1))
GROUPS = len(FLIPS)
PART = 4096 // GROUPS
ROWS, D, FF, LEN, VEC = 128, 1024, 4096, 1024, 144


def dot(a, b):
    return jnp.dot(a, b, preferred_element_type=f32)


def dot_t(a, b):
    return lax.dot_general(a, b, (((1,), (1,)), ((), ())), preferred_element_type=f32)


def dot_0(a, b):
    return lax.dot_general(a, b, (((0,), (0,)), ((), ())), preferred_element_type=f32)


def span(at, size):
    return pl.ds(pl.multiple_of(at * size, size), size)


def flip(bit, by):
    return bit + by * (1 - 2 * bit)


def group(ref, n):
    return ref.at[pl.ds(n * ROWS, ROWS)]


class Spot:
    def __init__(self):
        self.row, self.pos = lax.axis_index("batch"), lax.axis_index("blk")
        self.x, self.c = self.row // 2, self.row % 2
        self.z, self.y = self.pos // 2, self.pos % 2
        self.zl, self.zh = self.z % 2, self.z // 2
        self.place = self.c * 4 + self.zl * 2 + self.y
        self.moved = self.c != self.zh

    def flipped(self, c=0, x=0, y=0, zl=0, zh=0):
        row = flip(self.x, x) * 2 + flip(self.c, c)
        pos = flip(self.zh, zh) * 4 + flip(self.zl, zl) * 2 + flip(self.y, y)
        return {"batch": row, "blk": pos}

    def member(self, place):
        return {"batch": self.x * 2 + place // 4, "blk": self.zh * 4 + place % 4}

    def partner(self):
        return {"batch": self.x * 2 + self.zh, "blk": self.c * 4 + self.pos % 4}


BULK = 2**21


class Group:
    def __init__(self, at):
        self.at, self.bytes, self.waited = at, 0, False


def bytes_of(ref):
    return math.prod(ref.shape) * jnp.dtype(ref.dtype).itemsize


class Link:
    def __init__(self, send_sem, recv_sem, own_sem, *meters):
        self.send_sem, self.recv_sem, self.own_sem, self.meters = send_sem, recv_sem, own_sem, meters
        self.count, self.own_count = 0, 0
        self.groups, self.own_groups, self.swaps = [], [], []
        self.bulk, self.own_bulk = self.group(), self.own_group()

    def group(self):
        self.groups.append(Group(self.count))
        self.count += 1
        return self.groups[-1]

    def own_group(self):
        self.own_groups.append(Group(self.own_count))
        self.own_count += 1
        return self.own_groups[-1]

    def put(self, src, dst, device, group=None):
        if group is None:
            if self.bulk.bytes + bytes_of(src) > BULK:
                self.bulk = self.group()
            group = self.bulk
        group.bytes += bytes_of(src)
        pltpu.make_async_remote_copy(
            src_ref=src, dst_ref=dst, send_sem=self.send_sem.at[group.at], recv_sem=self.recv_sem.at[group.at],
            device_id=device, device_id_type=MESH,
        ).start()
        return group

    def keep(self, src, dst, group=None):
        if group is None:
            if self.own_bulk.bytes + bytes_of(src) > BULK:
                self.own_bulk = self.own_group()
            group = self.own_bulk
        group.bytes += bytes_of(src)
        pltpu.make_async_copy(src, dst, self.own_sem.at[group.at]).start()
        return group

    def wait(self, group, sem):
        if group.bytes:
            for meter in self.meters:
                row = bytes_of(meter) // meter.shape[0]
                tile = 8 if meter.dtype == f32 else 16
                if group.bytes % (tile * row) == 0 and group.bytes <= bytes_of(meter):
                    view = meter.at[pl.ds(0, group.bytes // row)]
                    pltpu.make_async_copy(view, view, sem.at[group.at]).wait()
                    return
            raise ValueError(group.bytes)

    def arrive(self, *groups):
        for group in groups:
            if not group.waited:
                group.waited = True
                self.wait(group, self.own_sem if any(group is own for own in self.own_groups) else self.recv_sem)

    def swap(self, spot, src, dst):
        far = pltpu.make_async_remote_copy(
            src_ref=src, dst_ref=dst, send_sem=self.send_sem.at[self.count], recv_sem=self.recv_sem.at[self.count],
            device_id=spot.partner(), device_id_type=MESH,
        )
        near = pltpu.make_async_copy(src, dst, self.own_sem.at[self.own_count])
        self.count += 1
        self.own_count += 1
        pl.when(spot.moved)(far.start)
        pl.when(jnp.logical_not(spot.moved))(near.start)
        self.swaps.append((spot, far, near))
        return far, near

    def arrive_swap(self, spot, pair):
        pl.when(spot.moved)(pair[0].wait_recv)
        pl.when(jnp.logical_not(spot.moved))(pair[1].wait)
        self.swaps = [(one, far, None if far is pair[0] else near) for one, far, near in self.swaps]

    def finish(self):
        self.arrive(*self.groups, *self.own_groups)
        for group in self.groups:
            self.wait(group, self.send_sem)
        for spot, far, near in self.swaps:
            if near is not None:
                self.arrive_swap(spot, (far, near))
            pl.when(spot.moved)(far.wait_send)


def greet(spot, devices):
    barrier = pltpu.get_barrier_semaphore()
    for device in devices:
        pl.semaphore_signal(barrier, inc=1, device_id=device, device_id_type=MESH)

    @pl.when(spot.moved)
    def _():
        pl.semaphore_signal(barrier, inc=1, device_id=spot.partner(), device_id_type=MESH)

    def meet():
        @pl.when(spot.moved)
        def _():
            pl.semaphore_wait(barrier, len(devices) + 1)

        @pl.when(jnp.logical_not(spot.moved))
        def _():
            pl.semaphore_wait(barrier, len(devices))

    return meet


def standard(values):
    centered = values - jnp.mean(values, axis=-1, keepdims=True)
    inverse = lax.rsqrt(jnp.mean(centered * centered, axis=-1, keepdims=True) + eps)
    return centered * inverse, inverse


def standard_back(unit, inverse, gain, grad):
    scaled = grad * gain
    inner = jnp.mean(scaled * unit, axis=-1, keepdims=True)
    return inverse * (scaled - jnp.mean(scaled, axis=-1, keepdims=True) - unit * inner)


def column_sum(x):
    return jnp.sum(x.astype(f32), axis=0, keepdims=True)


def gelu_pair(u):
    t = 1.0 / (1.0 + 0.23164188 * jnp.abs(u))
    bell = jnp.exp(-0.5 * u * u)
    poly = t * (0.127414796 + t * (-0.142248368 + t * (0.7107068705 + t * (-0.7265760135 + t * 0.5307027145))))
    tail = poly * bell
    cdf = jnp.where(u < 0, tail, 1.0 - tail)
    return u * cdf, cdf + u * bell * 0.3989422804


def low_lanes():
    return lax.broadcasted_iota(jnp.int32, (1, 128), 1) < 64


def valid_keys(length):
    return lax.broadcasted_iota(jnp.int32, (1, LEN), 1).astype(f32) < length


def attention_rows(qkv, rows, valid):
    queries, keys, values = qkv[rows, 0:128], qkv[:, 128:256], qkv[:, 256:384]
    low_half = low_lanes()
    outs, lses = [], []
    for half in range(2):
        mine = low_half if half == 0 else jnp.logical_not(low_half)
        part = jnp.where(mine, queries, jnp.zeros_like(queries)) * jnp.asarray(0.125, bf16)
        scores = jnp.where(valid, dot_t(part, keys), -1e30)
        top = jnp.max(scores, axis=1, keepdims=True)
        expd = jnp.exp(scores - top)
        total = jnp.sum(expd, axis=1, keepdims=True)
        probs = (expd * (1.0 / total)).astype(bf16)
        outs.append(dot(probs, values))
        lses.append(top + jnp.log(total))
    return jnp.where(low_half, outs[0], outs[1]), jnp.where(low_half, lses[0], lses[1])


def attention_back_keys(qkv, grads_ref, lse_rows, delta_rows, rows, first, length):
    low_half = low_lanes()
    keys, values = qkv[rows, 128:256], qkv[rows, 256:384]
    at = lax.broadcasted_iota(jnp.int32, (256, 1), 0) + first
    valid = at.astype(f32) < length
    dqs, dk, dv = [], None, None
    for half in range(2):
        mine = low_half if half == 0 else jnp.logical_not(low_half)
        k_part = jnp.where(mine, keys, jnp.zeros_like(keys)) * jnp.asarray(0.125, bf16)
        v_part = jnp.where(mine, values, jnp.zeros_like(values))
        queries, grads = qkv[:, 0:128], grads_ref[...]
        scores = dot_t(k_part, queries)
        probs = jnp.where(valid, jnp.exp(scores - lse_rows[half : half + 1, :]), 0.0)
        dp = dot_t(v_part, grads)
        ds = (probs * (dp - delta_rows[half : half + 1, :])).astype(bf16)
        dv_part = dot(probs.astype(bf16), grads)
        dk_part = dot(ds, queries)
        dv = dv_part if half == 0 else jnp.where(low_half, dv, dv_part)
        dk = dk_part if half == 0 else jnp.where(low_half, dk, dk_part)
        dqs.append(dot_0(ds, keys))
    return jnp.where(low_half, dqs[0], dqs[1]), (dk * 0.125).astype(bf16), dv.astype(bf16)


def attention_back_start(s, o, lse, grads):
    turned = lse[...].T
    s.lse_rows[0:1, :] = turned[0:1, :]
    s.lse_rows[1:2, :] = turned[64:65, :]
    product = (grads[...].astype(f32) * o[...]).T
    s.delta_rows[0:1, :] = jnp.sum(product[0:64, :], axis=0, keepdims=True)
    s.delta_rows[1:2, :] = jnp.sum(product[64:128, :], axis=0, keepdims=True)


def attention_back_step(link, spot, step, s, qkv, grads, dqkvh, group, own):
    pair = (spot.place // 2 + step) % 4
    rows = span(pair, 256)
    dq, dk, dv = attention_back_keys(
        qkv, grads, s.lse_rows, s.delta_rows, rows, pair * 256, s.length[0:1, 0:1]
    )
    dqkvh[rows, 128:256] = dk
    dqkvh[rows, 256:384] = dv
    s.dq[...] = dq if step == PAIR_STEPS[0] else s.dq[...] + dq
    for part in (1, 2):
        send_rows(link, spot, dqkvh, s.dqkv, step, part, group, own)


def attention_back_end(link, spot, s, dqkvh, group, own):
    dqkvh[:, 0:128] = (s.dq[...] * 0.125).astype(bf16)
    for step in PAIR_STEPS:
        send_rows(link, spot, dqkvh, s.dqkv, step, 0, group, own)


def send_columns(link, spot, source, target, part, landing, groups, own):
    for step in range(7, -1, -1):
        to = (spot.place + step) % 8
        src = source.at[:, pl.ds(pl.multiple_of(part * D + to * 128, 128), 128)]
        dst = target.at[span(spot.place, ROWS), pl.ds(landing * 128, 128)]
        if step:
            link.put(src, dst, spot.member(to), groups[step])
        else:
            link.keep(src, dst, own)


def pair_rows(spot, step):
    return span((spot.place // 2 + step) % 4, 256)


def send_rows(link, spot, source, target, step, part, group, own):
    same = (spot.place + 2 * step) % 8
    for n, to in enumerate((same, same + 1 - 2 * spot.y)):
        src = source.at[span(to, ROWS), pl.ds(part * 128, 128)]
        dst = target.at[:, pl.ds(pl.multiple_of(part * D + spot.place * 128, 128), 128)]
        if step or n:
            link.put(src, dst, spot.member(to), group)
        else:
            link.keep(src, dst, own)


PAIR_STEPS = (1, 2, 3, 0)


def spec(**named):
    return named


def two(*entry):
    return [entry, entry]


MAIN_OUT = spec(
    mixed=((ROWS, D), bf16), qkv1=((LEN, 384), bf16), lse1=((LEN, 128), f32), o1=((LEN, 128), f32),
    left_attn=((4, ROWS, D), bf16), right_attn=((4 * ROWS, 512), bf16),
    left_back=((2 * GROUPS, ROWS, D), bf16), right_back=((2 * GROUPS * ROWS, PART), bf16),
    left_in=((2 * GROUPS, ROWS, D), bf16), right_in=((2 * GROUPS * ROWS, PART), bf16),
    hidden=((2, LEN, D), bf16), dqkv2=((LEN, 384), bf16),
    du1=((ROWS, FF), bf16), dza1=((ROWS, D), bf16),
    do1=((ROWS, D), bf16), dr1=((ROWS, D), f32), vec=((8, D), f32), inb=((1, FF), f32),
    length=((16, 128), f32),
)
MAIN_SCRATCH = spec(
    w_qkv=((D, 3 * D), bf16), w_attn=((D, D), bf16), w_in=((D, FF), bf16), w_back=((FF, D), bf16),
    tok=((ROWS, D), bf16), cot=((ROWS, D), bf16), length=((16, 128), f32), sent_length=((16, 128), f32),
    proj=two((ROWS, 3 * D), bf16), qkv=two((LEN, 384), bf16), lse=two((LEN, 128), f32),
    o=two((LEN, 128), bf16), full_o=two((LEN, 128), f32), att=two((ROWS, D), bf16), n=two((ROWS, D), bf16),
    act=two((ROWS, FF), bf16), slope=two((ROWS, FF), bf16),
    unit_a=two((ROWS, D), f32), unit_b=two((ROWS, D), f32),
    inv_a=two((ROWS, 128), f32), inv_b=two((ROWS, 128), f32),
    hq2=((ROWS, D), bf16), h=((ROWS, D), f32), acc=((ROWS, D), f32), mixed=((ROWS, D), bf16),
    dzb=two((ROWS, D), bf16), du=two((ROWS, FF), bf16), dza=two((ROWS, D), bf16), do=two((ROWS, D), bf16),
    doh=((LEN, 128), bf16), dqkvh=((LEN, 384), bf16), dq=((LEN, 128), f32), lse_rows=((8, LEN), f32), delta_rows=((8, LEN), f32),
    dqkv=((ROWS, 3 * D), bf16), dr1=((ROWS, D), f32), vec=((8, D), f32), inb=((1, FF), f32),
)


class Refs:
    pass


def flat(entries):
    out = []
    for entry in entries.values():
        out += entry if isinstance(entry, list) else [entry]
    return out


def bind(entries, refs):
    got, it = Refs(), iter(refs)
    for name, entry in entries.items():
        setattr(got, name, [next(it) for _ in entry] if isinstance(entry, list) else next(it))
    return got


def main_kernel(*refs):
    (len_ref, tokens, cotangent, w_qkv, w_attn, w_in, w_back,
     qv_bias, out_bias, in_bias, gain, shift) = refs[:12]
    outs = bind(MAIN_OUT, refs[12 : 12 + len(MAIN_OUT)])
    rest = refs[12 + len(MAIN_OUT) :]
    s = bind(MAIN_SCRATCH, rest[:-4])
    load_sem, send_sem, recv_sem, own_sem = rest[-4:]
    spot = Spot()
    link = Link(send_sem, recv_sem, own_sem, outs.hidden.at[0], outs.lse1)
    others = [spot.member((spot.place + step) % 8) for step in range(1, 8)]
    others += [spot.flipped(x=1), spot.flipped(c=1, x=1)]
    meet = greet(spot, others)

    loads = []
    for n, (src, dst) in enumerate(
        [(w_qkv.at[:, pl.ds(D * part, D)], s.w_qkv.at[:, pl.ds(D * part, D)]) for part in (1, 2, 0)]
        + [(w_attn, s.w_attn), (w_in, s.w_in), (w_back, s.w_back)]
    ):
        loads.append(pltpu.make_async_copy(src, dst, load_sem.at[n]))
        loads[n].start()
    loaded = set()

    def need(n):
        if n not in loaded:
            loaded.add(n)
            loads[n].wait()

    s.sent_length[...] = jnp.full((16, 128), len_ref[0], jnp.int32).astype(f32)
    meet()
    first_in = [link.swap(spot, tokens, s.tok), link.swap(spot, s.sent_length, s.length)]
    for pair in first_in:
        link.arrive_swap(spot, pair)
    valid = valid_keys(s.length[0:1, 0:1])

    later = []

    def share(source, left, d):
        link.keep(source, left.at[d])
        link.put(source, left.at[2 + d], spot.flipped(c=1))
        link.put(source, left.at[4 + d], spot.flipped(x=1))

    def deal(source, right, d):
        link.keep(source.at[:, span(spot.c * 2 + spot.x, PART)], group(right, d))
        for n, (dc, dx) in enumerate(FLIPS[1:], 1):
            cols = span(flip(spot.c, dc) * 2 + flip(spot.x, dx), PART)
            link.put(source.at[:, cols], group(right, 2 * n + d), spot.flipped(c=dc, x=dx))

    def gather(hq, d, part):
        rows = pl.ds(part * 64, 64)
        block = outs.hidden.at[d, pl.ds(pl.multiple_of(spot.place * ROWS + part * 64, 64), 64)]
        for dz, dy in ((1, 0), (0, 1), (1, 1)):
            link.put(hq.at[rows], block, spot.flipped(zl=dz, y=dy))
        link.keep(hq.at[rows], block)

    def forward(d, hq, h):
        pair_of = [0, 3, 3, 2, 2, 1, 1, 1]
        both, pairs, own = link.group(), [link.group() for _ in range(4)], link.own_group()
        for part, number in ((1, 0), (2, 1), (0, 2)):
            need(number)

            def tile(i, carry):
                cols = span(2 * part + i, 512)
                value = dot(hq[...], s.w_qkv[:, cols])
                if part != 1:
                    value += qv_bias[part // 2 : part // 2 + 1, span(i, 512)]
                s.proj[d][:, cols] = value.astype(bf16)
                return carry

            lax.fori_loop(0, 2, tile, 0)
            to_groups = [both] * 8 if part else [pairs[pair] for pair in pair_of]
            send_columns(link, spot, s.proj[d], s.qkv[d], part, part, to_groups, own)
        link.arrive(both, own)
        if d == 0:
            later.append(link.swap(spot, cotangent, s.cot))
        to_rows, own_rows = link.group(), link.own_group()
        for step in PAIR_STEPS:
            link.arrive(pairs[step])
            rows = pair_rows(spot, step)
            s.full_o[d][rows, :], s.lse[d][rows, :] = attention_rows(s.qkv[d], rows, valid)
            s.o[d][rows, :] = s.full_o[d][rows, :].astype(bf16)
            send_rows(link, spot, s.o[d], s.att[d], step, 0, to_rows, own_rows)
        if d == 0:
            link.keep(s.qkv[0], outs.qkv1)
            link.keep(s.lse[0], outs.lse1)
            link.keep(s.full_o[0], outs.o1)
        link.arrive(to_rows, own_rows)
        gather(s.tok, 0, d)
        need(3)
        unit, inverse = standard(h[...].astype(f32) + dot(s.att[d][...], s.w_attn[...]) + out_bias[0:1])
        link.keep(s.att[d], outs.left_attn.at[d])
        link.put(s.att[d], outs.left_attn.at[2 + d], spot.flipped(c=1))
        s.unit_a[d][...] = unit
        s.inv_a[d][...] = jnp.broadcast_to(inverse, (ROWS, 128))
        first = unit * gain[0:1] + shift[0:1]
        s.n[d][...] = first.astype(bf16)
        share(s.n[d], outs.left_in, d)
        s.acc[...] = first + out_bias[1:2]
        need(4)
        need(5)

        def inner(i, carry):
            cols = span(i, 512)
            act, slope = gelu_pair(dot(s.n[d][...], s.w_in[:, cols]) + in_bias[:, cols])
            act = act.astype(bf16)
            s.act[d][:, cols] = act
            s.slope[d][:, cols] = slope.astype(bf16)
            s.acc[...] += dot(act, s.w_back[cols, :])
            return carry

        lax.fori_loop(0, 8, inner, 0)
        deal(s.act[d], outs.right_back, d)
        unit, inverse = standard(s.acc[...])
        s.unit_b[d][...] = unit
        s.inv_b[d][...] = jnp.broadcast_to(inverse, (ROWS, 128))
        return unit * gain[1:2] + shift[1:2]

    def add_vec(at, value, fresh):
        s.vec[at : at + 1, :] = value if fresh else s.vec[at : at + 1, :] + value

    def backward(d, grad, fresh):
        unit = s.unit_b[d][...]
        add_vec(3, column_sum(grad * unit), fresh)
        add_vec(5, column_sum(grad), fresh)
        dr = standard_back(unit, s.inv_b[d][:, 0:1], gain[1:2], grad)
        s.acc[...] = dr
        low = dr.astype(bf16)
        s.dzb[d][...] = low
        share(s.dzb[d], outs.left_back, d)
        add_vec(1, column_sum(low), fresh)

        def inner(i, carry):
            cols = span(i, 512)
            du = (dot_t(s.dzb[d][...], s.w_back[cols, :]) * s.slope[d][:, cols].astype(f32)).astype(bf16)
            s.du[d][:, cols] = du
            total = column_sum(du)
            s.inb[:, cols] = total if fresh else s.inb[:, cols] + total
            s.acc[...] += dot_t(du, s.w_in[:, cols])
            return carry

        lax.fori_loop(0, 8, inner, 0)
        if d:
            deal(s.du[d], outs.right_in, d)
        else:
            link.keep(s.du[d], outs.du1)
        grad = s.acc[...]
        unit = s.unit_a[d][...]
        add_vec(2, column_sum(grad * unit), fresh)
        add_vec(4, column_sum(grad), fresh)
        dr = standard_back(unit, s.inv_a[d][:, 0:1], gain[0:1], grad)
        s.dr1[...] = dr
        low = dr.astype(bf16)
        s.dza[d][...] = low
        if d:
            link.keep(s.dza[d].at[:, span(spot.c, 512)], group(outs.right_attn, d))
            link.put(s.dza[d].at[:, span(1 - spot.c, 512)], group(outs.right_attn, 2 + d), spot.flipped(c=1))
        else:
            link.keep(s.dza[d], outs.dza1)
        add_vec(0, column_sum(low), fresh)
        s.do[d][...] = dot_t(low, s.w_attn[...]).astype(bf16)

    out = forward(0, s.tok, s.tok)
    s.h[...] = out
    s.hq2[...] = out.astype(bf16)
    out = forward(1, s.hq2, s.h)
    s.mixed[...] = out.astype(bf16)
    link.swap(spot, s.mixed, outs.mixed)
    link.arrive_swap(spot, later[0])
    gather(s.hq2, 1, 0)
    backward(1, s.cot[...].astype(f32), True)
    to_heads, own_heads = link.group(), link.own_group()
    send_columns(link, spot, s.do[1], s.doh, 0, 0, [to_heads] * 8, own_heads)
    link.arrive(to_heads, own_heads)
    attention_back_start(s, s.full_o[1], s.lse[1], s.doh)
    to_rows, own_rows, last_rows, own_last = link.group(), link.own_group(), link.group(), link.own_group()
    for step in PAIR_STEPS:
        attention_back_step(link, spot, step, s, s.qkv[1], s.doh, s.dqkvh, to_rows, own_rows)
    attention_back_end(link, spot, s, s.dqkvh, last_rows, own_last)
    link.keep(s.dqkvh, outs.dqkv2)
    link.arrive(to_rows, own_rows)
    s.dr1[...] += dot_t(s.dqkv[:, D:], s.w_qkv[:, D:])
    link.arrive(last_rows, own_last)
    gather(s.hq2, 1, 1)
    backward(0, s.dr1[...] + dot_t(s.dqkv[:, :D], s.w_qkv[:, :D]), False)
    link.keep(s.do[0], outs.do1)
    link.keep(s.dr1, outs.dr1)
    small = link.own_group()
    link.keep(s.vec, outs.vec, small)
    link.keep(s.inb, outs.inb, small)
    link.keep(s.length, outs.length, small)
    link.finish()


def main_call(length, tokens, cotangent, params):
    w_qkv, qv_bias, w_attn, out_bias, w_in, in_bias, w_back, gain, shift = params
    dma = pltpu.SemaphoreType.DMA
    vmem, hbm = pl.BlockSpec(memory_space=pltpu.VMEM), pl.BlockSpec(memory_space=pl.ANY)
    results = pl.pallas_call(
        main_kernel,
        out_shape=[jax.ShapeDtypeStruct(*entry) for entry in MAIN_OUT.values()],
        in_specs=[pl.BlockSpec(memory_space=pltpu.SMEM), hbm, hbm] + [hbm] * 4 + [vmem] * 5,
        out_specs=[hbm] * len(MAIN_OUT),
        scratch_shapes=[pltpu.VMEM(*entry) for entry in flat(MAIN_SCRATCH)]
        + [dma((6,)), dma((32,)), dma((32,)), dma((20,))],
        compiler_params=pltpu.CompilerParams(
            collective_id=1, has_side_effects=True, vmem_limit_bytes=60 * 2**20
        ),
    )(length, tokens, cotangent, w_qkv, w_attn, w_in, w_back, qv_bias, out_bias, in_bias[None], gain, shift)
    return bind(MAIN_OUT, results)


PATHS = spec(A="yxabXC", B="xyabXC", C="abysC", F="yabVK", G="aybVK")
CHUNKS = (
    ("B", 0, 0, 512),
    ("F", 1, 0, 128),
    ("F", 1, 128, 128),
    ("F", 1, 256, 256),
    ("F", 1, 512, 256),
    ("F", 1, 768, 256),
    ("F", 2, 0, 256),
    ("F", 2, 256, 256),
    ("G", 2, 512, 256),
    ("F", 2, 768, 128),
    ("F", 2, 896, 128),
)
ORDER = (
    (100, 12), (100, 13), (100, 10), (100, 1), (100, 2), (100, 3), (100, 4), (100, 5), (100, 6), (8, -1),
    (100, 9), (9, -1), (0, -1), (7, -1), (6, -1), (100, 14), (9, 0), (5, -1), (7, 0), (4, -1),
    (8, 0), (2, -1), (6, 0), (3, -1), (0, 0), (1, -1), (100, 7), (9, 1), (7, 1), (5, 0),
    (10, -1), (6, 1), (9, 2), (4, 0), (7, 2), (5, 1), (100, 8), (9, 3), (8, 1), (7, 3),
    (9, 4), (6, 2), (2, 0), (7, 4), (4, 1), (6, 3), (5, 2), (6, 4), (3, 0), (5, 3),
    (5, 4), (8, 2), (2, 1), (0, 1), (8, 3), (4, 2), (3, 1), (8, 4), (1, 0), (2, 2),
    (4, 3), (2, 3), (0, 2), (4, 4), (10, 0), (2, 4), (3, 2), (1, 1), (100, 11), (3, 3),
    (10, 1), (0, 3), (1, 2), (3, 4), (10, 2), (0, 4), (1, 3), (10, 3), (0, 5), (1, 4),
    (10, 4),
)
IN_OUT = spec(back=0, fore=FF, attn=2 * FF, qkv=2 * FF + D)


def plan(path, width):
    slabs, steps = 8, []
    for stage in path:
        if stage in "yab":
            slabs //= 2
        elif stage == "x":
            width //= 2
        elif stage == "X":
            width *= 2
        steps.append((stage, slabs, width))
    return steps


def chunk_rows(c):
    return VEC if c == 0 else ROWS


SEMS = 20 + sum(len(PATHS[chunk[0]]) for chunk in CHUNKS)
PLANS = [plan(PATHS[chunk[0]], chunk[3]) for chunk in CHUNKS]
GRAD_SCRATCH = spec(
    left=[((4, ROWS, D), bf16)] + two((2 * GROUPS, ROWS, D), bf16),
    right=[((4 * ROWS, 512), bf16)] + two((2 * GROUPS * ROWS, PART), bf16),
    turned=[((D, 512), bf16)] + two((D, 256 * GROUPS), bf16),
    chunk=[((8, chunk_rows(c), CHUNKS[c][3]), bf16) for c in range(len(CHUNKS))],
    landing=[
        ((slabs, chunk_rows(c), width), bf16)
        for c, steps in enumerate(PLANS) for stage, slabs, width in steps if stage in "yabxs"
    ],
    hidden=two((LEN, D), bf16), dqkvh=two((LEN, 384), bf16),
    chunk_q=((8, VEC, 384), bf16), landing_q=two((4, VEC, 384), bf16),
    qkv=((LEN, 384), bf16), lse=((LEN, 128), f32), doh=((LEN, 128), bf16),
    o=((LEN, 128), f32), dq=((LEN, 128), f32), lse_rows=((8, LEN), f32), delta_rows=((8, LEN), f32),
    dqkv=((ROWS, 3 * D), bf16), w_qkv=((D, 3 * D), bf16),
    dr1=((ROWS, D), f32), grad=((ROWS, D), bf16), vec=((8, D), f32), inb=((1, FF), f32), length=((16, 128), f32),
)


def grad_kernel(*refs):
    src = bind(MAIN_OUT, refs[: len(MAIN_OUT)])
    w_qkv, sums, grad_out = refs[len(MAIN_OUT) : len(MAIN_OUT) + 3]
    rest = refs[len(MAIN_OUT) + 3 :]
    s = bind(GRAD_SCRATCH, rest[:-3])
    s.out = sums
    spot = Spot()
    link = Link(*rest[-3:], src.hidden.at[0], src.lse1, w_qkv)
    x, y, c, zl, zh = spot.x, spot.y, spot.c, spot.zl, spot.zh
    others = [spot.member((spot.place + step) % 8) for step in range(1, 8)]
    others += [spot.flipped(x=1), spot.flipped(c=1, x=1), spot.flipped(zh=1)]
    meet = greet(spot, others)
    mine = span(c * 2 + x, PART)
    heads_in, vec_in, hidden_in, dqkv_in, close_in, left_in, right_in, weight_in = [link.own_group() for _ in range(8)]
    length_in = link.own_group()
    own_ready = [link.own_group() for _ in range(3)]
    for one, other in ((src.o1, s.o), (src.qkv1, s.qkv), (src.lse1, s.lse)):
        link.keep(one, other, heads_in)
    link.keep(src.length, s.length, length_in)
    link.keep(src.left_attn, s.left[0], own_ready[0])
    for n in (1, 3):
        link.keep(group(src.right_attn, n), group(s.right[0], n), own_ready[0])
    link.keep(src.dza1.at[:, span(c, 512)], group(s.right[0], 0), own_ready[0])
    link.keep(src.right_back, s.right[1], right_in)
    first = pl.ds(0, 6)
    link.keep(src.left_back.at[first], s.left[1].at[first], own_ready[1])
    link.keep(src.left_in.at[first], s.left[2].at[first], left_in)
    link.keep(src.du1.at[:, mine], group(s.right[2], 0), own_ready[2])
    for n in range(GROUPS):
        link.keep(group(src.right_in, 2 * n + 1), group(s.right[2], 2 * n + 1), own_ready[2])
    link.keep(src.vec, s.vec, vec_in)
    link.keep(src.inb, s.inb, vec_in)
    rows = span(c, 512)
    for d in range(2):
        link.keep(src.hidden.at[d, rows], s.hidden[d].at[rows], hidden_in)
    link.keep(src.dqkv2, s.dqkvh[1], dqkv_in)
    link.keep(w_qkv, s.w_qkv, weight_in)
    link.keep(src.dr1, s.dr1, close_in)
    meet()
    to_heads, own_heads, far_hidden = link.group(), link.own_group(), link.group()
    far_ready = [link.group() for _ in range(3)]
    send_columns(link, spot, src.do1, s.doh, 0, 0, [to_heads] * 8, own_heads)
    link.put(src.dza1.at[:, span(1 - c, 512)], group(s.right[0], 2), spot.flipped(c=1), far_ready[0])
    far_left = link.group()
    here, there = pl.ds(4, 2), pl.ds(6, 2)
    link.put(src.left_back.at[here], s.left[1].at[there], spot.flipped(c=1), far_ready[1])
    link.put(src.left_in.at[here], s.left[2].at[there], spot.flipped(c=1), far_left)
    for n, (dc, dx) in enumerate(FLIPS[1:], 1):
        cols = span(flip(c, dc) * 2 + flip(x, dx), PART)
        link.put(src.du1.at[:, cols], group(s.right[2], 2 * n), spot.flipped(c=dc, x=dx), far_ready[2])
    for d in range(2):
        link.put(src.hidden.at[d, rows], s.hidden[d].at[rows], spot.flipped(c=1), far_hidden)

    bits = spec(y=y, a=zl, b=zh)
    across = spec(
        y=spot.flipped(y=1), a=spot.flipped(zl=1), b=spot.flipped(zh=1), x=spot.flipped(x=1), C=spot.flipped(c=1)
    )
    across.update(spec(X=across["x"], V=across["x"], s=across["x"], K=across["C"]))
    current, landing, copies = {}, {}, {}
    it = iter(s.landing)
    for n, steps in enumerate(PLANS):
        for i, step in enumerate(steps):
            if step[0] in "yabxs":
                landing[n, i] = next(it)
    waiting = [True, True, True]

    def turn(k):
        if k == 2:
            link.arrive(left_in, far_left)
        else:
            link.arrive(own_ready[k], far_ready[k])
            if k == 1:
                link.arrive(right_in)
        count = s.left[k].shape[0]
        for g in range(count):
            s.turned[k][:, pl.ds(ROWS * g, ROWS)] = s.left[k][g].T

    def compute(n):
        _, k, first, wide = CHUNKS[n]
        if k == 2 and waiting[2]:
            waiting[2] = False
            link.arrive(own_ready[2], far_ready[2])
        path = [stage for stage in PATHS[CHUNKS[n][0]] if stage in "yab"]
        path += [stage for stage in "yab" if stage not in path]

        def piece(i, carry):
            product = dot(s.turned[k][span(i, 256), :], s.right[k][:, pl.ds(first, wide)]).astype(bf16)
            for low in range(2):
                bit = spec(y=low, a=i % 2, b=i // 2)
                at_slab = (bit[path[0]] * 2 + bit[path[1]]) * 2 + bit[path[2]]
                s.chunk[n][at_slab, 0:ROWS] = product[ROWS * low : ROWS * (low + 1)]
            return carry

        lax.fori_loop(0, 4, piece, 0)
        if n == 0:
            link.arrive(vec_in)
            for shard in range(8):
                bit = spec(y=shard % 2, a=shard // 2 % 2, b=shard // 4)
                at_slab = (bit[path[0]] * 2 + bit[path[1]]) * 2 + bit[path[2]]
                vec = s.vec[:, pl.ds(shard * 128, 128)]
                top = jnp.concatenate([vec, jnp.zeros((8, 384), f32)], 1)
                low = jnp.broadcast_to(s.inb[:, pl.ds(shard * 512, 512)], (8, 512))
                s.chunk[n][at_slab, ROWS:VEC] = jnp.concatenate([top, low], 0).astype(bf16)
        current[n] = s.chunk[n]

    def base_of(n):
        _, k, first, _ = CHUNKS[n]
        if k == 0:
            return IN_OUT["attn"] + c * 512 + first, 0
        return IN_OUT["back" if k == 1 else "fore"] + c * 2 * PART + first, PART

    def columns(n, quarter, offset, width):
        start, stride = base_of(n)
        return pl.ds(pl.multiple_of(start + quarter * stride + offset, 128), width)

    def send(n, i):
        stage, slabs, width = PLANS[n][i]
        rows = pl.ds(0, chunk_rows(n))
        now, todo = current[n], []
        if stage in "yab":
            todo.append((now.at[pl.ds((1 - bits[stage]) * slabs, slabs)], landing[n, i]))
        elif stage == "x":
            todo.append((now.at[:, :, pl.ds(pl.multiple_of((1 - x) * width, 128), width)], landing[n, i]))
        elif stage == "s":
            todo.append((now, landing[n, i]))
        else:
            offset = x * (width // 2) if stage == "X" else 0
            width = width // 2 if stage == "X" else width
            for quarter in [x] if stage == "V" else range(2) if stage == "K" else [0]:
                where = s.out.at[rows, columns(n, quarter, offset, width)]
                todo.append((where, where))
        copies[n, i] = link.group()
        for here, there in todo:
            link.put(here, there, across[stage], copies[n, i])

    def advance(n, i):
        stage, slabs, width = PLANS[n][i]
        link.arrive(copies[n, i])
        if stage not in "yabxs":
            return
        got, old = landing[n, i], current[n]

        def add(m, carry):
            if stage in "yab":
                kept = old[bits[stage] * slabs + m]
            elif stage == "x":
                kept = old[m, :, pl.ds(pl.multiple_of(x * width, 128), width)]
            else:
                kept = old[m]
            got[m] = (got[m].astype(f32) + kept.astype(f32)).astype(bf16)
            return carry

        lax.fori_loop(0, slabs, add, 0)
        current[n] = got
        follow = PLANS[n][i + 1][0]
        if follow in "VXC":
            offset = x * width if follow == "X" else 0
            s.out[0 : chunk_rows(n), columns(n, x if follow == "V" else 0, offset, width)] = got[0]

    state = Refs()
    rows_kv, own_kv, rows_q, own_q = link.group(), link.own_group(), link.group(), link.own_group()

    def fold_q(n, bit):
        got = s.landing_q[n]
        slabs = got.shape[0]
        old = s.chunk_q if n == 0 else s.landing_q[0]

        def add(m, carry):
            got[m] = (got[m].astype(f32) + old[bit * slabs + m].astype(f32)).astype(bf16)
            return carry

        lax.fori_loop(0, slabs, add, 0)

    def task(k):
        if k == 1:
            link.arrive(to_heads, own_heads, heads_in, length_in)
            attention_back_start(s, s.o, s.lse, s.doh)
        if k <= 4:
            attention_back_step(link, spot, PAIR_STEPS[k - 1], s, s.qkv, s.doh, s.dqkvh[0], rows_kv, own_kv)
        elif k == 5:
            attention_back_end(link, spot, s, s.dqkvh[0], rows_q, own_q)
        elif k == 6:
            link.arrive(dqkv_in)

            def piece(i, carry):
                here = span(i, 256)
                product = dot_0(s.hidden[0][:, here], s.dqkvh[0][...])
                product += dot_0(s.hidden[1][:, here], s.dqkvh[1][...])
                product = product.astype(bf16)
                for low in range(2):
                    at_slab = i * 2 + low
                    s.chunk_q[at_slab, 0:ROWS] = product[ROWS * low : ROWS * (low + 1)]
                return carry

            lax.fori_loop(0, 4, piece, 0)
            total = column_sum(s.dqkvh[0][...]) + column_sum(s.dqkvh[1][...])
            extra = jnp.broadcast_to(total, (16, 384)).astype(bf16)
            for at_slab in range(8):
                s.chunk_q[at_slab, ROWS:VEC] = extra
            state.q = link.put(s.chunk_q.at[pl.ds((1 - zh) * 4, 4)], s.landing_q[0], across["b"], link.group())
        elif k == 7:
            link.arrive(state.q)
            fold_q(0, zh)
            state.q = link.put(s.landing_q[0], s.landing_q[1], across["x"], link.group())
        elif k == 8:
            link.arrive(state.q)
            fold_q(1, 0)
            cols = pl.ds(pl.multiple_of(IN_OUT["qkv"] + spot.place * 384, 128), 384)
            where = s.out.at[:, cols]
            state.q = link.group()
            for dz, dy in ((1, 1), (1, 0), (0, 1)):
                slab = s.landing_q[1].at[flip(zl, dz) * 2 + flip(y, dy)]
                link.put(slab, where, spot.flipped(zl=dz, y=dy), state.q)
            s.out[:, cols] = s.landing_q[1][zl * 2 + y]
        elif k == 11:
            link.arrive(state.q)
            where = s.out.at[:, pl.ds(pl.multiple_of(IN_OUT["qkv"] + c * 1536, 128), 1536)]
            link.put(where, where, across["C"])
        elif k == 9:
            link.arrive(rows_kv, own_kv, rows_q, own_q, close_in, weight_in)
            s.grad[...] = (s.dr1[...] + dot_t(s.dqkv[...], s.w_qkv[...])).astype(bf16)
            link.swap(spot, s.grad, grad_out)
        elif k == 10:
            link.arrive(hidden_in, far_hidden)
        elif k in (12, 13, 14):
            turn((0, 2, 1)[k - 12])

    for n, i in ORDER:
        if n == 100:
            task(i)
            continue
        if i < 0:
            compute(n)
        else:
            advance(n, i)
        if i + 1 < len(PLANS[n]):
            send(n, i + 1)
    link.finish()


def grad_call(main, w_qkv):
    dma = pltpu.SemaphoreType.DMA
    hbm = pl.BlockSpec(memory_space=pl.ANY)
    return pl.pallas_call(
        grad_kernel,
        out_shape=[jax.ShapeDtypeStruct((VEC, 12 * D), bf16), jax.ShapeDtypeStruct((ROWS, D), bf16)],
        in_specs=[hbm] * (len(MAIN_OUT) + 1),
        out_specs=[pl.BlockSpec(memory_space=pltpu.VMEM), hbm],
        scratch_shapes=[pltpu.VMEM(*entry) for entry in flat(GRAD_SCRATCH)]
        + [dma((SEMS,)), dma((SEMS,)), dma((20,))],
        compiler_params=pltpu.CompilerParams(
            collective_id=2, has_side_effects=True, vmem_limit_bytes=60 * 2**20
        ),
    )(*[getattr(main, name) for name in MAIN_OUT], w_qkv)


def finish_kernel(sums, mixed_in, grad_in, mixed, grad, qkv, attn, fore, back, qv, bias, fore_bias, gain, shift,
                  buf, thin_buf, qkv_buf, attn_buf, fore_buf, back_buf, in_sem, out_sem):
    at = IN_OUT
    pieces = [(at["qkv"], 1536, VEC), (at["qkv"] + 1536, 1536, VEC), (at["attn"], D, VEC)]
    for n in range(4):
        pieces += [(at["back"] + n * D, D, ROWS), (at["fore"] + n * D, D, ROWS)]
    loads, stores = [], []

    def store(src, dst):
        copy = pltpu.make_async_copy(src, dst, out_sem.at[len(stores)])
        copy.start()
        stores.append(copy)

    for n, (start, width, rows) in enumerate(pieces):
        here = (pl.ds(0, rows), pl.ds(start, width))
        loads.append(pltpu.make_async_copy(sums.at[here], buf.at[here], in_sem.at[n]))
        loads[n].start()
    for n, source in enumerate((mixed_in, grad_in)):
        loads.append(pltpu.make_async_copy(source, thin_buf.at[n], in_sem.at[11 + n]))
        loads[-1].start()
    total = jnp.zeros((16, 384), f32)
    for half in range(2):
        loads[half].wait()
        for place in range(4 * half, 4 * half + 4):
            start = at["qkv"] + place * 384
            for part in range(3):
                here = pl.ds(start + part * 128, 128)
                qkv_buf[:, pl.ds(part * D + place * 128, 128)] = buf[0:ROWS, here].astype(f32)
            block = buf[ROWS:VEC, pl.ds(start, 384)].astype(f32)
            total = total + jnp.where(lax.axis_index("blk") == place, block, 0.0)
        for part in range(3):
            here = pl.ds(part * D + half * 512, 512)
            store(qkv_buf.at[:, here], qkv.at[:, here])
    loads[2].wait()
    attn_buf[...] = buf[0:ROWS, pl.ds(at["attn"], D)].astype(f32)
    store(attn_buf, attn)
    for n in range(4):
        rows = pl.ds(n * D, D)
        loads[3 + 2 * n].wait()
        back_buf[rows, :] = buf[0:ROWS, pl.ds(at["back"] + n * D, D)].astype(f32).T
        store(back_buf.at[rows], back.at[rows])
        loads[4 + 2 * n].wait()
        fore_buf[:, rows] = buf[0:ROWS, pl.ds(at["fore"] + n * D, D)].astype(f32)
        store(fore_buf.at[:, rows], fore.at[:, rows])
    for n, target in enumerate((mixed, grad)):
        loads[11 + n].wait()
        store(thin_buf.at[n], target)
    qv[0:1, :] = total[0:1, 0:128]
    qv[1:2, :] = total[0:1, 256:384]
    start = at["attn"]
    small = buf[ROWS:VEC, pl.ds(start, 512)].astype(f32) + buf[ROWS:VEC, pl.ds(start + 512, 512)].astype(f32)
    bias[...] = small[0:2, 0:128]
    gain[...] = small[2:4, 0:128]
    shift[...] = small[4:6, 0:128]
    fore_bias[...] = small[8:9, :]
    for copy in stores:
        copy.wait()


def finish_call(sums, mixed, grad):
    large = [(ROWS, 3 * D), (ROWS, D), (ROWS, FF), (FF, 128)]
    small = [(2, 128), (2, 128), (1, 512), (2, 128), (2, 128)]
    hbm, vmem = pl.BlockSpec(memory_space=pl.ANY), pl.BlockSpec(memory_space=pltpu.VMEM)
    dma = pltpu.SemaphoreType.DMA
    return pl.pallas_call(
        finish_kernel,
        out_shape=[jax.ShapeDtypeStruct((ROWS, D), bf16)] * 2
        + [jax.ShapeDtypeStruct(shape, f32) for shape in large + small],
        in_specs=[hbm] * 3,
        out_specs=[hbm] * 6 + [vmem] * 5,
        scratch_shapes=[pltpu.VMEM((VEC, 12 * D), bf16), pltpu.VMEM((2, ROWS, D), bf16)] + [pltpu.VMEM(shape, f32) for shape in large]
        + [dma((13,)), dma((17,))],
        compiler_params=pltpu.CompilerParams(vmem_limit_bytes=63 * 2**20),
    )(sums, mixed, grad)


def fast_body(tokens, lengths, *rest):
    params, cotangent = rest[:-1], rest[-1]
    main = main_call(lengths, tokens[0], cotangent[0], params)
    sums, grad = grad_call(main, params[0])
    mixed, grad, qkv, attn, fore, back, qv, bias, fore_bias, gain, shift = finish_call(sums, main.mixed, grad)
    return (
        mixed[None], grad[None], qkv, qv, attn, bias, fore, fore_bias.reshape(512), back, gain, shift,
    )


def solution(mesh):
    placed = (
        P("batch", "blk", None),
        P("batch"),
        P(),
        P(),
        P(),
        P(),
        P(),
        P(),
        P(),
        P(),
        P(),
        P("batch", "blk", None),
    )
    fast = dict(mesh.shape) == {"batch": 4, "blk": 8}
    return jax.shard_map(
        fast_body if fast else body,
        mesh=mesh,
        in_specs=placed,
        out_specs=(
            P("batch", "blk", None),
            P("batch", "blk", None),
            P("blk", None),
            P(None, "blk"),
            P("blk", None),
            P(None, "blk"),
            P("blk", None),
            P("blk"),
            P(None, "blk"),
            P(None, "blk"),
            P(None, "blk"),
        ),
        check_vma=False,
    )
```

```python
import math

import jax
import jax.numpy as jnp
from jax import lax
from jax.experimental import pallas as pl
from jax.experimental.pallas import tpu as pltpu
from jax.sharding import PartitionSpec as P

HEADS = 16


eps = 1e-12


def from_partner(x, axis, distance):
    return lax.ppermute(x, axis, [(i, i ^ 1 << distance) for i in range(lax.axis_size(axis))])


def normalize(values, gain, shift):
    centered = values - jnp.mean(values, axis=-1, keepdims=True)
    variance = jnp.mean(centered * centered, axis=-1, keepdims=True)
    return centered * lax.rsqrt(variance + eps) * gain + shift


def gelu_exact(values):
    return jax.nn.gelu(values, approximate=False)


def head_split(matrix, head_count):
    row_count, model_width = matrix.shape
    return matrix.reshape(row_count, head_count // 4, 4, model_width // head_count).transpose(
        1, 2, 0, 3
    )


def head_merge(stacked):
    group_count, group_size, row_count, head_size = stacked.shape
    return stacked.transpose(2, 0, 1, 3).reshape(row_count, group_count * group_size * head_size)


def core_forward(query_part, key_part, value_part, key_valid, scale):
    scores = (
        jnp.einsum("hqd,hkd->hqk", query_part, key_part, preferred_element_type=jnp.float32) * scale
    )
    masked = jnp.where(key_valid, scores, -1e30)
    row_max = jnp.max(masked, axis=-1, keepdims=True)
    exp_scores = jnp.where(key_valid, jnp.exp(masked - row_max), 0.0)
    row_total = jnp.sum(exp_scores, axis=-1, keepdims=True)
    prob_low = (exp_scores / row_total).astype(jnp.bfloat16)
    output = jnp.einsum("hqk,hkd->hqd", prob_low, value_part, preferred_element_type=jnp.float32)
    return (output, (row_max + jnp.log(row_total))[..., 0])


def core_backward(query_part, key_part, value_part, grad_part, log_part, key_valid, scale):
    scores = (
        jnp.einsum("hqd,hkd->hqk", query_part, key_part, preferred_element_type=jnp.float32) * scale
    )
    probs = jnp.where(key_valid, jnp.exp(scores - log_part[..., None]), 0.0)
    grad_probs = jnp.einsum(
        "hqd,hkd->hqk", grad_part, value_part, preferred_element_type=jnp.float32
    )
    inner_sum = jnp.sum(probs * grad_probs, axis=-1, keepdims=True)
    grad_scores = (probs * (grad_probs - inner_sum)).astype(jnp.bfloat16)
    grad_query = (
        jnp.einsum("hqk,hkd->hqd", grad_scores, key_part, preferred_element_type=jnp.float32)
        * scale
    )
    grad_key = (
        jnp.einsum("hqk,hqd->hkd", grad_scores, query_part, preferred_element_type=jnp.float32)
        * scale
    )
    grad_value = jnp.einsum(
        "hqk,hqd->hkd", probs.astype(jnp.bfloat16), grad_part, preferred_element_type=jnp.float32
    )
    return (grad_query, grad_key, grad_value)


def gather_group(kv_pair, position, bit_count):
    buffer_rows = kv_pair
    for step_bit in range(bit_count):
        received = from_partner(buffer_rows, "blk", step_bit)
        high_side = position >> step_bit & 1 == 1
        buffer_rows = jnp.where(
            high_side,
            jnp.concatenate([received, buffer_rows], 0),
            jnp.concatenate([buffer_rows, received], 0),
        )
    return buffer_rows


def spread_group(partials, position, bit_count):
    for step_bit in reversed(range(bit_count)):
        half_rows = partials.shape[0] // 2
        high_side = position >> step_bit & 1 == 1
        lower_part = partials[:half_rows]
        upper_part = partials[half_rows:]
        kept_part = jnp.where(high_side, upper_part, lower_part)
        sent_part = jnp.where(high_side, lower_part, upper_part)
        partials = kept_part + from_partner(sent_part.astype(jnp.bfloat16), "blk", step_bit).astype(
            sent_part.dtype
        )
    return partials


def attend_forward(queries, gathered, key_valid, head_count):
    model_width = queries.shape[1]
    scale = (model_width // head_count) ** (-0.5)
    query_heads = head_split(queries, head_count)
    key_heads = head_split(gathered[:, :model_width], head_count)
    value_heads = head_split(gathered[:, model_width:], head_count)

    def one_group(operands):
        query_part, key_part, value_part = operands
        return core_forward(query_part, key_part, value_part, key_valid, scale)

    outputs, log_sums = lax.map(one_group, (query_heads, key_heads, value_heads))
    return (head_merge(outputs), log_sums)


def attend_backward(queries, gathered, key_valid, log_sums, grad_attended, head_count):
    model_width = queries.shape[1]
    scale = (model_width // head_count) ** (-0.5)
    query_heads = head_split(queries, head_count)
    key_heads = head_split(gathered[:, :model_width], head_count)
    value_heads = head_split(gathered[:, model_width:], head_count)
    grad_heads = head_split(grad_attended, head_count)

    def one_group(operands):
        query_part, key_part, value_part, grad_part, log_part = operands
        return core_backward(
            query_part, key_part, value_part, grad_part, log_part, key_valid, scale
        )

    grad_query, grad_key, grad_value = lax.map(
        one_group, (query_heads, key_heads, value_heads, grad_heads, log_sums)
    )
    return (
        head_merge(grad_query),
        jnp.concatenate([head_merge(grad_key), head_merge(grad_value)], 1),
    )


def layer_forward(hidden, params, key_valid, position, bit_count, head_count):
    w_qkv, qv_bias, w_attn, out_bias, w_in, in_bias, w_back, norm_gain, norm_shift = params
    model_width = hidden.shape[1]
    hidden_low = hidden.astype(jnp.bfloat16)
    bias_row = jnp.concatenate([qv_bias[0], jnp.zeros_like(qv_bias[0]), qv_bias[1]])
    projected = (jnp.dot(hidden_low, w_qkv, preferred_element_type=jnp.float32) + bias_row).astype(
        jnp.bfloat16
    )
    gathered = gather_group(projected[:, model_width:], position, bit_count)
    attended, log_sums = attend_forward(projected[:, :model_width], gathered, key_valid, head_count)
    attended_low = attended.astype(jnp.bfloat16)
    first_sum = (
        hidden + jnp.dot(attended_low, w_attn, preferred_element_type=jnp.float32) + out_bias[0]
    )
    first_norm = normalize(first_sum, norm_gain[0], norm_shift[0])
    first_low = first_norm.astype(jnp.bfloat16)
    inner_pre = jnp.dot(first_low, w_in, preferred_element_type=jnp.float32) + in_bias
    activated = gelu_exact(inner_pre).astype(jnp.bfloat16)
    second_sum = (
        first_norm + jnp.dot(activated, w_back, preferred_element_type=jnp.float32) + out_bias[1]
    )
    output = normalize(second_sum, norm_gain[1], norm_shift[1])
    saved_state = (
        hidden_low,
        projected,
        gathered,
        log_sums,
        attended_low,
        first_sum,
        first_low,
        inner_pre,
        activated,
        second_sum,
    )
    return (output, saved_state)


def layer_backward(grad_output, saved_state, params, key_valid, position, bit_count, head_count):
    w_qkv, qv_bias, w_attn, out_bias, w_in, in_bias, w_back, norm_gain, norm_shift = params
    (
        hidden_low,
        projected,
        gathered,
        log_sums,
        attended_low,
        first_sum,
        first_low,
        inner_pre,
        activated,
        second_sum,
    ) = saved_state
    model_width = hidden_low.shape[1]
    unused_two, pull_two = jax.vjp(normalize, second_sum, norm_gain[1], norm_shift[1])
    grad_second, gain_two, shift_two = pull_two(grad_output)
    grad_branch_two = grad_second.astype(jnp.bfloat16)
    back_grad = jnp.einsum(
        "ra,rb->ab", activated, grad_branch_two, preferred_element_type=jnp.float32
    )
    bias_two = jnp.sum(grad_branch_two.astype(jnp.float32), axis=0)
    grad_act = jnp.dot(grad_branch_two, w_back.T, preferred_element_type=jnp.float32)
    unused_gelu, pull_gelu = jax.vjp(gelu_exact, inner_pre)
    grad_inner = pull_gelu(grad_act)[0].astype(jnp.bfloat16)
    in_grad = jnp.einsum("ra,rb->ab", first_low, grad_inner, preferred_element_type=jnp.float32)
    in_bias_grad = jnp.sum(grad_inner.astype(jnp.float32), axis=0)
    grad_first_norm = grad_second + jnp.dot(grad_inner, w_in.T, preferred_element_type=jnp.float32)
    unused_one, pull_one = jax.vjp(normalize, first_sum, norm_gain[0], norm_shift[0])
    grad_first, gain_one, shift_one = pull_one(grad_first_norm)
    grad_branch = grad_first.astype(jnp.bfloat16)
    attn_grad = jnp.einsum(
        "ra,rb->ab", attended_low, grad_branch, preferred_element_type=jnp.float32
    )
    bias_one = jnp.sum(grad_branch.astype(jnp.float32), axis=0)
    grad_attended = jnp.dot(grad_branch, w_attn.T, preferred_element_type=jnp.float32).astype(
        jnp.bfloat16
    )
    grad_query, grad_pairs = attend_backward(
        projected[:, :model_width], gathered, key_valid, log_sums, grad_attended, head_count
    )
    own_pairs = spread_group(grad_pairs, position, bit_count)
    grad_proj = jnp.concatenate([grad_query, own_pairs], 1).astype(jnp.bfloat16)
    qkv_grad = jnp.einsum("ra,rb->ab", hidden_low, grad_proj, preferred_element_type=jnp.float32)
    column_sums = jnp.sum(grad_proj.astype(jnp.float32), axis=0)
    qv_grad = jnp.stack([column_sums[:model_width], column_sums[2 * model_width :]])
    grad_hidden = grad_first + jnp.dot(grad_proj, w_qkv.T, preferred_element_type=jnp.float32)
    grad_list = (
        qkv_grad,
        qv_grad,
        attn_grad,
        jnp.stack([bias_one, bias_two]),
        in_grad,
        in_bias_grad,
        back_grad,
        jnp.stack([gain_one, gain_two]),
        jnp.stack([shift_one, shift_two]),
    )
    return (grad_hidden, grad_list)


def scatter_once(grad_list):
    (
        qkv_grad,
        qv_grad,
        attn_grad,
        bias_grad,
        in_grad,
        in_bias_grad,
        back_grad,
        gain_grad,
        shift_grad,
    ) = grad_list
    return (
        lax.psum_scatter(qkv_grad, "blk", scatter_dimension=0, tiled=True),
        lax.psum_scatter(qv_grad, "blk", scatter_dimension=1, tiled=True),
        lax.psum_scatter(attn_grad, "blk", scatter_dimension=0, tiled=True),
        lax.psum_scatter(bias_grad, "blk", scatter_dimension=1, tiled=True),
        lax.psum_scatter(in_grad, "blk", scatter_dimension=0, tiled=True),
        lax.psum_scatter(in_bias_grad, "blk", scatter_dimension=0, tiled=True),
        lax.psum_scatter(back_grad, "blk", scatter_dimension=1, tiled=True),
        lax.psum_scatter(gain_grad, "blk", scatter_dimension=1, tiled=True),
        lax.psum_scatter(shift_grad, "blk", scatter_dimension=1, tiled=True),
    )


def body(
    tokens,
    lengths,
    w_qkv,
    qv_bias,
    w_attn,
    out_bias,
    w_in,
    in_bias,
    w_back,
    norm_gain,
    norm_shift,
    cotangent,
):
    row_count = tokens.shape[1]
    head_count = HEADS
    cycle_size = lax.axis_size("blk")
    bit_count = cycle_size.bit_length() - 1
    position = lax.axis_index("blk")
    length = lengths[0]
    key_valid = jnp.arange(cycle_size * row_count) < length
    params = (w_qkv, qv_bias, w_attn, out_bias, w_in, in_bias, w_back, norm_gain, norm_shift)
    out_one, saved_one = layer_forward(
        tokens[0].astype(jnp.float32), params, key_valid, position, bit_count, head_count
    )
    out_two, saved_two = layer_forward(out_one, params, key_valid, position, bit_count, head_count)
    grad_hidden, grads_two = layer_backward(
        cotangent[0].astype(jnp.float32),
        saved_two,
        params,
        key_valid,
        position,
        bit_count,
        head_count,
    )
    grad_hidden, grads_one = layer_backward(
        grad_hidden, saved_one, params, key_valid, position, bit_count, head_count
    )
    shards = scatter_once(jax.tree.map(jnp.add, grads_two, grads_one))
    (
        qkv_part,
        qv_part,
        attn_part,
        bias_part,
        in_part,
        in_bias_part,
        back_part,
        gain_part,
        shift_part,
    ) = shards
    totals = (
        lax.psum(qkv_part.astype(jnp.bfloat16), "batch").astype(jnp.float32),
        lax.psum(qv_part.astype(jnp.bfloat16), "batch").astype(jnp.float32),
        lax.psum(attn_part.astype(jnp.bfloat16), "batch").astype(jnp.float32),
        lax.psum(bias_part.astype(jnp.bfloat16), "batch").astype(jnp.float32),
        lax.psum(in_part.astype(jnp.bfloat16), "batch").astype(jnp.float32),
        lax.psum(in_bias_part.astype(jnp.bfloat16), "batch").astype(jnp.float32),
        lax.psum(back_part.astype(jnp.bfloat16), "batch").astype(jnp.float32),
        lax.psum(gain_part.astype(jnp.bfloat16), "batch").astype(jnp.float32),
        lax.psum(shift_part.astype(jnp.bfloat16), "batch").astype(jnp.float32),
    )
    return (
        out_two.astype(jnp.bfloat16)[None],
        grad_hidden.astype(jnp.bfloat16)[None],
        totals[0],
        totals[1],
        totals[2],
        totals[3],
        totals[4],
        totals[5],
        totals[6],
        totals[7],
        totals[8],
    )


MESH = pl.DeviceIdType.MESH
f32 = jnp.float32
bf16 = jnp.bfloat16
FLIPS = ((0, 0), (1, 0), (0, 1), (1, 1))
GROUPS = len(FLIPS)
PART = 4096 // GROUPS
ROWS, D, FF, LEN, VEC = 128, 1024, 4096, 1024, 144


def dot(a, b):
    return jnp.dot(a, b, preferred_element_type=f32)


def dot_t(a, b):
    return lax.dot_general(a, b, (((1,), (1,)), ((), ())), preferred_element_type=f32)


def dot_0(a, b):
    return lax.dot_general(a, b, (((0,), (0,)), ((), ())), preferred_element_type=f32)


def span(at, size):
    return pl.ds(pl.multiple_of(at * size, size), size)


def flip(bit, by):
    return bit + by * (1 - 2 * bit)


def group(ref, n):
    return ref.at[pl.ds(n * ROWS, ROWS)]


class Spot:
    def __init__(self):
        self.row, self.pos = lax.axis_index("batch"), lax.axis_index("blk")
        self.x, self.c = self.row // 2, self.row % 2
        self.z, self.y = self.pos // 2, self.pos % 2
        self.zl, self.zh = self.z % 2, self.z // 2
        self.place = self.c * 4 + self.zl * 2 + self.y
        self.moved = self.c != self.zh

    def flipped(self, c=0, x=0, y=0, zl=0, zh=0):
        row = flip(self.x, x) * 2 + flip(self.c, c)
        pos = flip(self.zh, zh) * 4 + flip(self.zl, zl) * 2 + flip(self.y, y)
        return {"batch": row, "blk": pos}

    def member(self, place):
        return {"batch": self.x * 2 + place // 4, "blk": self.zh * 4 + place % 4}

    def partner(self):
        return {"batch": self.x * 2 + self.zh, "blk": self.c * 4 + self.pos % 4}


BULK = 2**21


class Group:
    def __init__(self, at):
        self.at, self.bytes, self.waited = at, 0, False


def bytes_of(ref):
    return math.prod(ref.shape) * jnp.dtype(ref.dtype).itemsize


class Link:
    def __init__(self, send_sem, recv_sem, own_sem, *meters):
        self.send_sem, self.recv_sem, self.own_sem, self.meters = send_sem, recv_sem, own_sem, meters
        self.count, self.own_count = 0, 0
        self.groups, self.own_groups, self.swaps, self.last = [], [], [], []
        self.bulk, self.own_bulk = self.group(), self.own_group()

    def group(self):
        self.groups.append(Group(self.count))
        self.count += 1
        return self.groups[-1]

    def own_group(self):
        self.own_groups.append(Group(self.own_count))
        self.own_count += 1
        return self.own_groups[-1]

    def put(self, src, dst, device, group=None):
        if group is None:
            if self.bulk.bytes + bytes_of(src) > BULK:
                self.bulk = self.group()
            group = self.bulk
        group.bytes += bytes_of(src)
        pltpu.make_async_remote_copy(
            src_ref=src, dst_ref=dst, send_sem=self.send_sem.at[group.at], recv_sem=self.recv_sem.at[group.at],
            device_id=device, device_id_type=MESH,
        ).start()
        return group

    def keep(self, src, dst, group=None):
        if group is None:
            if self.own_bulk.bytes + bytes_of(src) > BULK:
                self.own_bulk = self.own_group()
            group = self.own_bulk
        group.bytes += bytes_of(src)
        pltpu.make_async_copy(src, dst, self.own_sem.at[group.at]).start()
        return group

    def wait(self, group, sem):
        if group.bytes:
            for meter in self.meters:
                row = bytes_of(meter) // meter.shape[0]
                tile = 8 if meter.dtype == f32 else 16
                if group.bytes % (tile * row) == 0 and group.bytes <= bytes_of(meter):
                    view = meter.at[pl.ds(0, group.bytes // row)]
                    pltpu.make_async_copy(view, view, sem.at[group.at]).wait()
                    return
            raise ValueError(group.bytes)

    def arrive(self, *groups):
        for group in groups:
            if not group.waited:
                group.waited = True
                self.wait(group, self.own_sem if any(group is own for own in self.own_groups) else self.recv_sem)

    def swap(self, spot, src, dst):
        far = pltpu.make_async_remote_copy(
            src_ref=src, dst_ref=dst, send_sem=self.send_sem.at[self.count], recv_sem=self.recv_sem.at[self.count],
            device_id=spot.partner(), device_id_type=MESH,
        )
        near = pltpu.make_async_copy(src, dst, self.own_sem.at[self.own_count])
        self.count += 1
        self.own_count += 1
        pl.when(spot.moved)(far.start)
        pl.when(jnp.logical_not(spot.moved))(near.start)
        self.swaps.append((spot, far, near))
        return far, near

    def arrive_swap(self, spot, pair):
        pl.when(spot.moved)(pair[0].wait_recv)
        pl.when(jnp.logical_not(spot.moved))(pair[1].wait)
        self.swaps = [(one, far, None if far is pair[0] else near) for one, far, near in self.swaps]

    def finish(self):
        self.arrive(*self.groups, *self.own_groups)
        for group in self.groups:
            self.wait(group, self.send_sem)
        for wait in self.last:
            wait()
        for spot, far, near in self.swaps:
            if near is not None:
                self.arrive_swap(spot, (far, near))
            pl.when(spot.moved)(far.wait_send)


def greet(spot, devices):
    barrier = pltpu.get_barrier_semaphore()
    for device in devices:
        pl.semaphore_signal(barrier, inc=1, device_id=device, device_id_type=MESH)

    @pl.when(spot.moved)
    def _():
        pl.semaphore_signal(barrier, inc=1, device_id=spot.partner(), device_id_type=MESH)

    def meet():
        @pl.when(spot.moved)
        def _():
            pl.semaphore_wait(barrier, len(devices) + 1)

        @pl.when(jnp.logical_not(spot.moved))
        def _():
            pl.semaphore_wait(barrier, len(devices))

    return meet


def standard(values):
    centered = values - jnp.mean(values, axis=-1, keepdims=True)
    inverse = lax.rsqrt(jnp.mean(centered * centered, axis=-1, keepdims=True) + eps)
    return centered * inverse, inverse


def standard_back(unit, inverse, gain, grad):
    scaled = grad * gain
    inner = jnp.mean(scaled * unit, axis=-1, keepdims=True)
    return inverse * (scaled - jnp.mean(scaled, axis=-1, keepdims=True) - unit * inner)


def column_sum(x):
    return jnp.sum(x.astype(f32), axis=0, keepdims=True)


def gelu_pair(u):
    t = 1.0 / (1.0 + 0.23164188 * jnp.abs(u))
    bell = jnp.exp(-0.5 * u * u)
    poly = t * (0.127414796 + t * (-0.142248368 + t * (0.7107068705 + t * (-0.7265760135 + t * 0.5307027145))))
    tail = poly * bell
    cdf = jnp.where(u < 0, tail, 1.0 - tail)
    return u * cdf, cdf + u * bell * 0.3989422804


def low_lanes():
    return lax.broadcasted_iota(jnp.int32, (1, 128), 1) < 64


def valid_keys(length):
    return lax.broadcasted_iota(jnp.int32, (1, LEN), 1).astype(f32) < length


def attention_rows(qkv, rows, valid):
    queries, keys, values = qkv[rows, 0:128], qkv[:, 128:256], qkv[:, 256:384]
    low_half = low_lanes()
    outs, lses = [], []
    for half in range(2):
        mine = low_half if half == 0 else jnp.logical_not(low_half)
        part = jnp.where(mine, queries, jnp.zeros_like(queries)) * jnp.asarray(0.125, bf16)
        scores = jnp.where(valid, dot_t(part, keys), -1e30)
        top = jnp.max(scores, axis=1, keepdims=True)
        expd = jnp.exp(scores - top)
        total = jnp.sum(expd, axis=1, keepdims=True)
        probs = (expd * (1.0 / total)).astype(bf16)
        outs.append(dot(probs, values))
        lses.append(top + jnp.log(total))
    return jnp.where(low_half, outs[0], outs[1]), jnp.where(low_half, lses[0], lses[1])


def attention_back_keys(qkv, grads_ref, lse_rows, delta_rows, rows, first, length):
    low_half = low_lanes()
    keys, values = qkv[rows, 128:256], qkv[rows, 256:384]
    at = lax.broadcasted_iota(jnp.int32, (256, 1), 0) + first
    valid = at.astype(f32) < length
    dqs, dk, dv = [], None, None
    for half in range(2):
        mine = low_half if half == 0 else jnp.logical_not(low_half)
        k_part = jnp.where(mine, keys, jnp.zeros_like(keys)) * jnp.asarray(0.125, bf16)
        v_part = jnp.where(mine, values, jnp.zeros_like(values))
        queries, grads = qkv[:, 0:128], grads_ref[...]
        scores = dot_t(k_part, queries)
        probs = jnp.where(valid, jnp.exp(scores - lse_rows[half : half + 1, :]), 0.0)
        dp = dot_t(v_part, grads)
        ds = (probs * (dp - delta_rows[half : half + 1, :])).astype(bf16)
        dv_part = dot(probs.astype(bf16), grads)
        dk_part = dot(ds, queries)
        dv = dv_part if half == 0 else jnp.where(low_half, dv, dv_part)
        dk = dk_part if half == 0 else jnp.where(low_half, dk, dk_part)
        dqs.append(dot_0(ds, keys))
    return jnp.where(low_half, dqs[0], dqs[1]), (dk * 0.125).astype(bf16), dv.astype(bf16)


def attention_back_start(s, o, lse, grads):
    turned = lse[...].T
    s.lse_rows[0:1, :] = turned[0:1, :]
    s.lse_rows[1:2, :] = turned[64:65, :]
    product = (grads[...].astype(f32) * o[...]).T
    s.delta_rows[0:1, :] = jnp.sum(product[0:64, :], axis=0, keepdims=True)
    s.delta_rows[1:2, :] = jnp.sum(product[64:128, :], axis=0, keepdims=True)


def attention_back_step(link, spot, step, s, qkv, grads, dqkvh, group, own):
    pair = (spot.place // 2 + step) % 4
    rows = span(pair, 256)
    dq, dk, dv = attention_back_keys(
        qkv, grads, s.lse_rows, s.delta_rows, rows, pair * 256, s.length[0:1, 0:1]
    )
    dqkvh[rows, 128:256] = dk
    dqkvh[rows, 256:384] = dv
    s.dq[...] = dq if step == PAIR_STEPS[0] else s.dq[...] + dq
    for part in (1, 2):
        send_rows(link, spot, dqkvh, s.dqkv, step, part, group, own)


def attention_back_end(link, spot, s, dqkvh, group, own):
    dqkvh[0:LEN, 0:128] = (s.dq[...] * 0.125).astype(bf16)
    for step in PAIR_STEPS:
        send_rows(link, spot, dqkvh, s.dqkv, step, 0, group, own)


def send_columns(link, spot, source, target, part, landing, groups, own):
    for step in range(7, -1, -1):
        to = (spot.place + step) % 8
        src = source.at[:, pl.ds(pl.multiple_of(part * D + to * 128, 128), 128)]
        dst = target.at[span(spot.place, ROWS), pl.ds(landing * 128, 128)]
        if step:
            link.put(src, dst, spot.member(to), groups[step])
        else:
            link.keep(src, dst, own)


def pair_rows(spot, step):
    return span((spot.place // 2 + step) % 4, 256)


def send_rows(link, spot, source, target, step, part, group, own):
    same = (spot.place + 2 * step) % 8
    for n, to in enumerate((same, same + 1 - 2 * spot.y)):
        src = source.at[span(to, ROWS), pl.ds(part * 128, 128)]
        dst = target.at[:, pl.ds(pl.multiple_of(part * D + spot.place * 128, 128), 128)]
        if step or n:
            link.put(src, dst, spot.member(to), group)
        else:
            link.keep(src, dst, own)


PAIR_STEPS = (1, 2, 3, 0)


def spec(**named):
    return named


def two(*entry):
    return [entry, entry]


MAIN_OUT = spec(
    mixed=((ROWS, D), bf16), qkv1=((LEN, 384), bf16), lse1=((LEN, 128), f32), o1=((LEN, 128), f32),
    left_attn=((4, ROWS, D), bf16), right_attn=((4 * ROWS, 512), bf16),
    left_back=((2 * GROUPS, ROWS, D), bf16), right_back=((2 * GROUPS * ROWS, PART), bf16),
    left_in=((2 * GROUPS, ROWS, D), bf16), right_in=((2 * GROUPS * ROWS, PART), bf16),
    hidden=((2, LEN, D), bf16), dqkv2=((LEN, 384), bf16),
    du1=((ROWS, FF), bf16), dza1=((ROWS, D), bf16),
    do1=((ROWS, D), bf16), dr1=((ROWS, D), f32), vec=((8, D), f32), inb=((1, FF), f32),
    length=((16, 128), f32),
)
MAIN_SCRATCH = spec(
    w_qkv=((D, 3 * D), bf16), w_attn=((D, D), bf16), w_in=((D, FF), bf16), w_back=((FF, D), bf16),
    tok=((ROWS, D), bf16), cot=((ROWS, D), bf16), length=((16, 128), f32), sent_length=((16, 128), f32),
    proj=two((ROWS, 3 * D), bf16), qkv=two((LEN, 384), bf16), lse=two((LEN, 128), f32),
    o=two((LEN, 128), bf16), full_o=two((LEN, 128), f32), att=two((ROWS, D), bf16), n=two((ROWS, D), bf16),
    act=two((ROWS, FF), bf16), slope=two((ROWS, FF), bf16),
    unit_a=two((ROWS, D), f32), unit_b=two((ROWS, D), f32),
    inv_a=two((ROWS, 128), f32), inv_b=two((ROWS, 128), f32),
    hq2=((ROWS, D), bf16), h=((ROWS, D), f32), acc=((ROWS, D), f32), mixed=((ROWS, D), bf16),
    dzb=two((ROWS, D), bf16), du=two((ROWS, FF), bf16), dza=two((ROWS, D), bf16), do=two((ROWS, D), bf16),
    doh=((LEN, 128), bf16), dqkvh=((LEN, 384), bf16), dq=((LEN, 128), f32), lse_rows=((8, LEN), f32), delta_rows=((8, LEN), f32),
    dqkv=((ROWS, 3 * D), bf16), dr1=((ROWS, D), f32), vec=((8, D), f32), inb=((1, FF), f32),
)


class Refs:
    pass


def flat(entries):
    out = []
    for entry in entries.values():
        out += entry if isinstance(entry, list) else [entry]
    return out


def bind(entries, refs):
    got, it = Refs(), iter(refs)
    for name, entry in entries.items():
        setattr(got, name, [next(it) for _ in entry] if isinstance(entry, list) else next(it))
    return got


def main_kernel(*refs):
    (len_ref, tokens, cotangent, w_qkv, w_attn, w_in, w_back,
     qv_bias, out_bias, in_bias, gain, shift) = refs[:12]
    outs = bind(MAIN_OUT, refs[12 : 12 + len(MAIN_OUT)])
    rest = refs[12 + len(MAIN_OUT) :]
    s = bind(MAIN_SCRATCH, rest[:-4])
    load_sem, send_sem, recv_sem, own_sem = rest[-4:]
    spot = Spot()
    link = Link(send_sem, recv_sem, own_sem, outs.hidden.at[0], outs.lse1)
    others = [spot.member((spot.place + step) % 8) for step in range(1, 8)]
    others += [spot.flipped(x=1), spot.flipped(c=1, x=1)]
    meet = greet(spot, others)

    loads = []
    for n, (src, dst) in enumerate(
        [(w_qkv.at[:, pl.ds(D * part, D)], s.w_qkv.at[:, pl.ds(D * part, D)]) for part in (1, 2, 0)]
        + [(w_attn, s.w_attn), (w_in, s.w_in), (w_back, s.w_back)]
    ):
        loads.append(pltpu.make_async_copy(src, dst, load_sem.at[n]))
        loads[n].start()
    loaded = set()

    def need(n):
        if n not in loaded:
            loaded.add(n)
            loads[n].wait()

    s.sent_length[...] = jnp.full((16, 128), len_ref[0], jnp.int32).astype(f32)
    meet()
    first_in = [link.swap(spot, tokens, s.tok), link.swap(spot, s.sent_length, s.length)]
    for pair in first_in:
        link.arrive_swap(spot, pair)
    valid = valid_keys(s.length[0:1, 0:1])

    later = []

    def share(source, left, d):
        link.keep(source, left.at[d])
        link.put(source, left.at[2 + d], spot.flipped(c=1))
        link.put(source, left.at[4 + d], spot.flipped(x=1))

    def deal(source, right, d):
        link.keep(source.at[:, span(spot.c * 2 + spot.x, PART)], group(right, d))
        for n, (dc, dx) in enumerate(FLIPS[1:], 1):
            cols = span(flip(spot.c, dc) * 2 + flip(spot.x, dx), PART)
            link.put(source.at[:, cols], group(right, 2 * n + d), spot.flipped(c=dc, x=dx))

    def gather(hq, d, part):
        rows = pl.ds(part * 64, 64)
        block = outs.hidden.at[d, pl.ds(pl.multiple_of(spot.place * ROWS + part * 64, 64), 64)]
        for dz, dy in ((1, 0), (0, 1), (1, 1)):
            link.put(hq.at[rows], block, spot.flipped(zl=dz, y=dy))
        link.keep(hq.at[rows], block)

    def forward(d, hq, h):
        pair_of = [0, 3, 3, 2, 2, 1, 1, 1]
        both, pairs, own = link.group(), [link.group() for _ in range(4)], link.own_group()
        for part, number in ((1, 0), (2, 1), (0, 2)):
            need(number)

            def tile(i, carry):
                cols = span(2 * part + i, 512)
                value = dot(hq[...], s.w_qkv[:, cols])
                if part != 1:
                    value += qv_bias[part // 2 : part // 2 + 1, span(i, 512)]
                s.proj[d][:, cols] = value.astype(bf16)
                return carry

            lax.fori_loop(0, 2, tile, 0)
            to_groups = [both] * 8 if part else [pairs[pair] for pair in pair_of]
            send_columns(link, spot, s.proj[d], s.qkv[d], part, part, to_groups, own)
        link.arrive(both, own)
        if d == 0:
            later.append(link.swap(spot, cotangent, s.cot))
        to_rows, own_rows = link.group(), link.own_group()
        for step in PAIR_STEPS:
            link.arrive(pairs[step])
            rows = pair_rows(spot, step)
            s.full_o[d][rows, :], s.lse[d][rows, :] = attention_rows(s.qkv[d], rows, valid)
            s.o[d][rows, :] = s.full_o[d][rows, :].astype(bf16)
            send_rows(link, spot, s.o[d], s.att[d], step, 0, to_rows, own_rows)
        if d == 0:
            link.keep(s.qkv[0], outs.qkv1)
            link.keep(s.lse[0], outs.lse1)
            link.keep(s.full_o[0], outs.o1)
        link.arrive(to_rows, own_rows)
        gather(s.tok, 0, d)
        need(3)
        unit, inverse = standard(h[...].astype(f32) + dot(s.att[d][...], s.w_attn[...]) + out_bias[0:1])
        link.keep(s.att[d], outs.left_attn.at[d])
        link.put(s.att[d], outs.left_attn.at[2 + d], spot.flipped(c=1))
        s.unit_a[d][...] = unit
        s.inv_a[d][...] = jnp.broadcast_to(inverse, (ROWS, 128))
        first = unit * gain[0:1] + shift[0:1]
        s.n[d][...] = first.astype(bf16)
        share(s.n[d], outs.left_in, d)
        s.acc[...] = first + out_bias[1:2]
        need(4)
        need(5)

        def inner(i, carry):
            cols = span(i, 512)
            act, slope = gelu_pair(dot(s.n[d][...], s.w_in[:, cols]) + in_bias[:, cols])
            act = act.astype(bf16)
            s.act[d][:, cols] = act
            s.slope[d][:, cols] = slope.astype(bf16)
            s.acc[...] += dot(act, s.w_back[cols, :])
            return carry

        lax.fori_loop(0, 8, inner, 0)
        deal(s.act[d], outs.right_back, d)
        unit, inverse = standard(s.acc[...])
        s.unit_b[d][...] = unit
        s.inv_b[d][...] = jnp.broadcast_to(inverse, (ROWS, 128))
        return unit * gain[1:2] + shift[1:2]

    def add_vec(at, value, fresh):
        s.vec[at : at + 1, :] = value if fresh else s.vec[at : at + 1, :] + value

    def backward(d, grad, fresh):
        unit = s.unit_b[d][...]
        add_vec(3, column_sum(grad * unit), fresh)
        add_vec(5, column_sum(grad), fresh)
        dr = standard_back(unit, s.inv_b[d][:, 0:1], gain[1:2], grad)
        s.acc[...] = dr
        low = dr.astype(bf16)
        s.dzb[d][...] = low
        share(s.dzb[d], outs.left_back, d)
        add_vec(1, column_sum(low), fresh)

        def inner(i, carry):
            cols = span(i, 512)
            du = (dot_t(s.dzb[d][...], s.w_back[cols, :]) * s.slope[d][:, cols].astype(f32)).astype(bf16)
            s.du[d][:, cols] = du
            total = column_sum(du)
            s.inb[:, cols] = total if fresh else s.inb[:, cols] + total
            s.acc[...] += dot_t(du, s.w_in[:, cols])
            return carry

        lax.fori_loop(0, 8, inner, 0)
        if d:
            deal(s.du[d], outs.right_in, d)
        else:
            link.keep(s.du[d], outs.du1)
        grad = s.acc[...]
        unit = s.unit_a[d][...]
        add_vec(2, column_sum(grad * unit), fresh)
        add_vec(4, column_sum(grad), fresh)
        dr = standard_back(unit, s.inv_a[d][:, 0:1], gain[0:1], grad)
        s.dr1[...] = dr
        low = dr.astype(bf16)
        s.dza[d][...] = low
        if d:
            link.keep(s.dza[d].at[:, span(spot.c, 512)], group(outs.right_attn, d))
            link.put(s.dza[d].at[:, span(1 - spot.c, 512)], group(outs.right_attn, 2 + d), spot.flipped(c=1))
        else:
            link.keep(s.dza[d], outs.dza1)
        add_vec(0, column_sum(low), fresh)
        s.do[d][...] = dot_t(low, s.w_attn[...]).astype(bf16)

    out = forward(0, s.tok, s.tok)
    s.h[...] = out
    s.hq2[...] = out.astype(bf16)
    out = forward(1, s.hq2, s.h)
    s.mixed[...] = out.astype(bf16)
    link.swap(spot, s.mixed, outs.mixed)
    link.arrive_swap(spot, later[0])
    gather(s.hq2, 1, 0)
    backward(1, s.cot[...].astype(f32), True)
    to_heads, own_heads = link.group(), link.own_group()
    send_columns(link, spot, s.do[1], s.doh, 0, 0, [to_heads] * 8, own_heads)
    link.arrive(to_heads, own_heads)
    attention_back_start(s, s.full_o[1], s.lse[1], s.doh)
    to_rows, own_rows, last_rows, own_last = link.group(), link.own_group(), link.group(), link.own_group()
    for step in PAIR_STEPS:
        attention_back_step(link, spot, step, s, s.qkv[1], s.doh, s.dqkvh, to_rows, own_rows)
    attention_back_end(link, spot, s, s.dqkvh, last_rows, own_last)
    link.keep(s.dqkvh, outs.dqkv2)
    link.arrive(to_rows, own_rows)
    s.dr1[...] += dot_t(s.dqkv[:, D:], s.w_qkv[:, D:])
    link.arrive(last_rows, own_last)
    gather(s.hq2, 1, 1)
    backward(0, s.dr1[...] + dot_t(s.dqkv[:, :D], s.w_qkv[:, :D]), False)
    link.keep(s.do[0], outs.do1)
    link.keep(s.dr1, outs.dr1)
    small = link.own_group()
    link.keep(s.vec, outs.vec, small)
    link.keep(s.inb, outs.inb, small)
    link.keep(s.length, outs.length, small)
    link.finish()


def main_call(length, tokens, cotangent, params):
    w_qkv, qv_bias, w_attn, out_bias, w_in, in_bias, w_back, gain, shift = params
    dma = pltpu.SemaphoreType.DMA
    vmem, hbm = pl.BlockSpec(memory_space=pltpu.VMEM), pl.BlockSpec(memory_space=pl.ANY)
    results = pl.pallas_call(
        main_kernel,
        out_shape=[jax.ShapeDtypeStruct(*entry) for entry in MAIN_OUT.values()],
        in_specs=[pl.BlockSpec(memory_space=pltpu.SMEM), hbm, hbm] + [hbm] * 4 + [vmem] * 5,
        out_specs=[hbm] * len(MAIN_OUT),
        scratch_shapes=[pltpu.VMEM(*entry) for entry in flat(MAIN_SCRATCH)]
        + [dma((6,)), dma((32,)), dma((32,)), dma((20,))],
        compiler_params=pltpu.CompilerParams(
            collective_id=1, has_side_effects=True, vmem_limit_bytes=60 * 2**20
        ),
    )(length, tokens, cotangent, w_qkv, w_attn, w_in, w_back, qv_bias, out_bias, in_bias[None], gain, shift)
    return bind(MAIN_OUT, results)


PATHS = spec(A="yxabXC", B="xyabXC", C="abysC", F="yabVK", G="aybVK")
CHUNKS = (
    ("A", 0, 0, 512),
    ("F", 1, 0, 256),
    ("F", 1, 256, 256),
    ("G", 1, 512, 256),
    ("G", 1, 768, 256),
    ("F", 2, 0, 256),
    ("F", 2, 256, 256),
    ("F", 2, 512, 256),
    ("F", 2, 768, 128),
    ("F", 2, 896, 128),
)
ORDER = (
    (100, 12), (0, -1), (100, 14), (3, -1), (100, 10), (1, -1), (100, 13), (100, 1), (4, -1), (100, 2),
    (100, 3), (100, 4), (100, 5), (100, 20), (3, 0), (100, 22), (0, 0), (7, -1), (6, -1), (4, 0),
    (100, 30), (5, -1), (1, 0), (8, -1), (100, 21), (100, 32), (100, 40), (1, 1), (100, 9), (0, 1),
    (100, 42), (3, 1), (100, 31), (1, 2), (7, 0), (2, -1), (1, 3), (0, 2), (1, 4), (6, 0),
    (9, -1), (3, 2), (4, 1), (100, 41), (3, 3), (7, 1), (3, 4), (5, 0), (0, 3), (6, 1),
    (8, 0), (0, 4), (4, 2), (100, 50), (100, 52), (0, 5), (4, 3), (7, 2), (5, 1), (4, 4),
    (2, 0), (7, 3), (6, 2), (8, 1), (7, 4), (9, 0), (5, 2), (6, 3), (100, 51), (2, 1),
    (8, 2), (6, 4), (5, 3), (9, 1), (8, 3), (5, 4), (2, 2), (9, 2), (8, 4), (2, 3),
    (9, 3), (2, 4), (9, 4),
)
IN_OUT = spec(back=0, fore=FF, attn=2 * FF, qkv=2 * FF + D)


def plan(path, width):
    slabs, steps = 8, []
    for stage in path:
        if stage in "yab":
            slabs //= 2
        elif stage == "x":
            width //= 2
        elif stage == "X":
            width *= 2
        steps.append((stage, slabs, width))
    return steps


def chunk_rows(c):
    return VEC if c == 0 else ROWS


SEMS = 24 + sum(len(PATHS[chunk[0]]) for chunk in CHUNKS)
PLANS = [plan(PATHS[chunk[0]], chunk[3]) for chunk in CHUNKS]
GRAD_SCRATCH = spec(
    left=[((4, ROWS, D), bf16)] + two((2 * GROUPS, ROWS, D), bf16),
    right=[((4 * ROWS, 512), bf16)] + two((2 * GROUPS * ROWS, PART), bf16),
    turned=[((D, 512), bf16)] + two((D, 256 * GROUPS), bf16),
    chunk=[((8, chunk_rows(c), CHUNKS[c][3]), bf16) for c in range(len(CHUNKS))],
    landing=[
        ((slabs, chunk_rows(c), width), bf16)
        for c, steps in enumerate(PLANS) for stage, slabs, width in steps if stage in "yabxs"
    ],
    hidden=two((LEN, D), bf16), turned_h=((D, 2 * LEN), bf16), dqkvh=((2 * LEN, 384), bf16),
    chunk_q=[((8, VEC, 128), bf16)] * 3, landing_x=[((4, VEC, 128), bf16)] * 3, landing_b=[((2, VEC, 128), bf16)] * 3,
    qkv=((LEN, 384), bf16), lse=((LEN, 128), f32), doh=((LEN, 128), bf16),
    o=((LEN, 128), f32), dq=((LEN, 128), f32), lse_rows=((8, LEN), f32), delta_rows=((8, LEN), f32),
    dqkv=((ROWS, 3 * D), bf16), w_qkv=((D, 3 * D), bf16),
    dr1=((ROWS, D), f32), grad=((ROWS, D), bf16), vec=((8, D), f32), inb=((1, FF), f32), length=((16, 128), f32),
)


def grad_kernel(*refs):
    src = bind(MAIN_OUT, refs[: len(MAIN_OUT)])
    w_qkv, sums, grad_out = refs[len(MAIN_OUT) : len(MAIN_OUT) + 3]
    rest = refs[len(MAIN_OUT) + 3 :]
    s = bind(GRAD_SCRATCH, rest[:-3])
    s.out = sums
    spot = Spot()
    link = Link(*rest[-3:], src.hidden.at[0], src.lse1, w_qkv)
    x, y, c, zl, zh = spot.x, spot.y, spot.c, spot.zl, spot.zh
    others = [spot.member((spot.place + step) % 8) for step in range(1, 8)]
    others += [spot.flipped(x=1), spot.flipped(c=1, x=1), spot.flipped(zh=1)]
    meet = greet(spot, others)
    mine = span(c * 2 + x, PART)
    heads_in, vec_in, hidden_in, dqkv_in, close_in, left_in, right_in, weight_in = [link.own_group() for _ in range(8)]
    length_in = link.own_group()
    own_ready = [link.own_group() for _ in range(3)]
    for one, other in ((src.o1, s.o), (src.qkv1, s.qkv), (src.lse1, s.lse)):
        link.keep(one, other, heads_in)
    link.keep(src.length, s.length, length_in)
    link.keep(src.left_attn, s.left[0], own_ready[0])
    for n in (1, 3):
        link.keep(group(src.right_attn, n), group(s.right[0], n), own_ready[0])
    link.keep(src.dza1.at[:, span(c, 512)], group(s.right[0], 0), own_ready[0])
    link.keep(src.right_back, s.right[1], right_in)
    first = pl.ds(0, 6)
    link.keep(src.left_back.at[first], s.left[1].at[first], own_ready[1])
    link.keep(src.vec, s.vec, vec_in)
    link.keep(src.inb, s.inb, vec_in)
    meet()
    to_heads, own_heads, far_hidden = link.group(), link.own_group(), link.group()
    far_ready = [link.group() for _ in range(3)]
    send_columns(link, spot, src.do1, s.doh, 0, 0, [to_heads] * 8, own_heads)
    link.put(src.dza1.at[:, span(1 - c, 512)], group(s.right[0], 2), spot.flipped(c=1), far_ready[0])
    far_left = link.group()
    here, there = pl.ds(4, 2), pl.ds(6, 2)
    link.put(src.left_back.at[here], s.left[1].at[there], spot.flipped(c=1), far_ready[1])
    for n, (dc, dx) in enumerate(FLIPS[1:], 1):
        cols = span(flip(c, dc) * 2 + flip(x, dx), PART)
        link.put(src.du1.at[:, cols], group(s.right[2], 2 * n), spot.flipped(c=dc, x=dx), far_ready[2])
    waves = [0]

    def wave(upto):
        if waves[0] < 1 <= upto:
            link.put(src.left_in.at[here], s.left[2].at[there], spot.flipped(c=1), far_left)
            link.keep(src.left_in.at[first], s.left[2].at[first], left_in)
            link.keep(src.du1.at[:, mine], group(s.right[2], 0), own_ready[2])
            for n in range(GROUPS):
                link.keep(group(src.right_in, 2 * n + 1), group(s.right[2], 2 * n + 1), own_ready[2])
        if waves[0] < 2 <= upto:
            rows = span(c, 512)
            for d in range(2):
                link.put(src.hidden.at[d, rows], s.hidden[d].at[rows], spot.flipped(c=1), far_hidden)
                link.keep(src.hidden.at[d, rows], s.hidden[d].at[rows], hidden_in)
            link.keep(src.dqkv2, s.dqkvh.at[pl.ds(LEN, LEN)], dqkv_in)
            link.keep(w_qkv, s.w_qkv, weight_in)
            link.keep(src.dr1, s.dr1, close_in)
        waves[0] = max(waves[0], upto)

    bits = spec(y=y, a=zl, b=zh)
    across = spec(
        y=spot.flipped(y=1), a=spot.flipped(zl=1), b=spot.flipped(zh=1), x=spot.flipped(x=1), C=spot.flipped(c=1)
    )
    across.update(spec(X=across["x"], V=across["x"], s=across["x"], K=across["C"]))
    current, landing, copies = {}, {}, {}
    it = iter(s.landing)
    for n, steps in enumerate(PLANS):
        for i, step in enumerate(steps):
            if step[0] in "yabxs":
                landing[n, i] = next(it)
    waiting = [True, True, True]

    def turn(k):
        if k == 2:
            wave(1)
            link.arrive(left_in, far_left)
        else:
            link.arrive(own_ready[k], far_ready[k])
            if k == 1:
                link.arrive(right_in)
        count = s.left[k].shape[0]
        for g in range(count):
            s.turned[k][:, pl.ds(ROWS * g, ROWS)] = s.left[k][g].T

    def compute(n):
        _, k, first, wide = CHUNKS[n]
        if k == 2 and waiting[2]:
            waiting[2] = False
            link.arrive(own_ready[2], far_ready[2])
        path = [stage for stage in PATHS[CHUNKS[n][0]] if stage in "yab"]
        path += [stage for stage in "yab" if stage not in path]

        def piece(i, carry):
            product = dot(s.turned[k][span(i, 256), :], s.right[k][:, pl.ds(first, wide)]).astype(bf16)
            for low in range(2):
                bit = spec(y=low, a=i % 2, b=i // 2)
                at_slab = (bit[path[0]] * 2 + bit[path[1]]) * 2 + bit[path[2]]
                s.chunk[n][at_slab, 0:ROWS] = product[ROWS * low : ROWS * (low + 1)]
            return carry

        lax.fori_loop(0, 4, piece, 0)
        if n == 0:
            link.arrive(vec_in)
            for shard in range(8):
                bit = spec(y=shard % 2, a=shard // 2 % 2, b=shard // 4)
                at_slab = (bit[path[0]] * 2 + bit[path[1]]) * 2 + bit[path[2]]
                vec = s.vec[:, pl.ds(shard * 128, 128)]
                top = jnp.concatenate([vec, jnp.zeros((8, 384), f32)], 1)
                low = jnp.broadcast_to(s.inb[:, pl.ds(shard * 512, 512)], (8, 512))
                s.chunk[n][at_slab, ROWS:VEC] = jnp.concatenate([top, low], 0).astype(bf16)
        current[n] = s.chunk[n]

    def base_of(n):
        _, k, first, _ = CHUNKS[n]
        if k == 0:
            return IN_OUT["attn"] + c * 512 + first, 0
        return IN_OUT["back" if k == 1 else "fore"] + c * 2 * PART + first, PART

    def columns(n, quarter, offset, width):
        start, stride = base_of(n)
        return pl.ds(pl.multiple_of(start + quarter * stride + offset, 128), width)

    def send(n, i):
        stage, slabs, width = PLANS[n][i]
        rows = pl.ds(0, chunk_rows(n))
        now, todo = current[n], []
        if stage in "yab":
            todo.append((now.at[pl.ds((1 - bits[stage]) * slabs, slabs)], landing[n, i]))
        elif stage == "x":
            todo.append((now.at[:, :, pl.ds(pl.multiple_of((1 - x) * width, 128), width)], landing[n, i]))
        elif stage == "s":
            todo.append((now, landing[n, i]))
        else:
            offset = x * (width // 2) if stage == "X" else 0
            width = width // 2 if stage == "X" else width
            for quarter in [x] if stage == "V" else range(2) if stage == "K" else [0]:
                where = s.out.at[rows, columns(n, quarter, offset, width)]
                todo.append((where, where))
        copies[n, i] = link.group()
        for here, there in todo:
            link.put(here, there, across[stage], copies[n, i])

    def advance(n, i):
        stage, slabs, width = PLANS[n][i]
        link.arrive(copies[n, i])
        if stage not in "yabxs":
            return
        got, old = landing[n, i], current[n]

        def add(m, carry):
            if stage in "yab":
                kept = old[bits[stage] * slabs + m]
            elif stage == "x":
                kept = old[m, :, pl.ds(pl.multiple_of(x * width, 128), width)]
            else:
                kept = old[m]
            got[m] = (got[m].astype(f32) + kept.astype(f32)).astype(bf16)
            return carry

        lax.fori_loop(0, slabs, add, 0)
        current[n] = got
        follow = PLANS[n][i + 1][0]
        if follow in "VXC":
            offset = x * width if follow == "X" else 0
            s.out[0 : chunk_rows(n), columns(n, x if follow == "V" else 0, offset, width)] = got[0]

    state = Refs()
    rows_kv, own_kv, rows_q, own_q = link.group(), link.own_group(), link.group(), link.own_group()

    def fold_q(got, old, bit):
        slabs = got.shape[0]

        def add(m, carry):
            got[m] = (got[m].astype(f32) + old[bit * slabs + m].astype(f32)).astype(bf16)
            return carry

        lax.fori_loop(0, slabs, add, 0)

    keeps = x == zl
    came_q = [None] * 3

    def wait_q(group, sem):
        def some(count):
            def wait():
                rows = count * VEC * 128 * 2 // 512
                view = src.lse1.at[pl.ds(0, rows)]
                pltpu.make_async_copy(view, view, sem.at[group.at]).wait()

            return wait

        pl.when(keeps)(some(3))
        pl.when(jnp.logical_not(keeps))(some(4))

    def out_q(part, first, width):
        return s.out.at[:, pl.ds(pl.multiple_of(IN_OUT["qkv"] + part * D + first * 128, 128), width)]

    def form_q(part):
        cols = pl.ds(part * 128, 128)

        def piece(i, carry):
            product = dot(s.turned_h[span(i, 256), :], s.dqkvh[:, cols]).astype(bf16)
            for low in range(2):
                at_slab = (i % 2) * 4 + (i // 2) * 2 + low
                s.chunk_q[part][at_slab, 0:ROWS] = product[ROWS * low : ROWS * (low + 1)]
            return carry

        lax.fori_loop(0, 4, piece, 0)
        extra = jnp.broadcast_to(column_sum(s.dqkvh[:, cols]), (16, 128)).astype(bf16)
        for at_slab in range(8):
            s.chunk_q[part][at_slab, ROWS:VEC] = extra
        came_q[part] = link.put(
            s.chunk_q[part].at[pl.ds((1 - x) * 4, 4)], s.landing_x[part], across["x"], link.group()
        )

    def second_q(part):
        link.arrive(came_q[part])
        fold_q(s.landing_x[part], s.chunk_q[part], x)
        came_q[part] = link.put(
            s.landing_x[part].at[pl.ds((1 - zh) * 2, 2)], s.landing_b[part], across["b"], link.group()
        )

    def deal_q(part):
        link.arrive(came_q[part])
        fold_q(s.landing_b[part], s.landing_x[part], zh)
        group = Group(link.count)
        link.count += 1
        where = out_q(part, spot.place, 128)

        def copy_to(fx, fy):
            y_to = flip(y, fy)
            return pltpu.make_async_remote_copy(
                src_ref=s.landing_b[part].at[y_to], dst_ref=where,
                send_sem=link.send_sem.at[group.at], recv_sem=link.recv_sem.at[group.at],
                device_id={"batch": flip(x, fx) * 2 + c, "blk": zh * 4 + x * 2 + y_to}, device_id_type=MESH,
            )

        for fx, fy in ((1, 1), (1, 0), (0, 1)):
            copy_to(fx, fy).start()
        pl.when(jnp.logical_not(keeps))(copy_to(0, 0).start)

        @pl.when(keeps)
        def _():
            where[...] = s.landing_b[part][y]

        link.last.append(lambda: wait_q(group, link.send_sem))
        came_q[part] = group

    def pass_q(part):
        wait_q(came_q[part], link.recv_sem)
        where = out_q(part, c * 4, 512)
        link.put(where, where, across["C"])

    def task(k):
        if k == 1:
            link.arrive(to_heads, own_heads, heads_in, length_in)
            attention_back_start(s, s.o, s.lse, s.doh)
        if k <= 4:
            attention_back_step(link, spot, PAIR_STEPS[k - 1], s, s.qkv, s.doh, s.dqkvh, rows_kv, own_kv)
        elif k == 5:
            attention_back_end(link, spot, s, s.dqkvh, rows_q, own_q)
        elif k >= 20:
            (form_q, second_q, deal_q, pass_q)[k // 10 - 2]((1, 2, 0)[k % 10])
        elif k == 9:
            link.arrive(rows_kv, own_kv, rows_q, own_q, close_in, weight_in)
            s.grad[...] = (s.dr1[...] + dot_t(s.dqkv[...], s.w_qkv[...])).astype(bf16)
            link.swap(spot, s.grad, grad_out)
        elif k == 10:
            wave(2)
            link.arrive(hidden_in, far_hidden, dqkv_in)
            for d in range(2):
                for g in range(8):
                    rows = pl.ds(g * ROWS, ROWS)
                    s.turned_h[:, pl.ds(d * LEN + g * ROWS, ROWS)] = s.hidden[d][rows, :].T
        elif k in (12, 13, 14):
            turn((0, 2, 1)[k - 12])

    for n, i in ORDER:
        if n == 100:
            task(i)
            continue
        if i < 0:
            compute(n)
            wave(waves[0] + 1)
        else:
            advance(n, i)
        if i + 1 < len(PLANS[n]):
            send(n, i + 1)
    link.finish()


def grad_call(main, w_qkv):
    dma = pltpu.SemaphoreType.DMA
    hbm = pl.BlockSpec(memory_space=pl.ANY)
    return pl.pallas_call(
        grad_kernel,
        out_shape=[jax.ShapeDtypeStruct((VEC, 12 * D), bf16), jax.ShapeDtypeStruct((ROWS, D), bf16)],
        in_specs=[hbm] * (len(MAIN_OUT) + 1),
        out_specs=[pl.BlockSpec(memory_space=pltpu.VMEM), hbm],
        scratch_shapes=[pltpu.VMEM(*entry) for entry in flat(GRAD_SCRATCH)]
        + [dma((SEMS,)), dma((SEMS,)), dma((20,))],
        compiler_params=pltpu.CompilerParams(
            collective_id=2, has_side_effects=True, vmem_limit_bytes=60 * 2**20
        ),
    )(*[getattr(main, name) for name in MAIN_OUT], w_qkv)


def finish_kernel(sums, mixed_in, grad_in, mixed, grad, qkv, attn, fore, back, qv, bias, fore_bias, gain, shift,
                  buf, thin_buf, qkv_buf, attn_buf, fore_buf, back_buf, in_sem, out_sem):
    at = IN_OUT
    pieces = [(at["qkv"] + part * D, D, VEC) for part in range(3)] + [(at["attn"], D, VEC)]
    for n in range(4):
        pieces += [(at["back"] + n * D, D, ROWS), (at["fore"] + n * D, D, ROWS)]
    loads, stores = [], []

    def store(src, dst):
        copy = pltpu.make_async_copy(src, dst, out_sem.at[len(stores)])
        copy.start()
        stores.append(copy)

    for n, (start, width, rows) in enumerate(pieces):
        here = (pl.ds(0, rows), pl.ds(start, width))
        loads.append(pltpu.make_async_copy(sums.at[here], buf.at[here], in_sem.at[n]))
        loads[n].start()
    for n, source in enumerate((mixed_in, grad_in)):
        loads.append(pltpu.make_async_copy(source, thin_buf.at[n], in_sem.at[12 + n]))
        loads[-1].start()
    mine = lax.axis_index("blk")
    for part in range(3):
        loads[part].wait()
        here = pl.ds(part * D, D)
        qkv_buf[:, here] = buf[0:ROWS, pl.ds(at["qkv"] + part * D, D)].astype(f32)
        store(qkv_buf.at[:, here], qkv.at[:, here])
        total = jnp.zeros((16, 128), f32)
        for place in range(8):
            block = buf[ROWS:VEC, pl.ds(at["qkv"] + part * D + place * 128, 128)].astype(f32)
            total = total + jnp.where(mine == place, block, 0.0)
        if part != 1:
            qv[part // 2 : part // 2 + 1, :] = total[0:1, :]
    loads[3].wait()
    attn_buf[...] = buf[0:ROWS, pl.ds(at["attn"], D)].astype(f32)
    store(attn_buf, attn)
    for n in range(4):
        rows = pl.ds(n * D, D)
        loads[4 + 2 * n].wait()
        back_buf[rows, :] = buf[0:ROWS, pl.ds(at["back"] + n * D, D)].astype(f32).T
        store(back_buf.at[rows], back.at[rows])
        loads[5 + 2 * n].wait()
        fore_buf[:, rows] = buf[0:ROWS, pl.ds(at["fore"] + n * D, D)].astype(f32)
        store(fore_buf.at[:, rows], fore.at[:, rows])
    for n, target in enumerate((mixed, grad)):
        loads[12 + n].wait()
        store(thin_buf.at[n], target)
    start = at["attn"]
    small = buf[ROWS:VEC, pl.ds(start, 512)].astype(f32) + buf[ROWS:VEC, pl.ds(start + 512, 512)].astype(f32)
    bias[...] = small[0:2, 0:128]
    gain[...] = small[2:4, 0:128]
    shift[...] = small[4:6, 0:128]
    fore_bias[...] = small[8:9, :]
    for copy in stores:
        copy.wait()


def finish_call(sums, mixed, grad):
    large = [(ROWS, 3 * D), (ROWS, D), (ROWS, FF), (FF, 128)]
    small = [(2, 128), (2, 128), (1, 512), (2, 128), (2, 128)]
    hbm, vmem = pl.BlockSpec(memory_space=pl.ANY), pl.BlockSpec(memory_space=pltpu.VMEM)
    dma = pltpu.SemaphoreType.DMA
    return pl.pallas_call(
        finish_kernel,
        out_shape=[jax.ShapeDtypeStruct((ROWS, D), bf16)] * 2
        + [jax.ShapeDtypeStruct(shape, f32) for shape in large + small],
        in_specs=[hbm] * 3,
        out_specs=[hbm] * 6 + [vmem] * 5,
        scratch_shapes=[pltpu.VMEM((VEC, 12 * D), bf16), pltpu.VMEM((2, ROWS, D), bf16)] + [pltpu.VMEM(shape, f32) for shape in large]
        + [dma((14,)), dma((14,))],
        compiler_params=pltpu.CompilerParams(vmem_limit_bytes=63 * 2**20),
    )(sums, mixed, grad)


def fast_body(tokens, lengths, *rest):
    params, cotangent = rest[:-1], rest[-1]
    main = main_call(lengths, tokens[0], cotangent[0], params)
    sums, grad = grad_call(main, params[0])
    mixed, grad, qkv, attn, fore, back, qv, bias, fore_bias, gain, shift = finish_call(sums, main.mixed, grad)
    return (
        mixed[None], grad[None], qkv, qv, attn, bias, fore, fore_bias.reshape(512), back, gain, shift,
    )


def solution(mesh):
    placed = (
        P("batch", "blk", None),
        P("batch"),
        P(),
        P(),
        P(),
        P(),
        P(),
        P(),
        P(),
        P(),
        P(),
        P("batch", "blk", None),
    )
    fast = dict(mesh.shape) == {"batch": 4, "blk": 8}
    return jax.shard_map(
        fast_body if fast else body,
        mesh=mesh,
        in_specs=placed,
        out_specs=(
            P("batch", "blk", None),
            P("batch", "blk", None),
            P("blk", None),
            P(None, "blk"),
            P("blk", None),
            P(None, "blk"),
            P("blk", None),
            P("blk"),
            P(None, "blk"),
            P(None, "blk"),
            P(None, "blk"),
        ),
        check_vma=False,
    )
```

```python
import math

import jax
import jax.numpy as jnp
from jax import lax
from jax.experimental import pallas as pl
from jax.experimental.pallas import tpu as pltpu
from jax.sharding import PartitionSpec as P

HEADS = 16


eps = 1e-12


def from_partner(x, axis, distance):
    return lax.ppermute(x, axis, [(i, i ^ 1 << distance) for i in range(lax.axis_size(axis))])


def normalize(values, gain, shift):
    centered = values - jnp.mean(values, axis=-1, keepdims=True)
    variance = jnp.mean(centered * centered, axis=-1, keepdims=True)
    return centered * lax.rsqrt(variance + eps) * gain + shift


def gelu_exact(values):
    return jax.nn.gelu(values, approximate=False)


def head_split(matrix, head_count):
    row_count, model_width = matrix.shape
    return matrix.reshape(row_count, head_count // 4, 4, model_width // head_count).transpose(
        1, 2, 0, 3
    )


def head_merge(stacked):
    group_count, group_size, row_count, head_size = stacked.shape
    return stacked.transpose(2, 0, 1, 3).reshape(row_count, group_count * group_size * head_size)


def core_forward(query_part, key_part, value_part, key_valid, scale):
    scores = (
        jnp.einsum("hqd,hkd->hqk", query_part, key_part, preferred_element_type=jnp.float32) * scale
    )
    masked = jnp.where(key_valid, scores, -1e30)
    row_max = jnp.max(masked, axis=-1, keepdims=True)
    exp_scores = jnp.where(key_valid, jnp.exp(masked - row_max), 0.0)
    row_total = jnp.sum(exp_scores, axis=-1, keepdims=True)
    prob_low = (exp_scores / row_total).astype(jnp.bfloat16)
    output = jnp.einsum("hqk,hkd->hqd", prob_low, value_part, preferred_element_type=jnp.float32)
    return (output, (row_max + jnp.log(row_total))[..., 0])


def core_backward(query_part, key_part, value_part, grad_part, log_part, key_valid, scale):
    scores = (
        jnp.einsum("hqd,hkd->hqk", query_part, key_part, preferred_element_type=jnp.float32) * scale
    )
    probs = jnp.where(key_valid, jnp.exp(scores - log_part[..., None]), 0.0)
    grad_probs = jnp.einsum(
        "hqd,hkd->hqk", grad_part, value_part, preferred_element_type=jnp.float32
    )
    inner_sum = jnp.sum(probs * grad_probs, axis=-1, keepdims=True)
    grad_scores = (probs * (grad_probs - inner_sum)).astype(jnp.bfloat16)
    grad_query = (
        jnp.einsum("hqk,hkd->hqd", grad_scores, key_part, preferred_element_type=jnp.float32)
        * scale
    )
    grad_key = (
        jnp.einsum("hqk,hqd->hkd", grad_scores, query_part, preferred_element_type=jnp.float32)
        * scale
    )
    grad_value = jnp.einsum(
        "hqk,hqd->hkd", probs.astype(jnp.bfloat16), grad_part, preferred_element_type=jnp.float32
    )
    return (grad_query, grad_key, grad_value)


def gather_group(kv_pair, position, bit_count):
    buffer_rows = kv_pair
    for step_bit in range(bit_count):
        received = from_partner(buffer_rows, "blk", step_bit)
        high_side = position >> step_bit & 1 == 1
        buffer_rows = jnp.where(
            high_side,
            jnp.concatenate([received, buffer_rows], 0),
            jnp.concatenate([buffer_rows, received], 0),
        )
    return buffer_rows


def spread_group(partials, position, bit_count):
    for step_bit in reversed(range(bit_count)):
        half_rows = partials.shape[0] // 2
        high_side = position >> step_bit & 1 == 1
        lower_part = partials[:half_rows]
        upper_part = partials[half_rows:]
        kept_part = jnp.where(high_side, upper_part, lower_part)
        sent_part = jnp.where(high_side, lower_part, upper_part)
        partials = kept_part + from_partner(sent_part.astype(jnp.bfloat16), "blk", step_bit).astype(
            sent_part.dtype
        )
    return partials


def attend_forward(queries, gathered, key_valid, head_count):
    model_width = queries.shape[1]
    scale = (model_width // head_count) ** (-0.5)
    query_heads = head_split(queries, head_count)
    key_heads = head_split(gathered[:, :model_width], head_count)
    value_heads = head_split(gathered[:, model_width:], head_count)

    def one_group(operands):
        query_part, key_part, value_part = operands
        return core_forward(query_part, key_part, value_part, key_valid, scale)

    outputs, log_sums = lax.map(one_group, (query_heads, key_heads, value_heads))
    return (head_merge(outputs), log_sums)


def attend_backward(queries, gathered, key_valid, log_sums, grad_attended, head_count):
    model_width = queries.shape[1]
    scale = (model_width // head_count) ** (-0.5)
    query_heads = head_split(queries, head_count)
    key_heads = head_split(gathered[:, :model_width], head_count)
    value_heads = head_split(gathered[:, model_width:], head_count)
    grad_heads = head_split(grad_attended, head_count)

    def one_group(operands):
        query_part, key_part, value_part, grad_part, log_part = operands
        return core_backward(
            query_part, key_part, value_part, grad_part, log_part, key_valid, scale
        )

    grad_query, grad_key, grad_value = lax.map(
        one_group, (query_heads, key_heads, value_heads, grad_heads, log_sums)
    )
    return (
        head_merge(grad_query),
        jnp.concatenate([head_merge(grad_key), head_merge(grad_value)], 1),
    )


def layer_forward(hidden, params, key_valid, position, bit_count, head_count):
    w_qkv, qv_bias, w_attn, out_bias, w_in, in_bias, w_back, norm_gain, norm_shift = params
    model_width = hidden.shape[1]
    hidden_low = hidden.astype(jnp.bfloat16)
    bias_row = jnp.concatenate([qv_bias[0], jnp.zeros_like(qv_bias[0]), qv_bias[1]])
    projected = (jnp.dot(hidden_low, w_qkv, preferred_element_type=jnp.float32) + bias_row).astype(
        jnp.bfloat16
    )
    gathered = gather_group(projected[:, model_width:], position, bit_count)
    attended, log_sums = attend_forward(projected[:, :model_width], gathered, key_valid, head_count)
    attended_low = attended.astype(jnp.bfloat16)
    first_sum = (
        hidden + jnp.dot(attended_low, w_attn, preferred_element_type=jnp.float32) + out_bias[0]
    )
    first_norm = normalize(first_sum, norm_gain[0], norm_shift[0])
    first_low = first_norm.astype(jnp.bfloat16)
    inner_pre = jnp.dot(first_low, w_in, preferred_element_type=jnp.float32) + in_bias
    activated = gelu_exact(inner_pre).astype(jnp.bfloat16)
    second_sum = (
        first_norm + jnp.dot(activated, w_back, preferred_element_type=jnp.float32) + out_bias[1]
    )
    output = normalize(second_sum, norm_gain[1], norm_shift[1])
    saved_state = (
        hidden_low,
        projected,
        gathered,
        log_sums,
        attended_low,
        first_sum,
        first_low,
        inner_pre,
        activated,
        second_sum,
    )
    return (output, saved_state)


def layer_backward(grad_output, saved_state, params, key_valid, position, bit_count, head_count):
    w_qkv, qv_bias, w_attn, out_bias, w_in, in_bias, w_back, norm_gain, norm_shift = params
    (
        hidden_low,
        projected,
        gathered,
        log_sums,
        attended_low,
        first_sum,
        first_low,
        inner_pre,
        activated,
        second_sum,
    ) = saved_state
    model_width = hidden_low.shape[1]
    unused_two, pull_two = jax.vjp(normalize, second_sum, norm_gain[1], norm_shift[1])
    grad_second, gain_two, shift_two = pull_two(grad_output)
    grad_branch_two = grad_second.astype(jnp.bfloat16)
    back_grad = jnp.einsum(
        "ra,rb->ab", activated, grad_branch_two, preferred_element_type=jnp.float32
    )
    bias_two = jnp.sum(grad_branch_two.astype(jnp.float32), axis=0)
    grad_act = jnp.dot(grad_branch_two, w_back.T, preferred_element_type=jnp.float32)
    unused_gelu, pull_gelu = jax.vjp(gelu_exact, inner_pre)
    grad_inner = pull_gelu(grad_act)[0].astype(jnp.bfloat16)
    in_grad = jnp.einsum("ra,rb->ab", first_low, grad_inner, preferred_element_type=jnp.float32)
    in_bias_grad = jnp.sum(grad_inner.astype(jnp.float32), axis=0)
    grad_first_norm = grad_second + jnp.dot(grad_inner, w_in.T, preferred_element_type=jnp.float32)
    unused_one, pull_one = jax.vjp(normalize, first_sum, norm_gain[0], norm_shift[0])
    grad_first, gain_one, shift_one = pull_one(grad_first_norm)
    grad_branch = grad_first.astype(jnp.bfloat16)
    attn_grad = jnp.einsum(
        "ra,rb->ab", attended_low, grad_branch, preferred_element_type=jnp.float32
    )
    bias_one = jnp.sum(grad_branch.astype(jnp.float32), axis=0)
    grad_attended = jnp.dot(grad_branch, w_attn.T, preferred_element_type=jnp.float32).astype(
        jnp.bfloat16
    )
    grad_query, grad_pairs = attend_backward(
        projected[:, :model_width], gathered, key_valid, log_sums, grad_attended, head_count
    )
    own_pairs = spread_group(grad_pairs, position, bit_count)
    grad_proj = jnp.concatenate([grad_query, own_pairs], 1).astype(jnp.bfloat16)
    qkv_grad = jnp.einsum("ra,rb->ab", hidden_low, grad_proj, preferred_element_type=jnp.float32)
    column_sums = jnp.sum(grad_proj.astype(jnp.float32), axis=0)
    qv_grad = jnp.stack([column_sums[:model_width], column_sums[2 * model_width :]])
    grad_hidden = grad_first + jnp.dot(grad_proj, w_qkv.T, preferred_element_type=jnp.float32)
    grad_list = (
        qkv_grad,
        qv_grad,
        attn_grad,
        jnp.stack([bias_one, bias_two]),
        in_grad,
        in_bias_grad,
        back_grad,
        jnp.stack([gain_one, gain_two]),
        jnp.stack([shift_one, shift_two]),
    )
    return (grad_hidden, grad_list)


def scatter_once(grad_list):
    (
        qkv_grad,
        qv_grad,
        attn_grad,
        bias_grad,
        in_grad,
        in_bias_grad,
        back_grad,
        gain_grad,
        shift_grad,
    ) = grad_list
    return (
        lax.psum_scatter(qkv_grad, "blk", scatter_dimension=0, tiled=True),
        lax.psum_scatter(qv_grad, "blk", scatter_dimension=1, tiled=True),
        lax.psum_scatter(attn_grad, "blk", scatter_dimension=0, tiled=True),
        lax.psum_scatter(bias_grad, "blk", scatter_dimension=1, tiled=True),
        lax.psum_scatter(in_grad, "blk", scatter_dimension=0, tiled=True),
        lax.psum_scatter(in_bias_grad, "blk", scatter_dimension=0, tiled=True),
        lax.psum_scatter(back_grad, "blk", scatter_dimension=1, tiled=True),
        lax.psum_scatter(gain_grad, "blk", scatter_dimension=1, tiled=True),
        lax.psum_scatter(shift_grad, "blk", scatter_dimension=1, tiled=True),
    )


def body(
    tokens,
    lengths,
    w_qkv,
    qv_bias,
    w_attn,
    out_bias,
    w_in,
    in_bias,
    w_back,
    norm_gain,
    norm_shift,
    cotangent,
):
    row_count = tokens.shape[1]
    head_count = HEADS
    cycle_size = lax.axis_size("blk")
    bit_count = cycle_size.bit_length() - 1
    position = lax.axis_index("blk")
    length = lengths[0]
    key_valid = jnp.arange(cycle_size * row_count) < length
    params = (w_qkv, qv_bias, w_attn, out_bias, w_in, in_bias, w_back, norm_gain, norm_shift)
    out_one, saved_one = layer_forward(
        tokens[0].astype(jnp.float32), params, key_valid, position, bit_count, head_count
    )
    out_two, saved_two = layer_forward(out_one, params, key_valid, position, bit_count, head_count)
    grad_hidden, grads_two = layer_backward(
        cotangent[0].astype(jnp.float32),
        saved_two,
        params,
        key_valid,
        position,
        bit_count,
        head_count,
    )
    grad_hidden, grads_one = layer_backward(
        grad_hidden, saved_one, params, key_valid, position, bit_count, head_count
    )
    shards = scatter_once(jax.tree.map(jnp.add, grads_two, grads_one))
    (
        qkv_part,
        qv_part,
        attn_part,
        bias_part,
        in_part,
        in_bias_part,
        back_part,
        gain_part,
        shift_part,
    ) = shards
    totals = (
        lax.psum(qkv_part.astype(jnp.bfloat16), "batch").astype(jnp.float32),
        lax.psum(qv_part.astype(jnp.bfloat16), "batch").astype(jnp.float32),
        lax.psum(attn_part.astype(jnp.bfloat16), "batch").astype(jnp.float32),
        lax.psum(bias_part.astype(jnp.bfloat16), "batch").astype(jnp.float32),
        lax.psum(in_part.astype(jnp.bfloat16), "batch").astype(jnp.float32),
        lax.psum(in_bias_part.astype(jnp.bfloat16), "batch").astype(jnp.float32),
        lax.psum(back_part.astype(jnp.bfloat16), "batch").astype(jnp.float32),
        lax.psum(gain_part.astype(jnp.bfloat16), "batch").astype(jnp.float32),
        lax.psum(shift_part.astype(jnp.bfloat16), "batch").astype(jnp.float32),
    )
    return (
        out_two.astype(jnp.bfloat16)[None],
        grad_hidden.astype(jnp.bfloat16)[None],
        totals[0],
        totals[1],
        totals[2],
        totals[3],
        totals[4],
        totals[5],
        totals[6],
        totals[7],
        totals[8],
    )


MESH = pl.DeviceIdType.MESH
f32 = jnp.float32
bf16 = jnp.bfloat16
FLIPS = ((0, 0), (1, 0), (0, 1), (1, 1))
GROUPS = len(FLIPS)
PART = 4096 // GROUPS
ROWS, D, FF, LEN, VEC = 128, 1024, 4096, 1024, 144


def dot(a, b):
    return jnp.dot(a, b, preferred_element_type=f32)


def dot_t(a, b):
    return lax.dot_general(a, b, (((1,), (1,)), ((), ())), preferred_element_type=f32)


def dot_0(a, b):
    return lax.dot_general(a, b, (((0,), (0,)), ((), ())), preferred_element_type=f32)


def span(at, size):
    return pl.ds(pl.multiple_of(at * size, size), size)


def flip(bit, by):
    return bit + by * (1 - 2 * bit)


def group(ref, n):
    return ref.at[pl.ds(n * ROWS, ROWS)]


class Spot:
    def __init__(self):
        self.row, self.pos = lax.axis_index("batch"), lax.axis_index("blk")
        self.x, self.c = self.row // 2, self.row % 2
        self.z, self.y = self.pos // 2, self.pos % 2
        self.zl, self.zh = self.z % 2, self.z // 2
        self.place = self.c * 4 + self.zl * 2 + self.y
        self.moved = self.c != self.zh

    def flipped(self, c=0, x=0, y=0, zl=0, zh=0):
        row = flip(self.x, x) * 2 + flip(self.c, c)
        pos = flip(self.zh, zh) * 4 + flip(self.zl, zl) * 2 + flip(self.y, y)
        return {"batch": row, "blk": pos}

    def member(self, place):
        return {"batch": self.x * 2 + place // 4, "blk": self.zh * 4 + place % 4}

    def partner(self):
        return {"batch": self.x * 2 + self.zh, "blk": self.c * 4 + self.pos % 4}


BULK = 2**21


class Group:
    def __init__(self, at):
        self.at, self.bytes, self.waited = at, 0, False


def bytes_of(ref):
    return math.prod(ref.shape) * jnp.dtype(ref.dtype).itemsize


class Link:
    def __init__(self, send_sem, recv_sem, own_sem, *meters):
        self.send_sem, self.recv_sem, self.own_sem, self.meters = send_sem, recv_sem, own_sem, meters
        self.count, self.own_count = 0, 0
        self.groups, self.own_groups, self.swaps, self.last = [], [], [], []
        self.bulk, self.own_bulk = self.group(), self.own_group()

    def group(self):
        self.groups.append(Group(self.count))
        self.count += 1
        return self.groups[-1]

    def own_group(self):
        self.own_groups.append(Group(self.own_count))
        self.own_count += 1
        return self.own_groups[-1]

    def put(self, src, dst, device, group=None):
        if group is None:
            if self.bulk.bytes + bytes_of(src) > BULK:
                self.bulk = self.group()
            group = self.bulk
        group.bytes += bytes_of(src)
        pltpu.make_async_remote_copy(
            src_ref=src, dst_ref=dst, send_sem=self.send_sem.at[group.at], recv_sem=self.recv_sem.at[group.at],
            device_id=device, device_id_type=MESH,
        ).start()
        return group

    def keep(self, src, dst, group=None):
        if group is None:
            if self.own_bulk.bytes + bytes_of(src) > BULK:
                self.own_bulk = self.own_group()
            group = self.own_bulk
        group.bytes += bytes_of(src)
        pltpu.make_async_copy(src, dst, self.own_sem.at[group.at]).start()
        return group

    def wait(self, group, sem):
        if group.bytes:
            for meter in self.meters:
                row = bytes_of(meter) // meter.shape[0]
                tile = 8 if meter.dtype == f32 else 16
                if group.bytes % (tile * row) == 0 and group.bytes <= bytes_of(meter):
                    view = meter.at[pl.ds(0, group.bytes // row)]
                    pltpu.make_async_copy(view, view, sem.at[group.at]).wait()
                    return
            raise ValueError(group.bytes)

    def arrive(self, *groups):
        for group in groups:
            if not group.waited:
                group.waited = True
                self.wait(group, self.own_sem if any(group is own for own in self.own_groups) else self.recv_sem)

    def swap(self, spot, src, dst):
        far = pltpu.make_async_remote_copy(
            src_ref=src, dst_ref=dst, send_sem=self.send_sem.at[self.count], recv_sem=self.recv_sem.at[self.count],
            device_id=spot.partner(), device_id_type=MESH,
        )
        near = pltpu.make_async_copy(src, dst, self.own_sem.at[self.own_count])
        self.count += 1
        self.own_count += 1
        pl.when(spot.moved)(far.start)
        pl.when(jnp.logical_not(spot.moved))(near.start)
        self.swaps.append((spot, far, near))
        return far, near

    def arrive_swap(self, spot, pair):
        pl.when(spot.moved)(pair[0].wait_recv)
        pl.when(jnp.logical_not(spot.moved))(pair[1].wait)
        self.swaps = [(one, far, None if far is pair[0] else near) for one, far, near in self.swaps]

    def finish(self):
        self.arrive(*self.groups, *self.own_groups)
        for group in self.groups:
            self.wait(group, self.send_sem)
        for wait in self.last:
            wait()
        for spot, far, near in self.swaps:
            if near is not None:
                self.arrive_swap(spot, (far, near))
            pl.when(spot.moved)(far.wait_send)


def greet(spot, devices):
    barrier = pltpu.get_barrier_semaphore()
    for device in devices:
        pl.semaphore_signal(barrier, inc=1, device_id=device, device_id_type=MESH)

    @pl.when(spot.moved)
    def _():
        pl.semaphore_signal(barrier, inc=1, device_id=spot.partner(), device_id_type=MESH)

    def meet():
        @pl.when(spot.moved)
        def _():
            pl.semaphore_wait(barrier, len(devices) + 1)

        @pl.when(jnp.logical_not(spot.moved))
        def _():
            pl.semaphore_wait(barrier, len(devices))

    return meet


def standard(values):
    centered = values - jnp.mean(values, axis=-1, keepdims=True)
    inverse = lax.rsqrt(jnp.mean(centered * centered, axis=-1, keepdims=True) + eps)
    return centered * inverse, inverse


def standard_back(unit, inverse, gain, grad):
    scaled = grad * gain
    inner = jnp.mean(scaled * unit, axis=-1, keepdims=True)
    return inverse * (scaled - jnp.mean(scaled, axis=-1, keepdims=True) - unit * inner)


def column_sum(x):
    return jnp.sum(x.astype(f32), axis=0, keepdims=True)


def gelu_pair(u):
    t = 1.0 / (1.0 + 0.23164188 * jnp.abs(u))
    bell = jnp.exp(-0.5 * u * u)
    poly = t * (0.127414796 + t * (-0.142248368 + t * (0.7107068705 + t * (-0.7265760135 + t * 0.5307027145))))
    tail = poly * bell
    cdf = jnp.where(u < 0, tail, 1.0 - tail)
    return u * cdf, cdf + u * bell * 0.3989422804


def low_lanes():
    return lax.broadcasted_iota(jnp.int32, (1, 128), 1) < 64


def valid_keys(length):
    return lax.broadcasted_iota(jnp.int32, (1, LEN), 1).astype(f32) < length


def attention_rows(qkv, rows, valid):
    queries, keys, values = qkv[rows, 0:128], qkv[:, 128:256], qkv[:, 256:384]
    low_half = low_lanes()
    outs, lses = [], []
    for half in range(2):
        mine = low_half if half == 0 else jnp.logical_not(low_half)
        part = jnp.where(mine, queries, jnp.zeros_like(queries)) * jnp.asarray(0.125, bf16)
        scores = jnp.where(valid, dot_t(part, keys), -1e30)
        top = jnp.max(scores, axis=1, keepdims=True)
        expd = jnp.exp(scores - top)
        total = jnp.sum(expd, axis=1, keepdims=True)
        probs = (expd * (1.0 / total)).astype(bf16)
        outs.append(dot(probs, values))
        lses.append(top + jnp.log(total))
    return jnp.where(low_half, outs[0], outs[1]), jnp.where(low_half, lses[0], lses[1])


def attention_back_keys(qkv, grads_ref, lse_rows, delta_rows, rows, first, length):
    low_half = low_lanes()
    keys, values = qkv[rows, 128:256], qkv[rows, 256:384]
    at = lax.broadcasted_iota(jnp.int32, (256, 1), 0) + first
    valid = at.astype(f32) < length
    dqs, dk, dv = [], None, None
    for half in range(2):
        mine = low_half if half == 0 else jnp.logical_not(low_half)
        k_part = jnp.where(mine, keys, jnp.zeros_like(keys)) * jnp.asarray(0.125, bf16)
        v_part = jnp.where(mine, values, jnp.zeros_like(values))
        queries, grads = qkv[:, 0:128], grads_ref[...]
        scores = dot_t(k_part, queries)
        probs = jnp.where(valid, jnp.exp(scores - lse_rows[half : half + 1, :]), 0.0)
        dp = dot_t(v_part, grads)
        ds = (probs * (dp - delta_rows[half : half + 1, :])).astype(bf16)
        dv_part = dot(probs.astype(bf16), grads)
        dk_part = dot(ds, queries)
        dv = dv_part if half == 0 else jnp.where(low_half, dv, dv_part)
        dk = dk_part if half == 0 else jnp.where(low_half, dk, dk_part)
        dqs.append(dot_0(ds, keys))
    return jnp.where(low_half, dqs[0], dqs[1]), (dk * 0.125).astype(bf16), dv.astype(bf16)


def attention_back_start(s, o, lse, grads):
    turned = lse[...].T
    s.lse_rows[0:1, :] = turned[0:1, :]
    s.lse_rows[1:2, :] = turned[64:65, :]
    product = (grads[...].astype(f32) * o[...]).T
    s.delta_rows[0:1, :] = jnp.sum(product[0:64, :], axis=0, keepdims=True)
    s.delta_rows[1:2, :] = jnp.sum(product[64:128, :], axis=0, keepdims=True)


def attention_back_step(link, spot, step, s, qkv, grads, dqkvh, group, own):
    pair = (spot.place // 2 + step) % 4
    rows = span(pair, 256)
    dq, dk, dv = attention_back_keys(
        qkv, grads, s.lse_rows, s.delta_rows, rows, pair * 256, s.length[0:1, 0:1]
    )
    dqkvh[rows, 128:256] = dk
    dqkvh[rows, 256:384] = dv
    s.dq[...] = dq if step == PAIR_STEPS[0] else s.dq[...] + dq
    for part in (1, 2):
        send_rows(link, spot, dqkvh, s.dqkv, step, part, group, own)


def attention_back_end(link, spot, s, dqkvh, group, own):
    dqkvh[0:LEN, 0:128] = (s.dq[...] * 0.125).astype(bf16)
    for step in PAIR_STEPS:
        send_rows(link, spot, dqkvh, s.dqkv, step, 0, group, own)


def send_columns(link, spot, source, target, part, landing, groups, own):
    for step in range(7, -1, -1):
        to = (spot.place + step) % 8
        src = source.at[:, pl.ds(pl.multiple_of(part * D + to * 128, 128), 128)]
        dst = target.at[span(spot.place, ROWS), pl.ds(landing * 128, 128)]
        if step:
            link.put(src, dst, spot.member(to), groups[step])
        else:
            link.keep(src, dst, own)


def pair_rows(spot, step):
    return span((spot.place // 2 + step) % 4, 256)


def send_rows(link, spot, source, target, step, part, group, own):
    same = (spot.place + 2 * step) % 8
    for n, to in enumerate((same, same + 1 - 2 * spot.y)):
        src = source.at[span(to, ROWS), pl.ds(part * 128, 128)]
        dst = target.at[:, pl.ds(pl.multiple_of(part * D + spot.place * 128, 128), 128)]
        if step or n:
            link.put(src, dst, spot.member(to), group)
        else:
            link.keep(src, dst, own)


PAIR_STEPS = (1, 2, 3, 0)


def spec(**named):
    return named


def two(*entry):
    return [entry, entry]


MAIN_OUT = spec(
    mixed=((ROWS, D), bf16), qkv1=((LEN, 384), bf16), lse1=((LEN, 128), f32), o1=((LEN, 128), f32),
    left_attn=((4, ROWS, D), bf16), right_attn=((4 * ROWS, 512), bf16),
    left_back=((2 * GROUPS, ROWS, D), bf16), right_back=((2 * GROUPS * ROWS, PART), bf16),
    left_in=((2 * GROUPS, ROWS, D), bf16), right_in=((2 * GROUPS * ROWS, PART), bf16),
    hidden=((2, LEN, D), bf16), dqkv2=((LEN, 384), bf16),
    du1=((ROWS, FF), bf16), dza1=((ROWS, D), bf16),
    do1=((ROWS, D), bf16), dr1=((ROWS, D), f32), vec=((8, D), f32), inb=((1, FF), f32),
    length=((16, 128), f32),
)
MAIN_SCRATCH = spec(
    w_qkv=((D, 3 * D), bf16), w_attn=((D, D), bf16), w_in=((D, FF), bf16), w_back=((FF, D), bf16),
    tok=((ROWS, D), bf16), cot=((ROWS, D), bf16), length=((16, 128), f32), sent_length=((16, 128), f32),
    proj=two((ROWS, 3 * D), bf16), qkv=two((LEN, 384), bf16), lse=two((LEN, 128), f32),
    o=two((LEN, 128), bf16), full_o=two((LEN, 128), f32), att=two((ROWS, D), bf16), n=two((ROWS, D), bf16),
    act=two((ROWS, FF), bf16), slope=two((ROWS, FF), bf16),
    unit_a=two((ROWS, D), f32), unit_b=two((ROWS, D), f32),
    inv_a=two((ROWS, 128), f32), inv_b=two((ROWS, 128), f32),
    hq2=((ROWS, D), bf16), h=((ROWS, D), f32), acc=((ROWS, D), f32), mixed=((ROWS, D), bf16),
    dzb=two((ROWS, D), bf16), du=two((ROWS, FF), bf16), dza=two((ROWS, D), bf16), do=two((ROWS, D), bf16),
    doh=((LEN, 128), bf16), dqkvh=((LEN, 384), bf16), dq=((LEN, 128), f32), lse_rows=((8, LEN), f32), delta_rows=((8, LEN), f32),
    dqkv=((ROWS, 3 * D), bf16), dr1=((ROWS, D), f32), vec=((8, D), f32), inb=((1, FF), f32),
)


class Refs:
    pass


def flat(entries):
    out = []
    for entry in entries.values():
        out += entry if isinstance(entry, list) else [entry]
    return out


def bind(entries, refs):
    got, it = Refs(), iter(refs)
    for name, entry in entries.items():
        setattr(got, name, [next(it) for _ in entry] if isinstance(entry, list) else next(it))
    return got


def main_kernel(*refs):
    (len_ref, tokens, cotangent, w_qkv, w_attn, w_in, w_back,
     qv_bias, out_bias, in_bias, gain, shift) = refs[:12]
    outs = bind(MAIN_OUT, refs[12 : 12 + len(MAIN_OUT)])
    rest = refs[12 + len(MAIN_OUT) :]
    s = bind(MAIN_SCRATCH, rest[:-4])
    load_sem, send_sem, recv_sem, own_sem = rest[-4:]
    spot = Spot()
    link = Link(send_sem, recv_sem, own_sem, outs.hidden.at[0], outs.lse1)
    others = [spot.member((spot.place + step) % 8) for step in range(1, 8)]
    others += [spot.flipped(x=1), spot.flipped(c=1, x=1)]
    meet = greet(spot, others)

    loads = []
    for n, (src, dst) in enumerate(
        [(w_qkv.at[:, pl.ds(D * part, D)], s.w_qkv.at[:, pl.ds(D * part, D)]) for part in (1, 2, 0)]
        + [(w_attn, s.w_attn), (w_in, s.w_in), (w_back, s.w_back)]
    ):
        loads.append(pltpu.make_async_copy(src, dst, load_sem.at[n]))
        loads[n].start()
    loaded = set()

    def need(n):
        if n not in loaded:
            loaded.add(n)
            loads[n].wait()

    s.sent_length[...] = jnp.full((16, 128), len_ref[0], jnp.int32).astype(f32)
    meet()
    first_in = [link.swap(spot, tokens, s.tok), link.swap(spot, s.sent_length, s.length)]
    for pair in first_in:
        link.arrive_swap(spot, pair)
    valid = valid_keys(s.length[0:1, 0:1])

    later = []

    def share(source, left, d):
        link.keep(source, left.at[d])
        link.put(source, left.at[2 + d], spot.flipped(c=1))
        link.put(source, left.at[4 + d], spot.flipped(x=1))

    def deal(source, right, d):
        link.keep(source.at[:, span(spot.c * 2 + spot.x, PART)], group(right, d))
        for n, (dc, dx) in enumerate(FLIPS[1:], 1):
            cols = span(flip(spot.c, dc) * 2 + flip(spot.x, dx), PART)
            link.put(source.at[:, cols], group(right, 2 * n + d), spot.flipped(c=dc, x=dx))

    def gather(hq, d, part):
        rows = pl.ds(part * 64, 64)
        block = outs.hidden.at[d, pl.ds(pl.multiple_of(spot.place * ROWS + part * 64, 64), 64)]
        for dz, dy in ((1, 0), (0, 1), (1, 1)):
            link.put(hq.at[rows], block, spot.flipped(zl=dz, y=dy))
        link.keep(hq.at[rows], block)

    def forward(d, hq, h):
        pair_of = [0, 3, 3, 2, 2, 1, 1, 1]
        both, pairs, own = link.group(), [link.group() for _ in range(4)], link.own_group()
        for part, number in ((1, 0), (2, 1), (0, 2)):
            need(number)

            def tile(i, carry):
                cols = span(2 * part + i, 512)
                value = dot(hq[...], s.w_qkv[:, cols])
                if part != 1:
                    value += qv_bias[part // 2 : part // 2 + 1, span(i, 512)]
                s.proj[d][:, cols] = value.astype(bf16)
                return carry

            lax.fori_loop(0, 2, tile, 0)
            to_groups = [both] * 8 if part else [pairs[pair] for pair in pair_of]
            send_columns(link, spot, s.proj[d], s.qkv[d], part, part, to_groups, own)
        link.arrive(both, own)
        if d == 0:
            later.append(link.swap(spot, cotangent, s.cot))
        to_rows, own_rows = link.group(), link.own_group()
        for step in PAIR_STEPS:
            link.arrive(pairs[step])
            rows = pair_rows(spot, step)
            s.full_o[d][rows, :], s.lse[d][rows, :] = attention_rows(s.qkv[d], rows, valid)
            s.o[d][rows, :] = s.full_o[d][rows, :].astype(bf16)
            send_rows(link, spot, s.o[d], s.att[d], step, 0, to_rows, own_rows)
        if d == 0:
            link.keep(s.qkv[0], outs.qkv1)
            link.keep(s.lse[0], outs.lse1)
            link.keep(s.full_o[0], outs.o1)
        link.arrive(to_rows, own_rows)
        gather(s.tok, 0, d)
        need(3)
        unit, inverse = standard(h[...].astype(f32) + dot(s.att[d][...], s.w_attn[...]) + out_bias[0:1])
        link.keep(s.att[d], outs.left_attn.at[d])
        link.put(s.att[d], outs.left_attn.at[2 + d], spot.flipped(c=1))
        s.unit_a[d][...] = unit
        s.inv_a[d][...] = jnp.broadcast_to(inverse, (ROWS, 128))
        first = unit * gain[0:1] + shift[0:1]
        s.n[d][...] = first.astype(bf16)
        share(s.n[d], outs.left_in, d)
        s.acc[...] = first + out_bias[1:2]
        need(4)
        need(5)

        def inner(i, carry):
            cols = span(i, 512)
            act, slope = gelu_pair(dot(s.n[d][...], s.w_in[:, cols]) + in_bias[:, cols])
            act = act.astype(bf16)
            s.act[d][:, cols] = act
            s.slope[d][:, cols] = slope.astype(bf16)
            s.acc[...] += dot(act, s.w_back[cols, :])
            return carry

        lax.fori_loop(0, 8, inner, 0)
        deal(s.act[d], outs.right_back, d)
        unit, inverse = standard(s.acc[...])
        s.unit_b[d][...] = unit
        s.inv_b[d][...] = jnp.broadcast_to(inverse, (ROWS, 128))
        return unit * gain[1:2] + shift[1:2]

    def add_vec(at, value, fresh):
        s.vec[at : at + 1, :] = value if fresh else s.vec[at : at + 1, :] + value

    def backward(d, grad, fresh):
        unit = s.unit_b[d][...]
        add_vec(3, column_sum(grad * unit), fresh)
        add_vec(5, column_sum(grad), fresh)
        dr = standard_back(unit, s.inv_b[d][:, 0:1], gain[1:2], grad)
        s.acc[...] = dr
        low = dr.astype(bf16)
        s.dzb[d][...] = low
        share(s.dzb[d], outs.left_back, d)
        add_vec(1, column_sum(low), fresh)

        def inner(i, carry):
            cols = span(i, 512)
            du = (dot_t(s.dzb[d][...], s.w_back[cols, :]) * s.slope[d][:, cols].astype(f32)).astype(bf16)
            s.du[d][:, cols] = du
            total = column_sum(du)
            s.inb[:, cols] = total if fresh else s.inb[:, cols] + total
            s.acc[...] += dot_t(du, s.w_in[:, cols])
            return carry

        lax.fori_loop(0, 8, inner, 0)
        if d:
            deal(s.du[d], outs.right_in, d)
        else:
            link.keep(s.du[d], outs.du1)
        grad = s.acc[...]
        unit = s.unit_a[d][...]
        add_vec(2, column_sum(grad * unit), fresh)
        add_vec(4, column_sum(grad), fresh)
        dr = standard_back(unit, s.inv_a[d][:, 0:1], gain[0:1], grad)
        s.dr1[...] = dr
        low = dr.astype(bf16)
        s.dza[d][...] = low
        if d:
            link.keep(s.dza[d].at[:, span(spot.c, 512)], group(outs.right_attn, d))
            link.put(s.dza[d].at[:, span(1 - spot.c, 512)], group(outs.right_attn, 2 + d), spot.flipped(c=1))
        else:
            link.keep(s.dza[d], outs.dza1)
        add_vec(0, column_sum(low), fresh)
        s.do[d][...] = dot_t(low, s.w_attn[...]).astype(bf16)

    out = forward(0, s.tok, s.tok)
    s.h[...] = out
    s.hq2[...] = out.astype(bf16)
    out = forward(1, s.hq2, s.h)
    s.mixed[...] = out.astype(bf16)
    link.swap(spot, s.mixed, outs.mixed)
    link.arrive_swap(spot, later[0])
    gather(s.hq2, 1, 0)
    backward(1, s.cot[...].astype(f32), True)
    to_heads, own_heads = link.group(), link.own_group()
    send_columns(link, spot, s.do[1], s.doh, 0, 0, [to_heads] * 8, own_heads)
    link.arrive(to_heads, own_heads)
    attention_back_start(s, s.full_o[1], s.lse[1], s.doh)
    to_rows, own_rows, last_rows, own_last = link.group(), link.own_group(), link.group(), link.own_group()
    for step in PAIR_STEPS:
        attention_back_step(link, spot, step, s, s.qkv[1], s.doh, s.dqkvh, to_rows, own_rows)
    attention_back_end(link, spot, s, s.dqkvh, last_rows, own_last)
    link.keep(s.dqkvh, outs.dqkv2)
    link.arrive(to_rows, own_rows)
    s.dr1[...] += dot_t(s.dqkv[:, D:], s.w_qkv[:, D:])
    link.arrive(last_rows, own_last)
    gather(s.hq2, 1, 1)
    backward(0, s.dr1[...] + dot_t(s.dqkv[:, :D], s.w_qkv[:, :D]), False)
    link.keep(s.do[0], outs.do1)
    link.keep(s.dr1, outs.dr1)
    small = link.own_group()
    link.keep(s.vec, outs.vec, small)
    link.keep(s.inb, outs.inb, small)
    link.keep(s.length, outs.length, small)
    link.finish()


def main_call(length, tokens, cotangent, params):
    w_qkv, qv_bias, w_attn, out_bias, w_in, in_bias, w_back, gain, shift = params
    dma = pltpu.SemaphoreType.DMA
    vmem, hbm = pl.BlockSpec(memory_space=pltpu.VMEM), pl.BlockSpec(memory_space=pl.ANY)
    results = pl.pallas_call(
        main_kernel,
        out_shape=[jax.ShapeDtypeStruct(*entry) for entry in MAIN_OUT.values()],
        in_specs=[pl.BlockSpec(memory_space=pltpu.SMEM), hbm, hbm] + [hbm] * 4 + [vmem] * 5,
        out_specs=[hbm] * len(MAIN_OUT),
        scratch_shapes=[pltpu.VMEM(*entry) for entry in flat(MAIN_SCRATCH)]
        + [dma((6,)), dma((32,)), dma((32,)), dma((20,))],
        compiler_params=pltpu.CompilerParams(
            collective_id=1, has_side_effects=True, vmem_limit_bytes=60 * 2**20
        ),
    )(length, tokens, cotangent, w_qkv, w_attn, w_in, w_back, qv_bias, out_bias, in_bias[None], gain, shift)
    return bind(MAIN_OUT, results)


PATHS = spec(A="yxabXC", B="xyabXC", C="abysC", F="yabZ", G="aybZ")
CHUNKS = (
    ("B", 0, 0, 512),
    ("F", 1, 0, 128),
    ("F", 1, 128, 128),
    ("F", 1, 256, 256),
    ("G", 1, 512, 256),
    ("F", 1, 768, 256),
    ("F", 2, 0, 256),
    ("F", 2, 256, 256),
    ("F", 2, 512, 256),
    ("F", 2, 768, 128),
    ("F", 2, 896, 128),
)
ORDER = (
    (100, 12), (0, -1), (100, 14), (4, -1), (5, -1), (100, 1), (1, -1), (100, 2), (100, 3), (100, 4),
    (4, 0), (100, 13), (8, -1), (5, 0), (7, -1), (6, -1), (100, 5), (1, 0), (3, -1), (100, 10),
    (5, 1), (100, 20), (100, 22), (4, 1), (1, 1), (100, 21), (0, 0), (5, 2), (2, -1), (100, 30),
    (8, 0), (4, 2), (9, -1), (1, 2), (100, 32), (100, 40), (100, 31), (7, 0), (8, 1), (10, -1),
    (5, 3), (100, 42), (4, 3), (6, 0), (1, 3), (100, 41), (100, 9), (7, 1), (8, 2), (3, 0),
    (6, 1), (8, 3), (0, 1), (7, 2), (2, 0), (3, 1), (9, 0), (6, 2), (7, 3), (100, 50),
    (0, 2), (10, 0), (2, 1), (6, 3), (100, 52), (3, 2), (9, 1), (100, 51), (10, 1), (0, 3),
    (2, 2), (3, 3), (9, 2), (0, 4), (10, 2), (2, 3), (0, 5), (9, 3), (10, 3),
)
IN_OUT = spec(back=0, fore=FF, attn=2 * FF, qkv=2 * FF + D)


def plan(path, width):
    slabs, steps = 8, []
    for stage in path:
        if stage in "yab":
            slabs //= 2
        elif stage == "x":
            width //= 2
        elif stage == "X":
            width *= 2
        steps.append((stage, slabs, width))
    return steps


def chunk_rows(c):
    return VEC if c == 0 else ROWS


SEMS = 24 + sum(len(PATHS[chunk[0]]) for chunk in CHUNKS)
PLANS = [plan(PATHS[chunk[0]], chunk[3]) for chunk in CHUNKS]
GRAD_SCRATCH = spec(
    left=[((4, ROWS, D), bf16)] + two((2 * GROUPS, ROWS, D), bf16),
    right=[((4 * ROWS, 512), bf16)] + two((2 * GROUPS * ROWS, PART), bf16),
    turned=[((D, 512), bf16)] + two((D, 256 * GROUPS), bf16),
    chunk=[((8, chunk_rows(c), CHUNKS[c][3]), bf16) for c in range(len(CHUNKS))],
    landing=[
        ((slabs, chunk_rows(c), width), bf16)
        for c, steps in enumerate(PLANS) for stage, slabs, width in steps if stage in "yabxs"
    ],
    hidden=two((LEN, D), bf16), turned_h=((D, 2 * LEN), bf16), dqkvh=((2 * LEN, 384), bf16),
    chunk_q=[((8, VEC, 128), bf16)] * 3, landing_x=[((4, VEC, 128), bf16)] * 3, landing_b=[((2, VEC, 128), bf16)] * 3,
    qkv=((LEN, 384), bf16), lse=((LEN, 128), f32), doh=((LEN, 128), bf16),
    o=((LEN, 128), f32), dq=((LEN, 128), f32), lse_rows=((8, LEN), f32), delta_rows=((8, LEN), f32),
    dqkv=((ROWS, 3 * D), bf16), w_qkv=((D, 3 * D), bf16),
    dr1=((ROWS, D), f32), grad=((ROWS, D), bf16), vec=((8, D), f32), inb=((1, FF), f32), length=((16, 128), f32),
)


def grad_kernel(*refs):
    src = bind(MAIN_OUT, refs[: len(MAIN_OUT)])
    w_qkv, sums, grad_out = refs[len(MAIN_OUT) : len(MAIN_OUT) + 3]
    rest = refs[len(MAIN_OUT) + 3 :]
    s = bind(GRAD_SCRATCH, rest[:-3])
    s.out = sums
    spot = Spot()
    link = Link(*rest[-3:], src.hidden.at[0], src.lse1, w_qkv)
    x, y, c, zl, zh = spot.x, spot.y, spot.c, spot.zl, spot.zh
    others = [spot.member((spot.place + step) % 8) for step in range(1, 8)]
    others += [spot.flipped(x=1), spot.flipped(c=1, x=1), spot.flipped(zh=1)]
    meet = greet(spot, others)
    mine = span(c * 2 + x, PART)
    heads_in, vec_in, hidden_in, dqkv_in, close_in, left_in, right_in, weight_in = [link.own_group() for _ in range(8)]
    length_in = link.own_group()
    own_ready = [link.own_group() for _ in range(3)]
    for one, other in ((src.o1, s.o), (src.qkv1, s.qkv), (src.lse1, s.lse)):
        link.keep(one, other, heads_in)
    link.keep(src.length, s.length, length_in)
    link.keep(src.left_attn, s.left[0], own_ready[0])
    for n in (1, 3):
        link.keep(group(src.right_attn, n), group(s.right[0], n), own_ready[0])
    link.keep(src.dza1.at[:, span(c, 512)], group(s.right[0], 0), own_ready[0])
    link.keep(src.right_back, s.right[1], right_in)
    first = pl.ds(0, 6)
    link.keep(src.left_back.at[first], s.left[1].at[first], own_ready[1])
    link.keep(src.vec, s.vec, vec_in)
    link.keep(src.inb, s.inb, vec_in)
    meet()
    to_heads, own_heads, far_hidden = link.group(), link.own_group(), link.group()
    far_ready = [link.group() for _ in range(3)]
    send_columns(link, spot, src.do1, s.doh, 0, 0, [to_heads] * 8, own_heads)
    link.put(src.dza1.at[:, span(1 - c, 512)], group(s.right[0], 2), spot.flipped(c=1), far_ready[0])
    far_left = link.group()
    here, there = pl.ds(4, 2), pl.ds(6, 2)
    link.put(src.left_back.at[here], s.left[1].at[there], spot.flipped(c=1), far_ready[1])
    for n, (dc, dx) in enumerate(FLIPS[1:], 1):
        cols = span(flip(c, dc) * 2 + flip(x, dx), PART)
        link.put(src.du1.at[:, cols], group(s.right[2], 2 * n), spot.flipped(c=dc, x=dx), far_ready[2])
    waves = [0]

    def wave(upto):
        if waves[0] < 1 <= upto:
            link.put(src.left_in.at[here], s.left[2].at[there], spot.flipped(c=1), far_left)
            link.keep(src.left_in.at[first], s.left[2].at[first], left_in)
            link.keep(src.du1.at[:, mine], group(s.right[2], 0), own_ready[2])
            for n in range(GROUPS):
                link.keep(group(src.right_in, 2 * n + 1), group(s.right[2], 2 * n + 1), own_ready[2])
        if waves[0] < 2 <= upto:
            rows = span(c, 512)
            for d in range(2):
                link.put(src.hidden.at[d, rows], s.hidden[d].at[rows], spot.flipped(c=1), far_hidden)
                link.keep(src.hidden.at[d, rows], s.hidden[d].at[rows], hidden_in)
            link.keep(src.dqkv2, s.dqkvh.at[pl.ds(LEN, LEN)], dqkv_in)
            link.keep(w_qkv, s.w_qkv, weight_in)
            link.keep(src.dr1, s.dr1, close_in)
        waves[0] = max(waves[0], upto)

    bits = spec(y=y, a=zl, b=zh)
    across = spec(
        y=spot.flipped(y=1), a=spot.flipped(zl=1), b=spot.flipped(zh=1), x=spot.flipped(x=1), C=spot.flipped(c=1)
    )
    across.update(spec(X=across["x"], s=across["x"]))
    current, landing, copies = {}, {}, {}
    it = iter(s.landing)
    for n, steps in enumerate(PLANS):
        for i, step in enumerate(steps):
            if step[0] in "yabxs":
                landing[n, i] = next(it)
    waiting = [True, True, True]

    def turn(k):
        if k == 2:
            wave(1)
            link.arrive(left_in, far_left)
        else:
            link.arrive(own_ready[k], far_ready[k])
            if k == 1:
                link.arrive(right_in)
        count = s.left[k].shape[0]
        for g in range(count):
            s.turned[k][:, pl.ds(ROWS * g, ROWS)] = s.left[k][g].T

    def compute(n):
        _, k, first, wide = CHUNKS[n]
        if k == 2 and waiting[2]:
            waiting[2] = False
            link.arrive(own_ready[2], far_ready[2])
        path = [stage for stage in PATHS[CHUNKS[n][0]] if stage in "yab"]
        path += [stage for stage in "yab" if stage not in path]

        def piece(i, carry):
            product = dot(s.turned[k][span(i, 256), :], s.right[k][:, pl.ds(first, wide)]).astype(bf16)
            for low in range(2):
                bit = spec(y=low, a=i % 2, b=i // 2)
                at_slab = (bit[path[0]] * 2 + bit[path[1]]) * 2 + bit[path[2]]
                s.chunk[n][at_slab, 0:ROWS] = product[ROWS * low : ROWS * (low + 1)]
            return carry

        lax.fori_loop(0, 4, piece, 0)
        if n == 0:
            link.arrive(vec_in)
            for shard in range(8):
                bit = spec(y=shard % 2, a=shard // 2 % 2, b=shard // 4)
                at_slab = (bit[path[0]] * 2 + bit[path[1]]) * 2 + bit[path[2]]
                vec = s.vec[:, pl.ds(shard * 128, 128)]
                top = jnp.concatenate([vec, jnp.zeros((8, 384), f32)], 1)
                low = jnp.broadcast_to(s.inb[:, pl.ds(shard * 512, 512)], (8, 512))
                s.chunk[n][at_slab, ROWS:VEC] = jnp.concatenate([top, low], 0).astype(bf16)
        current[n] = s.chunk[n]

    def base_of(n):
        _, k, first, _ = CHUNKS[n]
        if k == 0:
            return IN_OUT["attn"] + c * 512 + first, 0
        return IN_OUT["back" if k == 1 else "fore"] + c * 2 * PART + first, PART

    def columns(n, quarter, offset, width):
        start, stride = base_of(n)
        return pl.ds(pl.multiple_of(start + quarter * stride + offset, 128), width)

    def send(n, i):
        stage, slabs, width = PLANS[n][i]
        rows = pl.ds(0, chunk_rows(n))
        now, todo = current[n], []
        if stage in "yab":
            todo.append((now.at[pl.ds((1 - bits[stage]) * slabs, slabs)], landing[n, i]))
        elif stage == "x":
            todo.append((now.at[:, :, pl.ds(pl.multiple_of((1 - x) * width, 128), width)], landing[n, i]))
        elif stage == "s":
            todo.append((now, landing[n, i]))
        elif stage == "Z":
            where = s.out.at[rows, columns(n, x, 0, width)]
            copies[n, i] = link.group()
            for dc, dx in ((1, 1), (0, 1), (1, 0)):
                link.put(where, where, spot.flipped(c=dc, x=dx), copies[n, i])
            return
        else:
            offset = x * (width // 2) if stage == "X" else 0
            width = width // 2 if stage == "X" else width
            where = s.out.at[rows, columns(n, 0, offset, width)]
            todo.append((where, where))
        copies[n, i] = link.group()
        for here, there in todo:
            link.put(here, there, across[stage], copies[n, i])

    def advance(n, i):
        stage, slabs, width = PLANS[n][i]
        link.arrive(copies[n, i])
        if stage not in "yabxs":
            return
        got, old = landing[n, i], current[n]

        def add(m, carry):
            if stage in "yab":
                kept = old[bits[stage] * slabs + m]
            elif stage == "x":
                kept = old[m, :, pl.ds(pl.multiple_of(x * width, 128), width)]
            else:
                kept = old[m]
            got[m] = (got[m].astype(f32) + kept.astype(f32)).astype(bf16)
            return carry

        lax.fori_loop(0, slabs, add, 0)
        current[n] = got
        follow = PLANS[n][i + 1][0]
        if follow in "ZXC":
            offset = x * width if follow == "X" else 0
            s.out[0 : chunk_rows(n), columns(n, x if follow == "Z" else 0, offset, width)] = got[0]

    state = Refs()
    rows_kv, own_kv, rows_q, own_q = link.group(), link.own_group(), link.group(), link.own_group()

    def fold_q(got, old, bit):
        slabs = got.shape[0]

        def add(m, carry):
            got[m] = (got[m].astype(f32) + old[bit * slabs + m].astype(f32)).astype(bf16)
            return carry

        lax.fori_loop(0, slabs, add, 0)

    keeps = x == zl
    came_q = [None] * 3

    def wait_q(group, sem):
        def some(count):
            def wait():
                rows = count * VEC * 128 * 2 // 512
                view = src.lse1.at[pl.ds(0, rows)]
                pltpu.make_async_copy(view, view, sem.at[group.at]).wait()

            return wait

        pl.when(keeps)(some(3))
        pl.when(jnp.logical_not(keeps))(some(4))

    def out_q(part, first, width):
        return s.out.at[:, pl.ds(pl.multiple_of(IN_OUT["qkv"] + part * D + first * 128, 128), width)]

    def form_q(part):
        cols = pl.ds(part * 128, 128)

        def piece(i, carry):
            product = dot(s.turned_h[span(i, 256), :], s.dqkvh[:, cols]).astype(bf16)
            for low in range(2):
                at_slab = (i % 2) * 4 + (i // 2) * 2 + low
                s.chunk_q[part][at_slab, 0:ROWS] = product[ROWS * low : ROWS * (low + 1)]
            return carry

        lax.fori_loop(0, 4, piece, 0)
        extra = jnp.broadcast_to(column_sum(s.dqkvh[:, cols]), (16, 128)).astype(bf16)
        for at_slab in range(8):
            s.chunk_q[part][at_slab, ROWS:VEC] = extra
        came_q[part] = link.put(
            s.chunk_q[part].at[pl.ds((1 - x) * 4, 4)], s.landing_x[part], across["x"], link.group()
        )

    def second_q(part):
        link.arrive(came_q[part])
        fold_q(s.landing_x[part], s.chunk_q[part], x)
        came_q[part] = link.put(
            s.landing_x[part].at[pl.ds((1 - zh) * 2, 2)], s.landing_b[part], across["b"], link.group()
        )

    def deal_q(part):
        link.arrive(came_q[part])
        fold_q(s.landing_b[part], s.landing_x[part], zh)
        group = Group(link.count)
        link.count += 1
        where = out_q(part, spot.place, 128)

        def copy_to(fx, fy):
            y_to = flip(y, fy)
            return pltpu.make_async_remote_copy(
                src_ref=s.landing_b[part].at[y_to], dst_ref=where,
                send_sem=link.send_sem.at[group.at], recv_sem=link.recv_sem.at[group.at],
                device_id={"batch": flip(x, fx) * 2 + c, "blk": zh * 4 + x * 2 + y_to}, device_id_type=MESH,
            )

        for fx, fy in ((1, 1), (1, 0), (0, 1)):
            copy_to(fx, fy).start()
        pl.when(jnp.logical_not(keeps))(copy_to(0, 0).start)

        @pl.when(keeps)
        def _():
            where[...] = s.landing_b[part][y]

        link.last.append(lambda: wait_q(group, link.send_sem))
        came_q[part] = group

    def pass_q(part):
        wait_q(came_q[part], link.recv_sem)
        where = out_q(part, c * 4, 512)
        link.put(where, where, across["C"])

    def task(k):
        if k == 1:
            link.arrive(to_heads, own_heads, heads_in, length_in)
            attention_back_start(s, s.o, s.lse, s.doh)
        if k <= 4:
            attention_back_step(link, spot, PAIR_STEPS[k - 1], s, s.qkv, s.doh, s.dqkvh, rows_kv, own_kv)
        elif k == 5:
            attention_back_end(link, spot, s, s.dqkvh, rows_q, own_q)
        elif k >= 20:
            (form_q, second_q, deal_q, pass_q)[k // 10 - 2]((1, 2, 0)[k % 10])
        elif k == 9:
            link.arrive(rows_kv, own_kv, rows_q, own_q, close_in, weight_in)
            s.grad[...] = (s.dr1[...] + dot_t(s.dqkv[...], s.w_qkv[...])).astype(bf16)
            link.swap(spot, s.grad, grad_out)
        elif k == 10:
            wave(2)
            link.arrive(hidden_in, far_hidden, dqkv_in)
            for d in range(2):
                for g in range(8):
                    rows = pl.ds(g * ROWS, ROWS)
                    s.turned_h[:, pl.ds(d * LEN + g * ROWS, ROWS)] = s.hidden[d][rows, :].T
        elif k in (12, 13, 14):
            turn((0, 2, 1)[k - 12])

    for n, i in ORDER:
        if n == 100:
            task(i)
            continue
        if i < 0:
            compute(n)
            wave(waves[0] + 1)
        else:
            advance(n, i)
        if i + 1 < len(PLANS[n]):
            send(n, i + 1)
    link.finish()


def grad_call(main, w_qkv):
    dma = pltpu.SemaphoreType.DMA
    hbm = pl.BlockSpec(memory_space=pl.ANY)
    return pl.pallas_call(
        grad_kernel,
        out_shape=[jax.ShapeDtypeStruct((VEC, 12 * D), bf16), jax.ShapeDtypeStruct((ROWS, D), bf16)],
        in_specs=[hbm] * (len(MAIN_OUT) + 1),
        out_specs=[pl.BlockSpec(memory_space=pltpu.VMEM), hbm],
        scratch_shapes=[pltpu.VMEM(*entry) for entry in flat(GRAD_SCRATCH)]
        + [dma((SEMS,)), dma((SEMS,)), dma((20,))],
        compiler_params=pltpu.CompilerParams(
            collective_id=2, has_side_effects=True, vmem_limit_bytes=60 * 2**20
        ),
    )(*[getattr(main, name) for name in MAIN_OUT], w_qkv)


def finish_kernel(sums, mixed_in, grad_in, mixed, grad, qkv, attn, fore, back, qv, bias, fore_bias, gain, shift,
                  buf, thin_buf, qkv_buf, attn_buf, fore_buf, back_buf, in_sem, out_sem):
    at = IN_OUT
    pieces = [(at["qkv"] + part * D, D, VEC) for part in range(3)] + [(at["attn"], D, VEC)]
    for n in range(4):
        pieces += [(at["back"] + n * D, D, ROWS), (at["fore"] + n * D, D, ROWS)]
    loads, stores = [], []

    def store(src, dst):
        copy = pltpu.make_async_copy(src, dst, out_sem.at[len(stores)])
        copy.start()
        stores.append(copy)

    for n, (start, width, rows) in enumerate(pieces):
        here = (pl.ds(0, rows), pl.ds(start, width))
        loads.append(pltpu.make_async_copy(sums.at[here], buf.at[here], in_sem.at[n]))
        loads[n].start()
    for n, source in enumerate((mixed_in, grad_in)):
        loads.append(pltpu.make_async_copy(source, thin_buf.at[n], in_sem.at[12 + n]))
        loads[-1].start()
    mine = lax.axis_index("blk")
    for part in range(3):
        loads[part].wait()
        here = pl.ds(part * D, D)
        qkv_buf[:, here] = buf[0:ROWS, pl.ds(at["qkv"] + part * D, D)].astype(f32)
        store(qkv_buf.at[:, here], qkv.at[:, here])
        total = jnp.zeros((16, 128), f32)
        for place in range(8):
            block = buf[ROWS:VEC, pl.ds(at["qkv"] + part * D + place * 128, 128)].astype(f32)
            total = total + jnp.where(mine == place, block, 0.0)
        if part != 1:
            qv[part // 2 : part // 2 + 1, :] = total[0:1, :]
    loads[3].wait()
    attn_buf[...] = buf[0:ROWS, pl.ds(at["attn"], D)].astype(f32)
    store(attn_buf, attn)
    for n in range(4):
        rows = pl.ds(n * D, D)
        loads[4 + 2 * n].wait()
        back_buf[rows, :] = buf[0:ROWS, pl.ds(at["back"] + n * D, D)].astype(f32).T
        store(back_buf.at[rows], back.at[rows])
        loads[5 + 2 * n].wait()
        fore_buf[:, rows] = buf[0:ROWS, pl.ds(at["fore"] + n * D, D)].astype(f32)
        store(fore_buf.at[:, rows], fore.at[:, rows])
    for n, target in enumerate((mixed, grad)):
        loads[12 + n].wait()
        store(thin_buf.at[n], target)
    start = at["attn"]
    small = buf[ROWS:VEC, pl.ds(start, 512)].astype(f32) + buf[ROWS:VEC, pl.ds(start + 512, 512)].astype(f32)
    bias[...] = small[0:2, 0:128]
    gain[...] = small[2:4, 0:128]
    shift[...] = small[4:6, 0:128]
    fore_bias[...] = small[8:9, :]
    for copy in stores:
        copy.wait()


def finish_call(sums, mixed, grad):
    large = [(ROWS, 3 * D), (ROWS, D), (ROWS, FF), (FF, 128)]
    small = [(2, 128), (2, 128), (1, 512), (2, 128), (2, 128)]
    hbm, vmem = pl.BlockSpec(memory_space=pl.ANY), pl.BlockSpec(memory_space=pltpu.VMEM)
    dma = pltpu.SemaphoreType.DMA
    return pl.pallas_call(
        finish_kernel,
        out_shape=[jax.ShapeDtypeStruct((ROWS, D), bf16)] * 2
        + [jax.ShapeDtypeStruct(shape, f32) for shape in large + small],
        in_specs=[hbm] * 3,
        out_specs=[hbm] * 6 + [vmem] * 5,
        scratch_shapes=[pltpu.VMEM((VEC, 12 * D), bf16), pltpu.VMEM((2, ROWS, D), bf16)] + [pltpu.VMEM(shape, f32) for shape in large]
        + [dma((14,)), dma((14,))],
        compiler_params=pltpu.CompilerParams(vmem_limit_bytes=63 * 2**20),
    )(sums, mixed, grad)


def fast_body(tokens, lengths, *rest):
    params, cotangent = rest[:-1], rest[-1]
    main = main_call(lengths, tokens[0], cotangent[0], params)
    sums, grad = grad_call(main, params[0])
    mixed, grad, qkv, attn, fore, back, qv, bias, fore_bias, gain, shift = finish_call(sums, main.mixed, grad)
    return (
        mixed[None], grad[None], qkv, qv, attn, bias, fore, fore_bias.reshape(512), back, gain, shift,
    )


def solution(mesh):
    placed = (
        P("batch", "blk", None),
        P("batch"),
        P(),
        P(),
        P(),
        P(),
        P(),
        P(),
        P(),
        P(),
        P(),
        P("batch", "blk", None),
    )
    fast = dict(mesh.shape) == {"batch": 4, "blk": 8}
    return jax.shard_map(
        fast_body if fast else body,
        mesh=mesh,
        in_specs=placed,
        out_specs=(
            P("batch", "blk", None),
            P("batch", "blk", None),
            P("blk", None),
            P(None, "blk"),
            P("blk", None),
            P(None, "blk"),
            P("blk", None),
            P("blk"),
            P(None, "blk"),
            P(None, "blk"),
            P(None, "blk"),
        ),
        check_vma=False,
    )
```

```python
import math

import jax
import jax.numpy as jnp
from jax import lax
from jax.experimental import pallas as pl
from jax.experimental.pallas import tpu as pltpu
from jax.sharding import PartitionSpec as P

HEADS = 16


eps = 1e-12


def from_partner(x, axis, distance):
    return lax.ppermute(x, axis, [(i, i ^ 1 << distance) for i in range(lax.axis_size(axis))])


def normalize(values, gain, shift):
    centered = values - jnp.mean(values, axis=-1, keepdims=True)
    variance = jnp.mean(centered * centered, axis=-1, keepdims=True)
    return centered * lax.rsqrt(variance + eps) * gain + shift


def gelu_exact(values):
    return jax.nn.gelu(values, approximate=False)


def head_split(matrix, head_count):
    row_count, model_width = matrix.shape
    return matrix.reshape(row_count, head_count // 4, 4, model_width // head_count).transpose(
        1, 2, 0, 3
    )


def head_merge(stacked):
    group_count, group_size, row_count, head_size = stacked.shape
    return stacked.transpose(2, 0, 1, 3).reshape(row_count, group_count * group_size * head_size)


def core_forward(query_part, key_part, value_part, key_valid, scale):
    scores = (
        jnp.einsum("hqd,hkd->hqk", query_part, key_part, preferred_element_type=jnp.float32) * scale
    )
    masked = jnp.where(key_valid, scores, -1e30)
    row_max = jnp.max(masked, axis=-1, keepdims=True)
    exp_scores = jnp.where(key_valid, jnp.exp(masked - row_max), 0.0)
    row_total = jnp.sum(exp_scores, axis=-1, keepdims=True)
    prob_low = (exp_scores / row_total).astype(jnp.bfloat16)
    output = jnp.einsum("hqk,hkd->hqd", prob_low, value_part, preferred_element_type=jnp.float32)
    return (output, (row_max + jnp.log(row_total))[..., 0])


def core_backward(query_part, key_part, value_part, grad_part, log_part, key_valid, scale):
    scores = (
        jnp.einsum("hqd,hkd->hqk", query_part, key_part, preferred_element_type=jnp.float32) * scale
    )
    probs = jnp.where(key_valid, jnp.exp(scores - log_part[..., None]), 0.0)
    grad_probs = jnp.einsum(
        "hqd,hkd->hqk", grad_part, value_part, preferred_element_type=jnp.float32
    )
    inner_sum = jnp.sum(probs * grad_probs, axis=-1, keepdims=True)
    grad_scores = (probs * (grad_probs - inner_sum)).astype(jnp.bfloat16)
    grad_query = (
        jnp.einsum("hqk,hkd->hqd", grad_scores, key_part, preferred_element_type=jnp.float32)
        * scale
    )
    grad_key = (
        jnp.einsum("hqk,hqd->hkd", grad_scores, query_part, preferred_element_type=jnp.float32)
        * scale
    )
    grad_value = jnp.einsum(
        "hqk,hqd->hkd", probs.astype(jnp.bfloat16), grad_part, preferred_element_type=jnp.float32
    )
    return (grad_query, grad_key, grad_value)


def gather_group(kv_pair, position, bit_count):
    buffer_rows = kv_pair
    for step_bit in range(bit_count):
        received = from_partner(buffer_rows, "blk", step_bit)
        high_side = position >> step_bit & 1 == 1
        buffer_rows = jnp.where(
            high_side,
            jnp.concatenate([received, buffer_rows], 0),
            jnp.concatenate([buffer_rows, received], 0),
        )
    return buffer_rows


def spread_group(partials, position, bit_count):
    for step_bit in reversed(range(bit_count)):
        half_rows = partials.shape[0] // 2
        high_side = position >> step_bit & 1 == 1
        lower_part = partials[:half_rows]
        upper_part = partials[half_rows:]
        kept_part = jnp.where(high_side, upper_part, lower_part)
        sent_part = jnp.where(high_side, lower_part, upper_part)
        partials = kept_part + from_partner(sent_part.astype(jnp.bfloat16), "blk", step_bit).astype(
            sent_part.dtype
        )
    return partials


def attend_forward(queries, gathered, key_valid, head_count):
    model_width = queries.shape[1]
    scale = (model_width // head_count) ** (-0.5)
    query_heads = head_split(queries, head_count)
    key_heads = head_split(gathered[:, :model_width], head_count)
    value_heads = head_split(gathered[:, model_width:], head_count)

    def one_group(operands):
        query_part, key_part, value_part = operands
        return core_forward(query_part, key_part, value_part, key_valid, scale)

    outputs, log_sums = lax.map(one_group, (query_heads, key_heads, value_heads))
    return (head_merge(outputs), log_sums)


def attend_backward(queries, gathered, key_valid, log_sums, grad_attended, head_count):
    model_width = queries.shape[1]
    scale = (model_width // head_count) ** (-0.5)
    query_heads = head_split(queries, head_count)
    key_heads = head_split(gathered[:, :model_width], head_count)
    value_heads = head_split(gathered[:, model_width:], head_count)
    grad_heads = head_split(grad_attended, head_count)

    def one_group(operands):
        query_part, key_part, value_part, grad_part, log_part = operands
        return core_backward(
            query_part, key_part, value_part, grad_part, log_part, key_valid, scale
        )

    grad_query, grad_key, grad_value = lax.map(
        one_group, (query_heads, key_heads, value_heads, grad_heads, log_sums)
    )
    return (
        head_merge(grad_query),
        jnp.concatenate([head_merge(grad_key), head_merge(grad_value)], 1),
    )


def layer_forward(hidden, params, key_valid, position, bit_count, head_count):
    w_qkv, qv_bias, w_attn, out_bias, w_in, in_bias, w_back, norm_gain, norm_shift = params
    model_width = hidden.shape[1]
    hidden_low = hidden.astype(jnp.bfloat16)
    bias_row = jnp.concatenate([qv_bias[0], jnp.zeros_like(qv_bias[0]), qv_bias[1]])
    projected = (jnp.dot(hidden_low, w_qkv, preferred_element_type=jnp.float32) + bias_row).astype(
        jnp.bfloat16
    )
    gathered = gather_group(projected[:, model_width:], position, bit_count)
    attended, log_sums = attend_forward(projected[:, :model_width], gathered, key_valid, head_count)
    attended_low = attended.astype(jnp.bfloat16)
    first_sum = (
        hidden + jnp.dot(attended_low, w_attn, preferred_element_type=jnp.float32) + out_bias[0]
    )
    first_norm = normalize(first_sum, norm_gain[0], norm_shift[0])
    first_low = first_norm.astype(jnp.bfloat16)
    inner_pre = jnp.dot(first_low, w_in, preferred_element_type=jnp.float32) + in_bias
    activated = gelu_exact(inner_pre).astype(jnp.bfloat16)
    second_sum = (
        first_norm + jnp.dot(activated, w_back, preferred_element_type=jnp.float32) + out_bias[1]
    )
    output = normalize(second_sum, norm_gain[1], norm_shift[1])
    saved_state = (
        hidden_low,
        projected,
        gathered,
        log_sums,
        attended_low,
        first_sum,
        first_low,
        inner_pre,
        activated,
        second_sum,
    )
    return (output, saved_state)


def layer_backward(grad_output, saved_state, params, key_valid, position, bit_count, head_count):
    w_qkv, qv_bias, w_attn, out_bias, w_in, in_bias, w_back, norm_gain, norm_shift = params
    (
        hidden_low,
        projected,
        gathered,
        log_sums,
        attended_low,
        first_sum,
        first_low,
        inner_pre,
        activated,
        second_sum,
    ) = saved_state
    model_width = hidden_low.shape[1]
    unused_two, pull_two = jax.vjp(normalize, second_sum, norm_gain[1], norm_shift[1])
    grad_second, gain_two, shift_two = pull_two(grad_output)
    grad_branch_two = grad_second.astype(jnp.bfloat16)
    back_grad = jnp.einsum(
        "ra,rb->ab", activated, grad_branch_two, preferred_element_type=jnp.float32
    )
    bias_two = jnp.sum(grad_branch_two.astype(jnp.float32), axis=0)
    grad_act = jnp.dot(grad_branch_two, w_back.T, preferred_element_type=jnp.float32)
    unused_gelu, pull_gelu = jax.vjp(gelu_exact, inner_pre)
    grad_inner = pull_gelu(grad_act)[0].astype(jnp.bfloat16)
    in_grad = jnp.einsum("ra,rb->ab", first_low, grad_inner, preferred_element_type=jnp.float32)
    in_bias_grad = jnp.sum(grad_inner.astype(jnp.float32), axis=0)
    grad_first_norm = grad_second + jnp.dot(grad_inner, w_in.T, preferred_element_type=jnp.float32)
    unused_one, pull_one = jax.vjp(normalize, first_sum, norm_gain[0], norm_shift[0])
    grad_first, gain_one, shift_one = pull_one(grad_first_norm)
    grad_branch = grad_first.astype(jnp.bfloat16)
    attn_grad = jnp.einsum(
        "ra,rb->ab", attended_low, grad_branch, preferred_element_type=jnp.float32
    )
    bias_one = jnp.sum(grad_branch.astype(jnp.float32), axis=0)
    grad_attended = jnp.dot(grad_branch, w_attn.T, preferred_element_type=jnp.float32).astype(
        jnp.bfloat16
    )
    grad_query, grad_pairs = attend_backward(
        projected[:, :model_width], gathered, key_valid, log_sums, grad_attended, head_count
    )
    own_pairs = spread_group(grad_pairs, position, bit_count)
    grad_proj = jnp.concatenate([grad_query, own_pairs], 1).astype(jnp.bfloat16)
    qkv_grad = jnp.einsum("ra,rb->ab", hidden_low, grad_proj, preferred_element_type=jnp.float32)
    column_sums = jnp.sum(grad_proj.astype(jnp.float32), axis=0)
    qv_grad = jnp.stack([column_sums[:model_width], column_sums[2 * model_width :]])
    grad_hidden = grad_first + jnp.dot(grad_proj, w_qkv.T, preferred_element_type=jnp.float32)
    grad_list = (
        qkv_grad,
        qv_grad,
        attn_grad,
        jnp.stack([bias_one, bias_two]),
        in_grad,
        in_bias_grad,
        back_grad,
        jnp.stack([gain_one, gain_two]),
        jnp.stack([shift_one, shift_two]),
    )
    return (grad_hidden, grad_list)


def scatter_once(grad_list):
    (
        qkv_grad,
        qv_grad,
        attn_grad,
        bias_grad,
        in_grad,
        in_bias_grad,
        back_grad,
        gain_grad,
        shift_grad,
    ) = grad_list
    return (
        lax.psum_scatter(qkv_grad, "blk", scatter_dimension=0, tiled=True),
        lax.psum_scatter(qv_grad, "blk", scatter_dimension=1, tiled=True),
        lax.psum_scatter(attn_grad, "blk", scatter_dimension=0, tiled=True),
        lax.psum_scatter(bias_grad, "blk", scatter_dimension=1, tiled=True),
        lax.psum_scatter(in_grad, "blk", scatter_dimension=0, tiled=True),
        lax.psum_scatter(in_bias_grad, "blk", scatter_dimension=0, tiled=True),
        lax.psum_scatter(back_grad, "blk", scatter_dimension=1, tiled=True),
        lax.psum_scatter(gain_grad, "blk", scatter_dimension=1, tiled=True),
        lax.psum_scatter(shift_grad, "blk", scatter_dimension=1, tiled=True),
    )


def body(
    tokens,
    lengths,
    w_qkv,
    qv_bias,
    w_attn,
    out_bias,
    w_in,
    in_bias,
    w_back,
    norm_gain,
    norm_shift,
    cotangent,
):
    row_count = tokens.shape[1]
    head_count = HEADS
    cycle_size = lax.axis_size("blk")
    bit_count = cycle_size.bit_length() - 1
    position = lax.axis_index("blk")
    length = lengths[0]
    key_valid = jnp.arange(cycle_size * row_count) < length
    params = (w_qkv, qv_bias, w_attn, out_bias, w_in, in_bias, w_back, norm_gain, norm_shift)
    out_one, saved_one = layer_forward(
        tokens[0].astype(jnp.float32), params, key_valid, position, bit_count, head_count
    )
    out_two, saved_two = layer_forward(out_one, params, key_valid, position, bit_count, head_count)
    grad_hidden, grads_two = layer_backward(
        cotangent[0].astype(jnp.float32),
        saved_two,
        params,
        key_valid,
        position,
        bit_count,
        head_count,
    )
    grad_hidden, grads_one = layer_backward(
        grad_hidden, saved_one, params, key_valid, position, bit_count, head_count
    )
    shards = scatter_once(jax.tree.map(jnp.add, grads_two, grads_one))
    (
        qkv_part,
        qv_part,
        attn_part,
        bias_part,
        in_part,
        in_bias_part,
        back_part,
        gain_part,
        shift_part,
    ) = shards
    totals = (
        lax.psum(qkv_part.astype(jnp.bfloat16), "batch").astype(jnp.float32),
        lax.psum(qv_part.astype(jnp.bfloat16), "batch").astype(jnp.float32),
        lax.psum(attn_part.astype(jnp.bfloat16), "batch").astype(jnp.float32),
        lax.psum(bias_part.astype(jnp.bfloat16), "batch").astype(jnp.float32),
        lax.psum(in_part.astype(jnp.bfloat16), "batch").astype(jnp.float32),
        lax.psum(in_bias_part.astype(jnp.bfloat16), "batch").astype(jnp.float32),
        lax.psum(back_part.astype(jnp.bfloat16), "batch").astype(jnp.float32),
        lax.psum(gain_part.astype(jnp.bfloat16), "batch").astype(jnp.float32),
        lax.psum(shift_part.astype(jnp.bfloat16), "batch").astype(jnp.float32),
    )
    return (
        out_two.astype(jnp.bfloat16)[None],
        grad_hidden.astype(jnp.bfloat16)[None],
        totals[0],
        totals[1],
        totals[2],
        totals[3],
        totals[4],
        totals[5],
        totals[6],
        totals[7],
        totals[8],
    )


MESH = pl.DeviceIdType.MESH
f32 = jnp.float32
bf16 = jnp.bfloat16
FLIPS = ((0, 0), (1, 0), (0, 1), (1, 1))
GROUPS = len(FLIPS)
PART = 4096 // GROUPS
ROWS, D, FF, LEN, VEC = 128, 1024, 4096, 1024, 144


def dot(a, b):
    return jnp.dot(a, b, preferred_element_type=f32)


def dot_t(a, b):
    return lax.dot_general(a, b, (((1,), (1,)), ((), ())), preferred_element_type=f32)


def dot_0(a, b):
    return lax.dot_general(a, b, (((0,), (0,)), ((), ())), preferred_element_type=f32)


def span(at, size):
    return pl.ds(pl.multiple_of(at * size, size), size)


def flip(bit, by):
    return bit + by * (1 - 2 * bit)


def group(ref, n):
    return ref.at[pl.ds(n * ROWS, ROWS)]


class Spot:
    def __init__(self):
        self.row, self.pos = lax.axis_index("batch"), lax.axis_index("blk")
        self.x, self.c = self.row // 2, self.row % 2
        self.z, self.y = self.pos // 2, self.pos % 2
        self.zl, self.zh = self.z % 2, self.z // 2
        self.place = self.c * 4 + self.zl * 2 + self.y
        self.moved = self.c != self.zh

    def flipped(self, c=0, x=0, y=0, zl=0, zh=0):
        row = flip(self.x, x) * 2 + flip(self.c, c)
        pos = flip(self.zh, zh) * 4 + flip(self.zl, zl) * 2 + flip(self.y, y)
        return {"batch": row, "blk": pos}

    def member(self, place):
        return {"batch": self.x * 2 + place // 4, "blk": self.zh * 4 + place % 4}

    def partner(self):
        return {"batch": self.x * 2 + self.zh, "blk": self.c * 4 + self.pos % 4}


BULK = 2**21


class Group:
    def __init__(self, at):
        self.at, self.bytes, self.waited = at, 0, False


def bytes_of(ref):
    return math.prod(ref.shape) * jnp.dtype(ref.dtype).itemsize


class Link:
    def __init__(self, send_sem, recv_sem, own_sem, *meters):
        self.send_sem, self.recv_sem, self.own_sem, self.meters = send_sem, recv_sem, own_sem, meters
        self.count, self.own_count, self.send_count = 0, 0, 0
        self.sends, self.send_bulk = [], {}
        self.groups, self.own_groups, self.swaps, self.last = [], [], [], []
        self.bulk, self.own_bulk = self.group(), self.own_group()

    def group(self):
        self.groups.append(Group(self.count))
        self.count += 1
        return self.groups[-1]

    def send_slot(self, src):
        size = bytes_of(src)
        limit = BULK if size % 2**15 == 0 else BULK // 4
        bulk = self.send_bulk.get(limit)
        if bulk is None or bulk.bytes + size > limit:
            bulk = self.send_bulk[limit] = Group(self.send_count)
            self.sends.append(bulk)
            self.send_count += 1
        bulk.bytes += size
        return self.send_sem.at[bulk.at]

    def own_group(self):
        self.own_groups.append(Group(self.own_count))
        self.own_count += 1
        return self.own_groups[-1]

    def put(self, src, dst, device, group=None):
        if group is None:
            if self.bulk.bytes + bytes_of(src) > BULK:
                self.bulk = self.group()
            group = self.bulk
        group.bytes += bytes_of(src)
        pltpu.make_async_remote_copy(
            src_ref=src, dst_ref=dst, send_sem=self.send_slot(src), recv_sem=self.recv_sem.at[group.at],
            device_id=device, device_id_type=MESH,
        ).start()
        return group

    def keep(self, src, dst, group=None):
        if group is None:
            if self.own_bulk.bytes + bytes_of(src) > BULK:
                self.own_bulk = self.own_group()
            group = self.own_bulk
        group.bytes += bytes_of(src)
        pltpu.make_async_copy(src, dst, self.own_sem.at[group.at]).start()
        return group

    def wait(self, group, sem):
        if group.bytes:
            for meter in self.meters:
                row = bytes_of(meter) // meter.shape[0]
                tile = 8 if meter.dtype == f32 else 16
                if group.bytes % (tile * row) == 0 and group.bytes <= bytes_of(meter):
                    view = meter.at[pl.ds(0, group.bytes // row)]
                    pltpu.make_async_copy(view, view, sem.at[group.at]).wait()
                    return
            raise ValueError(group.bytes)

    def arrive(self, *groups):
        for group in groups:
            if not group.waited:
                group.waited = True
                self.wait(group, self.own_sem if any(group is own for own in self.own_groups) else self.recv_sem)

    def swap(self, spot, src, dst):
        far = pltpu.make_async_remote_copy(
            src_ref=src, dst_ref=dst, send_sem=self.send_sem.at[self.send_count], recv_sem=self.recv_sem.at[self.count],
            device_id=spot.partner(), device_id_type=MESH,
        )
        near = pltpu.make_async_copy(src, dst, self.own_sem.at[self.own_count])
        self.count += 1
        self.send_count += 1
        self.own_count += 1
        pl.when(spot.moved)(far.start)
        pl.when(jnp.logical_not(spot.moved))(near.start)
        self.swaps.append((spot, far, near))
        return far, near

    def arrive_swap(self, spot, pair):
        pl.when(spot.moved)(pair[0].wait_recv)
        pl.when(jnp.logical_not(spot.moved))(pair[1].wait)
        self.swaps = [(one, far, None if far is pair[0] else near) for one, far, near in self.swaps]

    def finish(self):
        self.arrive(*self.groups, *self.own_groups)
        for group in self.sends:
            self.wait(group, self.send_sem)
        for wait in self.last:
            wait()
        for spot, far, near in self.swaps:
            if near is not None:
                self.arrive_swap(spot, (far, near))
            pl.when(spot.moved)(far.wait_send)


def greet(spot, devices):
    barrier = pltpu.get_barrier_semaphore()
    for device in devices:
        pl.semaphore_signal(barrier, inc=1, device_id=device, device_id_type=MESH)

    @pl.when(spot.moved)
    def _():
        pl.semaphore_signal(barrier, inc=1, device_id=spot.partner(), device_id_type=MESH)

    def meet():
        @pl.when(spot.moved)
        def _():
            pl.semaphore_wait(barrier, len(devices) + 1)

        @pl.when(jnp.logical_not(spot.moved))
        def _():
            pl.semaphore_wait(barrier, len(devices))

    return meet


def standard(values):
    centered = values - jnp.mean(values, axis=-1, keepdims=True)
    inverse = lax.rsqrt(jnp.mean(centered * centered, axis=-1, keepdims=True) + eps)
    return centered * inverse, inverse


def standard_back(unit, inverse, gain, grad):
    scaled = grad * gain
    inner = jnp.mean(scaled * unit, axis=-1, keepdims=True)
    return inverse * (scaled - jnp.mean(scaled, axis=-1, keepdims=True) - unit * inner)


def column_sum(x):
    return jnp.sum(x.astype(f32), axis=0, keepdims=True)


def gelu_pair(u):
    t = 1.0 / (1.0 + 0.23164188 * jnp.abs(u))
    bell = jnp.exp(-0.5 * u * u)
    poly = t * (0.127414796 + t * (-0.142248368 + t * (0.7107068705 + t * (-0.7265760135 + t * 0.5307027145))))
    tail = poly * bell
    cdf = jnp.where(u < 0, tail, 1.0 - tail)
    return u * cdf, cdf + u * bell * 0.3989422804


def low_lanes():
    return lax.broadcasted_iota(jnp.int32, (1, 128), 1) < 64


def valid_keys(length):
    return lax.broadcasted_iota(jnp.int32, (1, LEN), 1).astype(f32) < length


def attention_rows(qkv, rows, valid):
    queries, keys, values = qkv[rows, 0:128], qkv[:, 128:256], qkv[:, 256:384]
    low_half = low_lanes()
    outs, lses = [], []
    for half in range(2):
        mine = low_half if half == 0 else jnp.logical_not(low_half)
        part = jnp.where(mine, queries, jnp.zeros_like(queries)) * jnp.asarray(0.125, bf16)
        scores = jnp.where(valid, dot_t(part, keys), -1e30)
        top = jnp.max(scores, axis=1, keepdims=True)
        expd = jnp.exp(scores - top)
        total = jnp.sum(expd, axis=1, keepdims=True)
        probs = (expd * (1.0 / total)).astype(bf16)
        outs.append(dot(probs, values))
        lses.append(top + jnp.log(total))
    return jnp.where(low_half, outs[0], outs[1]), jnp.where(low_half, lses[0], lses[1])


def attention_back_keys(qkv, grads_ref, lse_rows, delta_rows, rows, first, length):
    low_half = low_lanes()
    keys, values = qkv[rows, 128:256], qkv[rows, 256:384]
    at = lax.broadcasted_iota(jnp.int32, (256, 1), 0) + first
    valid = at.astype(f32) < length
    dqs, dk, dv = [], None, None
    for half in range(2):
        mine = low_half if half == 0 else jnp.logical_not(low_half)
        k_part = jnp.where(mine, keys, jnp.zeros_like(keys)) * jnp.asarray(0.125, bf16)
        v_part = jnp.where(mine, values, jnp.zeros_like(values))
        queries, grads = qkv[:, 0:128], grads_ref[...]
        scores = dot_t(k_part, queries)
        probs = jnp.where(valid, jnp.exp(scores - lse_rows[half : half + 1, :]), 0.0)
        dp = dot_t(v_part, grads)
        ds = (probs * (dp - delta_rows[half : half + 1, :])).astype(bf16)
        dv_part = dot(probs.astype(bf16), grads)
        dk_part = dot(ds, queries)
        dv = dv_part if half == 0 else jnp.where(low_half, dv, dv_part)
        dk = dk_part if half == 0 else jnp.where(low_half, dk, dk_part)
        dqs.append(dot_0(ds, keys))
    return jnp.where(low_half, dqs[0], dqs[1]), (dk * 0.125).astype(bf16), dv.astype(bf16)


def attention_back_start(s, o, lse, grads):
    turned = lse[...].T
    s.lse_rows[0:1, :] = turned[0:1, :]
    s.lse_rows[1:2, :] = turned[64:65, :]
    product = (grads[...].astype(f32) * o[...]).T
    s.delta_rows[0:1, :] = jnp.sum(product[0:64, :], axis=0, keepdims=True)
    s.delta_rows[1:2, :] = jnp.sum(product[64:128, :], axis=0, keepdims=True)


def attention_back_step(link, spot, step, s, qkv, grads, dqkvh, group, own):
    pair = (spot.place // 2 + step) % 4
    rows = span(pair, 256)
    dq, dk, dv = attention_back_keys(
        qkv, grads, s.lse_rows, s.delta_rows, rows, pair * 256, s.length[0:1, 0:1]
    )
    dqkvh[rows, 128:256] = dk
    dqkvh[rows, 256:384] = dv
    s.dq[...] = dq if step == PAIR_STEPS[0] else s.dq[...] + dq
    for part in (1, 2):
        send_rows(link, spot, dqkvh, s.dqkv, step, part, group, own)


def attention_back_end(link, spot, s, dqkvh, group, own):
    dqkvh[0:LEN, 0:128] = (s.dq[...] * 0.125).astype(bf16)
    for step in PAIR_STEPS:
        send_rows(link, spot, dqkvh, s.dqkv, step, 0, group, own)


def send_columns(link, spot, source, target, part, landing, groups, own):
    for step in range(7, -1, -1):
        to = (spot.place + step) % 8
        src = source.at[:, pl.ds(pl.multiple_of(part * D + to * 128, 128), 128)]
        dst = target.at[span(spot.place, ROWS), pl.ds(landing * 128, 128)]
        if step:
            link.put(src, dst, spot.member(to), groups[step])
        else:
            link.keep(src, dst, own)


def pair_rows(spot, step):
    return span((spot.place // 2 + step) % 4, 256)


def send_rows(link, spot, source, target, step, part, group, own):
    same = (spot.place + 2 * step) % 8
    for n, to in enumerate((same, same + 1 - 2 * spot.y)):
        src = source.at[span(to, ROWS), pl.ds(part * 128, 128)]
        dst = target.at[:, pl.ds(pl.multiple_of(part * D + spot.place * 128, 128), 128)]
        if step or n:
            link.put(src, dst, spot.member(to), group)
        else:
            link.keep(src, dst, own)


PAIR_STEPS = (1, 2, 3, 0)


def spec(**named):
    return named


def two(*entry):
    return [entry, entry]


MAIN_OUT = spec(
    mixed=((ROWS, D), bf16), qkv1=((LEN, 384), bf16), lse1=((LEN, 128), f32), o1=((LEN, 128), f32),
    left_attn=((4, ROWS, D), bf16), right_attn=((4 * ROWS, 512), bf16),
    left_back=((2 * GROUPS, ROWS, D), bf16), right_back=((2 * GROUPS * ROWS, PART), bf16),
    left_in=((2 * GROUPS, ROWS, D), bf16), right_in=((2 * GROUPS * ROWS, PART), bf16),
    hidden=((2, LEN, D), bf16), dqkv2=((LEN, 384), bf16),
    du1=((ROWS, FF), bf16), dza1=((ROWS, D), bf16),
    do1=((ROWS, D), bf16), dr1=((ROWS, D), f32), vec=((8, D), f32), inb=((1, FF), f32),
    length=((16, 128), f32),
)
MAIN_SCRATCH = spec(
    w_qkv=((D, 3 * D), bf16), w_attn=((D, D), bf16), w_in=((D, FF), bf16), w_back=((FF, D), bf16),
    tok=((ROWS, D), bf16), cot=((ROWS, D), bf16), length=((16, 128), f32), sent_length=((16, 128), f32),
    proj=two((ROWS, 3 * D), bf16), qkv=two((LEN, 384), bf16), lse=two((LEN, 128), f32),
    o=two((LEN, 128), bf16), full_o=two((LEN, 128), f32), att=two((ROWS, D), bf16), n=two((ROWS, D), bf16),
    act=two((ROWS, FF), bf16), slope=two((ROWS, FF), bf16),
    unit_a=two((ROWS, D), f32), unit_b=two((ROWS, D), f32),
    inv_a=two((ROWS, 128), f32), inv_b=two((ROWS, 128), f32),
    hq2=((ROWS, D), bf16), h=((ROWS, D), f32), acc=((ROWS, D), f32), mixed=((ROWS, D), bf16),
    dzb=two((ROWS, D), bf16), du=two((ROWS, FF), bf16), dza=two((ROWS, D), bf16), do=two((ROWS, D), bf16),
    doh=((LEN, 128), bf16), dqkvh=((LEN, 384), bf16), dq=((LEN, 128), f32), lse_rows=((8, LEN), f32), delta_rows=((8, LEN), f32),
    dqkv=((ROWS, 3 * D), bf16), dr1=((ROWS, D), f32), vec=((8, D), f32), inb=((1, FF), f32),
)


class Refs:
    pass


def flat(entries):
    out = []
    for entry in entries.values():
        out += entry if isinstance(entry, list) else [entry]
    return out


def bind(entries, refs):
    got, it = Refs(), iter(refs)
    for name, entry in entries.items():
        setattr(got, name, [next(it) for _ in entry] if isinstance(entry, list) else next(it))
    return got


def main_kernel(*refs):
    (len_ref, tokens, cotangent, w_qkv, w_attn, w_in, w_back,
     qv_bias, out_bias, in_bias, gain, shift) = refs[:12]
    outs = bind(MAIN_OUT, refs[12 : 12 + len(MAIN_OUT)])
    rest = refs[12 + len(MAIN_OUT) :]
    s = bind(MAIN_SCRATCH, rest[:-4])
    load_sem, send_sem, recv_sem, own_sem = rest[-4:]
    spot = Spot()
    link = Link(send_sem, recv_sem, own_sem, outs.hidden.at[0], outs.lse1)
    others = [spot.member((spot.place + step) % 8) for step in range(1, 8)]
    others += [spot.flipped(x=1), spot.flipped(c=1, x=1)]
    meet = greet(spot, others)

    loads = []
    for n, (src, dst) in enumerate(
        [(w_qkv.at[:, pl.ds(D * part, D)], s.w_qkv.at[:, pl.ds(D * part, D)]) for part in (1, 2, 0)]
        + [(w_attn, s.w_attn), (w_in, s.w_in), (w_back, s.w_back)]
    ):
        loads.append(pltpu.make_async_copy(src, dst, load_sem.at[n]))
        if n < 3:
            loads[n].start()
    loaded = set()

    def need(n):
        if n not in loaded:
            loaded.add(n)
            loads[n].wait()

    s.sent_length[...] = jnp.full((16, 128), len_ref[0], jnp.int32).astype(f32)
    meet()
    first_in = [link.swap(spot, tokens, s.tok), link.swap(spot, s.sent_length, s.length)]
    for n in range(3, 6):
        loads[n].start()
    for pair in first_in:
        link.arrive_swap(spot, pair)
    valid = valid_keys(s.length[0:1, 0:1])

    later = []

    def share(source, left, d):
        link.keep(source, left.at[d])
        link.put(source, left.at[2 + d], spot.flipped(c=1))
        link.put(source, left.at[4 + d], spot.flipped(x=1))

    def deal(source, right, d):
        link.keep(source.at[:, span(spot.c * 2 + spot.x, PART)], group(right, d))
        for n, (dc, dx) in enumerate(FLIPS[1:], 1):
            cols = span(flip(spot.c, dc) * 2 + flip(spot.x, dx), PART)
            link.put(source.at[:, cols], group(right, 2 * n + d), spot.flipped(c=dc, x=dx))

    def gather(hq, d, part):
        rows = pl.ds(part * 64, 64)
        block = outs.hidden.at[d, pl.ds(pl.multiple_of(spot.place * ROWS + part * 64, 64), 64)]
        for dz, dy in ((1, 0), (0, 1), (1, 1)):
            link.put(hq.at[rows], block, spot.flipped(zl=dz, y=dy))
        link.keep(hq.at[rows], block)

    def forward(d, hq, h):
        pair_of = [0, 3, 3, 2, 2, 1, 1, 1]
        both, pairs, own = link.group(), [link.group() for _ in range(4)], link.own_group()
        for part, number in ((1, 0), (2, 1), (0, 2)):
            need(number)

            def tile(i, carry):
                cols = span(2 * part + i, 512)
                value = dot(hq[...], s.w_qkv[:, cols])
                if part != 1:
                    value += qv_bias[part // 2 : part // 2 + 1, span(i, 512)]
                s.proj[d][:, cols] = value.astype(bf16)
                return carry

            lax.fori_loop(0, 2, tile, 0)
            to_groups = [both] * 8 if part else [pairs[pair] for pair in pair_of]
            send_columns(link, spot, s.proj[d], s.qkv[d], part, part, to_groups, own)
        link.arrive(both, own)
        if d == 0:
            later.append(link.swap(spot, cotangent, s.cot))
        to_rows, own_rows = link.group(), link.own_group()
        for step in PAIR_STEPS:
            link.arrive(pairs[step])
            rows = pair_rows(spot, step)
            s.full_o[d][rows, :], s.lse[d][rows, :] = attention_rows(s.qkv[d], rows, valid)
            s.o[d][rows, :] = s.full_o[d][rows, :].astype(bf16)
            send_rows(link, spot, s.o[d], s.att[d], step, 0, to_rows, own_rows)
        if d == 0:
            link.keep(s.qkv[0], outs.qkv1)
            link.keep(s.lse[0], outs.lse1)
            link.keep(s.full_o[0], outs.o1)
        link.arrive(to_rows, own_rows)
        gather(s.tok, 0, d)
        need(3)
        unit, inverse = standard(h[...].astype(f32) + dot(s.att[d][...], s.w_attn[...]) + out_bias[0:1])
        link.keep(s.att[d], outs.left_attn.at[d])
        link.put(s.att[d], outs.left_attn.at[2 + d], spot.flipped(c=1))
        s.unit_a[d][...] = unit
        s.inv_a[d][...] = jnp.broadcast_to(inverse, (ROWS, 128))
        first = unit * gain[0:1] + shift[0:1]
        s.n[d][...] = first.astype(bf16)
        share(s.n[d], outs.left_in, d)
        s.acc[...] = first + out_bias[1:2]
        need(4)
        need(5)

        def inner(i, carry):
            cols = span(i, 512)
            act, slope = gelu_pair(dot(s.n[d][...], s.w_in[:, cols]) + in_bias[:, cols])
            act = act.astype(bf16)
            s.act[d][:, cols] = act
            s.slope[d][:, cols] = slope.astype(bf16)
            s.acc[...] += dot(act, s.w_back[cols, :])
            return carry

        lax.fori_loop(0, 8, inner, 0)
        deal(s.act[d], outs.right_back, d)
        unit, inverse = standard(s.acc[...])
        s.unit_b[d][...] = unit
        s.inv_b[d][...] = jnp.broadcast_to(inverse, (ROWS, 128))
        return unit * gain[1:2] + shift[1:2]

    def add_vec(at, value, fresh):
        s.vec[at : at + 1, :] = value if fresh else s.vec[at : at + 1, :] + value

    def backward(d, grad, fresh):
        unit = s.unit_b[d][...]
        add_vec(3, column_sum(grad * unit), fresh)
        add_vec(5, column_sum(grad), fresh)
        dr = standard_back(unit, s.inv_b[d][:, 0:1], gain[1:2], grad)
        s.acc[...] = dr
        low = dr.astype(bf16)
        s.dzb[d][...] = low
        share(s.dzb[d], outs.left_back, d)
        add_vec(1, column_sum(low), fresh)

        def inner(i, carry):
            cols = span(i, 512)
            du = (dot_t(s.dzb[d][...], s.w_back[cols, :]) * s.slope[d][:, cols].astype(f32)).astype(bf16)
            s.du[d][:, cols] = du
            total = column_sum(du)
            s.inb[:, cols] = total if fresh else s.inb[:, cols] + total
            s.acc[...] += dot_t(du, s.w_in[:, cols])
            return carry

        lax.fori_loop(0, 8, inner, 0)
        if d:
            deal(s.du[d], outs.right_in, d)
        else:
            link.keep(s.du[d], outs.du1)
        grad = s.acc[...]
        unit = s.unit_a[d][...]
        add_vec(2, column_sum(grad * unit), fresh)
        add_vec(4, column_sum(grad), fresh)
        dr = standard_back(unit, s.inv_a[d][:, 0:1], gain[0:1], grad)
        s.dr1[...] = dr
        low = dr.astype(bf16)
        s.dza[d][...] = low
        if d:
            link.keep(s.dza[d].at[:, span(spot.c, 512)], group(outs.right_attn, d))
            link.put(s.dza[d].at[:, span(1 - spot.c, 512)], group(outs.right_attn, 2 + d), spot.flipped(c=1))
        else:
            link.keep(s.dza[d], outs.dza1)
        add_vec(0, column_sum(low), fresh)
        s.do[d][...] = dot_t(low, s.w_attn[...]).astype(bf16)

    out = forward(0, s.tok, s.tok)
    s.h[...] = out
    s.hq2[...] = out.astype(bf16)
    out = forward(1, s.hq2, s.h)
    s.mixed[...] = out.astype(bf16)
    link.swap(spot, s.mixed, outs.mixed)
    link.arrive_swap(spot, later[0])
    gather(s.hq2, 1, 0)
    backward(1, s.cot[...].astype(f32), True)
    to_heads, own_heads = link.group(), link.own_group()
    send_columns(link, spot, s.do[1], s.doh, 0, 0, [to_heads] * 8, own_heads)
    link.arrive(to_heads, own_heads)
    attention_back_start(s, s.full_o[1], s.lse[1], s.doh)
    to_rows, own_rows, last_rows, own_last = link.group(), link.own_group(), link.group(), link.own_group()
    for step in PAIR_STEPS:
        attention_back_step(link, spot, step, s, s.qkv[1], s.doh, s.dqkvh, to_rows, own_rows)
    attention_back_end(link, spot, s, s.dqkvh, last_rows, own_last)
    link.keep(s.dqkvh, outs.dqkv2)
    link.arrive(to_rows, own_rows)
    s.dr1[...] += dot_t(s.dqkv[:, D:], s.w_qkv[:, D:])
    link.arrive(last_rows, own_last)
    gather(s.hq2, 1, 1)
    backward(0, s.dr1[...] + dot_t(s.dqkv[:, :D], s.w_qkv[:, :D]), False)
    link.keep(s.do[0], outs.do1)
    link.keep(s.dr1, outs.dr1)
    small = link.own_group()
    link.keep(s.vec, outs.vec, small)
    link.keep(s.inb, outs.inb, small)
    link.keep(s.length, outs.length, small)
    link.finish()


def main_call(length, tokens, cotangent, params):
    w_qkv, qv_bias, w_attn, out_bias, w_in, in_bias, w_back, gain, shift = params
    dma = pltpu.SemaphoreType.DMA
    vmem, hbm = pl.BlockSpec(memory_space=pltpu.VMEM), pl.BlockSpec(memory_space=pl.ANY)
    results = pl.pallas_call(
        main_kernel,
        out_shape=[jax.ShapeDtypeStruct(*entry) for entry in MAIN_OUT.values()],
        in_specs=[pl.BlockSpec(memory_space=pltpu.SMEM), hbm, hbm] + [hbm] * 4 + [vmem] * 5,
        out_specs=[hbm] * len(MAIN_OUT),
        scratch_shapes=[pltpu.VMEM(*entry) for entry in flat(MAIN_SCRATCH)]
        + [dma((6,)), dma((16,)), dma((32,)), dma((20,))],
        compiler_params=pltpu.CompilerParams(
            collective_id=1, has_side_effects=True, vmem_limit_bytes=60 * 2**20
        ),
    )(length, tokens, cotangent, w_qkv, w_attn, w_in, w_back, qv_bias, out_bias, in_bias[None], gain, shift)
    return bind(MAIN_OUT, results)


PATHS = spec(A="yxabXC", B="xyabXC", C="abysC", F="yabZ", G="aybZ")
CHUNKS = (
    ("B", 0, 0, 512),
    ("F", 1, 0, 128),
    ("F", 1, 128, 128),
    ("F", 1, 256, 256),
    ("G", 1, 512, 256),
    ("F", 1, 768, 256),
    ("F", 2, 0, 256),
    ("F", 2, 256, 256),
    ("F", 2, 512, 256),
    ("F", 2, 768, 128),
    ("F", 2, 896, 128),
)
ORDER = (
    (100, 12), (0, -1), (100, 14), (4, -1), (5, -1), (100, 1), (1, -1), (100, 2), (100, 3), (100, 4),
    (4, 0), (100, 13), (8, -1), (5, 0), (7, -1), (6, -1), (100, 5), (1, 0), (3, -1), (100, 10),
    (5, 1), (100, 20), (100, 22), (4, 1), (1, 1), (100, 21), (0, 0), (5, 2), (2, -1), (100, 30),
    (8, 0), (4, 2), (9, -1), (1, 2), (100, 32), (100, 40), (100, 31), (7, 0), (8, 1), (10, -1),
    (5, 3), (100, 42), (4, 3), (6, 0), (1, 3), (100, 41), (100, 9), (7, 1), (8, 2), (3, 0),
    (6, 1), (8, 3), (0, 1), (7, 2), (2, 0), (3, 1), (9, 0), (6, 2), (7, 3), (100, 50),
    (0, 2), (10, 0), (2, 1), (6, 3), (100, 52), (3, 2), (9, 1), (100, 51), (10, 1), (0, 3),
    (2, 2), (3, 3), (9, 2), (0, 4), (10, 2), (2, 3), (0, 5), (9, 3), (10, 3),
)
IN_OUT = spec(back=0, fore=FF, attn=2 * FF, qkv=2 * FF + D)


def plan(path, width):
    slabs, steps = 8, []
    for stage in path:
        if stage in "yab":
            slabs //= 2
        elif stage == "x":
            width //= 2
        elif stage == "X":
            width *= 2
        steps.append((stage, slabs, width))
    return steps


def chunk_rows(c):
    return VEC if c == 0 else ROWS


SEMS = 24 + sum(len(PATHS[chunk[0]]) for chunk in CHUNKS)
PLANS = [plan(PATHS[chunk[0]], chunk[3]) for chunk in CHUNKS]
GRAD_SCRATCH = spec(
    left=[((4, ROWS, D), bf16)] + two((2 * GROUPS, ROWS, D), bf16),
    right=[((4 * ROWS, 512), bf16)] + two((2 * GROUPS * ROWS, PART), bf16),
    turned=[((D, 512), bf16)] + two((D, 256 * GROUPS), bf16),
    chunk=[((8, chunk_rows(c), CHUNKS[c][3]), bf16) for c in range(len(CHUNKS))],
    landing=[
        ((slabs, chunk_rows(c), width), bf16)
        for c, steps in enumerate(PLANS) for stage, slabs, width in steps if stage in "yabxs"
    ],
    out=((VEC, 12 * D), bf16), hidden=two((LEN, D), bf16), turned_h=((D, 2 * LEN), bf16), dqkvh=((2 * LEN, 384), bf16),
    chunk_q=[((8, VEC, 128), bf16)] * 3, landing_x=[((4, VEC, 128), bf16)] * 3, landing_b=[((2, VEC, 128), bf16)] * 3,
    qkv=((LEN, 384), bf16), lse=((LEN, 128), f32), doh=((LEN, 128), bf16),
    o=((LEN, 128), f32), dq=((LEN, 128), f32), lse_rows=((8, LEN), f32), delta_rows=((8, LEN), f32),
    dqkv=((ROWS, 3 * D), bf16), w_qkv=((D, 3 * D), bf16),
    dr1=((ROWS, D), f32), grad=((ROWS, D), bf16), vec=((8, D), f32), inb=((1, FF), f32), length=((16, 128), f32),
)


def grad_kernel(*refs):
    src = bind(MAIN_OUT, refs[: len(MAIN_OUT)])
    w_qkv, sums, grad_out = refs[len(MAIN_OUT) : len(MAIN_OUT) + 3]
    rest = refs[len(MAIN_OUT) + 3 :]
    s = bind(GRAD_SCRATCH, rest[:-3])
    spot = Spot()
    link = Link(*rest[-3:], src.hidden.at[0], src.lse1, w_qkv)
    x, y, c, zl, zh = spot.x, spot.y, spot.c, spot.zl, spot.zh
    others = [spot.member((spot.place + step) % 8) for step in range(1, 8)]
    others += [spot.flipped(x=1), spot.flipped(c=1, x=1), spot.flipped(zh=1)]
    meet = greet(spot, others)
    mine = span(c * 2 + x, PART)
    heads_in, vec_in, hidden_in, dqkv_in, close_in, left_in, right_in, weight_in = [link.own_group() for _ in range(8)]
    length_in = link.own_group()
    own_ready = [link.own_group() for _ in range(3)]
    for one, other in ((src.o1, s.o), (src.qkv1, s.qkv), (src.lse1, s.lse)):
        link.keep(one, other, heads_in)
    link.keep(src.length, s.length, length_in)
    link.keep(src.left_attn, s.left[0], own_ready[0])
    for n in (1, 3):
        link.keep(group(src.right_attn, n), group(s.right[0], n), own_ready[0])
    link.keep(src.dza1.at[:, span(c, 512)], group(s.right[0], 0), own_ready[0])
    link.keep(src.right_back, s.right[1], right_in)
    first = pl.ds(0, 6)
    link.keep(src.left_back.at[first], s.left[1].at[first], own_ready[1])
    link.keep(src.vec, s.vec, vec_in)
    link.keep(src.inb, s.inb, vec_in)
    meet()
    to_heads, own_heads, far_hidden = link.group(), link.own_group(), link.group()
    far_ready = [link.group() for _ in range(3)]
    send_columns(link, spot, src.do1, s.doh, 0, 0, [to_heads] * 8, own_heads)
    link.put(src.dza1.at[:, span(1 - c, 512)], group(s.right[0], 2), spot.flipped(c=1), far_ready[0])
    far_left = link.group()
    here, there = pl.ds(4, 2), pl.ds(6, 2)
    link.put(src.left_back.at[here], s.left[1].at[there], spot.flipped(c=1), far_ready[1])
    for n, (dc, dx) in enumerate(FLIPS[1:], 1):
        cols = span(flip(c, dc) * 2 + flip(x, dx), PART)
        link.put(src.du1.at[:, cols], group(s.right[2], 2 * n), spot.flipped(c=dc, x=dx), far_ready[2])
    waves = [0]

    def wave(upto):
        if waves[0] < 1 <= upto:
            link.put(src.left_in.at[here], s.left[2].at[there], spot.flipped(c=1), far_left)
            link.keep(src.left_in.at[first], s.left[2].at[first], left_in)
            link.keep(src.du1.at[:, mine], group(s.right[2], 0), own_ready[2])
            for n in range(GROUPS):
                link.keep(group(src.right_in, 2 * n + 1), group(s.right[2], 2 * n + 1), own_ready[2])
        if waves[0] < 2 <= upto:
            rows = span(c, 512)
            for d in range(2):
                link.put(src.hidden.at[d, rows], s.hidden[d].at[rows], spot.flipped(c=1), far_hidden)
                link.keep(src.hidden.at[d, rows], s.hidden[d].at[rows], hidden_in)
            link.keep(src.dqkv2, s.dqkvh.at[pl.ds(LEN, LEN)], dqkv_in)
            link.keep(w_qkv, s.w_qkv, weight_in)
            link.keep(src.dr1, s.dr1, close_in)
        waves[0] = max(waves[0], upto)

    bits = spec(y=y, a=zl, b=zh)
    across = spec(
        y=spot.flipped(y=1), a=spot.flipped(zl=1), b=spot.flipped(zh=1), x=spot.flipped(x=1), C=spot.flipped(c=1)
    )
    across.update(spec(X=across["x"], s=across["x"]))
    current, landing, copies = {}, {}, {}
    it = iter(s.landing)
    for n, steps in enumerate(PLANS):
        for i, step in enumerate(steps):
            if step[0] in "yabxs":
                landing[n, i] = next(it)
    waiting = [True, True, True]

    def turn(k):
        if k == 2:
            wave(1)
            link.arrive(left_in, far_left)
        else:
            link.arrive(own_ready[k], far_ready[k])
            if k == 1:
                link.arrive(right_in)
        count = s.left[k].shape[0]
        for g in range(count):
            s.turned[k][:, pl.ds(ROWS * g, ROWS)] = s.left[k][g].T

    def compute(n):
        _, k, first, wide = CHUNKS[n]
        if k == 2 and waiting[2]:
            waiting[2] = False
            link.arrive(own_ready[2], far_ready[2])
        path = [stage for stage in PATHS[CHUNKS[n][0]] if stage in "yab"]
        path += [stage for stage in "yab" if stage not in path]

        def piece(i, carry):
            product = dot(s.turned[k][span(i, 256), :], s.right[k][:, pl.ds(first, wide)]).astype(bf16)
            for low in range(2):
                bit = spec(y=low, a=i % 2, b=i // 2)
                at_slab = (bit[path[0]] * 2 + bit[path[1]]) * 2 + bit[path[2]]
                s.chunk[n][at_slab, 0:ROWS] = product[ROWS * low : ROWS * (low + 1)]
            return carry

        lax.fori_loop(0, 4, piece, 0)
        if n == 0:
            link.arrive(vec_in)
            for shard in range(8):
                bit = spec(y=shard % 2, a=shard // 2 % 2, b=shard // 4)
                at_slab = (bit[path[0]] * 2 + bit[path[1]]) * 2 + bit[path[2]]
                vec = s.vec[:, pl.ds(shard * 128, 128)]
                top = jnp.concatenate([vec, jnp.zeros((8, 384), f32)], 1)
                low = jnp.broadcast_to(s.inb[:, pl.ds(shard * 512, 512)], (8, 512))
                s.chunk[n][at_slab, ROWS:VEC] = jnp.concatenate([top, low], 0).astype(bf16)
        current[n] = s.chunk[n]

    def base_of(n):
        _, k, first, _ = CHUNKS[n]
        if k == 0:
            return IN_OUT["attn"] + c * 512 + first, 0
        return IN_OUT["back" if k == 1 else "fore"] + c * 2 * PART + first, PART

    def columns(n, quarter, offset, width):
        start, stride = base_of(n)
        return pl.ds(pl.multiple_of(start + quarter * stride + offset, 128), width)

    def send(n, i):
        stage, slabs, width = PLANS[n][i]
        rows = pl.ds(0, chunk_rows(n))
        now, todo = current[n], []
        if stage in "yab":
            todo.append((now.at[pl.ds((1 - bits[stage]) * slabs, slabs)], landing[n, i]))
        elif stage == "x":
            todo.append((now.at[:, :, pl.ds(pl.multiple_of((1 - x) * width, 128), width)], landing[n, i]))
        elif stage == "s":
            todo.append((now, landing[n, i]))
        elif stage == "Z":
            where = s.out.at[rows, columns(n, x, 0, width)]
            copies[n, i] = link.group()
            for dc, dx in ((1, 1), (0, 1), (1, 0)):
                link.put(where, where, spot.flipped(c=dc, x=dx), copies[n, i])
            return
        else:
            offset = x * (width // 2) if stage == "X" else 0
            width = width // 2 if stage == "X" else width
            where = s.out.at[rows, columns(n, 0, offset, width)]
            todo.append((where, where))
        copies[n, i] = link.group()
        for here, there in todo:
            link.put(here, there, across[stage], copies[n, i])

    def store(rows, start, width):
        here = (pl.ds(0, rows), pl.ds(start, width))
        link.keep(s.out.at[here], sums.at[here])

    def flush(n):
        _, k, first, wide = CHUNKS[n]
        if k == 0:
            store(VEC, IN_OUT["attn"], D)
        else:
            for quarter in range(4):
                store(ROWS, IN_OUT["back" if k == 1 else "fore"] + quarter * PART + first, wide)

    def advance(n, i):
        stage, slabs, width = PLANS[n][i]
        link.arrive(copies[n, i])
        if stage in "ZC":
            flush(n)
        if stage not in "yabxs":
            return
        got, old = landing[n, i], current[n]

        def add(m, carry):
            if stage in "yab":
                kept = old[bits[stage] * slabs + m]
            elif stage == "x":
                kept = old[m, :, pl.ds(pl.multiple_of(x * width, 128), width)]
            else:
                kept = old[m]
            got[m] = (got[m].astype(f32) + kept.astype(f32)).astype(bf16)
            return carry

        lax.fori_loop(0, slabs, add, 0)
        current[n] = got
        follow = PLANS[n][i + 1][0]
        if follow in "ZXC":
            offset = x * width if follow == "X" else 0
            s.out[0 : chunk_rows(n), columns(n, x if follow == "Z" else 0, offset, width)] = got[0]

    state = Refs()
    rows_kv, own_kv, rows_q, own_q = link.group(), link.own_group(), link.group(), link.own_group()

    def fold_q(got, old, bit):
        slabs = got.shape[0]

        def add(m, carry):
            got[m] = (got[m].astype(f32) + old[bit * slabs + m].astype(f32)).astype(bf16)
            return carry

        lax.fori_loop(0, slabs, add, 0)

    keeps = x == zl
    came_q, passed = [None] * 3, [None] * 3

    def wait_q(group, sem):
        def some(count):
            def wait():
                rows = count * VEC * 128 * 2 // 512
                view = src.lse1.at[pl.ds(0, rows)]
                pltpu.make_async_copy(view, view, sem.at[group.at]).wait()

            return wait

        pl.when(keeps)(some(3))
        pl.when(jnp.logical_not(keeps))(some(4))

    def out_q(part, first, width):
        return s.out.at[:, pl.ds(pl.multiple_of(IN_OUT["qkv"] + part * D + first * 128, 128), width)]

    def form_q(part):
        cols = pl.ds(part * 128, 128)

        def piece(i, carry):
            product = dot(s.turned_h[span(i, 256), :], s.dqkvh[:, cols]).astype(bf16)
            for low in range(2):
                at_slab = (i % 2) * 4 + (i // 2) * 2 + low
                s.chunk_q[part][at_slab, 0:ROWS] = product[ROWS * low : ROWS * (low + 1)]
            return carry

        lax.fori_loop(0, 4, piece, 0)
        extra = jnp.broadcast_to(column_sum(s.dqkvh[:, cols]), (16, 128)).astype(bf16)
        for at_slab in range(8):
            s.chunk_q[part][at_slab, ROWS:VEC] = extra
        came_q[part] = link.put(
            s.chunk_q[part].at[pl.ds((1 - x) * 4, 4)], s.landing_x[part], across["x"], link.group()
        )

    def second_q(part):
        link.arrive(came_q[part])
        fold_q(s.landing_x[part], s.chunk_q[part], x)
        came_q[part] = link.put(
            s.landing_x[part].at[pl.ds((1 - zh) * 2, 2)], s.landing_b[part], across["b"], link.group()
        )

    def deal_q(part):
        link.arrive(came_q[part])
        fold_q(s.landing_b[part], s.landing_x[part], zh)
        group, sent = Group(link.count), Group(link.send_count)
        link.count += 1
        link.send_count += 1
        where = out_q(part, spot.place, 128)

        def copy_to(fx, fy):
            y_to = flip(y, fy)
            return pltpu.make_async_remote_copy(
                src_ref=s.landing_b[part].at[y_to], dst_ref=where,
                send_sem=link.send_sem.at[sent.at], recv_sem=link.recv_sem.at[group.at],
                device_id={"batch": flip(x, fx) * 2 + c, "blk": zh * 4 + x * 2 + y_to}, device_id_type=MESH,
            )

        for fx, fy in ((1, 1), (1, 0), (0, 1)):
            copy_to(fx, fy).start()
        pl.when(jnp.logical_not(keeps))(copy_to(0, 0).start)

        @pl.when(keeps)
        def _():
            where[...] = s.landing_b[part][y]

        link.last.append(lambda: wait_q(sent, link.send_sem))
        came_q[part] = group

    def pass_q(part):
        wait_q(came_q[part], link.recv_sem)
        where = out_q(part, c * 4, 512)
        passed[part] = link.put(where, where, across["C"], link.group())

    def task(k):
        if k == 1:
            link.arrive(to_heads, own_heads, heads_in, length_in)
            attention_back_start(s, s.o, s.lse, s.doh)
        if k <= 4:
            attention_back_step(link, spot, PAIR_STEPS[k - 1], s, s.qkv, s.doh, s.dqkvh, rows_kv, own_kv)
        elif k == 5:
            attention_back_end(link, spot, s, s.dqkvh, rows_q, own_q)
        elif k >= 20:
            (form_q, second_q, deal_q, pass_q)[k // 10 - 2]((1, 2, 0)[k % 10])
        elif k == 9:
            link.arrive(rows_kv, own_kv, rows_q, own_q, close_in, weight_in)
            s.grad[...] = (s.dr1[...] + dot_t(s.dqkv[...], s.w_qkv[...])).astype(bf16)
            link.swap(spot, s.grad, grad_out)
        elif k == 10:
            wave(2)
            link.arrive(hidden_in, far_hidden, dqkv_in)
            for d in range(2):
                for g in range(8):
                    rows = pl.ds(g * ROWS, ROWS)
                    s.turned_h[:, pl.ds(d * LEN + g * ROWS, ROWS)] = s.hidden[d][rows, :].T
        elif k in (12, 13, 14):
            turn((0, 2, 1)[k - 12])

    for n, i in ORDER:
        if n == 100:
            task(i)
            continue
        if i < 0:
            compute(n)
            wave(waves[0] + 1)
        else:
            advance(n, i)
        if i + 1 < len(PLANS[n]):
            send(n, i + 1)
    for part in (1, 2, 0):
        link.arrive(passed[part])
        store(VEC, IN_OUT["qkv"] + part * D, D)
    link.finish()


def grad_call(main, w_qkv):
    dma = pltpu.SemaphoreType.DMA
    hbm = pl.BlockSpec(memory_space=pl.ANY)
    return pl.pallas_call(
        grad_kernel,
        out_shape=[jax.ShapeDtypeStruct((VEC, 12 * D), bf16), jax.ShapeDtypeStruct((ROWS, D), bf16)],
        in_specs=[hbm] * (len(MAIN_OUT) + 1),
        out_specs=[hbm, hbm],
        scratch_shapes=[pltpu.VMEM(*entry) for entry in flat(GRAD_SCRATCH)]
        + [dma((24,)), dma((SEMS,)), dma((24,))],
        compiler_params=pltpu.CompilerParams(
            collective_id=2, has_side_effects=True, vmem_limit_bytes=60 * 2**20
        ),
    )(*[getattr(main, name) for name in MAIN_OUT], w_qkv)


def finish_kernel(sums, mixed_in, grad_in, mixed, grad, qkv, attn, fore, back, qv, bias, fore_bias, gain, shift,
                  buf, thin_buf, qkv_buf, attn_buf, fore_buf, back_buf, in_sem, out_sem):
    at = IN_OUT
    pieces = [(at["qkv"] + part * D, D, VEC) for part in range(3)] + [(at["attn"], D, VEC)]
    for n in range(4):
        pieces += [(at["back"] + n * D, D, ROWS), (at["fore"] + n * D, D, ROWS)]
    loads, stores = [], []

    def store(src, dst):
        copy = pltpu.make_async_copy(src, dst, out_sem.at[len(stores)])
        copy.start()
        stores.append(copy)

    for n, (start, width, rows) in enumerate(pieces):
        here = (pl.ds(0, rows), pl.ds(start, width))
        loads.append(pltpu.make_async_copy(sums.at[here], buf.at[here], in_sem.at[n]))
        loads[n].start()
    for n, source in enumerate((mixed_in, grad_in)):
        loads.append(pltpu.make_async_copy(source, thin_buf.at[n], in_sem.at[12 + n]))
        loads[-1].start()
    mine = lax.axis_index("blk")
    for part in range(3):
        loads[part].wait()
        here = pl.ds(part * D, D)
        qkv_buf[:, here] = buf[0:ROWS, pl.ds(at["qkv"] + part * D, D)].astype(f32)
        store(qkv_buf.at[:, here], qkv.at[:, here])
        total = jnp.zeros((16, 128), f32)
        for place in range(8):
            block = buf[ROWS:VEC, pl.ds(at["qkv"] + part * D + place * 128, 128)].astype(f32)
            total = total + jnp.where(mine == place, block, 0.0)
        if part != 1:
            qv[part // 2 : part // 2 + 1, :] = total[0:1, :]
    loads[3].wait()
    attn_buf[...] = buf[0:ROWS, pl.ds(at["attn"], D)].astype(f32)
    store(attn_buf, attn)
    for n in range(4):
        rows = pl.ds(n * D, D)
        loads[4 + 2 * n].wait()
        back_buf[rows, :] = buf[0:ROWS, pl.ds(at["back"] + n * D, D)].astype(f32).T
        store(back_buf.at[rows], back.at[rows])
        loads[5 + 2 * n].wait()
        fore_buf[:, rows] = buf[0:ROWS, pl.ds(at["fore"] + n * D, D)].astype(f32)
        store(fore_buf.at[:, rows], fore.at[:, rows])
    for n, target in enumerate((mixed, grad)):
        loads[12 + n].wait()
        store(thin_buf.at[n], target)
    start = at["attn"]
    small = buf[ROWS:VEC, pl.ds(start, 512)].astype(f32) + buf[ROWS:VEC, pl.ds(start + 512, 512)].astype(f32)
    bias[...] = small[0:2, 0:128]
    gain[...] = small[2:4, 0:128]
    shift[...] = small[4:6, 0:128]
    fore_bias[...] = small[8:9, :]
    for copy in stores:
        copy.wait()


def finish_call(sums, mixed, grad):
    large = [(ROWS, 3 * D), (ROWS, D), (ROWS, FF), (FF, 128)]
    small = [(2, 128), (2, 128), (1, 512), (2, 128), (2, 128)]
    hbm, vmem = pl.BlockSpec(memory_space=pl.ANY), pl.BlockSpec(memory_space=pltpu.VMEM)
    dma = pltpu.SemaphoreType.DMA
    return pl.pallas_call(
        finish_kernel,
        out_shape=[jax.ShapeDtypeStruct((ROWS, D), bf16)] * 2
        + [jax.ShapeDtypeStruct(shape, f32) for shape in large + small],
        in_specs=[hbm] * 3,
        out_specs=[hbm] * 6 + [vmem] * 5,
        scratch_shapes=[pltpu.VMEM((VEC, 12 * D), bf16), pltpu.VMEM((2, ROWS, D), bf16)] + [pltpu.VMEM(shape, f32) for shape in large]
        + [dma((14,)), dma((14,))],
        compiler_params=pltpu.CompilerParams(vmem_limit_bytes=63 * 2**20),
    )(sums, mixed, grad)


def fast_body(tokens, lengths, *rest):
    params, cotangent = rest[:-1], rest[-1]
    main = main_call(lengths, tokens[0], cotangent[0], params)
    sums, grad = grad_call(main, params[0])
    mixed, grad, qkv, attn, fore, back, qv, bias, fore_bias, gain, shift = finish_call(sums, main.mixed, grad)
    return (
        mixed[None], grad[None], qkv, qv, attn, bias, fore, fore_bias.reshape(512), back, gain, shift,
    )


def solution(mesh):
    placed = (
        P("batch", "blk", None),
        P("batch"),
        P(),
        P(),
        P(),
        P(),
        P(),
        P(),
        P(),
        P(),
        P(),
        P("batch", "blk", None),
    )
    fast = dict(mesh.shape) == {"batch": 4, "blk": 8}
    return jax.shard_map(
        fast_body if fast else body,
        mesh=mesh,
        in_specs=placed,
        out_specs=(
            P("batch", "blk", None),
            P("batch", "blk", None),
            P("blk", None),
            P(None, "blk"),
            P("blk", None),
            P(None, "blk"),
            P("blk", None),
            P("blk"),
            P(None, "blk"),
            P(None, "blk"),
            P(None, "blk"),
        ),
        check_vma=False,
    )
```

```python
import math

import jax
import jax.numpy as jnp
from jax import lax
from jax.experimental import pallas as pl
from jax.experimental.pallas import tpu as pltpu
from jax.sharding import PartitionSpec as P

HEADS = 16


eps = 1e-12


def from_partner(x, axis, distance):
    return lax.ppermute(x, axis, [(i, i ^ 1 << distance) for i in range(lax.axis_size(axis))])


def normalize(values, gain, shift):
    centered = values - jnp.mean(values, axis=-1, keepdims=True)
    variance = jnp.mean(centered * centered, axis=-1, keepdims=True)
    return centered * lax.rsqrt(variance + eps) * gain + shift


def gelu_exact(values):
    return jax.nn.gelu(values, approximate=False)


def head_split(matrix, head_count):
    row_count, model_width = matrix.shape
    return matrix.reshape(row_count, head_count // 4, 4, model_width // head_count).transpose(
        1, 2, 0, 3
    )


def head_merge(stacked):
    group_count, group_size, row_count, head_size = stacked.shape
    return stacked.transpose(2, 0, 1, 3).reshape(row_count, group_count * group_size * head_size)


def core_forward(query_part, key_part, value_part, key_valid, scale):
    scores = (
        jnp.einsum("hqd,hkd->hqk", query_part, key_part, preferred_element_type=jnp.float32) * scale
    )
    masked = jnp.where(key_valid, scores, -1e30)
    row_max = jnp.max(masked, axis=-1, keepdims=True)
    exp_scores = jnp.where(key_valid, jnp.exp(masked - row_max), 0.0)
    row_total = jnp.sum(exp_scores, axis=-1, keepdims=True)
    prob_low = (exp_scores / row_total).astype(jnp.bfloat16)
    output = jnp.einsum("hqk,hkd->hqd", prob_low, value_part, preferred_element_type=jnp.float32)
    return (output, (row_max + jnp.log(row_total))[..., 0])


def core_backward(query_part, key_part, value_part, grad_part, log_part, key_valid, scale):
    scores = (
        jnp.einsum("hqd,hkd->hqk", query_part, key_part, preferred_element_type=jnp.float32) * scale
    )
    probs = jnp.where(key_valid, jnp.exp(scores - log_part[..., None]), 0.0)
    grad_probs = jnp.einsum(
        "hqd,hkd->hqk", grad_part, value_part, preferred_element_type=jnp.float32
    )
    inner_sum = jnp.sum(probs * grad_probs, axis=-1, keepdims=True)
    grad_scores = (probs * (grad_probs - inner_sum)).astype(jnp.bfloat16)
    grad_query = (
        jnp.einsum("hqk,hkd->hqd", grad_scores, key_part, preferred_element_type=jnp.float32)
        * scale
    )
    grad_key = (
        jnp.einsum("hqk,hqd->hkd", grad_scores, query_part, preferred_element_type=jnp.float32)
        * scale
    )
    grad_value = jnp.einsum(
        "hqk,hqd->hkd", probs.astype(jnp.bfloat16), grad_part, preferred_element_type=jnp.float32
    )
    return (grad_query, grad_key, grad_value)


def gather_group(kv_pair, position, bit_count):
    buffer_rows = kv_pair
    for step_bit in range(bit_count):
        received = from_partner(buffer_rows, "blk", step_bit)
        high_side = position >> step_bit & 1 == 1
        buffer_rows = jnp.where(
            high_side,
            jnp.concatenate([received, buffer_rows], 0),
            jnp.concatenate([buffer_rows, received], 0),
        )
    return buffer_rows


def spread_group(partials, position, bit_count):
    for step_bit in reversed(range(bit_count)):
        half_rows = partials.shape[0] // 2
        high_side = position >> step_bit & 1 == 1
        lower_part = partials[:half_rows]
        upper_part = partials[half_rows:]
        kept_part = jnp.where(high_side, upper_part, lower_part)
        sent_part = jnp.where(high_side, lower_part, upper_part)
        partials = kept_part + from_partner(sent_part.astype(jnp.bfloat16), "blk", step_bit).astype(
            sent_part.dtype
        )
    return partials


def attend_forward(queries, gathered, key_valid, head_count):
    model_width = queries.shape[1]
    scale = (model_width // head_count) ** (-0.5)
    query_heads = head_split(queries, head_count)
    key_heads = head_split(gathered[:, :model_width], head_count)
    value_heads = head_split(gathered[:, model_width:], head_count)

    def one_group(operands):
        query_part, key_part, value_part = operands
        return core_forward(query_part, key_part, value_part, key_valid, scale)

    outputs, log_sums = lax.map(one_group, (query_heads, key_heads, value_heads))
    return (head_merge(outputs), log_sums)


def attend_backward(queries, gathered, key_valid, log_sums, grad_attended, head_count):
    model_width = queries.shape[1]
    scale = (model_width // head_count) ** (-0.5)
    query_heads = head_split(queries, head_count)
    key_heads = head_split(gathered[:, :model_width], head_count)
    value_heads = head_split(gathered[:, model_width:], head_count)
    grad_heads = head_split(grad_attended, head_count)

    def one_group(operands):
        query_part, key_part, value_part, grad_part, log_part = operands
        return core_backward(
            query_part, key_part, value_part, grad_part, log_part, key_valid, scale
        )

    grad_query, grad_key, grad_value = lax.map(
        one_group, (query_heads, key_heads, value_heads, grad_heads, log_sums)
    )
    return (
        head_merge(grad_query),
        jnp.concatenate([head_merge(grad_key), head_merge(grad_value)], 1),
    )


def layer_forward(hidden, params, key_valid, position, bit_count, head_count):
    w_qkv, qv_bias, w_attn, out_bias, w_in, in_bias, w_back, norm_gain, norm_shift = params
    model_width = hidden.shape[1]
    hidden_low = hidden.astype(jnp.bfloat16)
    bias_row = jnp.concatenate([qv_bias[0], jnp.zeros_like(qv_bias[0]), qv_bias[1]])
    projected = (jnp.dot(hidden_low, w_qkv, preferred_element_type=jnp.float32) + bias_row).astype(
        jnp.bfloat16
    )
    gathered = gather_group(projected[:, model_width:], position, bit_count)
    attended, log_sums = attend_forward(projected[:, :model_width], gathered, key_valid, head_count)
    attended_low = attended.astype(jnp.bfloat16)
    first_sum = (
        hidden + jnp.dot(attended_low, w_attn, preferred_element_type=jnp.float32) + out_bias[0]
    )
    first_norm = normalize(first_sum, norm_gain[0], norm_shift[0])
    first_low = first_norm.astype(jnp.bfloat16)
    inner_pre = jnp.dot(first_low, w_in, preferred_element_type=jnp.float32) + in_bias
    activated = gelu_exact(inner_pre).astype(jnp.bfloat16)
    second_sum = (
        first_norm + jnp.dot(activated, w_back, preferred_element_type=jnp.float32) + out_bias[1]
    )
    output = normalize(second_sum, norm_gain[1], norm_shift[1])
    saved_state = (
        hidden_low,
        projected,
        gathered,
        log_sums,
        attended_low,
        first_sum,
        first_low,
        inner_pre,
        activated,
        second_sum,
    )
    return (output, saved_state)


def layer_backward(grad_output, saved_state, params, key_valid, position, bit_count, head_count):
    w_qkv, qv_bias, w_attn, out_bias, w_in, in_bias, w_back, norm_gain, norm_shift = params
    (
        hidden_low,
        projected,
        gathered,
        log_sums,
        attended_low,
        first_sum,
        first_low,
        inner_pre,
        activated,
        second_sum,
    ) = saved_state
    model_width = hidden_low.shape[1]
    unused_two, pull_two = jax.vjp(normalize, second_sum, norm_gain[1], norm_shift[1])
    grad_second, gain_two, shift_two = pull_two(grad_output)
    grad_branch_two = grad_second.astype(jnp.bfloat16)
    back_grad = jnp.einsum(
        "ra,rb->ab", activated, grad_branch_two, preferred_element_type=jnp.float32
    )
    bias_two = jnp.sum(grad_branch_two.astype(jnp.float32), axis=0)
    grad_act = jnp.dot(grad_branch_two, w_back.T, preferred_element_type=jnp.float32)
    unused_gelu, pull_gelu = jax.vjp(gelu_exact, inner_pre)
    grad_inner = pull_gelu(grad_act)[0].astype(jnp.bfloat16)
    in_grad = jnp.einsum("ra,rb->ab", first_low, grad_inner, preferred_element_type=jnp.float32)
    in_bias_grad = jnp.sum(grad_inner.astype(jnp.float32), axis=0)
    grad_first_norm = grad_second + jnp.dot(grad_inner, w_in.T, preferred_element_type=jnp.float32)
    unused_one, pull_one = jax.vjp(normalize, first_sum, norm_gain[0], norm_shift[0])
    grad_first, gain_one, shift_one = pull_one(grad_first_norm)
    grad_branch = grad_first.astype(jnp.bfloat16)
    attn_grad = jnp.einsum(
        "ra,rb->ab", attended_low, grad_branch, preferred_element_type=jnp.float32
    )
    bias_one = jnp.sum(grad_branch.astype(jnp.float32), axis=0)
    grad_attended = jnp.dot(grad_branch, w_attn.T, preferred_element_type=jnp.float32).astype(
        jnp.bfloat16
    )
    grad_query, grad_pairs = attend_backward(
        projected[:, :model_width], gathered, key_valid, log_sums, grad_attended, head_count
    )
    own_pairs = spread_group(grad_pairs, position, bit_count)
    grad_proj = jnp.concatenate([grad_query, own_pairs], 1).astype(jnp.bfloat16)
    qkv_grad = jnp.einsum("ra,rb->ab", hidden_low, grad_proj, preferred_element_type=jnp.float32)
    column_sums = jnp.sum(grad_proj.astype(jnp.float32), axis=0)
    qv_grad = jnp.stack([column_sums[:model_width], column_sums[2 * model_width :]])
    grad_hidden = grad_first + jnp.dot(grad_proj, w_qkv.T, preferred_element_type=jnp.float32)
    grad_list = (
        qkv_grad,
        qv_grad,
        attn_grad,
        jnp.stack([bias_one, bias_two]),
        in_grad,
        in_bias_grad,
        back_grad,
        jnp.stack([gain_one, gain_two]),
        jnp.stack([shift_one, shift_two]),
    )
    return (grad_hidden, grad_list)


def scatter_once(grad_list):
    (
        qkv_grad,
        qv_grad,
        attn_grad,
        bias_grad,
        in_grad,
        in_bias_grad,
        back_grad,
        gain_grad,
        shift_grad,
    ) = grad_list
    return (
        lax.psum_scatter(qkv_grad, "blk", scatter_dimension=0, tiled=True),
        lax.psum_scatter(qv_grad, "blk", scatter_dimension=1, tiled=True),
        lax.psum_scatter(attn_grad, "blk", scatter_dimension=0, tiled=True),
        lax.psum_scatter(bias_grad, "blk", scatter_dimension=1, tiled=True),
        lax.psum_scatter(in_grad, "blk", scatter_dimension=0, tiled=True),
        lax.psum_scatter(in_bias_grad, "blk", scatter_dimension=0, tiled=True),
        lax.psum_scatter(back_grad, "blk", scatter_dimension=1, tiled=True),
        lax.psum_scatter(gain_grad, "blk", scatter_dimension=1, tiled=True),
        lax.psum_scatter(shift_grad, "blk", scatter_dimension=1, tiled=True),
    )


def body(
    tokens,
    lengths,
    w_qkv,
    qv_bias,
    w_attn,
    out_bias,
    w_in,
    in_bias,
    w_back,
    norm_gain,
    norm_shift,
    cotangent,
):
    row_count = tokens.shape[1]
    head_count = HEADS
    cycle_size = lax.axis_size("blk")
    bit_count = cycle_size.bit_length() - 1
    position = lax.axis_index("blk")
    length = lengths[0]
    key_valid = jnp.arange(cycle_size * row_count) < length
    params = (w_qkv, qv_bias, w_attn, out_bias, w_in, in_bias, w_back, norm_gain, norm_shift)
    out_one, saved_one = layer_forward(
        tokens[0].astype(jnp.float32), params, key_valid, position, bit_count, head_count
    )
    out_two, saved_two = layer_forward(out_one, params, key_valid, position, bit_count, head_count)
    grad_hidden, grads_two = layer_backward(
        cotangent[0].astype(jnp.float32),
        saved_two,
        params,
        key_valid,
        position,
        bit_count,
        head_count,
    )
    grad_hidden, grads_one = layer_backward(
        grad_hidden, saved_one, params, key_valid, position, bit_count, head_count
    )
    shards = scatter_once(jax.tree.map(jnp.add, grads_two, grads_one))
    (
        qkv_part,
        qv_part,
        attn_part,
        bias_part,
        in_part,
        in_bias_part,
        back_part,
        gain_part,
        shift_part,
    ) = shards
    totals = (
        lax.psum(qkv_part.astype(jnp.bfloat16), "batch").astype(jnp.float32),
        lax.psum(qv_part.astype(jnp.bfloat16), "batch").astype(jnp.float32),
        lax.psum(attn_part.astype(jnp.bfloat16), "batch").astype(jnp.float32),
        lax.psum(bias_part.astype(jnp.bfloat16), "batch").astype(jnp.float32),
        lax.psum(in_part.astype(jnp.bfloat16), "batch").astype(jnp.float32),
        lax.psum(in_bias_part.astype(jnp.bfloat16), "batch").astype(jnp.float32),
        lax.psum(back_part.astype(jnp.bfloat16), "batch").astype(jnp.float32),
        lax.psum(gain_part.astype(jnp.bfloat16), "batch").astype(jnp.float32),
        lax.psum(shift_part.astype(jnp.bfloat16), "batch").astype(jnp.float32),
    )
    return (
        out_two.astype(jnp.bfloat16)[None],
        grad_hidden.astype(jnp.bfloat16)[None],
        totals[0],
        totals[1],
        totals[2],
        totals[3],
        totals[4],
        totals[5],
        totals[6],
        totals[7],
        totals[8],
    )


MESH = pl.DeviceIdType.MESH
f32 = jnp.float32
bf16 = jnp.bfloat16
FLIPS = ((0, 0), (1, 0), (0, 1), (1, 1))
GROUPS = len(FLIPS)
PART = 4096 // GROUPS
ROWS, D, FF, LEN, VEC = 128, 1024, 4096, 1024, 144


def dot(a, b):
    return jnp.dot(a, b, preferred_element_type=f32)


def dot_t(a, b):
    return lax.dot_general(a, b, (((1,), (1,)), ((), ())), preferred_element_type=f32)


def dot_0(a, b):
    return lax.dot_general(a, b, (((0,), (0,)), ((), ())), preferred_element_type=f32)


def span(at, size):
    return pl.ds(pl.multiple_of(at * size, size), size)


def flip(bit, by):
    return bit + by * (1 - 2 * bit)


def group(ref, n):
    return ref.at[pl.ds(n * ROWS, ROWS)]


class Spot:
    def __init__(self):
        self.row, self.pos = lax.axis_index("batch"), lax.axis_index("blk")
        self.x, self.c = self.row // 2, self.row % 2
        self.z, self.y = self.pos // 2, self.pos % 2
        self.zl, self.zh = self.z % 2, self.z // 2
        self.place = self.c * 4 + self.zl * 2 + self.y
        self.moved = self.c != self.zh

    def flipped(self, c=0, x=0, y=0, zl=0, zh=0):
        row = flip(self.x, x) * 2 + flip(self.c, c)
        pos = flip(self.zh, zh) * 4 + flip(self.zl, zl) * 2 + flip(self.y, y)
        return {"batch": row, "blk": pos}

    def member(self, place):
        return {"batch": self.x * 2 + place // 4, "blk": self.zh * 4 + place % 4}

    def partner(self):
        return {"batch": self.x * 2 + self.zh, "blk": self.c * 4 + self.pos % 4}


BULK = 2**21


class Group:
    def __init__(self, at):
        self.at, self.bytes, self.waited = at, 0, False


def bytes_of(ref):
    return math.prod(ref.shape) * jnp.dtype(ref.dtype).itemsize


class Link:
    def __init__(self, send_sem, recv_sem, own_sem, *meters):
        self.send_sem, self.recv_sem, self.own_sem, self.meters = send_sem, recv_sem, own_sem, meters
        self.count, self.own_count, self.send_count = 0, 0, 0
        self.sends, self.send_bulk = [], {}
        self.groups, self.own_groups, self.swaps, self.last = [], [], [], []
        self.bulk, self.own_bulk = self.group(), self.own_group()

    def group(self):
        self.groups.append(Group(self.count))
        self.count += 1
        return self.groups[-1]

    def send_slot(self, src):
        size = bytes_of(src)
        limit = BULK if size % 2**15 == 0 else BULK // 4
        bulk = self.send_bulk.get(limit)
        if bulk is None or bulk.bytes + size > limit:
            bulk = self.send_bulk[limit] = Group(self.send_count)
            self.sends.append(bulk)
            self.send_count += 1
        bulk.bytes += size
        return self.send_sem.at[bulk.at]

    def own_group(self):
        self.own_groups.append(Group(self.own_count))
        self.own_count += 1
        return self.own_groups[-1]

    def put(self, src, dst, device, group=None):
        if group is None:
            if self.bulk.bytes + bytes_of(src) > BULK:
                self.bulk = self.group()
            group = self.bulk
        group.bytes += bytes_of(src)
        pltpu.make_async_remote_copy(
            src_ref=src, dst_ref=dst, send_sem=self.send_slot(src), recv_sem=self.recv_sem.at[group.at],
            device_id=device, device_id_type=MESH,
        ).start()
        return group

    def keep(self, src, dst, group=None):
        if group is None:
            if self.own_bulk.bytes + bytes_of(src) > BULK:
                self.own_bulk = self.own_group()
            group = self.own_bulk
        group.bytes += bytes_of(src)
        pltpu.make_async_copy(src, dst, self.own_sem.at[group.at]).start()
        return group

    def wait(self, group, sem):
        if group.bytes:
            for meter in self.meters:
                row = bytes_of(meter) // meter.shape[0]
                tile = 8 if meter.dtype == f32 else 16
                if group.bytes % (tile * row) == 0 and group.bytes <= bytes_of(meter):
                    view = meter.at[pl.ds(0, group.bytes // row)]
                    pltpu.make_async_copy(view, view, sem.at[group.at]).wait()
                    return
            raise ValueError(group.bytes)

    def arrive(self, *groups):
        for group in groups:
            if not group.waited:
                group.waited = True
                self.wait(group, self.own_sem if any(group is own for own in self.own_groups) else self.recv_sem)

    def swap(self, spot, src, dst):
        far = pltpu.make_async_remote_copy(
            src_ref=src, dst_ref=dst, send_sem=self.send_sem.at[self.send_count], recv_sem=self.recv_sem.at[self.count],
            device_id=spot.partner(), device_id_type=MESH,
        )
        near = pltpu.make_async_copy(src, dst, self.own_sem.at[self.own_count])
        self.count += 1
        self.send_count += 1
        self.own_count += 1
        pl.when(spot.moved)(far.start)
        pl.when(jnp.logical_not(spot.moved))(near.start)
        self.swaps.append((spot, far, near))
        return far, near

    def arrive_swap(self, spot, pair):
        pl.when(spot.moved)(pair[0].wait_recv)
        pl.when(jnp.logical_not(spot.moved))(pair[1].wait)
        self.swaps = [(one, far, None if far is pair[0] else near) for one, far, near in self.swaps]

    def finish(self):
        self.arrive(*self.groups, *self.own_groups)
        for group in self.sends:
            self.wait(group, self.send_sem)
        for wait in self.last:
            wait()
        for spot, far, near in self.swaps:
            if near is not None:
                self.arrive_swap(spot, (far, near))
            pl.when(spot.moved)(far.wait_send)


def greet(spot, devices):
    barrier = pltpu.get_barrier_semaphore()
    for device in devices:
        pl.semaphore_signal(barrier, inc=1, device_id=device, device_id_type=MESH)

    @pl.when(spot.moved)
    def _():
        pl.semaphore_signal(barrier, inc=1, device_id=spot.partner(), device_id_type=MESH)

    def meet():
        @pl.when(spot.moved)
        def _():
            pl.semaphore_wait(barrier, len(devices) + 1)

        @pl.when(jnp.logical_not(spot.moved))
        def _():
            pl.semaphore_wait(barrier, len(devices))

    return meet


def standard(values):
    centered = values - jnp.mean(values, axis=-1, keepdims=True)
    inverse = lax.rsqrt(jnp.mean(centered * centered, axis=-1, keepdims=True) + eps)
    return centered * inverse, inverse


def standard_back(unit, inverse, gain, grad):
    scaled = grad * gain
    inner = jnp.mean(scaled * unit, axis=-1, keepdims=True)
    return inverse * (scaled - jnp.mean(scaled, axis=-1, keepdims=True) - unit * inner)


def column_sum(x):
    return jnp.sum(x.astype(f32), axis=0, keepdims=True)


def gelu_pair(u):
    t = 1.0 / (1.0 + 0.23164188 * jnp.abs(u))
    bell = jnp.exp(-0.5 * u * u)
    poly = t * (0.127414796 + t * (-0.142248368 + t * (0.7107068705 + t * (-0.7265760135 + t * 0.5307027145))))
    tail = poly * bell
    cdf = jnp.where(u < 0, tail, 1.0 - tail)
    return u * cdf, cdf + u * bell * 0.3989422804


def low_lanes():
    return lax.broadcasted_iota(jnp.int32, (1, 128), 1) < 64


def valid_keys(length):
    return lax.broadcasted_iota(jnp.int32, (1, LEN), 1).astype(f32) < length


def attention_rows(qkv, rows, valid):
    queries, keys, values = qkv[rows, 0:128], qkv[:, 128:256], qkv[:, 256:384]
    low_half = low_lanes()
    outs, lses = [], []
    for half in range(2):
        mine = low_half if half == 0 else jnp.logical_not(low_half)
        part = jnp.where(mine, queries, jnp.zeros_like(queries)) * jnp.asarray(0.125, bf16)
        scores = jnp.where(valid, dot_t(part, keys), -1e30)
        top = jnp.max(scores, axis=1, keepdims=True)
        expd = jnp.exp(scores - top)
        total = jnp.sum(expd, axis=1, keepdims=True)
        probs = (expd * (1.0 / total)).astype(bf16)
        outs.append(dot(probs, values))
        lses.append(top + jnp.log(total))
    return jnp.where(low_half, outs[0], outs[1]), jnp.where(low_half, lses[0], lses[1])


def attention_back_keys(qkv, grads_ref, lse_rows, delta_rows, rows, first, length):
    low_half = low_lanes()
    keys, values = qkv[rows, 128:256], qkv[rows, 256:384]
    at = lax.broadcasted_iota(jnp.int32, (256, 1), 0) + first
    valid = at.astype(f32) < length
    dqs, dk, dv = [], None, None
    for half in range(2):
        mine = low_half if half == 0 else jnp.logical_not(low_half)
        k_part = jnp.where(mine, keys, jnp.zeros_like(keys)) * jnp.asarray(0.125, bf16)
        v_part = jnp.where(mine, values, jnp.zeros_like(values))
        queries, grads = qkv[:, 0:128], grads_ref[...]
        scores = dot_t(k_part, queries)
        probs = jnp.where(valid, jnp.exp(scores - lse_rows[half : half + 1, :]), 0.0)
        dp = dot_t(v_part, grads)
        ds = (probs * (dp - delta_rows[half : half + 1, :])).astype(bf16)
        dv_part = dot(probs.astype(bf16), grads)
        dk_part = dot(ds, queries)
        dv = dv_part if half == 0 else jnp.where(low_half, dv, dv_part)
        dk = dk_part if half == 0 else jnp.where(low_half, dk, dk_part)
        dqs.append(dot_0(ds, keys))
    return jnp.where(low_half, dqs[0], dqs[1]), (dk * 0.125).astype(bf16), dv.astype(bf16)


def attention_back_start(s, o, lse, grads):
    turned = lse[...].T
    s.lse_rows[0:1, :] = turned[0:1, :]
    s.lse_rows[1:2, :] = turned[64:65, :]
    product = (grads[...].astype(f32) * o[...]).T
    s.delta_rows[0:1, :] = jnp.sum(product[0:64, :], axis=0, keepdims=True)
    s.delta_rows[1:2, :] = jnp.sum(product[64:128, :], axis=0, keepdims=True)


def attention_back_step(link, spot, step, s, qkv, grads, dqkvh, group, own):
    pair = (spot.place // 2 + step) % 4
    rows = span(pair, 256)
    dq, dk, dv = attention_back_keys(
        qkv, grads, s.lse_rows, s.delta_rows, rows, pair * 256, s.length[0:1, 0:1]
    )
    dqkvh[rows, 128:256] = dk
    dqkvh[rows, 256:384] = dv
    s.dq[...] = dq if step == PAIR_STEPS[0] else s.dq[...] + dq
    for part in (1, 2):
        send_rows(link, spot, dqkvh, s.dqkv, step, part, group, own)


def attention_back_end(link, spot, s, dqkvh, group, own):
    dqkvh[0:LEN, 0:128] = (s.dq[...] * 0.125).astype(bf16)
    for step in PAIR_STEPS:
        send_rows(link, spot, dqkvh, s.dqkv, step, 0, group, own)


def send_columns(link, spot, source, target, part, landing, groups, own):
    for step in range(7, -1, -1):
        to = (spot.place + step) % 8
        src = source.at[:, pl.ds(pl.multiple_of(part * D + to * 128, 128), 128)]
        dst = target.at[span(spot.place, ROWS), pl.ds(landing * 128, 128)]
        if step:
            link.put(src, dst, spot.member(to), groups[step])
        else:
            link.keep(src, dst, own)


def pair_rows(spot, step):
    return span((spot.place // 2 + step) % 4, 256)


def send_rows(link, spot, source, target, step, part, group, own):
    same = (spot.place + 2 * step) % 8
    for n, to in enumerate((same, same + 1 - 2 * spot.y)):
        src = source.at[span(to, ROWS), pl.ds(part * 128, 128)]
        dst = target.at[:, pl.ds(pl.multiple_of(part * D + spot.place * 128, 128), 128)]
        if step or n:
            link.put(src, dst, spot.member(to), group)
        else:
            link.keep(src, dst, own)


PAIR_STEPS = (1, 2, 3, 0)


def spec(**named):
    return named


def two(*entry):
    return [entry, entry]


MAIN_OUT = spec(
    mixed=((ROWS, D), bf16), qkv1=((LEN, 384), bf16), lse1=((LEN, 128), f32), o1=((LEN, 128), f32),
    left_attn=((4, ROWS, D), bf16), right_attn=((4 * ROWS, 512), bf16),
    left_back=((2 * GROUPS, ROWS, D), bf16), right_back=((2 * GROUPS * ROWS, PART), bf16),
    left_in=((2 * GROUPS, ROWS, D), bf16), right_in=((2 * GROUPS * ROWS, PART), bf16),
    hidden=((2, LEN, D), bf16), dqkv2=((LEN, 384), bf16),
    du1=((ROWS, FF), bf16), dza1=((ROWS, D), bf16),
    do1=((ROWS, D), bf16), dr1=((ROWS, D), f32), vec=((8, D), f32), inb=((1, FF), f32),
    length=((16, 128), f32),
)
MAIN_SCRATCH = spec(
    w_qkv=((D, 3 * D), bf16), w_attn=((D, D), bf16), w_in=((D, FF), bf16), w_back=((FF, D), bf16),
    tok=((ROWS, D), bf16), cot=((ROWS, D), bf16), length=((16, 128), f32), sent_length=((16, 128), f32),
    proj=two((ROWS, 3 * D), bf16), qkv=two((LEN, 384), bf16), lse=two((LEN, 128), f32),
    o=two((LEN, 128), bf16), full_o=two((LEN, 128), f32), att=two((ROWS, D), bf16), n=two((ROWS, D), bf16),
    act=two((ROWS, FF), bf16), slope=two((ROWS, FF), bf16),
    unit_a=two((ROWS, D), f32), unit_b=two((ROWS, D), f32),
    inv_a=two((ROWS, 128), f32), inv_b=two((ROWS, 128), f32),
    hq2=((ROWS, D), bf16), h=((ROWS, D), f32), acc=((ROWS, D), f32), mixed=((ROWS, D), bf16),
    dzb=two((ROWS, D), bf16), du=two((ROWS, FF), bf16), dza=two((ROWS, D), bf16), do=two((ROWS, D), bf16),
    doh=((LEN, 128), bf16), dqkvh=((LEN, 384), bf16), dq=((LEN, 128), f32), lse_rows=((8, LEN), f32), delta_rows=((8, LEN), f32),
    dqkv=((ROWS, 3 * D), bf16), dr1=((ROWS, D), f32), vec=((8, D), f32), inb=((1, FF), f32),
)


class Refs:
    pass


def flat(entries):
    out = []
    for entry in entries.values():
        out += entry if isinstance(entry, list) else [entry]
    return out


def bind(entries, refs):
    got, it = Refs(), iter(refs)
    for name, entry in entries.items():
        setattr(got, name, [next(it) for _ in entry] if isinstance(entry, list) else next(it))
    return got


def main_kernel(*refs):
    (len_ref, tokens, cotangent, w_qkv, w_attn, w_in, w_back,
     qv_bias, out_bias, in_bias, gain, shift) = refs[:12]
    outs = bind(MAIN_OUT, refs[12 : 12 + len(MAIN_OUT)])
    rest = refs[12 + len(MAIN_OUT) :]
    s = bind(MAIN_SCRATCH, rest[:-4])
    load_sem, send_sem, recv_sem, own_sem = rest[-4:]
    spot = Spot()
    link = Link(send_sem, recv_sem, own_sem, outs.hidden.at[0], outs.lse1)
    others = [spot.member((spot.place + step) % 8) for step in range(1, 8)]
    others += [spot.flipped(x=1), spot.flipped(c=1, x=1)]
    meet = greet(spot, others)

    loads = []
    for n, (src, dst) in enumerate(
        [(w_qkv.at[:, pl.ds(D * part, D)], s.w_qkv.at[:, pl.ds(D * part, D)]) for part in (1, 2, 0)]
        + [(w_attn, s.w_attn), (w_in, s.w_in), (w_back, s.w_back)]
    ):
        loads.append(pltpu.make_async_copy(src, dst, load_sem.at[n]))
        if n < 3:
            loads[n].start()
    loaded = set()

    def need(n):
        if n not in loaded:
            loaded.add(n)
            loads[n].wait()

    s.sent_length[...] = jnp.full((16, 128), len_ref[0], jnp.int32).astype(f32)
    meet()
    first_in = [link.swap(spot, tokens, s.tok), link.swap(spot, s.sent_length, s.length)]
    for n in range(3, 6):
        loads[n].start()
    for pair in first_in:
        link.arrive_swap(spot, pair)
    valid = valid_keys(s.length[0:1, 0:1])

    later = []

    def share(source, left, d):
        link.keep(source, left.at[d])
        link.put(source, left.at[2 + d], spot.flipped(c=1))
        link.put(source, left.at[4 + d], spot.flipped(x=1))

    def deal(source, right, d):
        link.keep(source.at[:, span(spot.c * 2 + spot.x, PART)], group(right, d))
        for n, (dc, dx) in enumerate(FLIPS[1:], 1):
            cols = span(flip(spot.c, dc) * 2 + flip(spot.x, dx), PART)
            link.put(source.at[:, cols], group(right, 2 * n + d), spot.flipped(c=dc, x=dx))

    def gather(hq, d, part):
        rows = pl.ds(part * 64, 64)
        block = outs.hidden.at[d, pl.ds(pl.multiple_of(spot.place * ROWS + part * 64, 64), 64)]
        for dz, dy in ((1, 0), (0, 1), (1, 1)):
            link.put(hq.at[rows], block, spot.flipped(zl=dz, y=dy))
        link.keep(hq.at[rows], block)

    def forward(d, hq, h):
        pair_of = [0, 3, 3, 2, 2, 1, 1, 1]
        both, pairs, own = link.group(), [link.group() for _ in range(4)], link.own_group()
        for part, number in ((1, 0), (2, 1), (0, 2)):
            need(number)

            def tile(i, carry):
                cols = span(2 * part + i, 512)
                value = dot(hq[...], s.w_qkv[:, cols])
                if part != 1:
                    value += qv_bias[part // 2 : part // 2 + 1, span(i, 512)]
                s.proj[d][:, cols] = value.astype(bf16)
                return carry

            lax.fori_loop(0, 2, tile, 0)
            to_groups = [both] * 8 if part else [pairs[pair] for pair in pair_of]
            send_columns(link, spot, s.proj[d], s.qkv[d], part, part, to_groups, own)
        link.arrive(both, own)
        if d == 0:
            later.append(link.swap(spot, cotangent, s.cot))
        to_rows, own_rows = link.group(), link.own_group()
        for step in PAIR_STEPS:
            link.arrive(pairs[step])
            rows = pair_rows(spot, step)
            s.full_o[d][rows, :], s.lse[d][rows, :] = attention_rows(s.qkv[d], rows, valid)
            s.o[d][rows, :] = s.full_o[d][rows, :].astype(bf16)
            send_rows(link, spot, s.o[d], s.att[d], step, 0, to_rows, own_rows)
        if d == 0:
            link.keep(s.qkv[0], outs.qkv1)
            link.keep(s.lse[0], outs.lse1)
            link.keep(s.full_o[0], outs.o1)
        link.arrive(to_rows, own_rows)
        gather(s.tok, 0, d)
        need(3)
        unit, inverse = standard(h[...].astype(f32) + dot(s.att[d][...], s.w_attn[...]) + out_bias[0:1])
        link.keep(s.att[d], outs.left_attn.at[d])
        link.put(s.att[d], outs.left_attn.at[2 + d], spot.flipped(c=1))
        s.unit_a[d][...] = unit
        s.inv_a[d][...] = jnp.broadcast_to(inverse, (ROWS, 128))
        first = unit * gain[0:1] + shift[0:1]
        s.n[d][...] = first.astype(bf16)
        share(s.n[d], outs.left_in, d)
        s.acc[...] = first + out_bias[1:2]
        need(4)
        need(5)

        def inner(i, carry):
            cols = span(i, 1024)
            act, slope = gelu_pair(dot(s.n[d][...], s.w_in[:, cols]) + in_bias[:, cols])
            act = act.astype(bf16)
            s.act[d][:, cols] = act
            s.slope[d][:, cols] = slope.astype(bf16)
            s.acc[...] += dot(act, s.w_back[cols, :])
            return carry

        lax.fori_loop(0, 4, inner, 0)
        deal(s.act[d], outs.right_back, d)
        unit, inverse = standard(s.acc[...])
        s.unit_b[d][...] = unit
        s.inv_b[d][...] = jnp.broadcast_to(inverse, (ROWS, 128))
        return unit * gain[1:2] + shift[1:2]

    def add_vec(at, value, fresh):
        s.vec[at : at + 1, :] = value if fresh else s.vec[at : at + 1, :] + value

    def backward(d, grad, fresh):
        unit = s.unit_b[d][...]
        add_vec(3, column_sum(grad * unit), fresh)
        add_vec(5, column_sum(grad), fresh)
        dr = standard_back(unit, s.inv_b[d][:, 0:1], gain[1:2], grad)
        s.acc[...] = dr
        low = dr.astype(bf16)
        s.dzb[d][...] = low
        share(s.dzb[d], outs.left_back, d)
        add_vec(1, column_sum(low), fresh)

        def inner(i, carry):
            cols = span(i, 1024)
            du = (dot_t(s.dzb[d][...], s.w_back[cols, :]) * s.slope[d][:, cols].astype(f32)).astype(bf16)
            s.du[d][:, cols] = du
            total = column_sum(du)
            s.inb[:, cols] = total if fresh else s.inb[:, cols] + total
            s.acc[...] += dot_t(du, s.w_in[:, cols])
            return carry

        lax.fori_loop(0, 4, inner, 0)
        if d:
            deal(s.du[d], outs.right_in, d)
        else:
            link.keep(s.du[d], outs.du1)
        grad = s.acc[...]
        unit = s.unit_a[d][...]
        add_vec(2, column_sum(grad * unit), fresh)
        add_vec(4, column_sum(grad), fresh)
        dr = standard_back(unit, s.inv_a[d][:, 0:1], gain[0:1], grad)
        s.dr1[...] = dr
        low = dr.astype(bf16)
        s.dza[d][...] = low
        if d:
            link.keep(s.dza[d].at[:, span(spot.c, 512)], group(outs.right_attn, d))
            link.put(s.dza[d].at[:, span(1 - spot.c, 512)], group(outs.right_attn, 2 + d), spot.flipped(c=1))
        else:
            link.keep(s.dza[d], outs.dza1)
        add_vec(0, column_sum(low), fresh)
        s.do[d][...] = dot_t(low, s.w_attn[...]).astype(bf16)

    out = forward(0, s.tok, s.tok)
    s.h[...] = out
    s.hq2[...] = out.astype(bf16)
    out = forward(1, s.hq2, s.h)
    s.mixed[...] = out.astype(bf16)
    link.swap(spot, s.mixed, outs.mixed)
    link.arrive_swap(spot, later[0])
    gather(s.hq2, 1, 0)
    backward(1, s.cot[...].astype(f32), True)
    to_heads, own_heads = link.group(), link.own_group()
    send_columns(link, spot, s.do[1], s.doh, 0, 0, [to_heads] * 8, own_heads)
    link.arrive(to_heads, own_heads)
    attention_back_start(s, s.full_o[1], s.lse[1], s.doh)
    to_rows, own_rows, last_rows, own_last = link.group(), link.own_group(), link.group(), link.own_group()
    for step in PAIR_STEPS:
        attention_back_step(link, spot, step, s, s.qkv[1], s.doh, s.dqkvh, to_rows, own_rows)
    attention_back_end(link, spot, s, s.dqkvh, last_rows, own_last)
    link.keep(s.dqkvh, outs.dqkv2)
    link.arrive(to_rows, own_rows)
    s.dr1[...] += dot_t(s.dqkv[:, D:], s.w_qkv[:, D:])
    link.arrive(last_rows, own_last)
    gather(s.hq2, 1, 1)
    backward(0, s.dr1[...] + dot_t(s.dqkv[:, :D], s.w_qkv[:, :D]), False)
    link.keep(s.do[0], outs.do1)
    link.keep(s.dr1, outs.dr1)
    small = link.own_group()
    link.keep(s.vec, outs.vec, small)
    link.keep(s.inb, outs.inb, small)
    link.keep(s.length, outs.length, small)
    link.finish()


def main_call(length, tokens, cotangent, params):
    w_qkv, qv_bias, w_attn, out_bias, w_in, in_bias, w_back, gain, shift = params
    dma = pltpu.SemaphoreType.DMA
    vmem, hbm = pl.BlockSpec(memory_space=pltpu.VMEM), pl.BlockSpec(memory_space=pl.ANY)
    results = pl.pallas_call(
        main_kernel,
        out_shape=[jax.ShapeDtypeStruct(*entry) for entry in MAIN_OUT.values()],
        in_specs=[pl.BlockSpec(memory_space=pltpu.SMEM), hbm, hbm] + [hbm] * 4 + [vmem] * 5,
        out_specs=[hbm] * len(MAIN_OUT),
        scratch_shapes=[pltpu.VMEM(*entry) for entry in flat(MAIN_SCRATCH)]
        + [dma((6,)), dma((16,)), dma((32,)), dma((20,))],
        compiler_params=pltpu.CompilerParams(
            collective_id=1, has_side_effects=True, vmem_limit_bytes=60 * 2**20
        ),
    )(length, tokens, cotangent, w_qkv, w_attn, w_in, w_back, qv_bias, out_bias, in_bias[None], gain, shift)
    return bind(MAIN_OUT, results)


PATHS = spec(A="yxabXC", B="xyabXC", C="abysC", F="yabZ", G="aybZ")
CHUNKS = (
    ("B", 0, 0, 512),
    ("F", 1, 0, 128),
    ("F", 1, 128, 128),
    ("F", 1, 256, 256),
    ("G", 1, 512, 256),
    ("F", 1, 768, 256),
    ("F", 2, 0, 256),
    ("F", 2, 256, 256),
    ("F", 2, 512, 256),
    ("F", 2, 768, 128),
    ("F", 2, 896, 128),
)
ORDER = (
    (100, 12), (0, -1), (100, 14), (4, -1), (5, -1), (100, 1), (1, -1), (100, 2), (100, 3), (100, 4),
    (4, 0), (100, 13), (8, -1), (5, 0), (7, -1), (6, -1), (100, 5), (1, 0), (3, -1), (100, 10),
    (5, 1), (100, 20), (100, 22), (4, 1), (1, 1), (100, 21), (0, 0), (5, 2), (2, -1), (100, 30),
    (8, 0), (4, 2), (9, -1), (1, 2), (100, 32), (100, 40), (100, 31), (7, 0), (8, 1), (10, -1),
    (5, 3), (100, 42), (4, 3), (6, 0), (1, 3), (100, 41), (100, 9), (7, 1), (8, 2), (3, 0),
    (6, 1), (8, 3), (0, 1), (7, 2), (2, 0), (3, 1), (9, 0), (6, 2), (7, 3), (100, 50),
    (0, 2), (10, 0), (2, 1), (6, 3), (100, 52), (3, 2), (9, 1), (100, 51), (10, 1), (0, 3),
    (2, 2), (3, 3), (9, 2), (0, 4), (10, 2), (2, 3), (0, 5), (9, 3), (10, 3),
)
IN_OUT = spec(back=0, fore=FF, attn=2 * FF, qkv=2 * FF + D)


def plan(path, width):
    slabs, steps = 8, []
    for stage in path:
        if stage in "yab":
            slabs //= 2
        elif stage == "x":
            width //= 2
        elif stage == "X":
            width *= 2
        steps.append((stage, slabs, width))
    return steps


def chunk_rows(c):
    return VEC if c == 0 else ROWS


SEMS = 24 + sum(len(PATHS[chunk[0]]) for chunk in CHUNKS)
PLANS = [plan(PATHS[chunk[0]], chunk[3]) for chunk in CHUNKS]
GRAD_SCRATCH = spec(
    left=[((4, ROWS, D), bf16)] + two((2 * GROUPS, ROWS, D), bf16),
    right=[((4 * ROWS, 512), bf16)] + two((2 * GROUPS * ROWS, PART), bf16),
    turned=[((D, 512), bf16)] + two((D, 256 * GROUPS), bf16),
    chunk=[((8, chunk_rows(c), CHUNKS[c][3]), bf16) for c in range(len(CHUNKS))],
    landing=[
        ((slabs, chunk_rows(c), width), bf16)
        for c, steps in enumerate(PLANS) for stage, slabs, width in steps if stage in "yabxs"
    ],
    out=((VEC, 12 * D), bf16), hidden=two((LEN, D), bf16), turned_h=((D, 2 * LEN), bf16), dqkvh=((2 * LEN, 384), bf16),
    chunk_q=[((8, VEC, 128), bf16)] * 3, landing_x=[((4, VEC, 128), bf16)] * 3, landing_b=[((2, VEC, 128), bf16)] * 3,
    qkv=((LEN, 384), bf16), lse=((LEN, 128), f32), doh=((LEN, 128), bf16),
    o=((LEN, 128), f32), dq=((LEN, 128), f32), lse_rows=((8, LEN), f32), delta_rows=((8, LEN), f32),
    dqkv=((ROWS, 3 * D), bf16), w_qkv=((D, 3 * D), bf16),
    dr1=((ROWS, D), f32), grad=((ROWS, D), bf16), vec=((8, D), f32), inb=((1, FF), f32), length=((16, 128), f32),
)


def grad_kernel(*refs):
    src = bind(MAIN_OUT, refs[: len(MAIN_OUT)])
    w_qkv, sums, grad_out = refs[len(MAIN_OUT) : len(MAIN_OUT) + 3]
    rest = refs[len(MAIN_OUT) + 3 :]
    s = bind(GRAD_SCRATCH, rest[:-3])
    spot = Spot()
    link = Link(*rest[-3:], src.hidden.at[0], src.lse1, w_qkv)
    x, y, c, zl, zh = spot.x, spot.y, spot.c, spot.zl, spot.zh
    others = [spot.member((spot.place + step) % 8) for step in range(1, 8)]
    others += [spot.flipped(x=1), spot.flipped(c=1, x=1), spot.flipped(zh=1)]
    meet = greet(spot, others)
    mine = span(c * 2 + x, PART)
    heads_in, vec_in, hidden_in, dqkv_in, close_in, left_in, right_in, weight_in = [link.own_group() for _ in range(8)]
    length_in = link.own_group()
    own_ready = [link.own_group() for _ in range(3)]
    for one, other in ((src.o1, s.o), (src.qkv1, s.qkv), (src.lse1, s.lse)):
        link.keep(one, other, heads_in)
    link.keep(src.length, s.length, length_in)
    link.keep(src.left_attn, s.left[0], own_ready[0])
    for n in (1, 3):
        link.keep(group(src.right_attn, n), group(s.right[0], n), own_ready[0])
    link.keep(src.dza1.at[:, span(c, 512)], group(s.right[0], 0), own_ready[0])
    link.keep(src.right_back, s.right[1], right_in)
    first = pl.ds(0, 6)
    link.keep(src.left_back.at[first], s.left[1].at[first], own_ready[1])
    link.keep(src.vec, s.vec, vec_in)
    link.keep(src.inb, s.inb, vec_in)
    meet()
    to_heads, own_heads, far_hidden = link.group(), link.own_group(), link.group()
    far_ready = [link.group() for _ in range(3)]
    send_columns(link, spot, src.do1, s.doh, 0, 0, [to_heads] * 8, own_heads)
    link.put(src.dza1.at[:, span(1 - c, 512)], group(s.right[0], 2), spot.flipped(c=1), far_ready[0])
    far_left = link.group()
    here, there = pl.ds(4, 2), pl.ds(6, 2)
    link.put(src.left_back.at[here], s.left[1].at[there], spot.flipped(c=1), far_ready[1])
    for n, (dc, dx) in enumerate(FLIPS[1:], 1):
        cols = span(flip(c, dc) * 2 + flip(x, dx), PART)
        link.put(src.du1.at[:, cols], group(s.right[2], 2 * n), spot.flipped(c=dc, x=dx), far_ready[2])
    waves = [0]

    def wave(upto):
        if waves[0] < 1 <= upto:
            link.put(src.left_in.at[here], s.left[2].at[there], spot.flipped(c=1), far_left)
            link.keep(src.left_in.at[first], s.left[2].at[first], left_in)
            link.keep(src.du1.at[:, mine], group(s.right[2], 0), own_ready[2])
            for n in range(GROUPS):
                link.keep(group(src.right_in, 2 * n + 1), group(s.right[2], 2 * n + 1), own_ready[2])
        if waves[0] < 2 <= upto:
            rows = span(c, 512)
            for d in range(2):
                link.put(src.hidden.at[d, rows], s.hidden[d].at[rows], spot.flipped(c=1), far_hidden)
                link.keep(src.hidden.at[d, rows], s.hidden[d].at[rows], hidden_in)
            link.keep(src.dqkv2, s.dqkvh.at[pl.ds(LEN, LEN)], dqkv_in)
            link.keep(w_qkv, s.w_qkv, weight_in)
            link.keep(src.dr1, s.dr1, close_in)
        waves[0] = max(waves[0], upto)

    bits = spec(y=y, a=zl, b=zh)
    across = spec(
        y=spot.flipped(y=1), a=spot.flipped(zl=1), b=spot.flipped(zh=1), x=spot.flipped(x=1), C=spot.flipped(c=1)
    )
    across.update(spec(X=across["x"], s=across["x"]))
    current, landing, copies = {}, {}, {}
    it = iter(s.landing)
    for n, steps in enumerate(PLANS):
        for i, step in enumerate(steps):
            if step[0] in "yabxs":
                landing[n, i] = next(it)
    waiting = [True, True, True]

    def turn(k):
        if k == 2:
            wave(1)
            link.arrive(left_in, far_left)
        else:
            link.arrive(own_ready[k], far_ready[k])
            if k == 1:
                link.arrive(right_in)
        count = s.left[k].shape[0]
        for g in range(count):
            s.turned[k][:, pl.ds(ROWS * g, ROWS)] = s.left[k][g].T

    def compute(n):
        _, k, first, wide = CHUNKS[n]
        if k == 2 and waiting[2]:
            waiting[2] = False
            link.arrive(own_ready[2], far_ready[2])
        path = [stage for stage in PATHS[CHUNKS[n][0]] if stage in "yab"]
        path += [stage for stage in "yab" if stage not in path]

        def piece(i, carry):
            product = dot(s.turned[k][span(i, 256), :], s.right[k][:, pl.ds(first, wide)]).astype(bf16)
            for low in range(2):
                bit = spec(y=low, a=i % 2, b=i // 2)
                at_slab = (bit[path[0]] * 2 + bit[path[1]]) * 2 + bit[path[2]]
                s.chunk[n][at_slab, 0:ROWS] = product[ROWS * low : ROWS * (low + 1)]
            return carry

        lax.fori_loop(0, 4, piece, 0)
        if n == 0:
            link.arrive(vec_in)
            for shard in range(8):
                bit = spec(y=shard % 2, a=shard // 2 % 2, b=shard // 4)
                at_slab = (bit[path[0]] * 2 + bit[path[1]]) * 2 + bit[path[2]]
                vec = s.vec[:, pl.ds(shard * 128, 128)]
                top = jnp.concatenate([vec, jnp.zeros((8, 384), f32)], 1)
                low = jnp.broadcast_to(s.inb[:, pl.ds(shard * 512, 512)], (8, 512))
                s.chunk[n][at_slab, ROWS:VEC] = jnp.concatenate([top, low], 0).astype(bf16)
        current[n] = s.chunk[n]

    def base_of(n):
        _, k, first, _ = CHUNKS[n]
        if k == 0:
            return IN_OUT["attn"] + c * 512 + first, 0
        return IN_OUT["back" if k == 1 else "fore"] + c * 2 * PART + first, PART

    def columns(n, quarter, offset, width):
        start, stride = base_of(n)
        return pl.ds(pl.multiple_of(start + quarter * stride + offset, 128), width)

    def send(n, i):
        stage, slabs, width = PLANS[n][i]
        rows = pl.ds(0, chunk_rows(n))
        now, todo = current[n], []
        if stage in "yab":
            todo.append((now.at[pl.ds((1 - bits[stage]) * slabs, slabs)], landing[n, i]))
        elif stage == "x":
            todo.append((now.at[:, :, pl.ds(pl.multiple_of((1 - x) * width, 128), width)], landing[n, i]))
        elif stage == "s":
            todo.append((now, landing[n, i]))
        elif stage == "Z":
            where = s.out.at[rows, columns(n, x, 0, width)]
            copies[n, i] = link.group()
            for dc, dx in ((1, 1), (0, 1), (1, 0)):
                link.put(where, where, spot.flipped(c=dc, x=dx), copies[n, i])
            return
        else:
            offset = x * (width // 2) if stage == "X" else 0
            width = width // 2 if stage == "X" else width
            where = s.out.at[rows, columns(n, 0, offset, width)]
            todo.append((where, where))
        copies[n, i] = link.group()
        for here, there in todo:
            link.put(here, there, across[stage], copies[n, i])

    def store(rows, start, width):
        here = (pl.ds(0, rows), pl.ds(start, width))
        link.keep(s.out.at[here], sums.at[here])

    def flush(n):
        _, k, first, wide = CHUNKS[n]
        if k == 0:
            store(VEC, IN_OUT["attn"], D)
        else:
            for quarter in range(4):
                store(ROWS, IN_OUT["back" if k == 1 else "fore"] + quarter * PART + first, wide)

    def advance(n, i):
        stage, slabs, width = PLANS[n][i]
        link.arrive(copies[n, i])
        if stage in "ZC":
            flush(n)
        if stage not in "yabxs":
            return
        got, old = landing[n, i], current[n]

        def add(m, carry):
            if stage in "yab":
                kept = old[bits[stage] * slabs + m]
            elif stage == "x":
                kept = old[m, :, pl.ds(pl.multiple_of(x * width, 128), width)]
            else:
                kept = old[m]
            got[m] = (got[m].astype(f32) + kept.astype(f32)).astype(bf16)
            return carry

        lax.fori_loop(0, slabs, add, 0)
        current[n] = got
        follow = PLANS[n][i + 1][0]
        if follow in "ZXC":
            offset = x * width if follow == "X" else 0
            s.out[0 : chunk_rows(n), columns(n, x if follow == "Z" else 0, offset, width)] = got[0]

    state = Refs()
    rows_kv, own_kv, rows_q, own_q = link.group(), link.own_group(), link.group(), link.own_group()

    def fold_q(got, old, bit):
        slabs = got.shape[0]

        def add(m, carry):
            got[m] = (got[m].astype(f32) + old[bit * slabs + m].astype(f32)).astype(bf16)
            return carry

        lax.fori_loop(0, slabs, add, 0)

    keeps = x == zl
    came_q, passed = [None] * 3, [None] * 3

    def wait_q(group, sem):
        def some(count):
            def wait():
                rows = count * VEC * 128 * 2 // 512
                view = src.lse1.at[pl.ds(0, rows)]
                pltpu.make_async_copy(view, view, sem.at[group.at]).wait()

            return wait

        pl.when(keeps)(some(3))
        pl.when(jnp.logical_not(keeps))(some(4))

    def out_q(part, first, width):
        return s.out.at[:, pl.ds(pl.multiple_of(IN_OUT["qkv"] + part * D + first * 128, 128), width)]

    def form_q(part):
        cols = pl.ds(part * 128, 128)

        def piece(i, carry):
            product = dot(s.turned_h[span(i, 256), :], s.dqkvh[:, cols]).astype(bf16)
            for low in range(2):
                at_slab = (i % 2) * 4 + (i // 2) * 2 + low
                s.chunk_q[part][at_slab, 0:ROWS] = product[ROWS * low : ROWS * (low + 1)]
            return carry

        lax.fori_loop(0, 4, piece, 0)
        extra = jnp.broadcast_to(column_sum(s.dqkvh[:, cols]), (16, 128)).astype(bf16)
        for at_slab in range(8):
            s.chunk_q[part][at_slab, ROWS:VEC] = extra
        came_q[part] = link.put(
            s.chunk_q[part].at[pl.ds((1 - x) * 4, 4)], s.landing_x[part], across["x"], link.group()
        )

    def second_q(part):
        link.arrive(came_q[part])
        fold_q(s.landing_x[part], s.chunk_q[part], x)
        came_q[part] = link.put(
            s.landing_x[part].at[pl.ds((1 - zh) * 2, 2)], s.landing_b[part], across["b"], link.group()
        )

    def deal_q(part):
        link.arrive(came_q[part])
        fold_q(s.landing_b[part], s.landing_x[part], zh)
        group, sent = Group(link.count), Group(link.send_count)
        link.count += 1
        link.send_count += 1
        where = out_q(part, spot.place, 128)

        def copy_to(fx, fy):
            y_to = flip(y, fy)
            return pltpu.make_async_remote_copy(
                src_ref=s.landing_b[part].at[y_to], dst_ref=where,
                send_sem=link.send_sem.at[sent.at], recv_sem=link.recv_sem.at[group.at],
                device_id={"batch": flip(x, fx) * 2 + c, "blk": zh * 4 + x * 2 + y_to}, device_id_type=MESH,
            )

        for fx, fy in ((1, 1), (1, 0), (0, 1)):
            copy_to(fx, fy).start()
        pl.when(jnp.logical_not(keeps))(copy_to(0, 0).start)

        @pl.when(keeps)
        def _():
            where[...] = s.landing_b[part][y]

        link.last.append(lambda: wait_q(sent, link.send_sem))
        came_q[part] = group

    def pass_q(part):
        wait_q(came_q[part], link.recv_sem)
        where = out_q(part, c * 4, 512)
        passed[part] = link.put(where, where, across["C"], link.group())

    def task(k):
        if k == 1:
            link.arrive(to_heads, own_heads, heads_in, length_in)
            attention_back_start(s, s.o, s.lse, s.doh)
        if k <= 4:
            attention_back_step(link, spot, PAIR_STEPS[k - 1], s, s.qkv, s.doh, s.dqkvh, rows_kv, own_kv)
        elif k == 5:
            attention_back_end(link, spot, s, s.dqkvh, rows_q, own_q)
        elif k >= 20:
            (form_q, second_q, deal_q, pass_q)[k // 10 - 2]((1, 2, 0)[k % 10])
        elif k == 9:
            link.arrive(rows_kv, own_kv, rows_q, own_q, close_in, weight_in)
            s.grad[...] = (s.dr1[...] + dot_t(s.dqkv[...], s.w_qkv[...])).astype(bf16)
            link.swap(spot, s.grad, grad_out)
        elif k == 10:
            wave(2)
            link.arrive(hidden_in, far_hidden, dqkv_in)
            for d in range(2):
                for g in range(8):
                    rows = pl.ds(g * ROWS, ROWS)
                    s.turned_h[:, pl.ds(d * LEN + g * ROWS, ROWS)] = s.hidden[d][rows, :].T
        elif k in (12, 13, 14):
            turn((0, 2, 1)[k - 12])

    for n, i in ORDER:
        if n == 100:
            task(i)
            continue
        if i < 0:
            compute(n)
            wave(waves[0] + 1)
        else:
            advance(n, i)
        if i + 1 < len(PLANS[n]):
            send(n, i + 1)
    for part in (1, 2, 0):
        link.arrive(passed[part])
        store(VEC, IN_OUT["qkv"] + part * D, D)
    link.finish()


def grad_call(main, w_qkv):
    dma = pltpu.SemaphoreType.DMA
    hbm = pl.BlockSpec(memory_space=pl.ANY)
    return pl.pallas_call(
        grad_kernel,
        out_shape=[jax.ShapeDtypeStruct((VEC, 12 * D), bf16), jax.ShapeDtypeStruct((ROWS, D), bf16)],
        in_specs=[hbm] * (len(MAIN_OUT) + 1),
        out_specs=[hbm, hbm],
        scratch_shapes=[pltpu.VMEM(*entry) for entry in flat(GRAD_SCRATCH)]
        + [dma((24,)), dma((SEMS,)), dma((24,))],
        compiler_params=pltpu.CompilerParams(
            collective_id=2, has_side_effects=True, vmem_limit_bytes=60 * 2**20
        ),
    )(*[getattr(main, name) for name in MAIN_OUT], w_qkv)


def finish_kernel(sums, mixed_in, grad_in, mixed, grad, qkv, attn, fore, back, qv, bias, fore_bias, gain, shift,
                  buf, thin_buf, qkv_buf, attn_buf, fore_buf, back_buf, in_sem, out_sem):
    at = IN_OUT
    pieces = [(at["qkv"] + part * D, D, VEC) for part in range(3)] + [(at["attn"], D, VEC)]
    for n in range(4):
        pieces += [(at["back"] + n * D, D, ROWS), (at["fore"] + n * D, D, ROWS)]
    loads, stores = [], []

    def store(src, dst):
        copy = pltpu.make_async_copy(src, dst, out_sem.at[len(stores)])
        copy.start()
        stores.append(copy)

    for n, (start, width, rows) in enumerate(pieces):
        here = (pl.ds(0, rows), pl.ds(start, width))
        loads.append(pltpu.make_async_copy(sums.at[here], buf.at[here], in_sem.at[n]))
        loads[n].start()
    for n, source in enumerate((mixed_in, grad_in)):
        loads.append(pltpu.make_async_copy(source, thin_buf.at[n], in_sem.at[12 + n]))
        loads[-1].start()
    mine = lax.axis_index("blk")
    for part in range(3):
        loads[part].wait()
        here = pl.ds(part * D, D)
        qkv_buf[:, here] = buf[0:ROWS, pl.ds(at["qkv"] + part * D, D)].astype(f32)
        store(qkv_buf.at[:, here], qkv.at[:, here])
        total = jnp.zeros((16, 128), f32)
        for place in range(8):
            block = buf[ROWS:VEC, pl.ds(at["qkv"] + part * D + place * 128, 128)].astype(f32)
            total = total + jnp.where(mine == place, block, 0.0)
        if part != 1:
            qv[part // 2 : part // 2 + 1, :] = total[0:1, :]
    loads[3].wait()
    attn_buf[...] = buf[0:ROWS, pl.ds(at["attn"], D)].astype(f32)
    store(attn_buf, attn)
    for n in range(4):
        rows = pl.ds(n * D, D)
        loads[4 + 2 * n].wait()
        back_buf[rows, :] = buf[0:ROWS, pl.ds(at["back"] + n * D, D)].astype(f32).T
        store(back_buf.at[rows], back.at[rows])
        loads[5 + 2 * n].wait()
        fore_buf[:, rows] = buf[0:ROWS, pl.ds(at["fore"] + n * D, D)].astype(f32)
        store(fore_buf.at[:, rows], fore.at[:, rows])
    for n, target in enumerate((mixed, grad)):
        loads[12 + n].wait()
        store(thin_buf.at[n], target)
    start = at["attn"]
    small = buf[ROWS:VEC, pl.ds(start, 512)].astype(f32) + buf[ROWS:VEC, pl.ds(start + 512, 512)].astype(f32)
    bias[...] = small[0:2, 0:128]
    gain[...] = small[2:4, 0:128]
    shift[...] = small[4:6, 0:128]
    fore_bias[...] = small[8:9, :]
    for copy in stores:
        copy.wait()


def finish_call(sums, mixed, grad):
    large = [(ROWS, 3 * D), (ROWS, D), (ROWS, FF), (FF, 128)]
    small = [(2, 128), (2, 128), (1, 512), (2, 128), (2, 128)]
    hbm, vmem = pl.BlockSpec(memory_space=pl.ANY), pl.BlockSpec(memory_space=pltpu.VMEM)
    dma = pltpu.SemaphoreType.DMA
    return pl.pallas_call(
        finish_kernel,
        out_shape=[jax.ShapeDtypeStruct((ROWS, D), bf16)] * 2
        + [jax.ShapeDtypeStruct(shape, f32) for shape in large + small],
        in_specs=[hbm] * 3,
        out_specs=[hbm] * 6 + [vmem] * 5,
        scratch_shapes=[pltpu.VMEM((VEC, 12 * D), bf16), pltpu.VMEM((2, ROWS, D), bf16)] + [pltpu.VMEM(shape, f32) for shape in large]
        + [dma((14,)), dma((14,))],
        compiler_params=pltpu.CompilerParams(vmem_limit_bytes=63 * 2**20),
    )(sums, mixed, grad)


def fast_body(tokens, lengths, *rest):
    params, cotangent = rest[:-1], rest[-1]
    main = main_call(lengths, tokens[0], cotangent[0], params)
    sums, grad = grad_call(main, params[0])
    mixed, grad, qkv, attn, fore, back, qv, bias, fore_bias, gain, shift = finish_call(sums, main.mixed, grad)
    return (
        mixed[None], grad[None], qkv, qv, attn, bias, fore, fore_bias.reshape(512), back, gain, shift,
    )


def solution(mesh):
    placed = (
        P("batch", "blk", None),
        P("batch"),
        P(),
        P(),
        P(),
        P(),
        P(),
        P(),
        P(),
        P(),
        P(),
        P("batch", "blk", None),
    )
    fast = dict(mesh.shape) == {"batch": 4, "blk": 8}
    return jax.shard_map(
        fast_body if fast else body,
        mesh=mesh,
        in_specs=placed,
        out_specs=(
            P("batch", "blk", None),
            P("batch", "blk", None),
            P("blk", None),
            P(None, "blk"),
            P("blk", None),
            P(None, "blk"),
            P("blk", None),
            P("blk"),
            P(None, "blk"),
            P(None, "blk"),
            P(None, "blk"),
        ),
        check_vma=False,
    )
```
